32 devices in a mesh: seq: 4 (over x, core), fsdp: 8 (over z, y).
Axes of the slice: x: 2, y: 2, z: 4, core: 2. Of those that a mesh axis runs over, the one named last changes fastest.
Arguments:
- tokens: bfloat16 [65536, 512], P(('fsdp', 'seq')), may hold values from -6 to 6
- doc_ids: int32 [8, 8192], P('fsdp', 'seq'), may hold values from 0 to 31, never falling along the last dimension, each value on 1 to 4096 neighbouring positions
- w_query: float32 [512, 512], P('fsdp'), may hold values from -0.375 to 0.375
- w_key: float32 [512, 512], P('fsdp'), may hold values from -0.375 to 0.375
- w_value: float32 [512, 512], P('fsdp'), may hold values from -0.25 to 0.25
- w_slots: float32 [512, 512], P('fsdp'), may hold values from -0.5 to 0.5
- w_output: float32 [512, 512], P('fsdp'), may hold values from -0.75 to 0.75
- w_hidden: float32 [512, 2048], P('fsdp'), may hold values from -0.25 to 0.25
- w_return: float32 [2048, 512], P('fsdp'), may hold values from -0.1875 to 0.1875
- gain_first: float32 [512], P('fsdp'), may hold values from 0.1 to 1.9
- shift_first: float32 [512], P('fsdp'), may hold values from -3 to 3
- gain_second: float32 [512], P('fsdp'), may hold values from 0.1 to 1.9
- shift_second: float32 [512], P('fsdp'), may hold values from -3 to 3
- bias_hidden: float32 [2048], P('fsdp'), may hold values from -3 to 3
- bias_return: float32 [512], P('fsdp'), may hold values from -3 to 3
- cotangent: bfloat16 [65536, 512], P(('fsdp', 'seq')), may hold values from -6 to 6
Outputs:
- layer_out: bfloat16 [65536, 512], P(('fsdp', 'seq'))
- grad_input: float32 [65536, 512], P(('fsdp', 'seq'))
- grad_w_query: float32 [512, 512], P('fsdp')
- grad_w_key: float32 [512, 512], P('fsdp')
- grad_w_value: float32 [512, 512], P('fsdp')
- grad_w_slots: float32 [512, 512], P('fsdp')
- grad_w_output: float32 [512, 512], P('fsdp')
- grad_w_hidden: float32 [512, 2048], P('fsdp')
- grad_w_return: float32 [2048, 512], P('fsdp')
- grad_gain_first: float32 [512], P('fsdp')
- grad_shift_first: float32 [512], P('fsdp')
- grad_gain_second: float32 [512], P('fsdp')
- grad_shift_second: float32 [512], P('fsdp')
- grad_bias_hidden: float32 [2048], P('fsdp')
- grad_bias_return: float32 [512], P('fsdp')
The draws below stay inside these ranges and needn't reach their ends.
Inputs may be any that keep to these rules, and one draw needn't show every extreme that they name: `doc_ids`: in each packed sequence the document numbers never fall, each document has at least one token, and at most 4096 tokens, with one document of exactly 4096 tokens.
All inputs are finite; a program needn't handle non-finite values.
Results may differ from the reference program's by a relative error of at most 0.01.
The reference program's roundings to bfloat16 on the way count: a program that leaves them out, or rounds other values in their place, can miss the bound.
Values may be sent and summed in bfloat16 or wider, within the bound.
A program may use at most 192 MiB of HBM per device.

```python
import math
import jax
import jax.numpy as jnp
import numpy as np
from jax import lax

D = 512
H = 8
M = 64
FF = 2048
BLOCK = 512
LEN = 8192
SEQS = 8
TOKENS = 65536
DOCS = 32
MOST = 4096


def block_scale(own_key, dims, cuts, smallest, top_value):
    level, own = 1.0, jax.random.fold_in(own_key, 6)
    for axis_at, shards_of in cuts:
        heights = jnp.exp(jax.random.uniform(jax.random.fold_in(own, axis_at), (shards_of,), jnp.float32, smallest / len(cuts), top_value / len(cuts)))
        level = level * jnp.repeat(heights, dims[axis_at] // shards_of).reshape([-1 if axis == axis_at else 1 for axis in range(len(dims))])
    return level


def length_profile(count, total, limit, lean):
    weights = [(1 << 20) // math.isqrt(rank ** lean) + 1 for rank in range(2, count + 1)]
    rest, given = total - limit - (count - 1), [1] * (count - 1)
    while rest > 0:
        movable = [i for i in range(count - 1) if given[i] < limit]
        mass, left = sum([weights[i] for i in movable]), rest
        for i in movable:
            more = min(limit - given[i], max(1, left * weights[i] // mass), rest)
            given[i] = given[i] + more
            rest = rest - more
    return np.array([limit] + given)


def ragged_sizes(rng, amount, total, reach, lean):
    if amount == 2:
        one = jax.random.randint(rng, (), max(1, total - reach), min(reach, total - 1) + 1)
        return jnp.stack([one, total - one])
    sizes = jnp.asarray(length_profile(amount, total, reach, lean), jnp.int32)
    pairs = (amount - 1) // 2
    source_of, receiver = sizes[1:1 + 2 * pairs:2], sizes[2:2 + 2 * pairs:2]
    room = jnp.minimum(source_of - 1, reach - receiver)
    passed = jax.random.randint(jax.random.fold_in(rng, 1), (pairs,), 0, 1 << 20) % (room + 1)
    sizes = sizes.at[1:1 + 2 * pairs:2].set(source_of - passed).at[2:2 + 2 * pairs:2].set(receiver + passed)
    return sizes[jax.random.permutation(jax.random.fold_in(rng, 2), amount)]


def bell_draw(own_key, extent, scale, limit, shards=(), kind=jnp.bfloat16):
    result = scale * jax.random.normal(own_key, extent, jnp.float32)
    if shards:
        result = result * block_scale(own_key, extent, shards, -0.22, 0.18)
    return jnp.clip(result, -limit, limit).astype(kind)


def setup_inputs(seed: int = 0) -> dict:
    key_list = jax.random.split(jax.random.key(seed), 17)
    tokens = bell_draw(key_list[0], (TOKENS, D), 1.0, 6.0, ((0, 32),))
    doc_ids = jax.vmap(lambda own: jnp.searchsorted(jnp.cumsum(ragged_sizes(own, DOCS, LEN, MOST, 2)), jnp.arange(LEN), side="right"))(jax.random.split(key_list[1], SEQS)).reshape((SEQS, LEN)).astype(jnp.int32)
    w_query = bell_draw(key_list[2], (D, D), (D // 2) ** -0.5, 0.375, ((0, 8),), jnp.float32)
    w_key = bell_draw(key_list[3], (D, D), (D // 2) ** -0.5, 0.375, ((0, 8),), jnp.float32)
    w_value = bell_draw(key_list[4], (D, D), D ** -0.5, 0.25, ((0, 8),), jnp.float32)
    w_slots = bell_draw(key_list[5], (D, H * M), (D // 4) ** -0.5, 0.5, ((0, 8),), jnp.float32)
    w_output = bell_draw(key_list[6], (D, D), (D // 8) ** -0.5, 0.75, ((0, 8),), jnp.float32)
    w_hidden = bell_draw(key_list[7], (D, FF), D ** -0.5, 0.25, ((0, 8),), jnp.float32)
    w_return = bell_draw(key_list[8], (FF, D), (FF // 2) ** -0.5, 0.1875, ((0, 8),), jnp.float32)
    gain_first = jnp.clip(1.0 + 0.18 * jax.random.normal(key_list[9], (D,), jnp.float32), 0.1, 1.9)
    shift_first = bell_draw(key_list[10], (D,), 0.5, 3.0, ((0, 8),), jnp.float32)
    gain_second = jnp.clip(1.0 + 0.18 * jax.random.normal(key_list[11], (D,), jnp.float32), 0.1, 1.9)
    shift_second = bell_draw(key_list[12], (D,), 0.5, 3.0, ((0, 8),), jnp.float32)
    bias_hidden = bell_draw(key_list[13], (FF,), 0.5, 3.0, ((0, 8),), jnp.float32)
    bias_return = bell_draw(key_list[14], (D,), 0.5, 3.0, ((0, 8),), jnp.float32)
    cotangent = bell_draw(key_list[15], (TOKENS, D), 1.0, 6.0, ((0, 32),))
    return dict(tokens=tokens, doc_ids=doc_ids, w_query=w_query, w_key=w_key, w_value=w_value, w_slots=w_slots, w_output=w_output, w_hidden=w_hidden, w_return=w_return, gain_first=gain_first, shift_first=shift_first, gain_second=gain_second, shift_second=shift_second, bias_hidden=bias_hidden, bias_return=bias_return, cotangent=cotangent)


EPS = 1e-05
HIGH = lax.Precision.HIGHEST

@jax.custom_vjp
def low(v):
    return lax.optimization_barrier(v.astype(jnp.bfloat16)).astype(jnp.float32)

@jax.custom_vjp
def low_back(v):
    return v

def low_keep(v):
    return (low(v), None)

def low_pass(kept, grad):
    return (grad,)

def back_keep(v):
    return (v, None)

def back_low(kept, grad):
    return (low(grad),)
low.defvjp(low_keep, low_pass)
low_back.defvjp(back_keep, back_low)

def normed(values, gain, shift):
    centre = lax.optimization_barrier(jnp.mean(values, axis=-1, keepdims=True))
    centred = values - centre
    spread = lax.optimization_barrier(jnp.mean(centred * centred, axis=-1, keepdims=True))
    return centred * lax.rsqrt(spread + EPS) * gain + shift

def smooth_gate(values):
    return jax.nn.gelu(values, approximate=True)

def mix_head(queries, key_rows, value_rows, slot_logits, doc_row):
    length, width = queries.shape
    slot_count = slot_logits.shape[1]
    block_rows = min(BLOCK, length)
    block_count = length // block_rows
    score_scale = width ** (-0.5)
    positions = jnp.arange(block_rows)
    causal = positions[:, None] >= positions[None, :]

    def advance(state, pieces):
        key_state, value_state, norm_state, last_doc = state
        q_rows, k_rows, v_rows, p_rows, d_rows = pieces
        written = jnp.exp(p_rows)
        visible = (causal & (d_rows[:, None] == d_rows[None, :])).astype(jnp.float32)
        carried = (d_rows == last_doc).astype(jnp.float32)[:, None]
        affinity = jnp.dot(q_rows, k_rows.T, precision=HIGH) * visible
        numer = jnp.dot(affinity, written, precision=HIGH) + carried * jnp.dot(q_rows, key_state.T, precision=HIGH)
        total = jnp.dot(visible, written, precision=HIGH) + carried * norm_state[None, :]
        probs = jax.nn.softmax(numer / total * score_scale, axis=-1)
        reading = probs / total
        mixed = jnp.dot(jnp.dot(reading, written.T, precision=HIGH) * visible, v_rows, precision=HIGH)
        mixed = mixed + carried * jnp.dot(reading, value_state, precision=HIGH)
        newest = d_rows[-1]
        tail = (d_rows == newest).astype(jnp.float32)[:, None] * written
        kept = (last_doc == newest).astype(jnp.float32)
        state = (kept * key_state + jnp.dot(tail.T, k_rows, precision=HIGH), kept * value_state + jnp.dot(tail.T, v_rows, precision=HIGH), kept * norm_state + lax.optimization_barrier(jnp.sum(tail, axis=0)), newest)
        return (state, mixed)
    start = (jnp.zeros((slot_count, width), jnp.float32), jnp.zeros((slot_count, width), jnp.float32), jnp.zeros((slot_count,), jnp.float32), jnp.array(-1, jnp.int32))
    pieces = (queries.reshape(block_count, block_rows, width), key_rows.reshape(block_count, block_rows, width), value_rows.reshape(block_count, block_rows, width), slot_logits.reshape(block_count, block_rows, slot_count), doc_row.astype(jnp.int32).reshape(block_count, block_rows))
    final, outputs = lax.scan(jax.checkpoint(advance), start, pieces)
    return outputs.reshape(length, width)

def layer(resid, doc_row, params):
    q_weight, k_weight, v_weight, s_weight, o_weight, h_weight, r_weight, gain_one, shift_one, gain_two, shift_two, b_hidden, b_return = [low(piece) for piece in params]
    length = resid.shape[0]
    width = D // H
    hidden_one = low(normed(resid, gain_one, shift_one))

    def project(weights):
        return low(low_back(jnp.dot(hidden_one, weights, precision=HIGH)))
    queries = project(q_weight).reshape(length, H, width).transpose(1, 0, 2)
    key_rows = project(k_weight).reshape(length, H, width).transpose(1, 0, 2)
    value_rows = project(v_weight).reshape(length, H, width).transpose(1, 0, 2)
    slot_rows = project(s_weight).reshape(length, H, M).transpose(1, 0, 2)
    mixed = jax.vmap(mix_head, in_axes=(0, 0, 0, 0, None))(queries, key_rows, value_rows, slot_rows, doc_row)
    attended = low(low_back(mixed.transpose(1, 0, 2).reshape(length, D)))
    middle = resid + low_back(jnp.dot(attended, o_weight, precision=HIGH))
    hidden_two = low(normed(middle, gain_two, shift_two))
    inner = low_back(jnp.dot(hidden_two, h_weight, precision=HIGH) + b_hidden)
    active = low(smooth_gate(inner))
    return middle + jnp.dot(active, r_weight, precision=HIGH) + b_return

def reference(tokens, doc_ids, w_query, w_key, w_value, w_slots, w_output, w_hidden, w_return, gain_first, shift_first, gain_second, shift_second, bias_hidden, bias_return, cotangent):
    params = (w_query, w_key, w_value, w_slots, w_output, w_hidden, w_return, gain_first, shift_first, gain_second, shift_second, bias_hidden, bias_return)
    inputs = tokens.astype(jnp.float32).reshape(SEQS, LEN, D)
    upstream = cotangent.astype(jnp.float32).reshape(SEQS, LEN, D)
    totals = tuple((jnp.zeros_like(piece) for piece in params))

    def one_sequence(running, item):
        resid, doc_row, grad_out = item

        def forward(values, weights):
            return layer(values, doc_row, weights)
        output, pull = jax.vjp(forward, resid, params)
        grad_resid, grad_params = pull(grad_out)
        running = tuple((total + extra for total, extra in zip(running, grad_params)))
        return (running, (output.astype(jnp.bfloat16), grad_resid))
    totals, (outputs, grad_inputs) = lax.scan(one_sequence, totals, (inputs, doc_ids, upstream))
    return (outputs.reshape(TOKENS, D), grad_inputs.reshape(TOKENS, D), totals[0], totals[1], totals[2], totals[3], totals[4], totals[5], totals[6], totals[7], totals[8], totals[9], totals[10], totals[11], totals[12])
```

```python
import functools

import jax
import jax.numpy as jnp
from jax import lax
from jax.experimental import pallas as pl
from jax.experimental.pallas import tpu as pltpu
from jax.sharding import PartitionSpec as P

D = 512
H = 8
M = 64
FF = 2048
C = 256
GROUP = 256
EPS = 1e-05
SCALE = 0.125
F32 = jnp.float32
BF16 = jnp.bfloat16
LIMIT = 60 * 1024 * 1024


def dot(a, b):
    return lax.dot_general(a, b, (((1,), (0,)), ((), ())), preferred_element_type=F32)


def dot_nt(a, b):
    return lax.dot_general(a, b, (((1,), (1,)), ((), ())), preferred_element_type=F32)


def dot_tn(a, b):
    return lax.dot_general(a, b, (((0,), (0,)), ((), ())), preferred_element_type=F32)


def lane_heads(rows, lanes):
    return lax.broadcasted_iota(jnp.int32, (rows, lanes), 1) // M


def stacked(values):
    heads = lane_heads(C, GROUP)
    zero = jnp.zeros_like(values)
    return jnp.concatenate([jnp.where(heads == h, values, zero) for h in range(4)], axis=0)


def select(values):
    heads = lane_heads(C, GROUP)
    out = values[3 * C :]
    for h in (2, 1, 0):
        out = jnp.where(heads == h, values[h * C : (h + 1) * C], out)
    return out


def masked(values, mask):
    return jnp.concatenate(
        [values[h * C : (h + 1) * C].astype(BF16) * mask for h in range(4)], axis=0
    )


def expand(compact):
    rows = lax.broadcasted_iota(jnp.int32, (GROUP, GROUP), 0) // M
    full = jnp.concatenate([compact] * 4, axis=0)
    return jnp.where(rows == lane_heads(GROUP, GROUP), full, jnp.zeros_like(full))


def compacted(full):
    heads = lane_heads(M, GROUP)
    out = full[3 * M :]
    for h in (2, 1, 0):
        out = jnp.where(heads == h, full[h * M : (h + 1) * M], out)
    return out


def split(values):
    high = values.astype(BF16)
    return high, (values - high.astype(F32)).astype(BF16)


def ones_block():
    rows = lax.broadcasted_iota(jnp.int32, (GROUP, GROUP), 0) // M
    return (rows == lane_heads(GROUP, GROUP)).astype(BF16)


def head_sums(values):
    high, low = split(values)
    ones = ones_block()
    return dot(high, ones) + dot(low, ones)


def head_max(values):
    left = lane_heads(C, 128) == 0
    out = []
    for p in range(2):
        pair = values[:, p * 128 : (p + 1) * 128]
        one = jnp.max(jnp.where(left, pair, -jnp.inf), axis=1, keepdims=True)
        two = jnp.max(jnp.where(left, -jnp.inf, pair), axis=1, keepdims=True)
        out.append(jnp.where(left, one, two))
    return jnp.concatenate(out, axis=1)


def wide(values, times):
    return jnp.concatenate([values] * times, axis=1)


def visible(doc_col, doc_row):
    same = wide(doc_col, 2) == doc_row
    here = lax.broadcasted_iota(jnp.int32, (C, C), 0)
    there = lax.broadcasted_iota(jnp.int32, (C, C), 1)
    return jnp.where(same & (here >= there), 1.0, 0.0).astype(BF16)


def visible_back(doc_col, doc_row):
    same = wide(doc_col, 2) == doc_row
    here = lax.broadcasted_iota(jnp.int32, (C, C), 0)
    there = lax.broadcasted_iota(jnp.int32, (C, C), 1)
    return jnp.where(same & (there >= here), 1.0, 0.0).astype(BF16)


def flag(doc_col, doc):
    return jnp.where(doc_col == doc[:, :128], 1.0, 0.0)


def norm_parts(values):
    centre = jnp.mean(values, axis=-1, keepdims=True)
    centred = values - centre
    spread = jnp.mean(centred * centred, axis=-1, keepdims=True)
    scale = lax.rsqrt(spread + EPS)
    return centred * scale, scale


def norm_back(unit, scale, gain, grad):
    inner = grad * gain
    return scale * (
        inner
        - jnp.mean(inner, axis=-1, keepdims=True)
        - unit * jnp.mean(inner * unit, axis=-1, keepdims=True)
    )


def groups(values):
    return values[:, :GROUP], values[:, GROUP:]


def state_terms(slots, left, right):
    one, two = [], []
    for g in range(2):
        lanes = slice(g * GROUP, (g + 1) * GROUP)
        both = dot_tn(slots[:, lanes], jnp.concatenate([left[:, lanes], right[:, lanes]], axis=1))
        one.append(compacted(both[:, :GROUP]))
        two.append(compacted(both[:, GROUP:]))
    return jnp.concatenate(one, axis=1), jnp.concatenate(two, axis=1)


def project_kernel(x_ref, col_ref, edge_ref, small_ref, w_ref, qkvf_ref, tail_ref):
    step = pl.program_id(0)
    unit, _ = norm_parts(x_ref[...].astype(F32))
    hidden = (unit * small_ref[0:1] + small_ref[1:2]).astype(BF16)
    rows = dot(hidden, w_ref[...]).astype(BF16)
    qkvf_ref[...] = rows
    written = jnp.exp(rows[:, 3 * D :].astype(F32))
    newest = edge_ref[15:16]
    tail = wide(flag(col_ref[...], newest), 4) * written
    slots = tail.astype(BF16)
    keys, values = state_terms(slots, rows[:, D : 2 * D], rows[:, 2 * D : 3 * D])

    @pl.when(step == 0)
    def _():
        tail_ref[...] = jnp.zeros_like(tail_ref)
        tail_ref[129:130] = newest.astype(F32)

    tail_ref[0:64] += keys
    tail_ref[64:128] += values
    tail_ref[128:129] += jnp.sum(slots.astype(F32), axis=0, keepdims=True)


def attend_kernel(
    qkvf_ref, col_ref, row_ref, edge_ref, start_ref, o_ref, p_ref, s_ref, z_ref, kept_ref, state
):
    step = pl.program_id(0)

    @pl.when(step == 0)
    def _():
        state[...] = start_ref[...]

    kept_ref[0] = state[0:128]
    first = edge_ref[pl.ds(0, 1)]
    before = edge_ref[pl.ds(8 + jnp.maximum(step - 1, 0), 1)]
    last = jnp.where(step == 0, first, before)
    newest = edge_ref[pl.ds(8 + step, 1)]
    col = col_ref[...]
    vis = visible(col, row_ref[...])
    carried = wide(flag(col, last), 2)
    written = jnp.exp(qkvf_ref[:, 3 * D :].astype(F32))
    slots = written.astype(BF16)
    norm = dot(vis, slots)
    for g in range(2):
        lanes = slice(g * GROUP, (g + 1) * GROUP)
        queries, keys, values = (
            qkvf_ref[:, part * D + g * GROUP : part * D + (g + 1) * GROUP] for part in range(3)
        )
        here = slots[:, lanes]
        affinity = masked(dot_nt(stacked(queries), keys), vis)
        numer = select(dot(affinity, here))
        numer = numer + carried * dot_nt(queries, expand(state[0:64, lanes]).astype(BF16))
        total = norm[:, lanes] + carried * state[128:129, lanes]
        inverse = 1.0 / total
        score = numer * inverse * SCALE
        grown = jnp.exp(score - head_max(score))
        probs = grown / head_sums(grown)
        reading = (probs * inverse).astype(BF16)
        mix = masked(dot_nt(stacked(reading), here), vis)
        mixed = select(dot(mix, values))
        mixed = mixed + carried * dot(reading, expand(state[64:128, lanes]).astype(BF16))
        o_ref[:, lanes] = mixed.astype(BF16)
        p_ref[:, lanes] = probs
        s_ref[:, lanes] = score
        z_ref[:, lanes] = inverse
    tail = (wide(flag(col, newest), 4) * written).astype(BF16)
    new_keys, new_values = state_terms(tail, qkvf_ref[:, D : 2 * D], qkvf_ref[:, 2 * D : 3 * D])
    same = jnp.where(last == newest, 1.0, 0.0)
    state[0:64] = same * state[0:64] + new_keys
    state[64:128] = same * state[64:128] + new_values
    state[128:129] = same * state[128:129] + jnp.sum(tail.astype(F32), axis=0, keepdims=True)


ROOT = 0.7978845608028654
CUBE = 0.044715


def gelu_both(u):
    square = u * u
    bent = jnp.tanh(ROOT * u * (1.0 + CUBE * square))
    half = 0.5 * (1.0 + bent)
    slope = half + 0.5 * u * (1.0 - bent * bent) * (ROOT * (1.0 + 3.0 * CUBE * square))
    return u * half, slope


def forward_kernel(
    x_ref, o_ref, g_ref, small_ref, bias_ref, wo_ref, wh_ref, wr_ref,
    y_ref, dy_ref, do_ref, gwo_ref, gwh_ref, gwr_ref, gsmall_ref, gbias_ref, dz_buf,
):
    step = pl.program_id(0)

    @pl.when(step == 0)
    def _():
        for ref in (gwo_ref, gwh_ref, gwr_ref, gsmall_ref, gbias_ref):
            ref[...] = jnp.zeros_like(ref)

    attended, cot = o_ref[...], g_ref[...]
    middle = x_ref[...].astype(F32) + dot(attended, wo_ref[...])
    unit, scale = norm_parts(middle)
    hidden = (unit * small_ref[2:3] + small_ref[3:4]).astype(BF16)
    out = middle + small_ref[4:5]
    grad_hidden = jnp.zeros((x_ref.shape[0], D), F32)
    cot32 = cot.astype(F32)
    for j in range(4):
        cols = slice(j * 512, (j + 1) * 512)
        inner = dot(hidden, wh_ref[:, cols]) + bias_ref[0:1, cols]
        gated, slope = gelu_both(inner)
        active = gated.astype(BF16)
        out = out + dot(active, wr_ref[cols, :])
        gwr_ref[:, cols] += dot_tn(cot, active)
        grad = dot_nt(cot, wr_ref[cols, :]) * slope
        low = grad.astype(BF16)
        gbias_ref[0:1, cols] += jnp.sum(low.astype(F32), axis=0, keepdims=True)
        gwh_ref[:, cols] += dot_tn(hidden, low)
        grad_hidden = grad_hidden + dot_nt(low, wh_ref[:, cols])
    y_ref[...] = out.astype(BF16)
    gsmall_ref[2:3] += jnp.sum(grad_hidden * unit, axis=0, keepdims=True)
    gsmall_ref[3:4] += jnp.sum(grad_hidden, axis=0, keepdims=True)
    gsmall_ref[4:5] += jnp.sum(cot32, axis=0, keepdims=True)
    grad_middle = cot32 + norm_back(unit, scale, small_ref[2:3], grad_hidden)
    dy_ref[...] = grad_middle
    branch = grad_middle.astype(BF16)
    gwo_ref[...] += dot_tn(attended, branch)
    do_ref[...] = dot_nt(branch, wo_ref[...]).astype(BF16)


def row_kernel(
    qkvf_ref, do_ref, p_ref, s_ref, z_ref, kept_ref, col_ref, row_ref, edge_ref,
    dq_ref, r_ref, dn_ref, dz_ref, head_ref,
):
    step = pl.program_id(0)
    first = edge_ref[pl.ds(0, 1)]
    before = edge_ref[pl.ds(8 + jnp.maximum(step - 1, 0), 1)]
    last = jnp.where(step == 0, first, before)
    col = col_ref[...]
    vis = visible(col, row_ref[...])
    carried = wide(flag(col, last), 2)
    slots = jnp.exp(qkvf_ref[:, 3 * D :].astype(F32)).astype(BF16)
    own = wide(flag(col, first), 4)

    @pl.when(step == 0)
    def _():
        head_ref[...] = jnp.zeros_like(head_ref)
        head_ref[129:130] = first.astype(F32)

    for g in range(2):
        lanes = slice(g * GROUP, (g + 1) * GROUP)
        queries, keys, values = (
            qkvf_ref[:, part * D + g * GROUP : part * D + (g + 1) * GROUP] for part in range(3)
        )
        here, grads = slots[:, lanes], do_ref[:, lanes]
        probs, score, inverse = p_ref[:, lanes], s_ref[:, lanes], z_ref[:, lanes]
        back_mix = masked(dot_nt(stacked(grads), values), vis)
        back_reading = select(dot(back_mix, here))
        back_reading = back_reading + carried * dot_nt(
            grads, expand(kept_ref[0, 64:128, lanes]).astype(BF16)
        )
        back_probs = back_reading * inverse
        shared = back_probs * probs
        back_score = shared - probs * head_sums(shared)
        back_numer = back_score * inverse * SCALE
        back_total = -(shared + back_score * score) * inverse
        low = back_numer.astype(BF16)
        back_affinity = masked(dot_nt(stacked(low), here), vis)
        back_queries = select(dot(back_affinity, keys))
        back_queries = back_queries + carried * dot(
            low, expand(kept_ref[0, 0:64, lanes]).astype(BF16)
        )
        dq_ref[:, lanes] = back_queries.astype(BF16)
        reading = (probs * inverse).astype(BF16)
        r_ref[:, lanes] = reading
        dn_ref[:, lanes] = back_numer
        dz_ref[:, lanes] = back_total
        mine = own[:, lanes]
        head_ref[0:64, lanes] += compacted(dot_tn((mine * back_numer).astype(BF16), queries))
        head_ref[64:128, lanes] += compacted(
            dot_tn((mine * reading.astype(F32)).astype(BF16), grads)
        )
        head_ref[128:129, lanes] += jnp.sum(mine * back_total, axis=0, keepdims=True)


def column_kernel(
    x_ref, qkvf_ref, do_ref, dq_ref, r_ref, dn_ref, dz_ref, col_ref, row_ref, edge_ref, small_ref,
    start_ref, d_ref, gw_ref, state,
):
    step = pl.program_id(0)
    here_at = 7 - step

    @pl.when(step == 0)
    def _():
        state[...] = start_ref[...]
        gw_ref[...] = jnp.zeros_like(gw_ref)

    newest = edge_ref[15:16]
    after = edge_ref[pl.ds(jnp.minimum(here_at + 1, 7), 1)]
    following = jnp.where(step == 0, newest, after)
    first = edge_ref[pl.ds(here_at, 1)]
    col = col_ref[...]
    vis = visible_back(col, row_ref[...])
    carried = wide(flag(col, following), 2)
    own = wide(flag(col, first), 2)
    same = jnp.where(following == first, 1.0, 0.0)
    written = jnp.exp(qkvf_ref[:, 3 * D :].astype(F32))
    slots = written.astype(BF16)
    total_high, total_low = split(dz_ref[...])
    back_norm = dot(vis, total_high) + dot(vis, total_low)
    d_ref[:, 0:D] = dq_ref[...]
    left = lane_heads(C, 128) == 0
    for g in range(2):
        lanes = slice(g * GROUP, (g + 1) * GROUP)
        queries, keys, values = (
            qkvf_ref[:, part * D + g * GROUP : part * D + (g + 1) * GROUP] for part in range(3)
        )
        here, grads, reading = slots[:, lanes], do_ref[:, lanes], r_ref[:, lanes]
        numer_high, numer_low = split(dn_ref[:, lanes])
        key_state = expand(state[0:64, lanes]).astype(BF16)
        value_state = expand(state[64:128, lanes]).astype(BF16)
        apart = stacked(here)
        mix = masked(dot_nt(apart, reading), vis)
        back_values = select(dot(mix, grads)) + carried * dot(here, value_state)
        d_ref[:, 2 * D + g * GROUP : 2 * D + (g + 1) * GROUP] = back_values.astype(BF16)
        back_affinity = masked(dot_nt(apart, numer_high), vis)
        back_keys = select(dot(back_affinity, queries)) + carried * dot(here, key_state)
        d_ref[:, D + g * GROUP : D + (g + 1) * GROUP] = back_keys.astype(BF16)
        back_mix = masked(dot_nt(stacked(values), grads), vis)
        back_slots = back_norm[:, lanes] + select(dot(back_mix, reading))
        affinity = masked(dot_nt(stacked(keys), queries), vis)
        parts = []
        for p in range(2):
            pair = slice(p * 128, (p + 1) * 128)
            both = dot(
                affinity[p * 512 : (p + 1) * 512],
                jnp.concatenate([numer_high[:, pair], numer_low[:, pair]], axis=1),
            )
            both = both[:, :128] + both[:, 128:]
            parts.append(jnp.where(left, both[:C], both[C:]))
        back_slots = back_slots + jnp.concatenate(parts, axis=1)
        back_slots = back_slots + carried * (
            dot_nt(keys, key_state) + dot_nt(values, value_state) + state[128:129, lanes]
        )
        d_ref[:, 3 * D + g * GROUP : 3 * D + (g + 1) * GROUP] = (
            back_slots * written[:, lanes]
        ).astype(BF16)
        kept = same[:, lanes]
        state[0:64, lanes] = kept * state[0:64, lanes] + compacted(
            dot_tn((own * dn_ref[:, lanes]).astype(BF16), queries)
        )
        state[64:128, lanes] = kept * state[64:128, lanes] + compacted(
            dot_tn((own * reading.astype(F32)).astype(BF16), grads)
        )
        state[128:129, lanes] = kept * state[128:129, lanes] + jnp.sum(
            own * dz_ref[:, lanes], axis=0, keepdims=True
        )
    unit, _ = norm_parts(x_ref[...].astype(F32))
    hidden = (unit * small_ref[0:1] + small_ref[1:2]).astype(BF16)
    gw_ref[...] += dot_tn(hidden, d_ref[...])


def input_kernel(x_ref, d_ref, dy_ref, w_ref, small_ref, gi_ref, gsmall_ref):
    step = pl.program_id(0)

    @pl.when(step == 0)
    def _():
        gsmall_ref[...] = jnp.zeros_like(gsmall_ref)

    grad = dot_nt(d_ref[...], w_ref[...])
    unit, scale = norm_parts(x_ref[...].astype(F32))
    gsmall_ref[0:1] += jnp.sum(grad * unit, axis=0, keepdims=True)
    gsmall_ref[1:2] += jnp.sum(grad, axis=0, keepdims=True)
    gi_ref[...] = dy_ref[...] + norm_back(unit, scale, small_ref[0:1], grad)


def rows_of(lanes, order=lambda i: i):
    return pl.BlockSpec((C, lanes), lambda i: (order(i), 0))


def whole(*shape):
    return pl.BlockSpec(shape, lambda i: (0,) * len(shape))


def row_of(order=lambda i: i):
    return pl.BlockSpec((1, C), lambda i: (0, order(i)))


def shape_of(shape, kind):
    return jax.ShapeDtypeStruct(shape, kind)


PARAMS = pltpu.CompilerParams(vmem_limit_bytes=LIMIT)


def on_device(
    tokens, doc_ids, w_query, w_key, w_value, w_slots, w_output, w_hidden, w_return,
    gain_first, shift_first, gain_second, shift_second, bias_hidden, bias_return, cotangent,
):
    rows = tokens.shape[0]
    steps = rows // C
    seq = lax.axis_index("seq")
    gather = lambda a: lax.all_gather(a.astype(BF16), "fsdp", axis=0, tiled=True)
    w_qkvf = gather(jnp.concatenate([w_query, w_key, w_value, w_slots], axis=1))
    w_o, w_h, w_r = gather(w_output), gather(w_hidden), gather(w_return)
    smalls = lax.all_gather(
        jnp.concatenate(
            [gain_first, shift_first, gain_second, shift_second, bias_return, bias_hidden]
        ).astype(BF16),
        "fsdp",
    ).astype(F32)
    part = gain_first.shape[0]
    small = jnp.stack([smalls[:, n * part : (n + 1) * part].reshape(-1) for n in range(5)])
    small = jnp.concatenate([small, jnp.zeros((3, D), F32)], axis=0)
    bias = smalls[:, 5 * part :].reshape(1, FF)
    doc_col = jnp.broadcast_to(doc_ids.reshape(rows, 1), (rows, 128))
    pieces = doc_ids.reshape(steps, C)
    edges = jnp.concatenate([pieces[:, 0], pieces[:, -1]])
    edges = jnp.broadcast_to(edges[:, None], (2 * steps, D))

    qkvf, tail = pl.pallas_call(
        project_kernel,
        grid=(steps,),
        in_specs=[rows_of(D), rows_of(128), whole(16, D), whole(8, D), whole(D, 4 * D)],
        out_specs=[rows_of(4 * D), whole(136, D)],
        out_shape=[shape_of((rows, 4 * D), BF16), shape_of((136, D), F32)],
        compiler_params=PARAMS,
        name="project",
    )(tokens, doc_col, edges, small, w_qkvf)
    tails = lax.all_gather(tail, "seq")
    use = (jnp.arange(4) < seq) & (tails[:, 129, 0] == edges[0, 0].astype(F32))
    start = jnp.sum(jnp.where(use[:, None, None], tails, 0.0), axis=0)

    attended, probs, score, inverse, kept = pl.pallas_call(
        attend_kernel,
        grid=(steps,),
        in_specs=[rows_of(4 * D), rows_of(128), row_of(), whole(16, D), whole(136, D)],
        out_specs=[rows_of(D)] * 4 + [pl.BlockSpec((1, 128, D), lambda i: (i, 0, 0))],
        out_shape=[shape_of((rows, D), BF16)]
        + [shape_of((rows, D), F32)] * 3
        + [shape_of((steps, 128, D), F32)],
        scratch_shapes=[pltpu.VMEM((136, D), F32)],
        compiler_params=PARAMS,
        name="attend",
    )(qkvf, doc_col, doc_ids, edges, start)

    out, grad_middle, grad_attended, g_wo, g_wh, g_wr, g_small, g_bias = pl.pallas_call(
        forward_kernel,
        grid=(steps,),
        in_specs=[rows_of(D)] * 3
        + [whole(8, D), whole(1, FF), whole(D, D), whole(D, FF), whole(FF, D)],
        out_specs=[rows_of(D)] * 3
        + [whole(D, D), whole(D, FF), whole(D, FF), whole(8, D), whole(1, FF)],
        out_shape=[
            shape_of((rows, D), BF16),
            shape_of((rows, D), F32),
            shape_of((rows, D), BF16),
            shape_of((D, D), F32),
            shape_of((D, FF), F32),
            shape_of((D, FF), F32),
            shape_of((8, D), F32),
            shape_of((1, FF), F32),
        ],
        scratch_shapes=[pltpu.VMEM((C, FF), BF16)],
        compiler_params=PARAMS,
        name="feed",
    )(tokens, attended, cotangent, small, bias, w_o, w_h, w_r)

    grad_q, reading, grad_numer, grad_total, head = pl.pallas_call(
        row_kernel,
        grid=(steps,),
        in_specs=[rows_of(4 * D)]
        + [rows_of(D)] * 4
        + [pl.BlockSpec((1, 128, D), lambda i: (i, 0, 0)), rows_of(128), row_of(), whole(16, D)],
        out_specs=[rows_of(D)] * 4 + [whole(136, D)],
        out_shape=[
            shape_of((rows, D), BF16),
            shape_of((rows, D), BF16),
            shape_of((rows, D), F32),
            shape_of((rows, D), F32),
            shape_of((136, D), F32),
        ],
        compiler_params=PARAMS,
        name="rowside",
    )(qkvf, grad_attended, probs, score, inverse, kept, doc_col, doc_ids, edges)
    heads = lax.all_gather(head, "seq")
    use = (jnp.arange(4) > seq) & (heads[:, 129, 0] == edges[-1, 0].astype(F32))
    finish = jnp.sum(jnp.where(use[:, None, None], heads, 0.0), axis=0)

    back = lambda i: steps - 1 - i
    grads, g_qkvf = pl.pallas_call(
        column_kernel,
        grid=(steps,),
        in_specs=[rows_of(D, back), rows_of(4 * D, back)]
        + [rows_of(D, back)] * 5
        + [rows_of(128, back), row_of(back), whole(16, D), whole(8, D), whole(136, D)],
        out_specs=[rows_of(4 * D, back), whole(D, 4 * D)],
        out_shape=[shape_of((rows, 4 * D), BF16), shape_of((D, 4 * D), F32)],
        scratch_shapes=[pltpu.VMEM((136, D), F32)],
        compiler_params=PARAMS,
        name="colside",
    )(
        tokens, qkvf, grad_attended, grad_q, reading, grad_numer, grad_total, doc_col, doc_ids,
        edges, small, finish,
    )

    grad_input, g_small_one = pl.pallas_call(
        input_kernel,
        grid=(steps,),
        in_specs=[rows_of(D), rows_of(4 * D), rows_of(D), whole(D, 4 * D), whole(8, D)],
        out_specs=[rows_of(D), whole(8, D)],
        out_shape=[shape_of((rows, D), F32), shape_of((8, D), F32)],
        compiler_params=PARAMS,
        name="inputside",
    )(tokens, grads, grad_middle, w_qkvf, small)

    scatter = lambda a, dim=0: lax.psum(
        lax.psum_scatter(a, "fsdp", scatter_dimension=dim, tiled=True), "seq"
    )
    g_qkvf = scatter(g_qkvf)
    g_wo, g_wh, g_wr = scatter(g_wo), scatter(g_wh), scatter(g_wr, 1).T
    vector = jnp.concatenate(
        [g_small_one[0], g_small_one[1], g_small[2], g_small[3], g_bias[0], g_small[4]]
    )
    vector = lax.psum(vector, ("fsdp", "seq"))
    at = lax.axis_index("fsdp")
    pick = lambda start, size: lax.dynamic_slice(vector, (start + at * size,), (size,))
    return (
        out,
        grad_input,
        g_qkvf[:, 0:D],
        g_qkvf[:, D : 2 * D],
        g_qkvf[:, 2 * D : 3 * D],
        g_qkvf[:, 3 * D :],
        g_wo,
        g_wh,
        g_wr,
        pick(0, part),
        pick(D, part),
        pick(2 * D, part),
        pick(3 * D, part),
        pick(4 * D, 4 * part),
        pick(4 * D + FF, part),
    )


def solution(mesh):
    tall, flat, one = P(("fsdp", "seq"), None), P("fsdp", None), P("fsdp")
    return jax.shard_map(
        on_device,
        mesh=mesh,
        in_specs=(tall, P("fsdp", "seq")) + (flat,) * 7 + (one,) * 6 + (tall,),
        out_specs=(tall, tall) + (flat,) * 7 + (one,) * 6,
        check_vma=False,
    )
```

```python
import functools

import jax
import jax.numpy as jnp
from jax import lax
from jax.experimental import pallas as pl
from jax.experimental.pallas import tpu as pltpu
from jax.sharding import PartitionSpec as P

D = 512
H = 8
M = 64
FF = 2048
C = 256
GROUP = 256
EPS = 1e-05
SCALE = 0.125
F32 = jnp.float32
BF16 = jnp.bfloat16
LIMIT = 60 * 1024 * 1024


def dot(a, b):
    return lax.dot_general(a, b, (((1,), (0,)), ((), ())), preferred_element_type=F32)


def dot_nt(a, b):
    return lax.dot_general(a, b, (((1,), (1,)), ((), ())), preferred_element_type=F32)


def dot_tn(a, b):
    return lax.dot_general(a, b, (((0,), (0,)), ((), ())), preferred_element_type=F32)


def lane_heads(rows, lanes):
    return lax.broadcasted_iota(jnp.int32, (rows, lanes), 1) // M


def stacked(values):
    heads = lane_heads(C, GROUP)
    zero = jnp.zeros_like(values)
    return jnp.concatenate([jnp.where(heads == h, values, zero) for h in range(4)], axis=0)


def select(values):
    heads = lane_heads(C, GROUP)
    out = values[3 * C :]
    for h in (2, 1, 0):
        out = jnp.where(heads == h, values[h * C : (h + 1) * C], out)
    return out


def masked(values, mask):
    return jnp.concatenate(
        [values[h * C : (h + 1) * C].astype(BF16) * mask for h in range(4)], axis=0
    )


def expand(compact):
    rows = lax.broadcasted_iota(jnp.int32, (GROUP, GROUP), 0) // M
    full = jnp.concatenate([compact] * 4, axis=0)
    return jnp.where(rows == lane_heads(GROUP, GROUP), full, jnp.zeros_like(full))


def compacted(full):
    heads = lane_heads(M, GROUP)
    out = full[3 * M :]
    for h in (2, 1, 0):
        out = jnp.where(heads == h, full[h * M : (h + 1) * M], out)
    return out


def split(values):
    high = values.astype(BF16)
    return high, (values - high.astype(F32)).astype(BF16)


def ones_block():
    rows = lax.broadcasted_iota(jnp.int32, (GROUP, GROUP), 0) // M
    return (rows == lane_heads(GROUP, GROUP)).astype(BF16)


def head_sums(values):
    high, low = split(values)
    ones = ones_block()
    return dot(high, ones) + dot(low, ones)


def head_max(values):
    left = lane_heads(C, 128) == 0
    out = []
    for p in range(2):
        pair = values[:, p * 128 : (p + 1) * 128]
        one = jnp.max(jnp.where(left, pair, -jnp.inf), axis=1, keepdims=True)
        two = jnp.max(jnp.where(left, -jnp.inf, pair), axis=1, keepdims=True)
        out.append(jnp.where(left, one, two))
    return jnp.concatenate(out, axis=1)


def wide(values, times):
    return jnp.concatenate([values] * times, axis=1)


def visible(doc_col, doc_row):
    same = wide(doc_col, 2) == doc_row
    here = lax.broadcasted_iota(jnp.int32, (C, C), 0)
    there = lax.broadcasted_iota(jnp.int32, (C, C), 1)
    return jnp.where(same & (here >= there), 1.0, 0.0).astype(BF16)


def visible_back(doc_col, doc_row):
    same = wide(doc_col, 2) == doc_row
    here = lax.broadcasted_iota(jnp.int32, (C, C), 0)
    there = lax.broadcasted_iota(jnp.int32, (C, C), 1)
    return jnp.where(same & (there >= here), 1.0, 0.0).astype(BF16)


def flag(doc_col, doc):
    return jnp.where(doc_col == doc[:, :128], 1.0, 0.0)


def norm_parts(values):
    centre = jnp.mean(values, axis=-1, keepdims=True)
    centred = values - centre
    spread = jnp.mean(centred * centred, axis=-1, keepdims=True)
    scale = lax.rsqrt(spread + EPS)
    return centred * scale, scale


def norm_back(unit, scale, gain, grad):
    inner = grad * gain
    return scale * (
        inner
        - jnp.mean(inner, axis=-1, keepdims=True)
        - unit * jnp.mean(inner * unit, axis=-1, keepdims=True)
    )


def groups(values):
    return values[:, :GROUP], values[:, GROUP:]


def state_terms(slots, left, right):
    one, two = [], []
    for g in range(2):
        lanes = slice(g * GROUP, (g + 1) * GROUP)
        both = dot_tn(slots[:, lanes], jnp.concatenate([left[:, lanes], right[:, lanes]], axis=1))
        one.append(compacted(both[:, :GROUP]))
        two.append(compacted(both[:, GROUP:]))
    return jnp.concatenate(one, axis=1), jnp.concatenate(two, axis=1)


def attend_body(
    n, qkvf_ref, col, row, edge_ref, state, o_ref, p_ref, s_ref, z_ref, kept_ref
):
    kept_ref[0] = state[0:128]
    first = edge_ref[pl.ds(0, 1)]
    before = edge_ref[pl.ds(8 + jnp.maximum(n - 1, 0), 1)]
    last = jnp.where(n == 0, first, before)
    newest = edge_ref[pl.ds(8 + n, 1)]
    vis = visible(col, row)
    carried = wide(flag(col, last), 2)
    written = jnp.exp(qkvf_ref[:, 3 * D :].astype(F32))
    slots = written.astype(BF16)
    norm = dot(vis, slots)
    for g in range(2):
        lanes = slice(g * GROUP, (g + 1) * GROUP)
        queries, keys, values = (
            qkvf_ref[:, part * D + g * GROUP : part * D + (g + 1) * GROUP] for part in range(3)
        )
        here = slots[:, lanes]
        affinity = masked(dot_nt(stacked(queries), keys), vis)
        numer = select(dot(affinity, here))
        numer = numer + carried * dot_nt(queries, expand(state[0:64, lanes]).astype(BF16))
        total = norm[:, lanes] + carried * state[128:129, lanes]
        inverse = 1.0 / total
        score = numer * inverse * SCALE
        grown = jnp.exp(score - head_max(score))
        probs = grown / head_sums(grown)
        reading = (probs * inverse).astype(BF16)
        mix = masked(dot_nt(stacked(reading), here), vis)
        mixed = select(dot(mix, values))
        mixed = mixed + carried * dot(reading, expand(state[64:128, lanes]).astype(BF16))
        o_ref[:, lanes] = mixed.astype(BF16)
        p_ref[:, lanes] = probs
        s_ref[:, lanes] = score
        z_ref[:, lanes] = inverse
    tail = (wide(flag(col, newest), 4) * written).astype(BF16)
    new_keys, new_values = state_terms(tail, qkvf_ref[:, D : 2 * D], qkvf_ref[:, 2 * D : 3 * D])
    same = jnp.where(last == newest, 1.0, 0.0)
    state[0:64] = same * state[0:64] + new_keys
    state[64:128] = same * state[64:128] + new_values
    state[128:129] = same * state[128:129] + jnp.sum(tail.astype(F32), axis=0, keepdims=True)


MESH_ID = pl.DeviceIdType.MESH


def places():
    seq, at = lax.axis_index("seq"), lax.axis_index("fsdp")
    core = lax.rem(seq, 2)
    return seq, at, seq + 1 - 2 * core, lax.rem(seq + 2, 4)


def push(src, dst, send, recv, **device):
    return pltpu.make_async_remote_copy(
        src_ref=src, dst_ref=dst, send_sem=send, recv_sem=recv,
        device_id=device, device_id_type=MESH_ID,
    )


def greet(count):
    seq, at, _, _ = places()
    barrier = pltpu.get_barrier_semaphore()
    for k in range(1, count):
        pl.semaphore_signal(barrier, inc=1, device_id={"fsdp": at ^ k}, device_id_type=MESH_ID)
    for k in range(1, 4):
        pl.semaphore_signal(barrier, inc=1, device_id={"seq": seq ^ k}, device_id_type=MESH_ID)
    pl.semaphore_wait(barrier, count - 1 + 3)


class Gather:
    def __init__(self, count, mine, held, sems):
        self.count, self.mine, self.held = count, mine, held
        self.across, self.core, self.chip, self.onward, self.local = sems
        self.seq, self.at, self.sibling, self.beside = places()
        self.quarter = held.shape[2] // 4

    def lanes(self, seq):
        return pl.ds(pl.multiple_of(seq * self.quarter, self.quarter), self.quarter)

    def part(self, owner, seq):
        return self.held.at[owner, :, self.lanes(seq)]

    def first(self, k):
        return push(
            self.mine.at[:, self.lanes(self.seq)], self.part(self.at, self.seq),
            self.across[0].at[k], self.across[1].at[k], fsdp=self.at ^ k,
        )

    def first_in(self, k):
        here = self.part(self.at ^ k, self.seq)
        return push(here, here, self.across[0].at[k], self.across[1].at[k], fsdp=self.at ^ k)

    def own(self):
        return pltpu.make_async_copy(
            self.mine.at[:, self.lanes(self.seq)], self.part(self.at, self.seq), self.local
        )

    def start(self):
        for k in range(1, self.count):
            self.first(k).start()
        self.own().start()

    def hop(self, sems, source, target, k):
        if k is None:
            ref, n = self.held.at[:, :, self.lanes(source)], 0
        else:
            ref, n = self.part(self.at ^ k, source), k
        return push(ref, ref, sems[0].at[n], sems[1].at[n], seq=target)

    def sent(self, n, k):
        if n == 0:
            return self.hop(self.core, self.seq, self.sibling, k)
        if n == 1:
            return self.hop(self.chip, self.seq, self.beside, k)
        return self.hop(self.onward, self.beside, self.sibling, k)

    def come(self, n, k):
        if n == 0:
            return self.hop(self.core, self.sibling, self.sibling, k)
        if n == 1:
            return self.hop(self.chip, self.beside, self.beside, k)
        return self.hop(self.onward, lax.rem(self.sibling + 2, 4), self.sibling, k)

    def second(self):
        self.own().wait()
        for k in range(1, self.count):
            self.first_in(k).wait_recv()
        self.sent(0, None).start()
        self.sent(1, None).start()

    def third(self):
        self.come(1, None).wait_recv()
        self.sent(2, None).start()

    def finish(self):
        for n in range(3):
            self.sent(n, None).wait_send()
        self.come(0, None).wait_recv()
        self.come(2, None).wait_recv()
        for k in range(1, self.count):
            self.first(k).wait_send()

    def second_each(self):
        for k in range(self.count):
            if k:
                self.first_in(k).wait_recv()
            else:
                self.own().wait()
            self.sent(0, k).start()
            self.sent(1, k).start()
        for k in range(self.count):
            self.come(1, k).wait_recv()
            self.sent(2, k).start()
        for k in range(self.count):
            self.come(0, k).wait_recv()
            self.come(2, k).wait_recv()

    def drain_each(self):
        for k in range(self.count):
            for n in range(3):
                self.sent(n, k).wait_send()
        for k in range(1, self.count):
            self.first(k).wait_send()


def gather_sems(count, each):
    n = count if each else 1
    pair = lambda size: [pltpu.SemaphoreType.DMA((size,)), pltpu.SemaphoreType.DMA((size,))]
    return pair(count) + pair(n) + pair(n) + pair(n) + [pltpu.SemaphoreType.DMA]


def bundle(refs):
    return (refs[0], refs[1]), (refs[2], refs[3]), (refs[4], refs[5]), (refs[6], refs[7]), refs[8]


class States:
    def __init__(self, big, small, sems):
        self.refs, self.sems = (big, small), sems
        self.seq, _, self.sibling, self.beside = places()

    def hop(self, n, source, target):
        out = []
        for m, ref in enumerate(self.refs):
            here = ref.at[source]
            out.append(push(here, here, self.sems[0].at[n, m], self.sems[1].at[n, m], seq=target))
        return out

    def start(self):
        for copy in self.hop(0, self.seq, self.sibling) + self.hop(1, self.seq, self.beside):
            copy.start()

    def finish(self):
        for copy in self.hop(1, self.beside, self.beside):
            copy.wait_recv()
        for copy in self.hop(2, self.beside, self.sibling):
            copy.start()
        for copy in self.hop(0, self.sibling, self.sibling):
            copy.wait_recv()
        for copy in self.hop(2, lax.rem(self.sibling + 2, 4), self.sibling):
            copy.wait_recv()

    def drain(self):
        for copy in (
            self.hop(0, self.seq, self.sibling)
            + self.hop(1, self.seq, self.beside)
            + self.hop(2, self.beside, self.sibling)
        ):
            copy.wait_send()


def doc_parts(doc_ref, col_ref, edge_ref):
    here = lax.broadcasted_iota(jnp.int32, (C, C), 0)
    there = lax.broadcasted_iota(jnp.int32, (C, C), 1)
    eye = jnp.where(here == there, 1.0, 0.0).astype(BF16)
    for n in range(doc_ref.shape[1] // C):
        row = doc_ref[:, n * C : (n + 1) * C].astype(F32)
        col_ref[n * C : (n + 1) * C] = dot_nt(eye, jnp.broadcast_to(row, (128, C)).astype(BF16))
        low = jnp.min(row, axis=1, keepdims=True)
        high = jnp.max(row, axis=1, keepdims=True)
        edge_ref[n : n + 1] = jnp.broadcast_to(low, (1, D))
        edge_ref[n + 8 : n + 9] = jnp.broadcast_to(high, (1, D))


def spread_small(vec_refs, bias_ref, out_ref):
    part = vec_refs[0].shape[1]

    def repeat(values):
        width = values.shape[1]
        rows = lax.broadcasted_iota(jnp.int32, (width, D), 0)
        lanes = lax.broadcasted_iota(jnp.int32, (width, D), 1)
        pick = jnp.where(lax.rem(lanes, width) == rows, 1.0, 0.0).astype(BF16)
        return dot(jnp.broadcast_to(values, (8, width)).astype(BF16), pick)[0:1]

    out_ref[...] = jnp.zeros_like(out_ref)
    for n, ref in enumerate(vec_refs):
        out_ref[n : n + 1] = repeat(ref[...])
    out_ref[5:6] = repeat(bias_ref[...])
    return part


def join_small(count, part, gathered, vec_ref, bias_ref):
    lanes = lax.broadcasted_iota(jnp.int32, (8, D), 1)
    total = jnp.zeros((8, D), F32)
    for f in range(count):
        total = jnp.where(lanes // part == f, gathered[f], total)
    vec_ref[...] = total
    for r in range(4):
        row = jnp.zeros((8, D), F32)
        for f in range(count):
            row = jnp.where((lanes + r * D) // (4 * part) == f, gathered[f], row)
        bias_ref[0:1, r * D : (r + 1) * D] = row[5:6]


def front_kernel(
    count, x_ref, doc_ref, wq_ref, wk_ref, wv_ref, ws_ref, wo_ref, wh_ref, wr_ref,
    v0, v1, v2, v3, v4, bias_in,
    qkvf_out, o_ref, p_ref, s_ref, z_ref, kept_ref, w_out, wo_out, wh_out, wr_out, vec_out, bias_out,
    qkvf, hidden, w_all, mine, mine_o, mine_h, mine_r, spread, smalls, col_ref, edge_ref, state,
    tail, tails, tail_rows, *sems,
):
    step = pl.program_id(0)
    seq, at, _, _ = places()
    link = mine.dtype
    first_sems, sems = bundle(sems[:9]), sems[9:]
    o_sems, sems = bundle(sems[:9]), sems[9:]
    h_sems, sems = bundle(sems[:9]), sems[9:]
    r_sems, sems = bundle(sems[:9]), sems[9:]
    small_send, small_recv, state_send, state_recv, out_sem = sems
    main = Gather(count, mine, w_all, first_sems)
    later = [
        Gather(count, mine_o, wo_out, o_sems),
        Gather(count, mine_h, wh_out, h_sems),
        Gather(count, mine_r, wr_out, r_sems),
    ]
    states = States(tails, tail_rows, (state_send, state_recv))

    def small_copy(k, owner):
        return push(
            spread, smalls.at[owner], small_send.at[k], small_recv.at[k], fsdp=at ^ k
        )

    def save():
        return (
            pltpu.make_async_copy(qkvf, qkvf_out, out_sem.at[0]),
            pltpu.make_async_copy(w_all, w_out, out_sem.at[1]),
        )

    @pl.when(step == 0)
    def _():
        greet(count)
        for n, ref in enumerate((wq_ref, wk_ref, wv_ref, ws_ref)):
            mine[:, n * D : (n + 1) * D] = ref[...].astype(BF16).astype(link)
        spread_small((v0, v1, v2, v3, v4), bias_in, spread)
        main.start()
        for k in range(1, count):
            small_copy(k, at).start()
        mine_o[...] = wo_ref[...].astype(BF16).astype(link)
        mine_h[...] = wh_ref[...].astype(BF16).astype(link)
        mine_r[...] = wr_ref[...].astype(BF16).astype(link)
        doc_parts(doc_ref, col_ref, edge_ref)
        tail[...] = jnp.zeros_like(tail)
        smalls[at] = spread[...]
        main.second_each()
        for k in range(1, count):
            small_copy(k, at ^ k).wait_recv()
        join_small(count, v0.shape[1], smalls, vec_out, bias_out)
        for piece in later:
            piece.start()

    @pl.when(step < 8)
    def _():
        unit, _ = norm_parts(x_ref[...].astype(F32))
        normed = (unit * vec_out[0:1] + vec_out[1:2]).astype(BF16)
        here = pl.ds(pl.multiple_of(step * C, C), C)
        hidden[here] = normed
        weights = w_all[:, :, D:].reshape(D, 3 * D).astype(BF16)
        rows = dot(normed, weights).astype(BF16)
        qkvf[here, D:] = rows
        slots = wide(flag(col_ref[here], edge_ref[15:16]), 4) * jnp.exp(rows[:, 2 * D :].astype(F32))
        slots = slots.astype(BF16)
        keys, values = state_terms(slots, rows[:, 0:D], rows[:, D : 2 * D])
        tail[0:64] += keys
        tail[64:128] += values
        tail[128:129] += jnp.sum(slots.astype(F32), axis=0, keepdims=True)

    @pl.when(step == 5)
    def _():
        for piece in later:
            piece.second()

    @pl.when(step == 7)
    def _():
        tails[seq] = tail[0:128].astype(link)
        tail_rows[seq, 0:1] = tail[128:129]
        tail_rows[seq, 1:2] = edge_ref[15:16]
        tail_rows[seq, 2:8] = jnp.zeros((6, D), F32)
        states.start()

    @pl.when(step == 8)
    def _():
        @pl.loop(0, 8)
        def _(n):
            here = pl.ds(pl.multiple_of(n * C, C), C)
            weights = w_all[:, :, 0:D].reshape(D, D).astype(BF16)
            qkvf[here, 0:D] = dot(hidden[here], weights).astype(BF16)

        for copy in save():
            copy.start()
        states.finish()
        first = edge_ref[0:1]
        state[...] = jnp.zeros_like(state)
        for n in range(4):
            use = jnp.where(tail_rows[n, 1:2] == first, 1.0, 0.0) * (n < seq).astype(F32)
            state[0:128] += use * tails[n].astype(F32)
            state[128:129] += use * tail_rows[n, 0:1]

    @pl.when(step == 12)
    def _():
        for piece in later:
            piece.third()

    @pl.when(step >= 9)
    def _():
        n = step - 9
        here = pl.ds(pl.multiple_of(n * C, C), C)
        attend_body(
            n, qkvf.at[here], col_ref[here], doc_ref[:, here].astype(F32), edge_ref,
            state, o_ref, p_ref, s_ref, z_ref, kept_ref,
        )

    @pl.when(step == 16)
    def _():
        for piece in later:
            piece.finish()
        main.drain_each()
        states.drain()
        for k in range(1, count):
            small_copy(k, at).wait_send()
        for copy in save():
            copy.wait()


def front(count, tokens, doc_ids, weights, vectors, bias):
    rows = tokens.shape[0]
    part = weights[0].shape[0]
    link = BF16 if part % 16 == 0 else F32
    once = lambda a: pl.BlockSpec(a.shape, lambda i: (0,) * a.ndim)
    early = lambda i: jnp.minimum(i, 7)
    late = lambda i: jnp.maximum(i - 9, 0)
    anywhere = pl.BlockSpec(memory_space=pl.ANY)
    vmem = pltpu.VMEM
    return pl.pallas_call(
        functools.partial(front_kernel, count),
        grid=(17,),
        in_specs=[rows_of(D, early), once(doc_ids)] + [once(a) for a in (*weights, *vectors, bias)],
        out_specs=[anywhere]
        + [rows_of(D, late)] * 4
        + [pl.BlockSpec((1, 128, D), lambda i: (late(i), 0, 0))]
        + [anywhere] * 4
        + [whole(8, D), whole(1, FF)],
        out_shape=[shape_of((rows, 4 * D), BF16), shape_of((rows, D), BF16)]
        + [shape_of((rows, D), F32)] * 3
        + [
            shape_of((8, 128, D), F32),
            shape_of((count, part, 4 * D), link),
            shape_of((count, part, D), link),
            shape_of((count, part, FF), link),
            shape_of((count, 4 * part, D), link),
            shape_of((8, D), F32),
            shape_of((1, FF), F32),
        ],
        scratch_shapes=[
            vmem((rows, 4 * D), BF16),
            vmem((rows, D), BF16),
            vmem((count, part, 4 * D), link),
            vmem((part, 4 * D), link),
            vmem((part, D), link),
            vmem((part, FF), link),
            vmem((4 * part, D), link),
            vmem((8, D), F32),
            vmem((count, 8, D), F32),
            vmem((rows, 128), F32),
            vmem((16, D), F32),
            vmem((136, D), F32),
            vmem((136, D), F32),
            vmem((4, 128, D), link),
            vmem((4, 8, D), F32),
        ]
        + gather_sems(count, True)
        + gather_sems(count, False) * 3
        + [
            pltpu.SemaphoreType.DMA((count,)),
            pltpu.SemaphoreType.DMA((count,)),
            pltpu.SemaphoreType.DMA((3, 2)),
            pltpu.SemaphoreType.DMA((3, 2)),
            pltpu.SemaphoreType.DMA((2,)),
        ],
        compiler_params=pltpu.CompilerParams(
            vmem_limit_bytes=LIMIT, collective_id=1, has_side_effects=True
        ),
        name="front",
    )(tokens, doc_ids, *weights, *vectors, bias)


ROOT = 0.7978845608028654
CUBE = 0.044715


def gelu_both(u):
    square = u * u
    bent = jnp.tanh(ROOT * u * (1.0 + CUBE * square))
    half = 0.5 * (1.0 + bent)
    slope = half + 0.5 * u * (1.0 - bent * bent) * (ROOT * (1.0 + 3.0 * CUBE * square))
    return u * half, slope


def forward_kernel(
    x_ref, o_ref, g_ref, small_ref, bias_ref, wo_ref, wh_ref, wr_ref,
    y_ref, dy_ref, do_ref, gwo_ref, gwh_ref, gwr_ref, gsmall_ref, gbias_ref, dz_buf,
):
    step = pl.program_id(0)

    @pl.when(step == 0)
    def _():
        for ref in (gwo_ref, gwh_ref, gwr_ref, gsmall_ref, gbias_ref):
            ref[...] = jnp.zeros_like(ref)

    attended, cot = o_ref[...], g_ref[...]
    middle = x_ref[...].astype(F32) + dot(attended, wo_ref[...])
    unit, scale = norm_parts(middle)
    hidden = (unit * small_ref[2:3] + small_ref[3:4]).astype(BF16)
    out = middle + small_ref[4:5]
    grad_hidden = jnp.zeros((x_ref.shape[0], D), F32)
    cot32 = cot.astype(F32)
    for j in range(4):
        cols = slice(j * 512, (j + 1) * 512)
        inner = dot(hidden, wh_ref[:, cols]) + bias_ref[0:1, cols]
        gated, slope = gelu_both(inner)
        active = gated.astype(BF16)
        out = out + dot(active, wr_ref[cols, :])
        gwr_ref[:, cols] += dot_tn(cot, active)
        grad = dot_nt(cot, wr_ref[cols, :]) * slope
        low = grad.astype(BF16)
        gbias_ref[0:1, cols] += jnp.sum(low.astype(F32), axis=0, keepdims=True)
        gwh_ref[:, cols] += dot_tn(hidden, low)
        grad_hidden = grad_hidden + dot_nt(low, wh_ref[:, cols])
    y_ref[...] = out.astype(BF16)
    gsmall_ref[2:3] += jnp.sum(grad_hidden * unit, axis=0, keepdims=True)
    gsmall_ref[3:4] += jnp.sum(grad_hidden, axis=0, keepdims=True)
    gsmall_ref[4:5] += jnp.sum(cot32, axis=0, keepdims=True)
    grad_middle = cot32 + norm_back(unit, scale, small_ref[2:3], grad_hidden)
    dy_ref[...] = grad_middle
    branch = grad_middle.astype(BF16)
    gwo_ref[...] += dot_tn(attended, branch)
    do_ref[...] = dot_nt(branch, wo_ref[...]).astype(BF16)


def row_kernel(
    qkvf_ref, do_ref, p_ref, s_ref, z_ref, kept_ref, col_ref, row_ref, edge_ref,
    dq_ref, r_ref, dn_ref, dz_ref, head_ref,
):
    step = pl.program_id(0)
    first = edge_ref[pl.ds(0, 1)]
    before = edge_ref[pl.ds(8 + jnp.maximum(step - 1, 0), 1)]
    last = jnp.where(step == 0, first, before)
    col = col_ref[...]
    vis = visible(col, row_ref[...])
    carried = wide(flag(col, last), 2)
    slots = jnp.exp(qkvf_ref[:, 3 * D :].astype(F32)).astype(BF16)
    own = wide(flag(col, first), 4)

    @pl.when(step == 0)
    def _():
        head_ref[...] = jnp.zeros_like(head_ref)
        head_ref[129:130] = first.astype(F32)

    for g in range(2):
        lanes = slice(g * GROUP, (g + 1) * GROUP)
        queries, keys, values = (
            qkvf_ref[:, part * D + g * GROUP : part * D + (g + 1) * GROUP] for part in range(3)
        )
        here, grads = slots[:, lanes], do_ref[:, lanes]
        probs, score, inverse = p_ref[:, lanes], s_ref[:, lanes], z_ref[:, lanes]
        back_mix = masked(dot_nt(stacked(grads), values), vis)
        back_reading = select(dot(back_mix, here))
        back_reading = back_reading + carried * dot_nt(
            grads, expand(kept_ref[0, 64:128, lanes]).astype(BF16)
        )
        back_probs = back_reading * inverse
        shared = back_probs * probs
        back_score = shared - probs * head_sums(shared)
        back_numer = back_score * inverse * SCALE
        back_total = -(shared + back_score * score) * inverse
        low = back_numer.astype(BF16)
        back_affinity = masked(dot_nt(stacked(low), here), vis)
        back_queries = select(dot(back_affinity, keys))
        back_queries = back_queries + carried * dot(
            low, expand(kept_ref[0, 0:64, lanes]).astype(BF16)
        )
        dq_ref[:, lanes] = back_queries.astype(BF16)
        reading = (probs * inverse).astype(BF16)
        r_ref[:, lanes] = reading
        dn_ref[:, lanes] = back_numer
        dz_ref[:, lanes] = back_total
        mine = own[:, lanes]
        head_ref[0:64, lanes] += compacted(dot_tn((mine * back_numer).astype(BF16), queries))
        head_ref[64:128, lanes] += compacted(
            dot_tn((mine * reading.astype(F32)).astype(BF16), grads)
        )
        head_ref[128:129, lanes] += jnp.sum(mine * back_total, axis=0, keepdims=True)


def column_kernel(
    x_ref, qkvf_ref, do_ref, dq_ref, r_ref, dn_ref, dz_ref, col_ref, row_ref, edge_ref, small_ref,
    start_ref, d_ref, gw_ref, state,
):
    step = pl.program_id(0)
    here_at = 7 - step

    @pl.when(step == 0)
    def _():
        state[...] = start_ref[...]
        gw_ref[...] = jnp.zeros_like(gw_ref)

    newest = edge_ref[15:16]
    after = edge_ref[pl.ds(jnp.minimum(here_at + 1, 7), 1)]
    following = jnp.where(step == 0, newest, after)
    first = edge_ref[pl.ds(here_at, 1)]
    col = col_ref[...]
    vis = visible_back(col, row_ref[...])
    carried = wide(flag(col, following), 2)
    own = wide(flag(col, first), 2)
    same = jnp.where(following == first, 1.0, 0.0)
    written = jnp.exp(qkvf_ref[:, 3 * D :].astype(F32))
    slots = written.astype(BF16)
    total_high, total_low = split(dz_ref[...])
    back_norm = dot(vis, total_high) + dot(vis, total_low)
    d_ref[:, 0:D] = dq_ref[...]
    left = lane_heads(C, 128) == 0
    for g in range(2):
        lanes = slice(g * GROUP, (g + 1) * GROUP)
        queries, keys, values = (
            qkvf_ref[:, part * D + g * GROUP : part * D + (g + 1) * GROUP] for part in range(3)
        )
        here, grads, reading = slots[:, lanes], do_ref[:, lanes], r_ref[:, lanes]
        numer_high, numer_low = split(dn_ref[:, lanes])
        key_state = expand(state[0:64, lanes]).astype(BF16)
        value_state = expand(state[64:128, lanes]).astype(BF16)
        apart = stacked(here)
        mix = masked(dot_nt(apart, reading), vis)
        back_values = select(dot(mix, grads)) + carried * dot(here, value_state)
        d_ref[:, 2 * D + g * GROUP : 2 * D + (g + 1) * GROUP] = back_values.astype(BF16)
        back_affinity = masked(dot_nt(apart, numer_high), vis)
        back_keys = select(dot(back_affinity, queries)) + carried * dot(here, key_state)
        d_ref[:, D + g * GROUP : D + (g + 1) * GROUP] = back_keys.astype(BF16)
        back_mix = masked(dot_nt(stacked(values), grads), vis)
        back_slots = back_norm[:, lanes] + select(dot(back_mix, reading))
        affinity = masked(dot_nt(stacked(keys), queries), vis)
        parts = []
        for p in range(2):
            pair = slice(p * 128, (p + 1) * 128)
            both = dot(
                affinity[p * 512 : (p + 1) * 512],
                jnp.concatenate([numer_high[:, pair], numer_low[:, pair]], axis=1),
            )
            both = both[:, :128] + both[:, 128:]
            parts.append(jnp.where(left, both[:C], both[C:]))
        back_slots = back_slots + jnp.concatenate(parts, axis=1)
        back_slots = back_slots + carried * (
            dot_nt(keys, key_state) + dot_nt(values, value_state) + state[128:129, lanes]
        )
        d_ref[:, 3 * D + g * GROUP : 3 * D + (g + 1) * GROUP] = (
            back_slots * written[:, lanes]
        ).astype(BF16)
        kept = same[:, lanes]
        state[0:64, lanes] = kept * state[0:64, lanes] + compacted(
            dot_tn((own * dn_ref[:, lanes]).astype(BF16), queries)
        )
        state[64:128, lanes] = kept * state[64:128, lanes] + compacted(
            dot_tn((own * reading.astype(F32)).astype(BF16), grads)
        )
        state[128:129, lanes] = kept * state[128:129, lanes] + jnp.sum(
            own * dz_ref[:, lanes], axis=0, keepdims=True
        )
    unit, _ = norm_parts(x_ref[...].astype(F32))
    hidden = (unit * small_ref[0:1] + small_ref[1:2]).astype(BF16)
    gw_ref[...] += dot_tn(hidden, d_ref[...])


def input_kernel(x_ref, d_ref, dy_ref, w_ref, small_ref, gi_ref, gsmall_ref):
    step = pl.program_id(0)

    @pl.when(step == 0)
    def _():
        gsmall_ref[...] = jnp.zeros_like(gsmall_ref)

    grad = dot_nt(d_ref[...], w_ref[...])
    unit, scale = norm_parts(x_ref[...].astype(F32))
    gsmall_ref[0:1] += jnp.sum(grad * unit, axis=0, keepdims=True)
    gsmall_ref[1:2] += jnp.sum(grad, axis=0, keepdims=True)
    gi_ref[...] = dy_ref[...] + norm_back(unit, scale, small_ref[0:1], grad)


def rows_of(lanes, order=lambda i: i):
    return pl.BlockSpec((C, lanes), lambda i: (order(i), 0))


def whole(*shape):
    return pl.BlockSpec(shape, lambda i: (0,) * len(shape))


def row_of(order=lambda i: i):
    return pl.BlockSpec((1, C), lambda i: (0, order(i)))


def shape_of(shape, kind):
    return jax.ShapeDtypeStruct(shape, kind)


PARAMS = pltpu.CompilerParams(vmem_limit_bytes=LIMIT)


def on_device(
    tokens, doc_ids, w_query, w_key, w_value, w_slots, w_output, w_hidden, w_return,
    gain_first, shift_first, gain_second, shift_second, bias_hidden, bias_return, cotangent,
):
    rows = tokens.shape[0]
    steps = rows // C
    seq = lax.axis_index("seq")
    count = lax.axis_size("fsdp")
    part = gain_first.shape[0]
    flat = lambda a: a.reshape(1, a.shape[0])
    qkvf, attended, probs, score, inverse, kept, w_qkvf, w_o, w_h, w_r, small, bias = front(
        count, tokens, doc_ids,
        (w_query, w_key, w_value, w_slots, w_output, w_hidden, w_return),
        [flat(a) for a in (gain_first, shift_first, gain_second, shift_second, bias_return)],
        flat(bias_hidden),
    )
    w_qkvf, w_o, w_h, w_r = (
        a.reshape(-1, a.shape[2]).astype(BF16) for a in (w_qkvf, w_o, w_h, w_r)
    )
    doc_col = jnp.broadcast_to(doc_ids.reshape(rows, 1), (rows, 128))
    pieces = doc_ids.reshape(steps, C)
    edges = jnp.concatenate([pieces[:, 0], pieces[:, -1]])
    edges = jnp.broadcast_to(edges[:, None], (2 * steps, D))

    out, grad_middle, grad_attended, g_wo, g_wh, g_wr, g_small, g_bias = pl.pallas_call(
        forward_kernel,
        grid=(steps,),
        in_specs=[rows_of(D)] * 3
        + [whole(8, D), whole(1, FF), whole(D, D), whole(D, FF), whole(FF, D)],
        out_specs=[rows_of(D)] * 3
        + [whole(D, D), whole(D, FF), whole(D, FF), whole(8, D), whole(1, FF)],
        out_shape=[
            shape_of((rows, D), BF16),
            shape_of((rows, D), F32),
            shape_of((rows, D), BF16),
            shape_of((D, D), F32),
            shape_of((D, FF), F32),
            shape_of((D, FF), F32),
            shape_of((8, D), F32),
            shape_of((1, FF), F32),
        ],
        scratch_shapes=[pltpu.VMEM((C, FF), BF16)],
        compiler_params=PARAMS,
        name="feed",
    )(tokens, attended, cotangent, small, bias, w_o, w_h, w_r)

    grad_q, reading, grad_numer, grad_total, head = pl.pallas_call(
        row_kernel,
        grid=(steps,),
        in_specs=[rows_of(4 * D)]
        + [rows_of(D)] * 4
        + [pl.BlockSpec((1, 128, D), lambda i: (i, 0, 0)), rows_of(128), row_of(), whole(16, D)],
        out_specs=[rows_of(D)] * 4 + [whole(136, D)],
        out_shape=[
            shape_of((rows, D), BF16),
            shape_of((rows, D), BF16),
            shape_of((rows, D), F32),
            shape_of((rows, D), F32),
            shape_of((136, D), F32),
        ],
        compiler_params=PARAMS,
        name="rowside",
    )(qkvf, grad_attended, probs, score, inverse, kept, doc_col, doc_ids, edges)
    heads = lax.all_gather(head, "seq")
    use = (jnp.arange(4) > seq) & (heads[:, 129, 0] == edges[-1, 0].astype(F32))
    finish = jnp.sum(jnp.where(use[:, None, None], heads, 0.0), axis=0)

    back = lambda i: steps - 1 - i
    grads, g_qkvf = pl.pallas_call(
        column_kernel,
        grid=(steps,),
        in_specs=[rows_of(D, back), rows_of(4 * D, back)]
        + [rows_of(D, back)] * 5
        + [rows_of(128, back), row_of(back), whole(16, D), whole(8, D), whole(136, D)],
        out_specs=[rows_of(4 * D, back), whole(D, 4 * D)],
        out_shape=[shape_of((rows, 4 * D), BF16), shape_of((D, 4 * D), F32)],
        scratch_shapes=[pltpu.VMEM((136, D), F32)],
        compiler_params=PARAMS,
        name="colside",
    )(
        tokens, qkvf, grad_attended, grad_q, reading, grad_numer, grad_total, doc_col, doc_ids,
        edges, small, finish,
    )

    grad_input, g_small_one = pl.pallas_call(
        input_kernel,
        grid=(steps,),
        in_specs=[rows_of(D), rows_of(4 * D), rows_of(D), whole(D, 4 * D), whole(8, D)],
        out_specs=[rows_of(D), whole(8, D)],
        out_shape=[shape_of((rows, D), F32), shape_of((8, D), F32)],
        compiler_params=PARAMS,
        name="inputside",
    )(tokens, grads, grad_middle, w_qkvf, small)

    scatter = lambda a, dim=0: lax.psum(
        lax.psum_scatter(a, "fsdp", scatter_dimension=dim, tiled=True), "seq"
    )
    g_qkvf = scatter(g_qkvf)
    g_wo, g_wh, g_wr = scatter(g_wo), scatter(g_wh), scatter(g_wr, 1).T
    vector = jnp.concatenate(
        [g_small_one[0], g_small_one[1], g_small[2], g_small[3], g_bias[0], g_small[4]]
    )
    vector = lax.psum(vector, ("fsdp", "seq"))
    at = lax.axis_index("fsdp")
    pick = lambda start, size: lax.dynamic_slice(vector, (start + at * size,), (size,))
    return (
        out,
        grad_input,
        g_qkvf[:, 0:D],
        g_qkvf[:, D : 2 * D],
        g_qkvf[:, 2 * D : 3 * D],
        g_qkvf[:, 3 * D :],
        g_wo,
        g_wh,
        g_wr,
        pick(0, part),
        pick(D, part),
        pick(2 * D, part),
        pick(3 * D, part),
        pick(4 * D, 4 * part),
        pick(4 * D + FF, part),
    )


def solution(mesh):
    tall, flat, one = P(("fsdp", "seq"), None), P("fsdp", None), P("fsdp")
    return jax.shard_map(
        on_device,
        mesh=mesh,
        in_specs=(tall, P("fsdp", "seq")) + (flat,) * 7 + (one,) * 6 + (tall,),
        out_specs=(tall, tall) + (flat,) * 7 + (one,) * 6,
        check_vma=False,
    )
```

```python
import functools

import jax
import jax.numpy as jnp
from jax import lax
from jax.experimental import pallas as pl
from jax.experimental.pallas import tpu as pltpu
from jax.sharding import PartitionSpec as P

D = 512
H = 8
M = 64
FF = 2048
C = 256
GROUP = 256
EPS = 1e-05
SCALE = 0.125
F32 = jnp.float32
BF16 = jnp.bfloat16
FEED_ROWS = 512
LIMIT = 62 * 1024 * 1024


def dot(a, b):
    return lax.dot_general(a, b, (((1,), (0,)), ((), ())), preferred_element_type=F32)


def dot_nt(a, b):
    return lax.dot_general(a, b, (((1,), (1,)), ((), ())), preferred_element_type=F32)


def dot_tn(a, b):
    return lax.dot_general(a, b, (((0,), (0,)), ((), ())), preferred_element_type=F32)


def lane_heads(rows, lanes):
    return lax.broadcasted_iota(jnp.int32, (rows, lanes), 1) // M


def stacked(values):
    heads = lane_heads(C, GROUP)
    zero = jnp.zeros_like(values)
    return jnp.concatenate([jnp.where(heads == h, values, zero) for h in range(4)], axis=0)


def select(values):
    heads = lane_heads(C, GROUP)
    out = values[3 * C :]
    for h in (2, 1, 0):
        out = jnp.where(heads == h, values[h * C : (h + 1) * C], out)
    return out


def masked(values, mask):
    return jnp.concatenate(
        [values[h * C : (h + 1) * C].astype(BF16) * mask for h in range(4)], axis=0
    )


def expand(compact):
    rows = lax.broadcasted_iota(jnp.int32, (GROUP, GROUP), 0) // M
    full = jnp.concatenate([compact] * 4, axis=0)
    return jnp.where(rows == lane_heads(GROUP, GROUP), full, jnp.zeros_like(full))


def compacted(full):
    heads = lane_heads(M, GROUP)
    out = full[3 * M :]
    for h in (2, 1, 0):
        out = jnp.where(heads == h, full[h * M : (h + 1) * M], out)
    return out


def split(values):
    high = values.astype(BF16)
    return high, (values - high.astype(F32)).astype(BF16)


def ones_block():
    rows = lax.broadcasted_iota(jnp.int32, (GROUP, GROUP), 0) // M
    return (rows == lane_heads(GROUP, GROUP)).astype(BF16)


def head_sums(values):
    high, low = split(values)
    ones = ones_block()
    return dot(high, ones) + dot(low, ones)


def head_max(values):
    left = lane_heads(C, 128) == 0
    out = []
    for p in range(2):
        pair = values[:, p * 128 : (p + 1) * 128]
        one = jnp.max(jnp.where(left, pair, -jnp.inf), axis=1, keepdims=True)
        two = jnp.max(jnp.where(left, -jnp.inf, pair), axis=1, keepdims=True)
        out.append(jnp.where(left, one, two))
    return jnp.concatenate(out, axis=1)


def wide(values, times):
    return jnp.concatenate([values] * times, axis=1)


def visible(doc_col, doc_row):
    same = wide(doc_col, 2) == doc_row
    here = lax.broadcasted_iota(jnp.int32, (C, C), 0)
    there = lax.broadcasted_iota(jnp.int32, (C, C), 1)
    return jnp.where(same & (here >= there), 1.0, 0.0).astype(BF16)


def visible_back(doc_col, doc_row):
    same = wide(doc_col, 2) == doc_row
    here = lax.broadcasted_iota(jnp.int32, (C, C), 0)
    there = lax.broadcasted_iota(jnp.int32, (C, C), 1)
    return jnp.where(same & (there >= here), 1.0, 0.0).astype(BF16)


def flag(doc_col, doc):
    return jnp.where(doc_col == doc[:, :128], 1.0, 0.0)


def norm_parts(values):
    centre = jnp.mean(values, axis=-1, keepdims=True)
    centred = values - centre
    spread = jnp.mean(centred * centred, axis=-1, keepdims=True)
    scale = lax.rsqrt(spread + EPS)
    return centred * scale, scale


def norm_back(unit, scale, gain, grad):
    inner = grad * gain
    return scale * (
        inner
        - jnp.mean(inner, axis=-1, keepdims=True)
        - unit * jnp.mean(inner * unit, axis=-1, keepdims=True)
    )


def groups(values):
    return values[:, :GROUP], values[:, GROUP:]


def state_terms(slots, left, right):
    one, two = [], []
    for g in range(2):
        lanes = slice(g * GROUP, (g + 1) * GROUP)
        both = dot_tn(slots[:, lanes], jnp.concatenate([left[:, lanes], right[:, lanes]], axis=1))
        one.append(compacted(both[:, :GROUP]))
        two.append(compacted(both[:, GROUP:]))
    return jnp.concatenate(one, axis=1), jnp.concatenate(two, axis=1)


def attend_body(
    n, qkvf_ref, col, row, edge_ref, state, o_ref, p_ref, s_ref, z_ref, kept_ref
):
    kept_ref[0] = state[0:128]
    first = edge_ref[pl.ds(0, 1)]
    before = edge_ref[pl.ds(8 + jnp.maximum(n - 1, 0), 1)]
    last = jnp.where(n == 0, first, before)
    newest = edge_ref[pl.ds(8 + n, 1)]
    vis = visible(col, row)
    carried = wide(flag(col, last), 2)
    written = jnp.exp(qkvf_ref[:, 3 * D :].astype(F32))
    slots = written.astype(BF16)
    norm = dot(vis, slots)
    for g in range(2):
        lanes = slice(g * GROUP, (g + 1) * GROUP)
        queries, keys, values = (
            qkvf_ref[:, part * D + g * GROUP : part * D + (g + 1) * GROUP] for part in range(3)
        )
        here = slots[:, lanes]
        affinity = masked(dot_nt(stacked(queries), keys), vis)
        numer = select(dot(affinity, here))
        numer = numer + carried * dot_nt(queries, expand(state[0:64, lanes]).astype(BF16))
        total = norm[:, lanes] + carried * state[128:129, lanes]
        inverse = 1.0 / total
        score = numer * inverse * SCALE
        grown = jnp.exp(score - head_max(score))
        probs = grown / head_sums(grown)
        reading = (probs * inverse).astype(BF16)
        mix = masked(dot_nt(stacked(reading), here), vis)
        mixed = select(dot(mix, values))
        mixed = mixed + carried * dot(reading, expand(state[64:128, lanes]).astype(BF16))
        o_ref[:, lanes] = mixed.astype(BF16)
        p_ref[:, lanes] = probs
        s_ref[:, lanes] = score
        z_ref[:, lanes] = inverse
    tail = (wide(flag(col, newest), 4) * written).astype(BF16)
    new_keys, new_values = state_terms(tail, qkvf_ref[:, D : 2 * D], qkvf_ref[:, 2 * D : 3 * D])
    same = jnp.where(last == newest, 1.0, 0.0)
    state[0:64] = same * state[0:64] + new_keys
    state[64:128] = same * state[64:128] + new_values
    state[128:129] = same * state[128:129] + jnp.sum(tail.astype(F32), axis=0, keepdims=True)


MESH_ID = pl.DeviceIdType.MESH


def places():
    seq, at = lax.axis_index("seq"), lax.axis_index("fsdp")
    core = lax.rem(seq, 2)
    return seq, at, seq + 1 - 2 * core, lax.rem(seq + 2, 4)


def push(src, dst, send, recv, **device):
    return pltpu.make_async_remote_copy(
        src_ref=src, dst_ref=dst, send_sem=send, recv_sem=recv,
        device_id=device, device_id_type=MESH_ID,
    )


def greet(count):
    seq, at, _, _ = places()
    barrier = pltpu.get_barrier_semaphore()
    for k in range(1, count):
        pl.semaphore_signal(barrier, inc=1, device_id={"fsdp": at ^ k}, device_id_type=MESH_ID)
    for k in range(1, 4):
        pl.semaphore_signal(barrier, inc=1, device_id={"seq": seq ^ k}, device_id_type=MESH_ID)
    pl.semaphore_wait(barrier, count - 1 + 3)


class Gather:
    def __init__(self, count, mine, held, sems):
        self.count, self.mine, self.held = count, mine, held
        self.across, self.core, self.chip, self.onward, self.local = sems
        self.seq, self.at, self.sibling, self.beside = places()
        self.quarter = held.shape[2] // 4

    def lanes(self, seq):
        return pl.ds(pl.multiple_of(seq * self.quarter, self.quarter), self.quarter)

    def part(self, owner, seq):
        return self.held.at[owner, :, self.lanes(seq)]

    def first(self, k):
        return push(
            self.mine.at[:, self.lanes(self.seq)], self.part(self.at, self.seq),
            self.across[0].at[k], self.across[1].at[k], fsdp=self.at ^ k,
        )

    def first_in(self, k):
        here = self.part(self.at ^ k, self.seq)
        return push(here, here, self.across[0].at[k], self.across[1].at[k], fsdp=self.at ^ k)

    def own(self):
        return pltpu.make_async_copy(
            self.mine.at[:, self.lanes(self.seq)], self.part(self.at, self.seq), self.local
        )

    def start(self):
        for k in range(1, self.count):
            self.first(k).start()
        self.own().start()

    def hop(self, sems, source, target, k):
        if k is None:
            ref, n = self.held.at[:, :, self.lanes(source)], 0
        else:
            ref, n = self.part(self.at ^ k, source), k
        return push(ref, ref, sems[0].at[n], sems[1].at[n], seq=target)

    def sent(self, n, k):
        if n == 0:
            return self.hop(self.core, self.seq, self.sibling, k)
        if n == 1:
            return self.hop(self.chip, self.seq, self.beside, k)
        return self.hop(self.onward, self.beside, self.sibling, k)

    def come(self, n, k):
        if n == 0:
            return self.hop(self.core, self.sibling, self.sibling, k)
        if n == 1:
            return self.hop(self.chip, self.beside, self.beside, k)
        return self.hop(self.onward, lax.rem(self.sibling + 2, 4), self.sibling, k)

    def second(self):
        self.own().wait()
        for k in range(1, self.count):
            self.first_in(k).wait_recv()
        self.sent(0, None).start()
        self.sent(1, None).start()

    def third(self):
        self.come(1, None).wait_recv()
        self.sent(2, None).start()

    def finish(self):
        for n in range(3):
            self.sent(n, None).wait_send()
        self.come(0, None).wait_recv()
        self.come(2, None).wait_recv()
        for k in range(1, self.count):
            self.first(k).wait_send()

    def second_each(self):
        for k in range(self.count):
            if k:
                self.first_in(k).wait_recv()
            else:
                self.own().wait()
            self.sent(0, k).start()
            self.sent(1, k).start()
        for k in range(self.count):
            self.come(1, k).wait_recv()
            self.sent(2, k).start()
        for k in range(self.count):
            self.come(0, k).wait_recv()
            self.come(2, k).wait_recv()

    def drain_each(self):
        for k in range(self.count):
            for n in range(3):
                self.sent(n, k).wait_send()
        for k in range(1, self.count):
            self.first(k).wait_send()


def gather_sems(count, each):
    n = count if each else 1
    pair = lambda size: [pltpu.SemaphoreType.DMA((size,)), pltpu.SemaphoreType.DMA((size,))]
    return pair(count) + pair(n) + pair(n) + pair(n) + [pltpu.SemaphoreType.DMA]


def bundle(refs):
    return (refs[0], refs[1]), (refs[2], refs[3]), (refs[4], refs[5]), (refs[6], refs[7]), refs[8]


class States:
    def __init__(self, big, small, sems):
        self.refs, self.sems = (big, small), sems
        self.seq, _, self.sibling, self.beside = places()

    def hop(self, n, source, target):
        out = []
        for m, ref in enumerate(self.refs):
            here = ref.at[source]
            out.append(push(here, here, self.sems[0].at[n, m], self.sems[1].at[n, m], seq=target))
        return out

    def start(self):
        for copy in self.hop(0, self.seq, self.sibling) + self.hop(1, self.seq, self.beside):
            copy.start()

    def finish(self):
        for copy in self.hop(1, self.beside, self.beside):
            copy.wait_recv()
        for copy in self.hop(2, self.beside, self.sibling):
            copy.start()
        for copy in self.hop(0, self.sibling, self.sibling):
            copy.wait_recv()
        for copy in self.hop(2, lax.rem(self.sibling + 2, 4), self.sibling):
            copy.wait_recv()

    def drain(self):
        for copy in (
            self.hop(0, self.seq, self.sibling)
            + self.hop(1, self.seq, self.beside)
            + self.hop(2, self.beside, self.sibling)
        ):
            copy.wait_send()


def doc_parts(doc_ref, col_ref, edge_ref):
    here = lax.broadcasted_iota(jnp.int32, (C, C), 0)
    there = lax.broadcasted_iota(jnp.int32, (C, C), 1)
    eye = jnp.where(here == there, 1.0, 0.0).astype(BF16)
    for n in range(doc_ref.shape[1] // C):
        row = doc_ref[:, n * C : (n + 1) * C].astype(F32)
        col_ref[n * C : (n + 1) * C] = dot_nt(eye, jnp.broadcast_to(row, (128, C)).astype(BF16))
        low = jnp.min(row, axis=1, keepdims=True)
        high = jnp.max(row, axis=1, keepdims=True)
        edge_ref[n : n + 1] = jnp.broadcast_to(low, (1, D))
        edge_ref[n + 8 : n + 9] = jnp.broadcast_to(high, (1, D))


def spread_small(vec_refs, bias_ref, out_ref):
    part = vec_refs[0].shape[1]

    def repeat(values):
        width = values.shape[1]
        rows = lax.broadcasted_iota(jnp.int32, (width, D), 0)
        lanes = lax.broadcasted_iota(jnp.int32, (width, D), 1)
        pick = jnp.where(lax.rem(lanes, width) == rows, 1.0, 0.0).astype(BF16)
        return dot(jnp.broadcast_to(values, (8, width)).astype(BF16), pick)[0:1]

    out_ref[...] = jnp.zeros_like(out_ref)
    for n, ref in enumerate(vec_refs):
        out_ref[n : n + 1] = repeat(ref[...])
    out_ref[5:6] = repeat(bias_ref[...])
    return part


def join_small(count, part, gathered, vec_ref, bias_ref):
    lanes = lax.broadcasted_iota(jnp.int32, (8, D), 1)
    total = jnp.zeros((8, D), F32)
    for f in range(count):
        total = jnp.where(lanes // part == f, gathered[f], total)
    vec_ref[...] = total
    for r in range(4):
        row = jnp.zeros((8, D), F32)
        for f in range(count):
            row = jnp.where((lanes + r * D) // (4 * part) == f, gathered[f], row)
        bias_ref[0:1, r * D : (r + 1) * D] = row[5:6]


def front_kernel(
    count, x_ref, doc_ref, wq_ref, wk_ref, wv_ref, ws_ref, wo_ref, wh_ref, wr_ref,
    v0, v1, v2, v3, v4, bias_in,
    qkvf_out, o_ref, p_ref, s_ref, z_ref, kept_ref, w_out, wo_out, wh_out, wr_out, vec_out, bias_out,
    qkvf, hidden, w_all, mine, mine_o, mine_h, mine_r, spread, smalls, col_ref, edge_ref, state,
    tail, tails, tail_rows, *sems,
):
    step = pl.program_id(0)
    seq, at, _, _ = places()
    link = mine.dtype
    first_sems, sems = bundle(sems[:9]), sems[9:]
    o_sems, sems = bundle(sems[:9]), sems[9:]
    h_sems, sems = bundle(sems[:9]), sems[9:]
    r_sems, sems = bundle(sems[:9]), sems[9:]
    small_send, small_recv, state_send, state_recv, out_sem = sems
    main = Gather(count, mine, w_all, first_sems)
    later = [
        Gather(count, mine_o, wo_out, o_sems),
        Gather(count, mine_h, wh_out, h_sems),
        Gather(count, mine_r, wr_out, r_sems),
    ]
    states = States(tails, tail_rows, (state_send, state_recv))

    def small_copy(k, owner):
        return push(
            spread, smalls.at[owner], small_send.at[k], small_recv.at[k], fsdp=at ^ k
        )

    def save():
        return (
            pltpu.make_async_copy(qkvf, qkvf_out, out_sem.at[0]),
            pltpu.make_async_copy(w_all, w_out, out_sem.at[1]),
        )

    @pl.when(step == 0)
    def _():
        greet(count)
        for n, ref in enumerate((wq_ref, wk_ref, wv_ref, ws_ref)):
            mine[:, n * D : (n + 1) * D] = ref[...].astype(BF16).astype(link)
        spread_small((v0, v1, v2, v3, v4), bias_in, spread)
        main.start()
        for k in range(1, count):
            small_copy(k, at).start()
        mine_o[...] = wo_ref[...].astype(BF16).astype(link)
        mine_h[...] = wh_ref[...].astype(BF16).astype(link)
        mine_r[...] = wr_ref[...].astype(BF16).astype(link)
        doc_parts(doc_ref, col_ref, edge_ref)
        tail[...] = jnp.zeros_like(tail)
        smalls[at] = spread[...]
        main.second_each()
        for k in range(1, count):
            small_copy(k, at ^ k).wait_recv()
        join_small(count, v0.shape[1], smalls, vec_out, bias_out)
        for piece in later:
            piece.start()

    @pl.when(step < 8)
    def _():
        unit, _ = norm_parts(x_ref[...].astype(F32))
        normed = (unit * vec_out[0:1] + vec_out[1:2]).astype(BF16)
        here = pl.ds(pl.multiple_of(step * C, C), C)
        hidden[here] = normed
        weights = w_all[:, :, D:].reshape(D, 3 * D).astype(BF16)
        rows = dot(normed, weights).astype(BF16)
        qkvf[here, D:] = rows
        slots = wide(flag(col_ref[here], edge_ref[15:16]), 4) * jnp.exp(rows[:, 2 * D :].astype(F32))
        slots = slots.astype(BF16)
        keys, values = state_terms(slots, rows[:, 0:D], rows[:, D : 2 * D])
        tail[0:64] += keys
        tail[64:128] += values
        tail[128:129] += jnp.sum(slots.astype(F32), axis=0, keepdims=True)

    @pl.when(step == 5)
    def _():
        for piece in later:
            piece.second()

    @pl.when(step == 7)
    def _():
        tails[seq] = tail[0:128].astype(link)
        tail_rows[seq, 0:1] = tail[128:129]
        tail_rows[seq, 1:2] = edge_ref[15:16]
        tail_rows[seq, 2:8] = jnp.zeros((6, D), F32)
        states.start()

    @pl.when(step == 8)
    def _():
        @pl.loop(0, 8)
        def _(n):
            here = pl.ds(pl.multiple_of(n * C, C), C)
            weights = w_all[:, :, 0:D].reshape(D, D).astype(BF16)
            qkvf[here, 0:D] = dot(hidden[here], weights).astype(BF16)

        for copy in save():
            copy.start()
        states.finish()
        first = edge_ref[0:1]
        state[...] = jnp.zeros_like(state)
        for n in range(4):
            use = jnp.where(tail_rows[n, 1:2] == first, 1.0, 0.0) * (n < seq).astype(F32)
            state[0:128] += use * tails[n].astype(F32)
            state[128:129] += use * tail_rows[n, 0:1]

    @pl.when(step == 12)
    def _():
        for piece in later:
            piece.third()

    @pl.when(step >= 9)
    def _():
        n = step - 9
        here = pl.ds(pl.multiple_of(n * C, C), C)
        attend_body(
            n, qkvf.at[here], col_ref[here], doc_ref[:, here].astype(F32), edge_ref,
            state, o_ref, p_ref, s_ref, z_ref, kept_ref,
        )

    @pl.when(step == 16)
    def _():
        for piece in later:
            piece.finish()
        main.drain_each()
        states.drain()
        for k in range(1, count):
            small_copy(k, at).wait_send()
        for copy in save():
            copy.wait()


def front(count, tokens, doc_ids, weights, vectors, bias):
    rows = tokens.shape[0]
    part = weights[0].shape[0]
    link = BF16 if part % 16 == 0 else F32
    once = lambda a: pl.BlockSpec(a.shape, lambda i: (0,) * a.ndim)
    early = lambda i: jnp.minimum(i, 7)
    late = lambda i: jnp.maximum(i - 9, 0)
    anywhere = pl.BlockSpec(memory_space=pl.ANY)
    vmem = pltpu.VMEM
    return pl.pallas_call(
        functools.partial(front_kernel, count),
        grid=(17,),
        in_specs=[rows_of(D, early), once(doc_ids)] + [once(a) for a in (*weights, *vectors, bias)],
        out_specs=[anywhere]
        + [rows_of(D, late)] * 4
        + [pl.BlockSpec((1, 128, D), lambda i: (late(i), 0, 0))]
        + [anywhere] * 4
        + [whole(8, D), whole(1, FF)],
        out_shape=[shape_of((rows, 4 * D), BF16), shape_of((rows, D), BF16)]
        + [shape_of((rows, D), F32)] * 3
        + [
            shape_of((8, 128, D), F32),
            shape_of((count, part, 4 * D), link),
            shape_of((count, part, D), link),
            shape_of((count, part, FF), link),
            shape_of((count, 4 * part, D), link),
            shape_of((8, D), F32),
            shape_of((1, FF), F32),
        ],
        scratch_shapes=[
            vmem((rows, 4 * D), BF16),
            vmem((rows, D), BF16),
            vmem((count, part, 4 * D), link),
            vmem((part, 4 * D), link),
            vmem((part, D), link),
            vmem((part, FF), link),
            vmem((4 * part, D), link),
            vmem((8, D), F32),
            vmem((count, 8, D), F32),
            vmem((rows, 128), F32),
            vmem((16, D), F32),
            vmem((136, D), F32),
            vmem((136, D), F32),
            vmem((4, 128, D), link),
            vmem((4, 8, D), F32),
        ]
        + gather_sems(count, True)
        + gather_sems(count, False) * 3
        + [
            pltpu.SemaphoreType.DMA((count,)),
            pltpu.SemaphoreType.DMA((count,)),
            pltpu.SemaphoreType.DMA((3, 2)),
            pltpu.SemaphoreType.DMA((3, 2)),
            pltpu.SemaphoreType.DMA((2,)),
        ],
        compiler_params=pltpu.CompilerParams(
            vmem_limit_bytes=LIMIT, collective_id=1, has_side_effects=True
        ),
        name="front",
    )(tokens, doc_ids, *weights, *vectors, bias)


ROOT = 0.7978845608028654
CUBE = 0.044715


def gelu_both(u):
    square = u * u
    bent = jnp.tanh(ROOT * u * (1.0 + CUBE * square))
    half = 0.5 * (1.0 + bent)
    slope = half + 0.5 * u * (1.0 - bent * bent) * (ROOT * (1.0 + 3.0 * CUBE * square))
    return u * half, slope


def forward_kernel(
    x_ref, o_ref, g_ref, small_ref, bias_ref, wo_ref, wh_ref, wr_ref,
    y_ref, dy_ref, do_ref, pack_ref, gsmall_ref, gwo_ref, gwh_ref, gwr_ref,
):
    step = pl.program_id(0)

    @pl.when(step == 0)
    def _():
        for ref in (gwo_ref, gwh_ref, gwr_ref, gsmall_ref):
            ref[...] = jnp.zeros_like(ref)

    attended, cot = o_ref[...], g_ref[...]
    middle = x_ref[...].astype(F32) + dot(attended, wo_ref[...])
    unit, scale = norm_parts(middle)
    hidden = (unit * small_ref[2:3] + small_ref[3:4]).astype(BF16)
    out = middle + small_ref[4:5]
    grad_hidden = jnp.zeros((x_ref.shape[0], D), F32)
    cot32 = cot.astype(F32)
    for j in range(4):
        cols = slice(j * 512, (j + 1) * 512)
        inner = dot(hidden, wh_ref[:, cols]) + bias_ref[0:1, cols]
        gated, slope = gelu_both(inner)
        active = gated.astype(BF16)
        out = out + dot(active, wr_ref[cols, :])
        gwr_ref[:, cols] += dot_tn(cot, active)
        grad = dot_nt(cot, wr_ref[cols, :]) * slope
        low = grad.astype(BF16)
        gsmall_ref[8 + j : 9 + j] += jnp.sum(low.astype(F32), axis=0, keepdims=True)
        gwh_ref[:, cols] += dot_tn(hidden, low)
        grad_hidden = grad_hidden + dot_nt(low, wh_ref[:, cols])
    y_ref[...] = out.astype(BF16)
    gsmall_ref[2:3] += jnp.sum(grad_hidden * unit, axis=0, keepdims=True)
    gsmall_ref[3:4] += jnp.sum(grad_hidden, axis=0, keepdims=True)
    gsmall_ref[4:5] += jnp.sum(cot32, axis=0, keepdims=True)
    grad_middle = cot32 + norm_back(unit, scale, small_ref[2:3], grad_hidden)
    dy_ref[...] = grad_middle
    branch = grad_middle.astype(BF16)
    gwo_ref[...] += dot_tn(attended, branch)
    do_ref[...] = dot_nt(branch, wo_ref[...]).astype(BF16)

    @pl.when(step == pl.num_programs(0) - 1)
    def _():
        _, count, part, _ = pack_ref.shape
        for q in range(4):
            hidden_part = gwh_ref[:, q * 512 : (q + 1) * 512].reshape(count, part, 512)
            pack_ref[q, :, :, 0:512] = hidden_part.astype(pack_ref.dtype)
            out_part = gwo_ref[:, q * 128 : (q + 1) * 128].reshape(count, part, 128)
            pack_ref[q, :, :, 512:640] = out_part.astype(pack_ref.dtype)
            turned = gwr_ref[q * 128 : (q + 1) * 128].T.reshape(count, 4, part, 128)
            for j in range(4):
                pack_ref[q, :, :, 640 + j * 128 : 768 + j * 128] = turned[:, j].astype(
                    pack_ref.dtype
                )


def row_body(
    n, qkvf_ref, do_ref, p_ref, s_ref, z_ref, kept_ref, col, row, edge_ref,
    dq_ref, r_ref, dn_ref, dz_ref, head_ref,
):
    first = edge_ref[pl.ds(0, 1)]
    before = edge_ref[pl.ds(8 + jnp.maximum(n - 1, 0), 1)]
    last = jnp.where(n == 0, first, before)
    vis = visible(col, row)
    carried = wide(flag(col, last), 2)
    slots = jnp.exp(qkvf_ref[:, 3 * D :].astype(F32)).astype(BF16)
    own = wide(flag(col, first), 4)
    for g in range(2):
        lanes = slice(g * GROUP, (g + 1) * GROUP)
        queries, keys, values = (
            qkvf_ref[:, part * D + g * GROUP : part * D + (g + 1) * GROUP] for part in range(3)
        )
        here, grads = slots[:, lanes], do_ref[:, lanes]
        probs, score, inverse = p_ref[:, lanes], s_ref[:, lanes], z_ref[:, lanes]
        back_mix = masked(dot_nt(stacked(grads), values), vis)
        back_reading = select(dot(back_mix, here))
        back_reading = back_reading + carried * dot_nt(
            grads, expand(kept_ref[0, 64:128, lanes]).astype(BF16)
        )
        back_probs = back_reading * inverse
        shared = back_probs * probs
        back_score = shared - probs * head_sums(shared)
        back_numer = back_score * inverse * SCALE
        back_total = -(shared + back_score * score) * inverse
        low = back_numer.astype(BF16)
        back_affinity = masked(dot_nt(stacked(low), here), vis)
        back_queries = select(dot(back_affinity, keys))
        back_queries = back_queries + carried * dot(
            low, expand(kept_ref[0, 0:64, lanes]).astype(BF16)
        )
        dq_ref[:, lanes] = back_queries.astype(BF16)
        reading = (probs * inverse).astype(BF16)
        r_ref[:, lanes] = reading
        dn_ref[:, lanes] = back_numer
        dz_ref[:, lanes] = back_total
        mine = own[:, lanes]
        head_ref[0:64, lanes] += compacted(dot_tn((mine * back_numer).astype(BF16), queries))
        head_ref[64:128, lanes] += compacted(
            dot_tn((mine * reading.astype(F32)).astype(BF16), grads)
        )
        head_ref[128:129, lanes] += jnp.sum(mine * back_total, axis=0, keepdims=True)


def column_body(
    n, g, qkvf_ref, do_ref, r_ref, dn_ref, dz_ref, col, row, edge_ref, state, d_ref
):
    newest = edge_ref[15:16]
    after = edge_ref[pl.ds(jnp.minimum(n + 1, 7), 1)]
    following = jnp.where(n == 7, newest, after)
    first = edge_ref[pl.ds(n, 1)]
    vis = visible_back(col, row)
    carried = wide(flag(col, following), 2)
    own = wide(flag(col, first), 2)
    kept = jnp.where(following == first, 1.0, 0.0)[:, :GROUP]
    left = lane_heads(C, 128) == 0

    def lanes_of(part):
        return pl.ds(pl.multiple_of(part * D + g * GROUP, GROUP), GROUP)

    lanes = lanes_of(0)
    queries, keys, values = (qkvf_ref[:, lanes_of(part)] for part in range(3))
    written = jnp.exp(qkvf_ref[:, lanes_of(3)].astype(F32))
    here = written.astype(BF16)
    back_total = dz_ref[:, lanes]
    total_high, total_low = split(back_total)
    back_norm = dot(vis, total_high) + dot(vis, total_low)
    grads, reading, back_numer = do_ref[:, lanes], r_ref[:, lanes], dn_ref[:, lanes]
    numer_high, numer_low = split(back_numer)
    key_state = expand(state[0:64, lanes]).astype(BF16)
    value_state = expand(state[64:128, lanes]).astype(BF16)
    apart = stacked(here)
    mix = masked(dot_nt(apart, reading), vis)
    back_values = select(dot(mix, grads)) + carried * dot(here, value_state)
    d_ref[:, lanes_of(2)] = back_values.astype(BF16)
    back_affinity = masked(dot_nt(apart, numer_high), vis)
    back_keys = select(dot(back_affinity, queries)) + carried * dot(here, key_state)
    d_ref[:, lanes_of(1)] = back_keys.astype(BF16)
    back_mix = masked(dot_nt(stacked(values), grads), vis)
    back_slots = back_norm + select(dot(back_mix, reading))
    affinity = masked(dot_nt(stacked(keys), queries), vis)
    parts = []
    for p in range(2):
        pair = slice(p * 128, (p + 1) * 128)
        both = dot(
            affinity[p * 512 : (p + 1) * 512],
            jnp.concatenate([numer_high[:, pair], numer_low[:, pair]], axis=1),
        )
        both = both[:, :128] + both[:, 128:]
        parts.append(jnp.where(left, both[:C], both[C:]))
    back_slots = back_slots + jnp.concatenate(parts, axis=1)
    back_slots = back_slots + carried * (
        dot_nt(keys, key_state) + dot_nt(values, value_state) + state[128:129, lanes]
    )
    d_ref[:, lanes_of(3)] = (back_slots * written).astype(BF16)
    state[0:64, lanes] = kept * state[0:64, lanes] + compacted(
        dot_tn((own * back_numer).astype(BF16), queries)
    )
    state[64:128, lanes] = kept * state[64:128, lanes] + compacted(
        dot_tn((own * reading.astype(F32)).astype(BF16), grads)
    )
    state[128:129, lanes] = kept * state[128:129, lanes] + jnp.sum(
        own * back_total, axis=0, keepdims=True
    )


class Scatter:
    def __init__(self, count, source, own, from_core, to_chip, from_chip, from_row, total, out, sems):
        self.count, self.source, self.own, self.out = count, source, own, out
        self.from_core, self.to_chip, self.from_chip = from_core, to_chip, from_chip
        self.to_row, self.from_row, self.total = to_chip, from_row, total
        (self.core, self.local, self.chip, self.row, self.last, self.done) = sems
        self.seq, self.at, self.sibling, self.beside = places()
        self.c = lax.rem(self.seq, 2)
        self.x = self.seq // 2

    def copy_core(self, n):
        return push(
            self.source.at[2 * n + 1 - self.c], self.from_core.at[n],
            self.core.at[0, n], self.core.at[1, n], seq=self.sibling,
        )

    def copy_own(self, n):
        return pltpu.make_async_copy(self.source.at[2 * n + self.c], self.own, self.local)

    def copy_chip(self):
        return push(
            self.to_chip, self.from_chip, self.chip.at[0], self.chip.at[1], seq=self.beside
        )

    def copy_row(self, k):
        return push(
            self.to_row.at[self.at ^ k], self.from_row.at[self.at],
            self.row.at[0, k], self.row.at[1, k], fsdp=self.at ^ k,
        )

    def row_in(self, k):
        here = self.from_row.at[self.at ^ k]
        return push(here, here, self.row.at[0, k], self.row.at[1, k], fsdp=self.at ^ k)

    def copy_done(self):
        return pltpu.make_async_copy(self.total, self.out.at[self.seq], self.done)

    def sent(self, n):
        if n == 2:
            here = self.out.at[self.beside]
            return push(here, here, self.last.at[0, 2], self.last.at[1, 2], seq=self.sibling)
        target = (self.sibling, self.beside)[n]
        return push(
            self.total, self.out.at[self.seq], self.last.at[0, n], self.last.at[1, n], seq=target
        )

    def come(self, n):
        if n == 2:
            here = self.out.at[lax.rem(self.sibling + 2, 4)]
            return push(here, here, self.last.at[0, 2], self.last.at[1, 2], seq=self.sibling)
        source = (self.sibling, self.beside)[n]
        here = self.out.at[source]
        return push(here, here, self.last.at[0, n], self.last.at[1, n], seq=source)

    def mine(self, n, f):
        if self.own is None:
            return self.source[2 * n + self.c, f].astype(F32)
        return self.own[f].astype(F32)

    def start(self):
        for n in range(2):
            self.copy_core(n).start()
        if self.own is not None:
            self.copy_own(1 - self.x).start()

    def second(self):
        for n in range(2):
            self.copy_core(n).wait_recv()
        n = 1 - self.x
        if self.own is not None:
            self.copy_own(n).wait()

        @pl.loop(0, self.count)
        def _(f):
            both = self.mine(n, f) + self.from_core[n, f].astype(F32)
            self.to_chip[f] = both.astype(self.to_chip.dtype)

        self.copy_chip().start()
        if self.own is not None:
            self.copy_own(self.x).start()

    def third(self):
        self.copy_chip().wait_recv()
        self.copy_chip().wait_send()
        n = self.x
        if self.own is not None:
            self.copy_own(n).wait()

        @pl.loop(0, self.count)
        def _(f):
            three = self.mine(n, f) + self.from_core[n, f].astype(F32) + self.from_chip[f].astype(F32)
            self.to_row[f] = three.astype(self.to_row.dtype)

        for k in range(1, self.count):
            self.copy_row(k).start()
        self.total[...] = (
            self.mine(n, self.at)
            + self.from_core[n, self.at].astype(F32)
            + self.from_chip[self.at].astype(F32)
        )

    def fourth(self):
        for k in range(1, self.count):
            self.row_in(k).wait_recv()
        total = self.total[...]
        for k in range(1, self.count):
            total = total + self.from_row[self.at ^ k].astype(F32)
        self.total[...] = total
        self.copy_done().start()
        self.sent(0).start()
        self.sent(1).start()

    def fifth(self):
        self.come(1).wait_recv()
        self.sent(2).start()

    def finish(self):
        self.come(0).wait_recv()
        self.come(2).wait_recv()
        self.copy_done().wait()
        for n in range(3):
            self.sent(n).wait_send()
        for n in range(2):
            self.copy_core(n).wait_send()
        for k in range(1, self.count):
            self.copy_row(k).wait_send()


def scatter_scratch(count, part, lanes, link, hbm):
    vmem, dma = pltpu.VMEM, pltpu.SemaphoreType.DMA
    block = (count, part, lanes)
    own = [vmem(block, link)] if hbm else []
    return (
        own
        + [vmem((2, *block), link)]
        + [vmem(block, link)] * 3
        + [vmem((part, lanes), F32)]
        + [dma((2, 2)), dma, dma((2,)), dma((2, count)), dma((2, 3)), dma]
    )


class SmallSum:
    def __init__(self, count, mine, from_seq, half, from_fsdp, sems):
        self.count, self.mine, self.from_seq = count, mine, from_seq
        self.half, self.from_fsdp, self.sems = half, from_fsdp, sems
        self.seq, self.at, _, _ = places()

    def over_seq(self, k, slot):
        return push(
            self.mine, self.from_seq.at[slot], self.sems[0].at[0, k], self.sems[0].at[1, k],
            seq=self.seq ^ k,
        )

    def over_fsdp(self, k, slot):
        return push(
            self.half, self.from_fsdp.at[slot], self.sems[1].at[0, k], self.sems[1].at[1, k],
            fsdp=self.at ^ k,
        )

    def start(self):
        for k in range(1, 4):
            self.over_seq(k, self.seq).start()
        self.from_seq[self.seq] = self.mine[...]

    def second(self):
        for k in range(1, 4):
            self.over_seq(k, self.seq ^ k).wait_recv()
        total = self.from_seq[0]
        for n in range(1, 4):
            total = total + self.from_seq[n]
        self.half[...] = total
        for k in range(1, self.count):
            self.over_fsdp(k, self.at).start()
        self.from_fsdp[self.at] = total

    def finish(self, out_ref):
        for k in range(1, self.count):
            self.over_fsdp(k, self.at ^ k).wait_recv()
        total = self.from_fsdp[0]
        for n in range(1, self.count):
            total = total + self.from_fsdp[n]
        out_ref[...] = total
        for k in range(1, 4):
            self.over_seq(k, self.seq).wait_send()
        for k in range(1, self.count):
            self.over_fsdp(k, self.at).wait_send()


def small_scratch(count, rows):
    vmem, dma = pltpu.VMEM, pltpu.SemaphoreType.DMA
    return [
        vmem((4, rows, D), F32), vmem((rows, D), F32), vmem((count, rows, D), F32),
        dma((2, 4)), dma((2, count)),
    ]


ROW_STEPS, COLUMN_STEPS = 8, 16
FIRST_COLUMN = ROW_STEPS + 1
FIRST_INPUT = FIRST_COLUMN + COLUMN_STEPS


def back_kernel(
    count, last_step, x_ref, xs_ref, qkvf_ref, do_ref, p_ref, s_ref, z_ref, kept_ref, dy_ref, doc_ref,
    small_ref, w_ref, ffg_ref, ffs_ref,
    gi_ref, ff_out, g0_out, g1_out, s1_out, s2_out,
    d_all, h_turned, reading, numer, total, col_ref, edge_ref, head, state, heads, head_rows,
    piece0, piece1, last_small, *rest,
):
    step = pl.program_id(0)
    seq, at, _, _ = places()
    link = piece0.dtype
    ff = Scatter(count, ffg_ref, *rest[:6], ff_out, rest[6:12])
    rest = rest[12:]
    first_piece = Scatter(count, piece0, None, *rest[:5], g0_out, rest[5:11])
    rest = rest[11:]
    second_piece = Scatter(count, piece1, None, *rest[:5], g1_out, rest[5:11])
    rest = rest[11:]
    small_one = SmallSum(count, ffs_ref, *rest[:3], rest[3:5])
    small_two = SmallSum(count, last_small, *rest[5:8], rest[8:10])
    states = States(heads, head_rows, (rest[10], rest[11]))

    @pl.when(step == 0)
    def _():
        greet(count)
        ff.start()
        small_one.start()
        doc_parts(doc_ref, col_ref, edge_ref)
        head[...] = jnp.zeros_like(head)
        last_small[...] = jnp.zeros_like(last_small)

    @pl.when(step < ROW_STEPS)
    def _():
        n = step
        here = pl.ds(pl.multiple_of(n * C, C), C)
        unit, _ = norm_parts(x_ref[...].astype(F32))
        h_turned[:, here] = (unit * small_ref[0:1] + small_ref[1:2]).astype(BF16).T
        row_body(
            n, qkvf_ref, do_ref, p_ref, s_ref, z_ref, kept_ref, col_ref[here],
            doc_ref[:, here].astype(F32), edge_ref,
            d_all.at[here, 0:D], reading.at[here], numer.at[here], total.at[here], head,
        )

    @pl.when(step == 2)
    def _():
        ff.second()
        small_one.second()

    @pl.when(step == 5)
    def _():
        small_one.finish(s1_out)

    @pl.when(step == ROW_STEPS - 1)
    def _():
        heads[seq] = head[0:128].astype(link)
        head_rows[seq, 0:1] = head[128:129]
        head_rows[seq, 1:2] = edge_ref[0:1]
        head_rows[seq, 2:8] = jnp.zeros((6, D), F32)
        states.start()

    def weight_grad(piece, n, lanes):
        grad = dot(h_turned[...], d_all[:, lanes])
        piece[n] = grad.reshape(count, D // count, GROUP).astype(link)

    @pl.when(step == ROW_STEPS)
    def _():
        weight_grad(piece0, 0, slice(0, GROUP))
        weight_grad(piece1, 0, slice(GROUP, D))
        states.finish()
        newest = edge_ref[15:16]
        state[...] = jnp.zeros_like(state)
        for n in range(4):
            use = jnp.where(head_rows[n, 1:2] == newest, 1.0, 0.0) * (n > seq).astype(F32)
            state[0:128] += use * heads[n].astype(F32)
            state[128:129] += use * head_rows[n, 0:1]

    @pl.when((step >= FIRST_COLUMN) & (step < FIRST_INPUT))
    def _():
        n = 7 - lax.rem(step - FIRST_COLUMN, 8)
        g = (step - FIRST_COLUMN) // 8
        here = pl.ds(pl.multiple_of(n * C, C), C)
        column_body(
            n, g, qkvf_ref, do_ref, reading.at[here], numer.at[here], total.at[here], col_ref[here],
            doc_ref[:, here].astype(F32), edge_ref, state, d_all.at[here],
        )

    @pl.when(step == FIRST_COLUMN + 2)
    def _():
        ff.third()

    @pl.when(step == FIRST_COLUMN + 7)
    def _():
        for w in range(1, 4):
            weight_grad(piece0, w, slice(w * D, w * D + GROUP))
        first_piece.start()

    @pl.when(step == FIRST_COLUMN + 9)
    def _():
        first_piece.second()

    @pl.when(step == FIRST_COLUMN + 12)
    def _():
        first_piece.third()

    @pl.when(step == FIRST_COLUMN + 15)
    def _():
        for w in range(1, 4):
            weight_grad(piece1, w, slice(w * D + GROUP, (w + 1) * D))
        second_piece.start()
        first_piece.fourth()
        ff.fourth()

    @pl.when(step >= FIRST_INPUT)
    def _():
        n = step - FIRST_INPUT
        size = xs_ref.shape[0]
        here = pl.ds(pl.multiple_of(n * size, size), size)
        grad = dot_nt(d_all[here], w_ref[...])
        unit, scale = norm_parts(xs_ref[...].astype(F32))
        last_small[0:1] += jnp.sum(grad * unit, axis=0, keepdims=True)
        last_small[1:2] += jnp.sum(grad, axis=0, keepdims=True)
        gi_ref[...] = dy_ref[...] + norm_back(unit, scale, small_ref[0:1], grad)

    @pl.when(step == FIRST_INPUT)
    def _():
        second_piece.second()
        first_piece.fifth()
        ff.fifth()

    @pl.when(step == last_step - 1)
    def _():
        second_piece.third()

    @pl.when(step == last_step)
    def _():
        small_two.start()
        ff.finish()
        first_piece.finish()
        small_two.second()
        second_piece.fourth()
        second_piece.fifth()
        small_two.finish(s2_out)
        second_piece.finish()
        states.drain()


def back(count, tokens, qkvf, do, probs, score, inverse, kept, dy, doc_ids, small, w_all, ffg, ffs):
    rows = tokens.shape[0]
    part, link = ffg.shape[2], ffg.dtype
    size = 512 if link == BF16 else 256
    last = FIRST_INPUT + rows // size - 1
    once = lambda a: pl.BlockSpec(a.shape, lambda i: (0,) * a.ndim)
    anywhere = pl.BlockSpec(memory_space=pl.ANY)
    vmem, dma = pltpu.VMEM, pltpu.SemaphoreType.DMA

    def early(i):
        return jnp.minimum(i, ROW_STEPS - 1)

    def both(i):
        turned = 7 - lax.rem(jnp.clip(i - FIRST_COLUMN, 0, COLUMN_STEPS - 1), 8)
        return jnp.where(i < ROW_STEPS, i, turned)

    late = lambda i: (jnp.maximum(i - FIRST_INPUT, 0), 0)
    tall = pl.BlockSpec((size, D), late)
    return pl.pallas_call(
        functools.partial(back_kernel, count, last),
        grid=(last + 1,),
        in_specs=[rows_of(D, early), tall, rows_of(4 * D, both), rows_of(D, both)]
        + [rows_of(D, early)] * 3
        + [pl.BlockSpec((1, 128, D), lambda i: (early(i), 0, 0)), tall]
        + [once(doc_ids), once(small), once(w_all), anywhere, once(ffs)],
        out_specs=[tall] + [anywhere] * 3 + [whole(16, D), whole(8, D)],
        out_shape=[
            shape_of((rows, D), F32),
            shape_of((4, part, 1152), F32),
            shape_of((4, part, GROUP), F32),
            shape_of((4, part, GROUP), F32),
            shape_of((16, D), F32),
            shape_of((8, D), F32),
        ],
        scratch_shapes=[
            vmem((rows, 4 * D), BF16),
            vmem((D, rows), BF16),
            vmem((rows, D), BF16),
            vmem((rows, D), F32),
            vmem((rows, D), F32),
            vmem((rows, 128), F32),
            vmem((16, D), F32),
            vmem((136, D), F32),
            vmem((136, D), F32),
            vmem((4, 128, D), link),
            vmem((4, 8, D), F32),
            vmem((4, count, part, GROUP), link),
            vmem((4, count, part, GROUP), link),
            vmem((8, D), F32),
        ]
        + scatter_scratch(count, part, 1152, link, True)
        + scatter_scratch(count, part, GROUP, link, False) * 2
        + small_scratch(count, 16)
        + small_scratch(count, 8)
        + [dma((3, 2)), dma((3, 2))],
        compiler_params=pltpu.CompilerParams(
            vmem_limit_bytes=LIMIT, collective_id=2, has_side_effects=True
        ),
        name="back",
    )(
        tokens, tokens, qkvf, do, probs, score, inverse, kept, dy, doc_ids, small, w_all, ffg, ffs
    )


def finish_kernel(count, part, ff_ref, g0_ref, g1_ref, s1_ref, s2_ref, *outs):
    at = lax.axis_index("fsdp")
    for n in range(4):
        outs[n][:, 0:GROUP] = g0_ref[n]
        outs[n][:, GROUP:D] = g1_ref[n]
        outs[4][:, n * 128 : (n + 1) * 128] = ff_ref[n, :, 512:640]
        outs[5][:, n * 512 : (n + 1) * 512] = ff_ref[n, :, 0:512]
        for j in range(4):
            outs[6][j * part : (j + 1) * part, n * 128 : (n + 1) * 128] = ff_ref[
                n, :, 640 + j * 128 : 768 + j * 128
            ]

    def pick(row, size):
        out = row(0, size)
        for f in range(1, count):
            out = jnp.where(at == f, row(f * size, size), out)
        return out

    def bias(start, size):
        r = start // D
        return s1_ref[8 + r : 9 + r, start - r * D : start - r * D + size]

    def row_of_sums(ref, n):
        return lambda start, size: ref[n : n + 1, start : start + size]

    outs[7][...] = pick(row_of_sums(s2_ref, 0), part)
    outs[8][...] = pick(row_of_sums(s2_ref, 1), part)
    outs[9][...] = pick(row_of_sums(s1_ref, 2), part)
    outs[10][...] = pick(row_of_sums(s1_ref, 3), part)
    outs[11][...] = pick(bias, 4 * part)
    outs[12][...] = pick(row_of_sums(s1_ref, 4), part)


def finish(count, part, ff, g0, g1, s1, s2):
    once = lambda shape: pl.BlockSpec(shape, lambda: (0,) * len(shape))
    shapes = [(part, D)] * 5 + [(part, FF), (4 * part, D)]
    shapes += [(1, part)] * 4 + [(1, 4 * part), (1, part)]
    args = (ff, g0, g1, s1, s2)
    return pl.pallas_call(
        functools.partial(finish_kernel, count, part),
        in_specs=[once(a.shape) for a in args],
        out_specs=[once(s) for s in shapes],
        out_shape=[shape_of(s, F32) for s in shapes],
        compiler_params=PARAMS,
        name="finish",
    )(*args)


def rows_of(lanes, order=lambda i: i):
    return pl.BlockSpec((C, lanes), lambda i: (order(i), 0))


def whole(*shape):
    return pl.BlockSpec(shape, lambda i: (0,) * len(shape))


def row_of(order=lambda i: i):
    return pl.BlockSpec((1, C), lambda i: (0, order(i)))


def shape_of(shape, kind):
    return jax.ShapeDtypeStruct(shape, kind)


PARAMS = pltpu.CompilerParams(vmem_limit_bytes=LIMIT)


def on_device(
    tokens, doc_ids, w_query, w_key, w_value, w_slots, w_output, w_hidden, w_return,
    gain_first, shift_first, gain_second, shift_second, bias_hidden, bias_return, cotangent,
):
    rows = tokens.shape[0]
    count = lax.axis_size("fsdp")
    part = gain_first.shape[0]
    flat = lambda a: a.reshape(1, a.shape[0])
    qkvf, attended, probs, score, inverse, kept, w_qkvf, w_o, w_h, w_r, small, bias = front(
        count, tokens, doc_ids,
        (w_query, w_key, w_value, w_slots, w_output, w_hidden, w_return),
        [flat(a) for a in (gain_first, shift_first, gain_second, shift_second, bias_return)],
        flat(bias_hidden),
    )
    link = w_qkvf.dtype
    w_qkvf, w_o, w_h, w_r = (
        a.reshape(-1, a.shape[2]).astype(BF16) for a in (w_qkvf, w_o, w_h, w_r)
    )
    tall = pl.BlockSpec((FEED_ROWS, D), lambda i: (i, 0))
    out, grad_middle, grad_attended, pack, ff_small = pl.pallas_call(
        forward_kernel,
        grid=(rows // FEED_ROWS,),
        in_specs=[tall] * 3
        + [whole(8, D), whole(1, FF), whole(D, D), whole(D, FF), whole(FF, D)],
        out_specs=[tall] * 3 + [whole(4, count, part, 1152), whole(16, D)],
        out_shape=[
            shape_of((rows, D), BF16),
            shape_of((rows, D), F32),
            shape_of((rows, D), BF16),
            shape_of((4, count, part, 1152), link),
            shape_of((16, D), F32),
        ],
        scratch_shapes=[
            pltpu.VMEM((D, D), F32),
            pltpu.VMEM((D, FF), F32),
            pltpu.VMEM((D, FF), F32),
        ],
        compiler_params=PARAMS,
        name="feed",
    )(tokens, attended, cotangent, small, bias, w_o, w_h, w_r)

    grad_input, ff, g0, g1, s1, s2 = back(
        count, tokens, qkvf, grad_attended, probs, score, inverse, kept, grad_middle, doc_ids,
        small, w_qkvf, pack, ff_small,
    )
    grads = finish(count, part, ff, g0, g1, s1, s2)
    return (out, grad_input, *grads[:7], *(a.reshape(-1) for a in grads[7:]))


def solution(mesh):
    tall, flat, one = P(("fsdp", "seq"), None), P("fsdp", None), P("fsdp")
    return jax.shard_map(
        on_device,
        mesh=mesh,
        in_specs=(tall, P("fsdp", "seq")) + (flat,) * 7 + (one,) * 6 + (tall,),
        out_specs=(tall, tall) + (flat,) * 7 + (one,) * 6,
        check_vma=False,
    )
```

```python
import functools

import jax
import jax.numpy as jnp
from jax import lax
from jax.experimental import pallas as pl
from jax.experimental.pallas import tpu as pltpu
from jax.sharding import PartitionSpec as P

D = 512
H = 8
M = 64
FF = 2048
C = 256
GROUP = 256
EPS = 1e-05
SCALE = 0.125
F32 = jnp.float32
BF16 = jnp.bfloat16
FEED_ROWS = 512
LIMIT = 62 * 1024 * 1024


def dot(a, b):
    return lax.dot_general(a, b, (((1,), (0,)), ((), ())), preferred_element_type=F32)


def dot_nt(a, b):
    return lax.dot_general(a, b, (((1,), (1,)), ((), ())), preferred_element_type=F32)


def dot_tn(a, b):
    return lax.dot_general(a, b, (((0,), (0,)), ((), ())), preferred_element_type=F32)


def lane_heads(rows, lanes):
    return lax.broadcasted_iota(jnp.int32, (rows, lanes), 1) // M


def stacked(values):
    heads = lane_heads(C, GROUP)
    zero = jnp.zeros_like(values)
    return jnp.concatenate([jnp.where(heads == h, values, zero) for h in range(4)], axis=0)


def select(values):
    heads = lane_heads(C, GROUP)
    out = values[3 * C :]
    for h in (2, 1, 0):
        out = jnp.where(heads == h, values[h * C : (h + 1) * C], out)
    return out


def masked(values, mask):
    return jnp.concatenate(
        [values[h * C : (h + 1) * C].astype(BF16) * mask for h in range(4)], axis=0
    )


def expand(compact):
    rows = lax.broadcasted_iota(jnp.int32, (GROUP, GROUP), 0) // M
    full = jnp.concatenate([compact] * 4, axis=0)
    return jnp.where(rows == lane_heads(GROUP, GROUP), full, jnp.zeros_like(full))


def compacted(full):
    heads = lane_heads(M, GROUP)
    out = full[3 * M :]
    for h in (2, 1, 0):
        out = jnp.where(heads == h, full[h * M : (h + 1) * M], out)
    return out


def split(values):
    high = values.astype(BF16)
    return high, (values - high.astype(F32)).astype(BF16)


def ones_block():
    rows = lax.broadcasted_iota(jnp.int32, (GROUP, GROUP), 0) // M
    return (rows == lane_heads(GROUP, GROUP)).astype(BF16)


def head_sums(values):
    high, low = split(values)
    ones = ones_block()
    return dot(high, ones) + dot(low, ones)


def head_max(values):
    left = lane_heads(C, 128) == 0
    out = []
    for p in range(2):
        pair = values[:, p * 128 : (p + 1) * 128]
        one = jnp.max(jnp.where(left, pair, -jnp.inf), axis=1, keepdims=True)
        two = jnp.max(jnp.where(left, -jnp.inf, pair), axis=1, keepdims=True)
        out.append(jnp.where(left, one, two))
    return jnp.concatenate(out, axis=1)


def wide(values, times):
    return jnp.concatenate([values] * times, axis=1)


def visible(doc_col, doc_row):
    same = wide(doc_col, 2) == doc_row
    here = lax.broadcasted_iota(jnp.int32, (C, C), 0)
    there = lax.broadcasted_iota(jnp.int32, (C, C), 1)
    return jnp.where(same & (here >= there), 1.0, 0.0).astype(BF16)


def visible_back(doc_col, doc_row):
    same = wide(doc_col, 2) == doc_row
    here = lax.broadcasted_iota(jnp.int32, (C, C), 0)
    there = lax.broadcasted_iota(jnp.int32, (C, C), 1)
    return jnp.where(same & (there >= here), 1.0, 0.0).astype(BF16)


def flag(doc_col, doc):
    return jnp.where(doc_col == doc[:, :128], 1.0, 0.0)


def norm_parts(values):
    centre = jnp.mean(values, axis=-1, keepdims=True)
    centred = values - centre
    spread = jnp.mean(centred * centred, axis=-1, keepdims=True)
    scale = lax.rsqrt(spread + EPS)
    return centred * scale, scale


def norm_back(unit, scale, gain, grad):
    inner = grad * gain
    return scale * (
        inner
        - jnp.mean(inner, axis=-1, keepdims=True)
        - unit * jnp.mean(inner * unit, axis=-1, keepdims=True)
    )


def groups(values):
    return values[:, :GROUP], values[:, GROUP:]


def state_terms(slots, left, right):
    one, two = [], []
    for g in range(2):
        lanes = slice(g * GROUP, (g + 1) * GROUP)
        both = dot_tn(slots[:, lanes], jnp.concatenate([left[:, lanes], right[:, lanes]], axis=1))
        one.append(compacted(both[:, :GROUP]))
        two.append(compacted(both[:, GROUP:]))
    return jnp.concatenate(one, axis=1), jnp.concatenate(two, axis=1)


def attend_body(
    n, qkvf_ref, col, row, edge_ref, state, o_ref, p_ref, s_ref, z_ref, kept_ref
):
    kept_ref[0] = state[0:128]
    first = edge_ref[pl.ds(0, 1)]
    before = edge_ref[pl.ds(8 + jnp.maximum(n - 1, 0), 1)]
    last = jnp.where(n == 0, first, before)
    newest = edge_ref[pl.ds(8 + n, 1)]
    vis = visible(col, row)
    carried = wide(flag(col, last), 2)
    written = jnp.exp(qkvf_ref[:, 3 * D :].astype(F32))
    slots = written.astype(BF16)
    norm = dot(vis, slots)
    for g in range(2):
        lanes = slice(g * GROUP, (g + 1) * GROUP)
        queries, keys, values = (
            qkvf_ref[:, part * D + g * GROUP : part * D + (g + 1) * GROUP] for part in range(3)
        )
        here = slots[:, lanes]
        affinity = masked(dot_nt(stacked(queries), keys), vis)
        numer = select(dot(affinity, here))
        numer = numer + carried * dot_nt(queries, expand(state[0:64, lanes]).astype(BF16))
        total = norm[:, lanes] + carried * state[128:129, lanes]
        inverse = 1.0 / total
        score = numer * inverse * SCALE
        grown = jnp.exp(score - head_max(score))
        probs = grown / head_sums(grown)
        reading = (probs * inverse).astype(BF16)
        mix = masked(dot_nt(stacked(reading), here), vis)
        mixed = select(dot(mix, values))
        mixed = mixed + carried * dot(reading, expand(state[64:128, lanes]).astype(BF16))
        o_ref[:, lanes] = mixed.astype(BF16)
        p_ref[:, lanes] = probs
        s_ref[:, lanes] = score
        z_ref[:, lanes] = inverse
    tail = (wide(flag(col, newest), 4) * written).astype(BF16)
    new_keys, new_values = state_terms(tail, qkvf_ref[:, D : 2 * D], qkvf_ref[:, 2 * D : 3 * D])
    same = jnp.where(last == newest, 1.0, 0.0)
    state[0:64] = same * state[0:64] + new_keys
    state[64:128] = same * state[64:128] + new_values
    state[128:129] = same * state[128:129] + jnp.sum(tail.astype(F32), axis=0, keepdims=True)


MESH_ID = pl.DeviceIdType.MESH


def places():
    seq, at = lax.axis_index("seq"), lax.axis_index("fsdp")
    core = lax.rem(seq, 2)
    return seq, at, seq + 1 - 2 * core, lax.rem(seq + 2, 4)


def push(src, dst, send, recv, **device):
    return pltpu.make_async_remote_copy(
        src_ref=src, dst_ref=dst, send_sem=send, recv_sem=recv,
        device_id=device, device_id_type=MESH_ID,
    )


def greet(count):
    seq, at, _, _ = places()
    barrier = pltpu.get_barrier_semaphore()
    for k in range(1, count):
        pl.semaphore_signal(barrier, inc=1, device_id={"fsdp": at ^ k}, device_id_type=MESH_ID)
    for k in range(1, 4):
        pl.semaphore_signal(barrier, inc=1, device_id={"seq": seq ^ k}, device_id_type=MESH_ID)
    pl.semaphore_wait(barrier, count - 1 + 3)


class Gather:
    def __init__(self, count, mine, held, base, width, four, sems):
        self.count, self.mine, self.held, self.four = count, mine, held, four
        self.far, self.near, self.core, self.chip, self.onward, self.local = sems
        self.seq, self.at, self.sibling, self.beside = places()
        self.base, self.share = base, width // (4 if four else 2)
        self.evens = range(0, count, 2)

    def lanes(self, seq):
        place = seq if self.four else lax.rem(seq, 2)
        return pl.ds(pl.multiple_of(self.base + place * self.share, 128), self.share)

    def part(self, k, seq):
        return self.held.at[self.at ^ k, :, self.lanes(seq)]

    def source(self, k):
        if k:
            return self.part(k, self.seq)
        return self.mine.at[:, self.lanes(self.seq)]

    def own(self):
        return pltpu.make_async_copy(self.source(0), self.part(0, self.seq), self.local)

    def over(self, sems, k, **device):
        return push(self.source(k), self.part(k, self.seq), sems[0].at[k], sems[1].at[k], **device)

    def come(self, sems, k, owner):
        here = self.part(owner, self.seq)
        return push(here, here, sems[0].at[k], sems[1].at[k], seq=self.sibling)

    def far_out(self, k):
        return push(
            self.source(0), self.part(0, self.seq), self.far[0].at[k], self.far[1].at[k],
            fsdp=self.at ^ k,
        )

    def far_in(self, k):
        return self.come(self.far, k, k)

    def near_out(self, k):
        return self.over(self.near, k, fsdp=self.at ^ 1)

    def near_in(self, k):
        return self.come(self.near, k, k ^ 1)

    def start(self):
        self.own().start()
        for k in self.evens[1:]:
            self.far_out(k).start()
        self.near_out(0).start()

    def second(self):
        for k in self.evens[1:]:
            self.far_in(k).wait_recv()
            self.near_out(k).start()

    def hop(self, sems, source, target):
        here = self.held.at[:, :, self.lanes(source)]
        return push(here, here, sems[0].at[0], sems[1].at[0], seq=target)

    def third(self):
        self.own().wait()
        for k in self.evens:
            self.near_in(k).wait_recv()
        self.hop(self.core, self.seq, self.sibling).start()
        if self.four:
            self.hop(self.chip, self.seq, self.beside).start()

    def fourth(self):
        self.hop(self.chip, self.beside, self.beside).wait_recv()
        self.hop(self.onward, self.beside, self.sibling).start()

    def finish(self):
        self.hop(self.core, self.sibling, self.sibling).wait_recv()
        self.hop(self.core, self.seq, self.sibling).wait_send()
        if self.four:
            self.hop(self.onward, lax.rem(self.sibling + 2, 4), self.sibling).wait_recv()
            self.hop(self.chip, self.seq, self.beside).wait_send()
            self.hop(self.onward, self.beside, self.sibling).wait_send()

    def core_out(self, k):
        return self.over(self.core, k, seq=self.sibling)

    def core_in(self, k):
        here = self.part(k, self.sibling)
        return push(here, here, self.core[0].at[k], self.core[1].at[k], seq=self.sibling)

    def at_once(self, between):
        self.start()
        self.core_out(0).start()
        for k in self.evens[1:]:
            self.far_in(k).wait_recv()
            self.near_out(k).start()
            self.core_out(k).start()
        between()
        for k in self.evens:
            self.near_in(k).wait_recv()
            self.core_out(k ^ 1).start()
        self.own().wait()
        for k in range(self.count):
            self.core_in(k).wait_recv()

    def drain(self, each=False):
        for k in self.evens:
            self.near_out(k).wait_send()
            if k:
                self.far_out(k).wait_send()
        if each:
            for k in range(self.count):
                self.core_out(k).wait_send()


def gather_sems(count, each):
    n = count if each else 1
    pair = lambda size: [pltpu.SemaphoreType.DMA((size,)), pltpu.SemaphoreType.DMA((size,))]
    return pair(count) + pair(count) + pair(n) + pair(1) + pair(1) + [pltpu.SemaphoreType.DMA]


def bundle(refs):
    return [(refs[2 * n], refs[2 * n + 1]) for n in range(5)] + [refs[10]]


class States:
    def __init__(self, big, small, sems):
        self.refs, self.sems = (big, small), sems
        self.seq, _, self.sibling, self.beside = places()

    def hop(self, n, source, target):
        out = []
        for m, ref in enumerate(self.refs):
            here = ref.at[source]
            out.append(push(here, here, self.sems[0].at[n, m], self.sems[1].at[n, m], seq=target))
        return out

    def start(self):
        for copy in self.hop(0, self.seq, self.sibling) + self.hop(1, self.seq, self.beside):
            copy.start()

    def finish(self):
        for copy in self.hop(1, self.beside, self.beside):
            copy.wait_recv()
        for copy in self.hop(2, self.beside, self.sibling):
            copy.start()
        for copy in self.hop(0, self.sibling, self.sibling):
            copy.wait_recv()
        for copy in self.hop(2, lax.rem(self.sibling + 2, 4), self.sibling):
            copy.wait_recv()

    def drain(self):
        for copy in (
            self.hop(0, self.seq, self.sibling)
            + self.hop(1, self.seq, self.beside)
            + self.hop(2, self.beside, self.sibling)
        ):
            copy.wait_send()


def doc_parts(doc_ref, col_ref, edge_ref):
    here = lax.broadcasted_iota(jnp.int32, (C, C), 0)
    there = lax.broadcasted_iota(jnp.int32, (C, C), 1)
    eye = jnp.where(here == there, 1.0, 0.0).astype(BF16)
    for n in range(doc_ref.shape[1] // C):
        row = doc_ref[:, n * C : (n + 1) * C].astype(F32)
        col_ref[n * C : (n + 1) * C] = dot_nt(eye, jnp.broadcast_to(row, (128, C)).astype(BF16))
        low = jnp.min(row, axis=1, keepdims=True)
        high = jnp.max(row, axis=1, keepdims=True)
        edge_ref[n : n + 1] = jnp.broadcast_to(low, (1, D))
        edge_ref[n + 8 : n + 9] = jnp.broadcast_to(high, (1, D))


def spread_small(vec_refs, bias_ref, out_ref):
    def repeat(values):
        width = values.shape[1]
        rows = lax.broadcasted_iota(jnp.int32, (width, 128), 0)
        lanes = lax.broadcasted_iota(jnp.int32, (width, 128), 1)
        pick = jnp.where(lax.rem(lanes, width) == rows, 1.0, 0.0).astype(BF16)
        return dot(jnp.broadcast_to(values, (8, width)).astype(BF16), pick)[0:1]

    out_ref[...] = jnp.zeros_like(out_ref)
    for n, ref in enumerate(vec_refs):
        out_ref[n : n + 1] = repeat(ref[...])
    for b in range(max(bias_ref.shape[1] // 128, 1)):
        out_ref[5 + b : 6 + b] = repeat(bias_ref[:, b * 128 : (b + 1) * 128])


def join_small(count, part, gathered, vec_ref, bias_ref):
    lanes = lax.broadcasted_iota(jnp.int32, (8, D), 1)
    total = jnp.zeros((8, D), F32)
    for f in range(count):
        total = jnp.where(lanes // part == f, wide(gathered[f], 4), total)
    vec_ref[...] = total
    size = 4 * part
    for r in range(4):
        at = lanes[0:1] + r * D
        row = jnp.zeros((1, D), F32)
        for f in range(r * D // size, -(-(r + 1) * D // size)):
            for b in range(max(size // 128, 1)):
                use = (at // size == f) & (lax.rem(at, size) // 128 == b)
                row = jnp.where(use, wide(gathered[f, 5 + b : 6 + b], 4), row)
        bias_ref[0:1, r * D : (r + 1) * D] = row


def front_kernel(
    count, x_ref, doc_ref, wq_ref, wk_ref, wv_ref, ws_ref, wo_ref, wh_ref, wr_ref,
    v0, v1, v2, v3, v4, bias_in,
    qkvf_out, o_ref, p_ref, s_ref, z_ref, kept_ref, w_out, wo_out, wh_out, wr_out, vec_out, bias_out,
    qkvf, hidden, w_all, mine, mine_o, mine_h, mine_r, spread, smalls, col_ref, edge_ref, state,
    tail, tails, tail_rows, *sems,
):
    step = pl.program_id(0)
    seq, at, _, _ = places()
    link = mine.dtype
    groups_of_sems = []
    for _ in range(5):
        groups_of_sems.append(bundle(sems[:11]))
        sems = sems[11:]
    small_send, small_recv, state_send, state_recv, out_sem = sems
    main = Gather(count, mine, w_all, D, 3 * D, False, groups_of_sems[0])
    q_piece = Gather(count, mine, w_all, 0, D, False, groups_of_sems[1])
    o_piece = Gather(count, mine_o, wo_out, 0, D, True, groups_of_sems[2])
    h_piece = Gather(count, mine_h, wh_out, 0, FF, True, groups_of_sems[3])
    r_piece = Gather(count, mine_r, wr_out, 0, D, False, groups_of_sems[4])
    later = (q_piece, o_piece, h_piece, r_piece)
    states = States(tails, tail_rows, (state_send, state_recv))

    def small_copy(k, owner):
        return push(
            spread, smalls.at[owner], small_send.at[k], small_recv.at[k], fsdp=at ^ k
        )

    def save():
        return (
            pltpu.make_async_copy(qkvf, qkvf_out, out_sem.at[0]),
            pltpu.make_async_copy(w_all, w_out, out_sem.at[1]),
        )

    @pl.when(step == 0)
    def _():
        greet(count)
        for n, ref in enumerate((wq_ref, wk_ref, wv_ref, ws_ref)):
            mine[:, n * D : (n + 1) * D] = ref[...].astype(BF16).astype(link)
        spread_small((v0, v1, v2, v3, v4), bias_in, spread)
        for k in range(1, count):
            small_copy(k, at).start()

        def between():
            mine_o[...] = wo_ref[...].astype(BF16).astype(link)
            mine_h[...] = wh_ref[...].astype(BF16).astype(link)
            mine_r[...] = wr_ref[...].astype(BF16).astype(link)
            doc_parts(doc_ref, col_ref, edge_ref)
            tail[...] = jnp.zeros_like(tail)
            smalls[at] = spread[...]
            for k in range(1, count):
                small_copy(k, at ^ k).wait_recv()
            join_small(count, v0.shape[1], smalls, vec_out, bias_out)
            for piece in later:
                piece.start()

        main.at_once(between)

    @pl.when(step < 8)
    def _():
        unit, _ = norm_parts(x_ref[...].astype(F32))
        normed = (unit * vec_out[0:1] + vec_out[1:2]).astype(BF16)
        here = pl.ds(pl.multiple_of(step * C, C), C)
        hidden[here] = normed
        weights = w_all[:, :, D:].reshape(D, 3 * D).astype(BF16)
        rows = dot(normed, weights).astype(BF16)
        qkvf[here, D:] = rows
        slots = wide(flag(col_ref[here], edge_ref[15:16]), 4) * jnp.exp(rows[:, 2 * D :].astype(F32))
        slots = slots.astype(BF16)
        keys, values = state_terms(slots, rows[:, 0:D], rows[:, D : 2 * D])
        tail[0:64] += keys
        tail[64:128] += values
        tail[128:129] += jnp.sum(slots.astype(F32), axis=0, keepdims=True)

    @pl.when(step == 1)
    def _():
        q_piece.second()
        o_piece.second()

    @pl.when(step == 4)
    def _():
        q_piece.third()
        o_piece.third()
        h_piece.second()

    @pl.when(step == 6)
    def _():
        o_piece.fourth()

    @pl.when(step == 7)
    def _():
        tails[seq] = tail[0:128].astype(link)
        tail_rows[seq, 0:1] = tail[128:129]
        tail_rows[seq, 1:2] = edge_ref[15:16]
        tail_rows[seq, 2:8] = jnp.zeros((6, D), F32)
        states.start()

    @pl.when(step == 8)
    def _():
        q_piece.finish()

        @pl.loop(0, 8)
        def _(n):
            here = pl.ds(pl.multiple_of(n * C, C), C)
            weights = w_all[:, :, 0:D].reshape(D, D).astype(BF16)
            qkvf[here, 0:D] = dot(hidden[here], weights).astype(BF16)

        for copy in save():
            copy.start()
        states.finish()
        first = edge_ref[0:1]
        state[...] = jnp.zeros_like(state)
        for n in range(4):
            use = jnp.where(tail_rows[n, 1:2] == first, 1.0, 0.0) * (n < seq).astype(F32)
            state[0:128] += use * tails[n].astype(F32)
            state[128:129] += use * tail_rows[n, 0:1]

    @pl.when(step == 9)
    def _():
        h_piece.third()
        r_piece.second()

    @pl.when(step == 13)
    def _():
        r_piece.third()
        h_piece.fourth()

    @pl.when(step >= 9)
    def _():
        n = step - 9
        here = pl.ds(pl.multiple_of(n * C, C), C)
        attend_body(
            n, qkvf.at[here], col_ref[here], doc_ref[:, here].astype(F32), edge_ref,
            state, o_ref, p_ref, s_ref, z_ref, kept_ref,
        )

    @pl.when(step == 16)
    def _():
        for piece in (o_piece, h_piece, r_piece):
            piece.finish()
        for piece in later:
            piece.drain()
        main.drain(True)
        states.drain()
        for k in range(1, count):
            small_copy(k, at).wait_send()
        for copy in save():
            copy.wait()


def front(count, tokens, doc_ids, weights, vectors, bias):
    rows = tokens.shape[0]
    part = weights[0].shape[0]
    link = BF16 if part % 16 == 0 else F32
    once = lambda a: pl.BlockSpec(a.shape, lambda i: (0,) * a.ndim)
    early = lambda i: jnp.minimum(i, 7)
    late = lambda i: jnp.maximum(i - 9, 0)
    anywhere = pl.BlockSpec(memory_space=pl.ANY)
    vmem = pltpu.VMEM
    return pl.pallas_call(
        functools.partial(front_kernel, count),
        grid=(17,),
        in_specs=[rows_of(D, early), once(doc_ids)] + [once(a) for a in (*weights, *vectors, bias)],
        out_specs=[anywhere]
        + [rows_of(D, late)] * 4
        + [pl.BlockSpec((1, 128, D), lambda i: (late(i), 0, 0))]
        + [anywhere] * 4
        + [whole(8, D), whole(1, FF)],
        out_shape=[shape_of((rows, 4 * D), BF16), shape_of((rows, D), BF16)]
        + [shape_of((rows, D), F32)] * 3
        + [
            shape_of((8, 128, D), F32),
            shape_of((count, part, 4 * D), link),
            shape_of((count, part, D), link),
            shape_of((count, part, FF), link),
            shape_of((count, 4 * part, D), link),
            shape_of((8, D), F32),
            shape_of((1, FF), F32),
        ],
        scratch_shapes=[
            vmem((rows, 4 * D), BF16),
            vmem((rows, D), BF16),
            vmem((count, part, 4 * D), link),
            vmem((part, 4 * D), link),
            vmem((part, D), link),
            vmem((part, FF), link),
            vmem((4 * part, D), link),
            vmem((8, 128), F32),
            vmem((count, 8, 128), F32),
            vmem((rows, 128), F32),
            vmem((16, D), F32),
            vmem((136, D), F32),
            vmem((136, D), F32),
            vmem((4, 128, D), link),
            vmem((4, 8, D), F32),
        ]
        + gather_sems(count, True)
        + gather_sems(count, False) * 4
        + [
            pltpu.SemaphoreType.DMA((count,)),
            pltpu.SemaphoreType.DMA((count,)),
            pltpu.SemaphoreType.DMA((3, 2)),
            pltpu.SemaphoreType.DMA((3, 2)),
            pltpu.SemaphoreType.DMA((2,)),
        ],
        compiler_params=pltpu.CompilerParams(
            vmem_limit_bytes=LIMIT, collective_id=1, has_side_effects=True
        ),
        name="front",
    )(tokens, doc_ids, *weights, *vectors, bias)


ROOT = 0.7978845608028654
CUBE = 0.044715


def gelu_both(u):
    square = u * u
    bent = jnp.tanh(ROOT * u * (1.0 + CUBE * square))
    half = 0.5 * (1.0 + bent)
    slope = half + 0.5 * u * (1.0 - bent * bent) * (ROOT * (1.0 + 3.0 * CUBE * square))
    return u * half, slope


def forward_kernel(
    x_ref, o_ref, g_ref, small_ref, bias_ref, wo_ref, wh_ref, wr_ref,
    y_ref, dy_ref, do_ref, pack_ref, pack_r_ref, gsmall_ref, gwo_ref, gwh_ref, gwr_ref,
):
    step = pl.program_id(0)

    @pl.when(step == 0)
    def _():
        for ref in (gwo_ref, gwh_ref, gwr_ref, gsmall_ref):
            ref[...] = jnp.zeros_like(ref)

    attended, cot = o_ref[...], g_ref[...]
    middle = x_ref[...].astype(F32) + dot(attended, wo_ref[...])
    unit, scale = norm_parts(middle)
    hidden = (unit * small_ref[2:3] + small_ref[3:4]).astype(BF16)
    out = middle + small_ref[4:5]
    grad_hidden = jnp.zeros((x_ref.shape[0], D), F32)
    cot32 = cot.astype(F32)
    for j in range(4):
        cols = slice(j * 512, (j + 1) * 512)
        inner = dot(hidden, wh_ref[:, cols]) + bias_ref[0:1, cols]
        gated, slope = gelu_both(inner)
        active = gated.astype(BF16)
        out = out + dot(active, wr_ref[cols, :])
        gwr_ref[:, cols] += dot_tn(cot, active)
        grad = dot_nt(cot, wr_ref[cols, :]) * slope
        low = grad.astype(BF16)
        gsmall_ref[8 + j : 9 + j] += jnp.sum(low.astype(F32), axis=0, keepdims=True)
        gwh_ref[:, cols] += dot_tn(hidden, low)
        grad_hidden = grad_hidden + dot_nt(low, wh_ref[:, cols])
    y_ref[...] = out.astype(BF16)
    gsmall_ref[2:3] += jnp.sum(grad_hidden * unit, axis=0, keepdims=True)
    gsmall_ref[3:4] += jnp.sum(grad_hidden, axis=0, keepdims=True)
    gsmall_ref[4:5] += jnp.sum(cot32, axis=0, keepdims=True)
    grad_middle = cot32 + norm_back(unit, scale, small_ref[2:3], grad_hidden)
    dy_ref[...] = grad_middle
    branch = grad_middle.astype(BF16)
    gwo_ref[...] += dot_tn(attended, branch)
    do_ref[...] = dot_nt(branch, wo_ref[...]).astype(BF16)

    @pl.when(step == pl.num_programs(0) - 1)
    def _():
        half, part = pack_ref.shape[3], pack_ref.shape[4]
        kind = pack_ref.dtype
        for q in range(4):
            x, c = q // 2, q % 2
            hidden_part = gwh_ref[:, q * 512 : (q + 1) * 512].reshape(half, 2, part, 512)
            out_part = gwo_ref[:, q * 128 : (q + 1) * 128].reshape(half, 2, part, 128)
            turned = gwr_ref[q * 128 : (q + 1) * 128].T.reshape(half, 2, 4, part, 128)
            for y in range(2):
                pack_ref[c, x, y, :, :, 0:512] = hidden_part[:, y].astype(kind)
                pack_ref[c, x, y, :, :, 512:640] = out_part[:, y].astype(kind)
                for j in range(4):
                    pack_r_ref[c, y, :, x, :, j * 128 : (j + 1) * 128] = turned[:, y, j].astype(kind)


def row_body(
    n, qkvf_ref, do_ref, p_ref, s_ref, z_ref, kept_ref, col, row, edge_ref,
    r_ref, dn_ref, dz_ref, head_ref,
):
    first = edge_ref[pl.ds(0, 1)]
    before = edge_ref[pl.ds(8 + jnp.maximum(n - 1, 0), 1)]
    last = jnp.where(n == 0, first, before)
    vis = visible(col, row)
    carried = wide(flag(col, last), 2)
    slots = jnp.exp(qkvf_ref[:, 3 * D :].astype(F32)).astype(BF16)
    own = wide(flag(col, first), 4)
    for g in range(2):
        lanes = slice(g * GROUP, (g + 1) * GROUP)
        queries, values = (
            qkvf_ref[:, part * D + g * GROUP : part * D + (g + 1) * GROUP] for part in (0, 2)
        )
        here, grads = slots[:, lanes], do_ref[:, lanes]
        probs, score, inverse = p_ref[:, lanes], s_ref[:, lanes], z_ref[:, lanes]
        back_mix = masked(dot_nt(stacked(grads), values), vis)
        back_reading = select(dot(back_mix, here))
        back_reading = back_reading + carried * dot_nt(
            grads, expand(kept_ref[0, 64:128, lanes]).astype(BF16)
        )
        back_probs = back_reading * inverse
        shared = back_probs * probs
        back_score = shared - probs * head_sums(shared)
        back_numer = back_score * inverse * SCALE
        back_total = -(shared + back_score * score) * inverse
        reading = (probs * inverse).astype(BF16)
        r_ref[:, lanes] = reading
        dn_ref[:, lanes] = back_numer
        dz_ref[:, lanes] = back_total
        mine = own[:, lanes]
        head_ref[0:64, lanes] += compacted(dot_tn((mine * back_numer).astype(BF16), queries))
        head_ref[64:128, lanes] += compacted(
            dot_tn((mine * reading.astype(F32)).astype(BF16), grads)
        )
        head_ref[128:129, lanes] += jnp.sum(mine * back_total, axis=0, keepdims=True)


def query_body(n, qkvf_ref, kept_ref, col, row, edge_ref, dn_ref, dq_ref):
    first = edge_ref[pl.ds(0, 1)]
    before = edge_ref[pl.ds(8 + jnp.maximum(n - 1, 0), 1)]
    last = jnp.where(n == 0, first, before)
    vis = visible(col, row)
    carried = wide(flag(col, last), 2)
    slots = jnp.exp(qkvf_ref[:, 3 * D :].astype(F32)).astype(BF16)
    for g in range(2):
        lanes = slice(g * GROUP, (g + 1) * GROUP)
        keys = qkvf_ref[:, D + g * GROUP : D + (g + 1) * GROUP]
        low = dn_ref[:, lanes].astype(BF16)
        back_affinity = masked(dot_nt(stacked(low), slots[:, lanes]), vis)
        back_queries = select(dot(back_affinity, keys))
        back_queries = back_queries + carried * dot(
            low, expand(kept_ref[0, 0:64, lanes]).astype(BF16)
        )
        dq_ref[:, lanes] = back_queries.astype(BF16)


def column_body(
    n, qkvf_ref, do_ref, r_ref, dn_ref, dz_ref, col, row, edge_ref, state, snap, snap_rows, d_ref
):
    newest = edge_ref[15:16]
    after = edge_ref[pl.ds(jnp.minimum(n + 1, 7), 1)]
    following = jnp.where(n == 7, newest, after)
    first = edge_ref[pl.ds(n, 1)]
    vis = visible_back(col, row)
    carried = wide(flag(col, following), 2)
    own = wide(flag(col, first), 2)
    kept = jnp.where(following == first, 1.0, 0.0)[:, :GROUP]
    snap[n] = state[0:128].astype(BF16)
    snap_rows[pl.ds(n, 1)] = state[128:129]
    for g in range(2):
        lanes = slice(g * GROUP, (g + 1) * GROUP)
        queries = qkvf_ref[:, lanes]
        here = jnp.exp(qkvf_ref[:, 3 * D + g * GROUP : 3 * D + (g + 1) * GROUP].astype(F32))
        here = here.astype(BF16)
        grads, reading, back_numer = do_ref[:, lanes], r_ref[:, lanes], dn_ref[:, lanes]
        key_state = expand(state[0:64, lanes]).astype(BF16)
        value_state = expand(state[64:128, lanes]).astype(BF16)
        apart = stacked(here)
        mix = masked(dot_nt(apart, reading), vis)
        back_values = select(dot(mix, grads)) + carried * dot(here, value_state)
        d_ref[:, 2 * D + g * GROUP : 2 * D + (g + 1) * GROUP] = back_values.astype(BF16)
        back_affinity = masked(dot_nt(apart, back_numer.astype(BF16)), vis)
        back_keys = select(dot(back_affinity, queries)) + carried * dot(here, key_state)
        d_ref[:, D + g * GROUP : D + (g + 1) * GROUP] = back_keys.astype(BF16)
        state[0:64, lanes] = kept * state[0:64, lanes] + compacted(
            dot_tn((own * back_numer).astype(BF16), queries)
        )
        state[64:128, lanes] = kept * state[64:128, lanes] + compacted(
            dot_tn((own * reading.astype(F32)).astype(BF16), grads)
        )
        state[128:129, lanes] = kept * state[128:129, lanes] + jnp.sum(
            own * dz_ref[:, lanes], axis=0, keepdims=True
        )


def slot_body(n, qkvf_ref, do_ref, r_ref, dn_ref, dz_ref, col, row, edge_ref, snap, snap_rows, d_ref):
    newest = edge_ref[15:16]
    after = edge_ref[pl.ds(jnp.minimum(n + 1, 7), 1)]
    following = jnp.where(n == 7, newest, after)
    vis = visible_back(col, row)
    carried = wide(flag(col, following), 2)
    left = lane_heads(C, 128) == 0
    total_high, total_low = split(dz_ref[...])
    back_norm = dot(vis, total_high) + dot(vis, total_low)
    norm_state = snap_rows[pl.ds(n, 1)]
    for g in range(2):
        lanes = slice(g * GROUP, (g + 1) * GROUP)
        queries, keys, values, logits = (
            qkvf_ref[:, part * D + g * GROUP : part * D + (g + 1) * GROUP] for part in range(4)
        )
        grads, reading = do_ref[:, lanes], r_ref[:, lanes]
        numer_high, numer_low = split(dn_ref[:, lanes])
        key_state = expand(snap[n, 0:64, lanes])
        value_state = expand(snap[n, 64:128, lanes])
        back_mix = masked(dot_nt(stacked(values), grads), vis)
        back_slots = back_norm[:, lanes] + select(dot(back_mix, reading))
        affinity = masked(dot_nt(stacked(keys), queries), vis)
        parts = []
        for p in range(2):
            pair = slice(p * 128, (p + 1) * 128)
            both = dot(
                affinity[p * 512 : (p + 1) * 512],
                jnp.concatenate([numer_high[:, pair], numer_low[:, pair]], axis=1),
            )
            both = both[:, :128] + both[:, 128:]
            parts.append(jnp.where(left, both[:C], both[C:]))
        back_slots = back_slots + jnp.concatenate(parts, axis=1)
        back_slots = back_slots + carried * (
            dot_nt(keys, key_state) + dot_nt(values, value_state) + norm_state[:, lanes]
        )
        d_ref[:, 3 * D + g * GROUP : 3 * D + (g + 1) * GROUP] = (
            back_slots * jnp.exp(logits.astype(F32))
        ).astype(BF16)


class Scatter:
    def __init__(self, count, source, own, axes, direct, out, buffers):
        self.axes, self.direct, self.out = axes, direct, out
        self.seq, self.at, self.sibling, self.beside = places()
        self.source, self.own = source, own
        self.core = lax.rem(self.seq, 2)
        self.total, self.local, self.last, self.done = buffers[:4]
        self.stages = []
        size = source.shape[0]
        base = 0
        for n, axis in enumerate(axes):
            ways = {"core": 2, "x": 2, "y": 2, "z": count // 2, "all": count}[axis]
            size = size // ways
            me = {
                "core": self.core, "x": self.seq // 2, "y": lax.rem(self.at, 2), "z": self.at // 2,
                "all": self.at,
            }[axis]
            held = source
            if own is not None and n > 0:
                held = own
            come, sems = buffers[4 + 2 * n], buffers[5 + 2 * n]
            self.stages.append((axis, ways, size, base, me, held, come, sems))
            if own is None or n > 0:
                base = base + me * size

    def copies(self, n):
        axis, ways, size, base, me, held, come, sems = self.stages[n]
        for k in range(1, ways):
            if axis in ("core", "x"):
                device = {"seq": self.sibling if axis == "core" else self.beside}
            else:
                device = {"fsdp": self.at ^ (2 * k if axis == "z" else k)}
            yield push(
                held.at[pl.ds(base + (me ^ k) * size, size)], come.at[k - 1],
                sems.at[0, k - 1], sems.at[1, k - 1], **device,
            )

    def copy_own(self):
        size = self.source.shape[0] // 2
        return pltpu.make_async_copy(
            self.source.at[pl.ds(self.core * size, size)], self.own, self.local
        )

    def start(self):
        for copy in self.copies(0):
            copy.start()
        if self.own is not None:
            self.copy_own().start()

    def advance(self, n):
        axis, ways, size, base, me, held, come, sems = self.stages[n]
        for copy in self.copies(n):
            copy.wait_recv()
        mine = held
        first = base + me * size
        if n == 0 and self.own is not None:
            self.copy_own().wait()
            mine, first = self.own, 0

        def added(slab):
            total = mine[first + slab].astype(F32)
            for k in range(1, ways):
                total = total + come[k - 1, slab].astype(F32)
            return total

        if n + 1 == len(self.stages):
            self.total[...] = added(0)
            self.copy_done().start()
            for copy in self.sent():
                copy.start()
            return

        @pl.loop(0, size)
        def _(slab):
            mine[first + slab] = added(slab).astype(mine.dtype)

        for copy in self.copies(n + 1):
            copy.start()

    def copy_done(self):
        return pltpu.make_async_copy(self.total, self.out.at[self.seq], self.done)

    def sent(self):
        other = lax.rem(self.sibling + 2, 4)
        for n, target in enumerate((self.sibling, self.beside, other)[: 3 if self.direct else 2]):
            yield push(
                self.total, self.out.at[self.seq], self.last.at[0, n], self.last.at[1, n], seq=target
            )

    def forwarded(self, source):
        here = self.out.at[source]
        return push(here, here, self.last.at[0, 2], self.last.at[1, 2], seq=self.sibling)

    def come_in(self, n, source):
        here = self.out.at[source]
        return push(here, here, self.last.at[0, n], self.last.at[1, n], seq=source)

    def forward(self):
        self.come_in(1, self.beside).wait_recv()
        self.forwarded(self.beside).start()

    def finish(self):
        other = lax.rem(self.sibling + 2, 4)
        self.come_in(0, self.sibling).wait_recv()
        if self.direct:
            self.come_in(1, self.beside).wait_recv()
        else:
            self.forwarded(self.beside).wait_send()
        self.forwarded(other).wait_recv()
        self.copy_done().wait()
        for copy in self.sent():
            copy.wait_send()
        for n in range(len(self.stages)):
            for copy in self.copies(n):
                copy.wait_send()


def scatter_scratch(count, part, lanes, link, axes, hbm):
    vmem, dma = pltpu.VMEM, pltpu.SemaphoreType.DMA
    size = 2 * 4 * count // 2
    out = [vmem((size // 2, part, lanes), link)] if hbm else []
    out += [vmem((part, lanes), F32), dma, dma((2, 3)), dma]
    for axis in axes:
        ways = {"core": 2, "x": 2, "y": 2, "z": count // 2, "all": count}[axis]
        size = size // ways
        out += [vmem((ways - 1, size, part, lanes), link), dma((2, ways - 1))]
    return out


OVER_X = ("core", "x", "y", "z")
OVER_Y = ("core", "y", "z", "x")
SHORT = ("core", "x", "all")


class SmallSum:
    def __init__(self, count, mine, from_seq, half, from_fsdp, sems):
        self.count, self.mine, self.from_seq = count, mine, from_seq
        self.half, self.from_fsdp, self.sems = half, from_fsdp, sems
        self.seq, self.at, _, _ = places()

    def over_seq(self, k, slot):
        return push(
            self.mine, self.from_seq.at[slot], self.sems[0].at[0, k], self.sems[0].at[1, k],
            seq=self.seq ^ k,
        )

    def over_fsdp(self, k, slot):
        return push(
            self.half, self.from_fsdp.at[slot], self.sems[1].at[0, k], self.sems[1].at[1, k],
            fsdp=self.at ^ k,
        )

    def start(self):
        for k in range(1, 4):
            self.over_seq(k, self.seq).start()
        self.from_seq[self.seq] = self.mine[...]

    def second(self):
        for k in range(1, 4):
            self.over_seq(k, self.seq ^ k).wait_recv()
        total = self.from_seq[0]
        for n in range(1, 4):
            total = total + self.from_seq[n]
        self.half[...] = total
        for k in range(1, self.count):
            self.over_fsdp(k, self.at).start()
        self.from_fsdp[self.at] = total

    def finish(self, out_ref):
        for k in range(1, self.count):
            self.over_fsdp(k, self.at ^ k).wait_recv()
        total = self.from_fsdp[0]
        for n in range(1, self.count):
            total = total + self.from_fsdp[n]
        out_ref[...] = total
        for k in range(1, 4):
            self.over_seq(k, self.seq).wait_send()
        for k in range(1, self.count):
            self.over_fsdp(k, self.at).wait_send()


def small_scratch(count, rows):
    vmem, dma = pltpu.VMEM, pltpu.SemaphoreType.DMA
    return [
        vmem((4, rows, D), F32), vmem((rows, D), F32), vmem((count, rows, D), F32),
        dma((2, 4)), dma((2, count)),
    ]


FIRST_QUERY, TURN = 8, 16
FIRST_COLUMN, FIRST_SLOT, FIRST_INPUT = 17, 25, 33


def back_kernel(
    count, last_step, x_ref, xs_ref, qkvf_ref, do_ref, p_ref, s_ref, z_ref, kept_ref, dy_ref, doc_ref,
    small_ref, w_ref, ffg_ref, ffr_ref, ffs_ref,
    gi_ref, ff_out, fr_out, q_out, kv_out, f_out, s1_out, s2_out,
    d_all, h_turned, reading, numer, total, col_ref, edge_ref, head, state, heads, head_rows,
    snap, snap_rows, q_piece, kv_piece, f_piece, last_small, *rest,
):
    step = pl.program_id(0)
    seq, at, _, _ = places()
    link = q_piece.dtype

    def take(size):
        nonlocal rest
        out, rest = rest[:size], rest[size:]
        return out

    (own,) = take(1)
    ff = Scatter(count, ffg_ref, own, OVER_X, False, ff_out, take(12))
    (own,) = take(1)
    fr = Scatter(count, ffr_ref, own, OVER_Y, False, fr_out, take(12))
    for_q = Scatter(count, q_piece, None, OVER_X, False, q_out, take(12))
    for_kv = Scatter(count, kv_piece, None, OVER_X, False, kv_out, take(12))
    for_f = Scatter(count, f_piece, None, SHORT, True, f_out, take(10))
    small_one = SmallSum(count, ffs_ref, *take(3), take(2))
    small_two = SmallSum(count, last_small, *take(3), take(2))
    states = States(heads, head_rows, take(2))

    def chunk(first, turned=False):
        n = step - first
        n = 7 - n if turned else n
        here = pl.ds(pl.multiple_of(n * C, C), C)
        return n, here, col_ref[here], doc_ref[:, here].astype(F32)

    def weight_grad(piece, d_lanes, lanes, short=False):
        grad = dot(h_turned[...], d_all[:, d_lanes])
        half, part = count // 2, piece.shape[1]
        for q in range(4):
            x, c = q // 2, q % 2
            share = grad[:, q * 128 : (q + 1) * 128].reshape(half, 2, part, 128).astype(link)
            if short:
                first = (c * 2 + x) * count
                piece[first : first + count, :, lanes] = share.reshape(count, part, 128)
                continue
            for y in range(2):
                first = ((c * 2 + x) * 2 + y) * half
                piece[first : first + half, :, lanes] = share[:, y]

    @pl.when(step == 0)
    def _():
        greet(count)
        ff.start()
        fr.start()
        small_one.start()
        doc_parts(doc_ref, col_ref, edge_ref)
        head[...] = jnp.zeros_like(head)
        last_small[...] = jnp.zeros_like(last_small)

    @pl.when(step < FIRST_QUERY)
    def _():
        n, here, col, row = chunk(0)
        unit, _ = norm_parts(x_ref[...].astype(F32))
        h_turned[:, here] = (unit * small_ref[0:1] + small_ref[1:2]).astype(BF16).T
        row_body(
            n, qkvf_ref, do_ref, p_ref, s_ref, z_ref, kept_ref, col, row, edge_ref,
            reading.at[here], numer.at[here], total.at[here], head,
        )

    @pl.when(step == 3)
    def _():
        ff.advance(0)
        fr.advance(0)
        small_one.second()

    @pl.when(step == 6)
    def _():
        small_one.finish(s1_out)

    @pl.when(step == FIRST_QUERY - 1)
    def _():
        heads[seq] = head[0:128].astype(link)
        head_rows[seq, 0:1] = head[128:129]
        head_rows[seq, 1:2] = edge_ref[0:1]
        head_rows[seq, 2:8] = jnp.zeros((6, D), F32)
        states.start()

    @pl.when((step >= FIRST_QUERY) & (step < TURN))
    def _():
        n, here, col, row = chunk(FIRST_QUERY)
        query_body(n, qkvf_ref, kept_ref, col, row, edge_ref, numer.at[here], d_all.at[here, 0:D])

    @pl.when(step == FIRST_QUERY + 1)
    def _():
        fr.advance(1)

    @pl.when(step == FIRST_QUERY + 4)
    def _():
        ff.advance(1)

    @pl.when(step == TURN)
    def _():
        weight_grad(q_piece, slice(0, D), slice(0, 128))
        for_q.start()
        states.finish()
        newest = edge_ref[15:16]
        state[...] = jnp.zeros_like(state)
        for n in range(4):
            use = jnp.where(head_rows[n, 1:2] == newest, 1.0, 0.0) * (n > seq).astype(F32)
            state[0:128] += use * heads[n].astype(F32)
            state[128:129] += use * head_rows[n, 0:1]

    @pl.when((step >= FIRST_COLUMN) & (step < FIRST_SLOT))
    def _():
        n, here, col, row = chunk(FIRST_COLUMN, True)
        column_body(
            n, qkvf_ref, do_ref, reading.at[here], numer.at[here], total.at[here], col, row, edge_ref,
            state, snap, snap_rows, d_all.at[here],
        )

    @pl.when(step == FIRST_COLUMN)
    def _():
        ff.advance(2)
        for_q.advance(0)

    @pl.when(step == FIRST_COLUMN + 1)
    def _():
        fr.advance(2)

    @pl.when(step == FIRST_COLUMN + 2)
    def _():
        for_q.advance(1)

    @pl.when(step == FIRST_COLUMN + 4)
    def _():
        fr.advance(3)
        for_q.advance(2)

    @pl.when(step == FIRST_COLUMN + 5)
    def _():
        ff.advance(3)

    @pl.when(step == FIRST_COLUMN + 6)
    def _():
        for_q.advance(3)
        fr.forward()

    @pl.when(step == FIRST_COLUMN + 7)
    def _():
        weight_grad(kv_piece, slice(D, 2 * D), slice(0, 128))
        weight_grad(kv_piece, slice(2 * D, 3 * D), slice(128, 256))
        for_kv.start()
        ff.forward()

    @pl.when((step >= FIRST_SLOT) & (step < FIRST_INPUT))
    def _():
        n, here, col, row = chunk(FIRST_SLOT, True)
        slot_body(
            n, qkvf_ref, do_ref, reading.at[here], numer.at[here], total.at[here], col, row, edge_ref,
            snap, snap_rows, d_all.at[here],
        )

    @pl.when(step == FIRST_SLOT)
    def _():
        for_kv.advance(0)
        for_q.forward()

    @pl.when(step == FIRST_SLOT + 3)
    def _():
        for_kv.advance(1)

    @pl.when(step == FIRST_SLOT + 5)
    def _():
        for_kv.advance(2)

    @pl.when(step == FIRST_SLOT + 7)
    def _():
        weight_grad(f_piece, slice(3 * D, 4 * D), slice(0, 128), True)
        for_f.start()
        for_kv.advance(3)

    @pl.when(step >= FIRST_INPUT)
    def _():
        n = step - FIRST_INPUT
        size = xs_ref.shape[0]
        here = pl.ds(pl.multiple_of(n * size, size), size)
        grad = dot_nt(d_all[here], w_ref[...])
        unit, scale = norm_parts(xs_ref[...].astype(F32))
        last_small[0:1] += jnp.sum(grad * unit, axis=0, keepdims=True)
        last_small[1:2] += jnp.sum(grad, axis=0, keepdims=True)
        gi_ref[...] = dy_ref[...] + norm_back(unit, scale, small_ref[0:1], grad)

    @pl.when(step == FIRST_INPUT)
    def _():
        for_f.advance(0)
        for_kv.forward()

    @pl.when(step == last_step - 1)
    def _():
        for_f.advance(1)

    @pl.when(step == last_step)
    def _():
        small_two.start()
        for piece in (ff, fr, for_q, for_kv):
            piece.finish()
        states.drain()
        small_two.second()
        for_f.advance(2)
        small_two.finish(s2_out)
        for_f.finish()


def back(
    count, tokens, qkvf, do, probs, score, inverse, kept, dy, doc_ids, small, w_all, ffg, ffr, ffs
):
    rows = tokens.shape[0]
    part, link = ffg.shape[1], ffg.dtype
    size = 512 if link == BF16 else 256
    last = FIRST_INPUT + rows // size - 1
    once = lambda a: pl.BlockSpec(a.shape, lambda i: (0,) * a.ndim)
    anywhere = pl.BlockSpec(memory_space=pl.ANY)
    vmem, dma = pltpu.VMEM, pltpu.SemaphoreType.DMA

    def early(i):
        return jnp.minimum(i, FIRST_QUERY - 1)

    def twice(i):
        return jnp.where(i < FIRST_QUERY, i, jnp.clip(i - FIRST_QUERY, 0, 7))

    def always(i):
        turned = 7 - lax.rem(jnp.clip(i - FIRST_COLUMN, 0, 15), 8)
        return jnp.where(i < TURN, twice(i), turned)

    def both(i):
        turned = 7 - lax.rem(jnp.clip(i - FIRST_COLUMN, 0, 15), 8)
        return jnp.where(i < FIRST_QUERY, i, turned)

    late = lambda i: (jnp.maximum(i - FIRST_INPUT, 0), 0)
    tall = pl.BlockSpec((size, D), late)
    slabs = 4 * count
    return pl.pallas_call(
        functools.partial(back_kernel, count, last),
        grid=(last + 1,),
        in_specs=[rows_of(D, early), tall, rows_of(4 * D, always), rows_of(D, both)]
        + [rows_of(D, early)] * 3
        + [pl.BlockSpec((1, 128, D), lambda i: (twice(i), 0, 0)), tall]
        + [once(doc_ids), once(small), once(w_all), anywhere, anywhere, once(ffs)],
        out_specs=[tall] + [anywhere] * 5 + [whole(16, D), whole(8, D)],
        out_shape=[
            shape_of((rows, D), F32),
            shape_of((4, part, 640), F32),
            shape_of((4, part, D), F32),
            shape_of((4, part, 128), F32),
            shape_of((4, part, 256), F32),
            shape_of((4, part, 128), F32),
            shape_of((16, D), F32),
            shape_of((8, D), F32),
        ],
        scratch_shapes=[
            vmem((rows, 4 * D), BF16),
            vmem((D, rows), BF16),
            vmem((rows, D), BF16),
            vmem((rows, D), F32),
            vmem((rows, D), F32),
            vmem((rows, 128), F32),
            vmem((16, D), F32),
            vmem((136, D), F32),
            vmem((136, D), F32),
            vmem((4, 128, D), link),
            vmem((4, 8, D), F32),
            vmem((8, 128, D), BF16),
            vmem((8, D), F32),
            vmem((slabs, part, 128), link),
            vmem((slabs, part, 256), link),
            vmem((slabs, part, 128), link),
            vmem((8, D), F32),
        ]
        + scatter_scratch(count, part, 640, link, OVER_X, True)
        + scatter_scratch(count, part, D, link, OVER_Y, True)
        + scatter_scratch(count, part, 128, link, OVER_X, False)
        + scatter_scratch(count, part, 256, link, OVER_X, False)
        + scatter_scratch(count, part, 128, link, SHORT, False)
        + small_scratch(count, 16)
        + small_scratch(count, 8)
        + [dma((3, 2)), dma((3, 2))],
        compiler_params=pltpu.CompilerParams(
            vmem_limit_bytes=LIMIT, collective_id=2, has_side_effects=True
        ),
        name="back",
    )(
        tokens, tokens, qkvf, do, probs, score, inverse, kept, dy, doc_ids, small, w_all, ffg, ffr,
        ffs,
    )


def finish_kernel(count, part, gi_ref, ff_ref, fr_ref, q_ref, kv_ref, f_ref, s1_ref, s2_ref, gi_out, *outs):
    at = lax.axis_index("fsdp")
    gi_out[...] = gi_ref[...]

    def pick(row, size):
        out = row(0, size)
        for f in range(1, count):
            out = jnp.where(at == f, row(f * size, size), out)
        return out

    def bias(start, size):
        r = start // D
        return s1_ref[8 + r : 9 + r, start - r * D : start - r * D + size]

    def row_of_sums(ref, n):
        return lambda start, size: ref[n : n + 1, start : start + size]

    @pl.when(pl.program_id(0) == 0)
    def _():
        for n in range(4):
            lanes = slice(n * 128, (n + 1) * 128)
            outs[0][:, lanes] = q_ref[n]
            outs[1][:, lanes] = kv_ref[n, :, 0:128]
            outs[2][:, lanes] = kv_ref[n, :, 128:256]
            outs[3][:, lanes] = f_ref[n]
            outs[4][:, lanes] = ff_ref[n, :, 512:640]
            outs[5][:, n * 512 : (n + 1) * 512] = ff_ref[n, :, 0:512]
            for j in range(4):
                outs[6][j * part : (j + 1) * part, lanes] = fr_ref[n, :, j * 128 : (j + 1) * 128]
        outs[7][...] = pick(row_of_sums(s2_ref, 0), part)
        outs[8][...] = pick(row_of_sums(s2_ref, 1), part)
        outs[9][...] = pick(row_of_sums(s1_ref, 2), part)
        outs[10][...] = pick(row_of_sums(s1_ref, 3), part)
        outs[11][...] = pick(bias, 4 * part)
        outs[12][...] = pick(row_of_sums(s1_ref, 4), part)


def finish(count, part, grad_input, *sums):
    once = lambda shape: pl.BlockSpec(shape, lambda i: (0,) * len(shape))
    tall = pl.BlockSpec((512, D), lambda i: (i, 0))
    shapes = [(part, D)] * 5 + [(part, FF), (4 * part, D)]
    shapes += [(1, part)] * 4 + [(1, 4 * part), (1, part)]
    return pl.pallas_call(
        functools.partial(finish_kernel, count, part),
        grid=(grad_input.shape[0] // 512,),
        in_specs=[tall] + [once(a.shape) for a in sums],
        out_specs=[tall] + [once(s) for s in shapes],
        out_shape=[shape_of(s, F32) for s in (grad_input.shape, *shapes)],
        compiler_params=PARAMS,
        name="finish",
    )(grad_input, *sums)


def rows_of(lanes, order=lambda i: i):
    return pl.BlockSpec((C, lanes), lambda i: (order(i), 0))


def whole(*shape):
    return pl.BlockSpec(shape, lambda i: (0,) * len(shape))


def row_of(order=lambda i: i):
    return pl.BlockSpec((1, C), lambda i: (0, order(i)))


def shape_of(shape, kind):
    return jax.ShapeDtypeStruct(shape, kind)


PARAMS = pltpu.CompilerParams(vmem_limit_bytes=LIMIT)


def on_device(
    tokens, doc_ids, w_query, w_key, w_value, w_slots, w_output, w_hidden, w_return,
    gain_first, shift_first, gain_second, shift_second, bias_hidden, bias_return, cotangent,
):
    rows = tokens.shape[0]
    count = lax.axis_size("fsdp")
    part = gain_first.shape[0]
    flat = lambda a: a.reshape(1, a.shape[0])
    qkvf, attended, probs, score, inverse, kept, w_qkvf, w_o, w_h, w_r, small, bias = front(
        count, tokens, doc_ids,
        (w_query, w_key, w_value, w_slots, w_output, w_hidden, w_return),
        [flat(a) for a in (gain_first, shift_first, gain_second, shift_second, bias_return)],
        flat(bias_hidden),
    )
    link = w_qkvf.dtype
    w_qkvf, w_o, w_h, w_r = (
        a.reshape(-1, a.shape[2]).astype(BF16) for a in (w_qkvf, w_o, w_h, w_r)
    )
    tall = pl.BlockSpec((FEED_ROWS, D), lambda i: (i, 0))
    half = count // 2
    out, grad_middle, grad_attended, pack, pack_r, ff_small = pl.pallas_call(
        forward_kernel,
        grid=(rows // FEED_ROWS,),
        in_specs=[tall] * 3
        + [whole(8, D), whole(1, FF), whole(D, D), whole(D, FF), whole(FF, D)],
        out_specs=[tall] * 3
        + [whole(2, 2, 2, half, part, 640), whole(2, 2, half, 2, part, D), whole(16, D)],
        out_shape=[
            shape_of((rows, D), BF16),
            shape_of((rows, D), F32),
            shape_of((rows, D), BF16),
            shape_of((2, 2, 2, half, part, 640), link),
            shape_of((2, 2, half, 2, part, D), link),
            shape_of((16, D), F32),
        ],
        scratch_shapes=[
            pltpu.VMEM((D, D), F32),
            pltpu.VMEM((D, FF), F32),
            pltpu.VMEM((D, FF), F32),
        ],
        compiler_params=PARAMS,
        name="feed",
    )(tokens, attended, cotangent, small, bias, w_o, w_h, w_r)

    grad_input, *sums = back(
        count, tokens, qkvf, grad_attended, probs, score, inverse, kept, grad_middle, doc_ids,
        small, w_qkvf, pack.reshape(-1, part, 640), pack_r.reshape(-1, part, D), ff_small,
    )
    grad_input, *grads = finish(count, part, grad_input, *sums)
    return (out, grad_input, *grads[:7], *(a.reshape(-1) for a in grads[7:]))


def solution(mesh):
    tall, flat, one = P(("fsdp", "seq"), None), P("fsdp", None), P("fsdp")
    return jax.shard_map(
        on_device,
        mesh=mesh,
        in_specs=(tall, P("fsdp", "seq")) + (flat,) * 7 + (one,) * 6 + (tall,),
        out_specs=(tall, tall) + (flat,) * 7 + (one,) * 6,
        check_vma=False,
    )
```

```python
import functools

import jax
import jax.numpy as jnp
from jax import lax
from jax.experimental import pallas as pl
from jax.experimental.pallas import tpu as pltpu
from jax.sharding import PartitionSpec as P

D = 512
H = 8
M = 64
FF = 2048
C = 256
GROUP = 256
EPS = 1e-05
SCALE = 0.125
F32 = jnp.float32
BF16 = jnp.bfloat16
FEED_ROWS = 512
FEED_LANES = 256
FRONT = 4
MIB = 1024 * 1024


def dot(a, b):
    return lax.dot_general(a, b, (((1,), (0,)), ((), ())), preferred_element_type=F32)


def dot_nt(a, b):
    return lax.dot_general(a, b, (((1,), (1,)), ((), ())), preferred_element_type=F32)


def dot_tn(a, b):
    return lax.dot_general(a, b, (((0,), (0,)), ((), ())), preferred_element_type=F32)


def lane_heads(rows, lanes):
    return lax.broadcasted_iota(jnp.int32, (rows, lanes), 1) // M


def stacked(values):
    heads = lane_heads(C, GROUP)
    zero = jnp.zeros_like(values)
    return jnp.concatenate([jnp.where(heads == h, values, zero) for h in range(4)], axis=0)


def select(values):
    heads = lane_heads(C, GROUP)
    out = values[3 * C :]
    for h in (2, 1, 0):
        out = jnp.where(heads == h, values[h * C : (h + 1) * C], out)
    return out


def masked(values, mask):
    return jnp.concatenate(
        [values[h * C : (h + 1) * C].astype(BF16) * mask for h in range(4)], axis=0
    )


def expand(compact):
    rows = lax.broadcasted_iota(jnp.int32, (GROUP, GROUP), 0) // M
    full = jnp.concatenate([compact] * 4, axis=0)
    return jnp.where(rows == lane_heads(GROUP, GROUP), full, jnp.zeros_like(full))


def compacted(full):
    heads = lane_heads(M, GROUP)
    out = full[3 * M :]
    for h in (2, 1, 0):
        out = jnp.where(heads == h, full[h * M : (h + 1) * M], out)
    return out


def split(values):
    high = values.astype(BF16)
    return high, (values - high.astype(F32)).astype(BF16)


def ones_block():
    rows = lax.broadcasted_iota(jnp.int32, (GROUP, GROUP), 0) // M
    return (rows == lane_heads(GROUP, GROUP)).astype(BF16)


def head_sums(values):
    high, low = split(values)
    ones = ones_block()
    return dot(high, ones) + dot(low, ones)


def head_max(values):
    left = lane_heads(C, 128) == 0
    out = []
    for p in range(2):
        pair = values[:, p * 128 : (p + 1) * 128]
        one = jnp.max(jnp.where(left, pair, -jnp.inf), axis=1, keepdims=True)
        two = jnp.max(jnp.where(left, -jnp.inf, pair), axis=1, keepdims=True)
        out.append(jnp.where(left, one, two))
    return jnp.concatenate(out, axis=1)


def wide(values, times):
    return jnp.concatenate([values] * times, axis=1)


def visible(doc_col, doc_row):
    same = wide(doc_col, 2) == doc_row
    here = lax.broadcasted_iota(jnp.int32, (C, C), 0)
    there = lax.broadcasted_iota(jnp.int32, (C, C), 1)
    return jnp.where(same & (here >= there), 1.0, 0.0).astype(BF16)


def visible_back(doc_col, doc_row):
    same = wide(doc_col, 2) == doc_row
    here = lax.broadcasted_iota(jnp.int32, (C, C), 0)
    there = lax.broadcasted_iota(jnp.int32, (C, C), 1)
    return jnp.where(same & (there >= here), 1.0, 0.0).astype(BF16)


def flag(doc_col, doc):
    return jnp.where(doc_col == doc[:, :128], 1.0, 0.0)


def norm_parts(values):
    centre = jnp.mean(values, axis=-1, keepdims=True)
    centred = values - centre
    spread = jnp.mean(centred * centred, axis=-1, keepdims=True)
    scale = lax.rsqrt(spread + EPS)
    return centred * scale, scale


def norm_back(unit, scale, gain, grad):
    inner = grad * gain
    return scale * (
        inner
        - jnp.mean(inner, axis=-1, keepdims=True)
        - unit * jnp.mean(inner * unit, axis=-1, keepdims=True)
    )


def groups(values):
    return values[:, :GROUP], values[:, GROUP:]


def state_terms(slots, left, right):
    one, two = [], []
    for g in range(2):
        lanes = slice(g * GROUP, (g + 1) * GROUP)
        both = dot_tn(slots[:, lanes], jnp.concatenate([left[:, lanes], right[:, lanes]], axis=1))
        one.append(compacted(both[:, :GROUP]))
        two.append(compacted(both[:, GROUP:]))
    return jnp.concatenate(one, axis=1), jnp.concatenate(two, axis=1)


def lanes_of(g):
    return slice(g * GROUP, (g + 1) * GROUP)


def part_of(ref, part, g):
    return ref[:, part * D + g * GROUP : part * D + (g + 1) * GROUP]


def attend_body(
    n, qkvf_ref, col, row, edge_ref, state, o_ref, p_ref, s_ref, z_ref, kept_ref
):
    kept_ref[0] = state[0:128]
    first = edge_ref[pl.ds(0, 1)]
    before = edge_ref[pl.ds(8 + jnp.maximum(n - 1, 0), 1)]
    last = jnp.where(n == 0, first, before)
    newest = edge_ref[pl.ds(8 + n, 1)]
    vis = visible(col, row)
    carried = wide(flag(col, last), 2)
    written = jnp.exp(qkvf_ref[:, 3 * D :].astype(F32))
    slots = written.astype(BF16)
    norm = dot(vis, slots)
    key_states = [expand(state[0:64, lanes_of(g)]).astype(BF16) for g in range(2)]
    value_states = [expand(state[64:128, lanes_of(g)]).astype(BF16) for g in range(2)]
    norm_state = state[128:129]

    def affine(g):
        return masked(dot_nt(stacked(part_of(qkvf_ref, 0, g)), part_of(qkvf_ref, 1, g)), vis)

    def scores(g, affinity):
        lanes = lanes_of(g)
        numer = select(dot(affinity, slots[:, lanes]))
        numer = numer + carried * dot_nt(part_of(qkvf_ref, 0, g), key_states[g])
        inverse = 1.0 / (norm[:, lanes] + carried * norm_state[:, lanes])
        return numer * inverse * SCALE, inverse

    def grow(score):
        return jnp.exp(score - head_max(score))

    def read(g, score, inverse, grown):
        lanes = lanes_of(g)
        probs = grown / head_sums(grown)
        p_ref[:, lanes] = probs
        s_ref[:, lanes] = score
        z_ref[:, lanes] = inverse
        return (probs * inverse).astype(BF16)

    def mixing(g, reading):
        return masked(dot_nt(stacked(reading), slots[:, lanes_of(g)]), vis)

    def mixed(g, reading, mix):
        out = select(dot(mix, part_of(qkvf_ref, 2, g))) + carried * dot(reading, value_states[g])
        o_ref[:, lanes_of(g)] = out.astype(BF16)

    affinity = affine(0)
    score, inverse = scores(0, affinity)
    affinity = affine(1)
    grown = grow(score)
    score_two, inverse_two = scores(1, affinity)
    reading = read(0, score, inverse, grown)
    tail = (wide(flag(col, newest), 4) * written).astype(BF16)
    new_keys, new_values = state_terms(tail, qkvf_ref[:, D : 2 * D], qkvf_ref[:, 2 * D : 3 * D])
    same = jnp.where(last == newest, 1.0, 0.0)
    state[0:64] = same * state[0:64] + new_keys
    state[64:128] = same * state[64:128] + new_values
    state[128:129] = same * state[128:129] + jnp.sum(tail.astype(F32), axis=0, keepdims=True)
    grown = grow(score_two)
    mix = mixing(0, reading)
    reading_two = read(1, score_two, inverse_two, grown)
    mixed(0, reading, mix)
    mix = mixing(1, reading_two)
    mixed(1, reading_two, mix)


MESH_ID = pl.DeviceIdType.MESH


def places():
    seq, at = lax.axis_index("seq"), lax.axis_index("fsdp")
    core = lax.rem(seq, 2)
    return seq, at, seq + 1 - 2 * core, lax.rem(seq + 2, 4)


def push(src, dst, send, recv, **device):
    return pltpu.make_async_remote_copy(
        src_ref=src, dst_ref=dst, send_sem=send, recv_sem=recv,
        device_id=device, device_id_type=MESH_ID,
    )


def greet(count):
    seq, at, _, _ = places()
    barrier = pltpu.get_barrier_semaphore()
    for k in range(1, count):
        pl.semaphore_signal(barrier, inc=1, device_id={"fsdp": at ^ k}, device_id_type=MESH_ID)
    for k in range(1, 4):
        pl.semaphore_signal(barrier, inc=1, device_id={"seq": seq ^ k}, device_id_type=MESH_ID)
    pl.semaphore_wait(barrier, count - 1 + 3)


class Gather:
    def __init__(self, count, mine, held, base, width, four, sems):
        self.count, self.mine, self.held, self.four = count, mine, held, four
        self.far, self.near, self.core, self.chip, self.onward, self.local = sems
        self.seq, self.at, self.sibling, self.beside = places()
        self.base, self.share = base, width // (4 if four else 2)
        self.evens = range(0, count, 2)

    def lanes(self, seq):
        place = seq if self.four else lax.rem(seq, 2)
        return pl.ds(pl.multiple_of(self.base + place * self.share, 128), self.share)

    def part(self, k, seq):
        return self.held.at[self.at ^ k, :, self.lanes(seq)]

    def source(self, k):
        if k:
            return self.part(k, self.seq)
        return self.mine.at[:, self.lanes(self.seq)]

    def own(self):
        return pltpu.make_async_copy(self.source(0), self.part(0, self.seq), self.local)

    def over(self, sems, k, **device):
        return push(self.source(k), self.part(k, self.seq), sems[0].at[k], sems[1].at[k], **device)

    def come(self, sems, k, owner):
        here = self.part(owner, self.seq)
        return push(here, here, sems[0].at[k], sems[1].at[k], seq=self.sibling)

    def far_out(self, k):
        return push(
            self.source(0), self.part(0, self.seq), self.far[0].at[k], self.far[1].at[k],
            fsdp=self.at ^ k,
        )

    def far_in(self, k):
        return self.come(self.far, k, k)

    def near_out(self, k):
        return self.over(self.near, k, fsdp=self.at ^ 1)

    def near_in(self, k):
        return self.come(self.near, k, k ^ 1)

    def start(self):
        self.own().start()
        for k in self.evens[1:]:
            self.far_out(k).start()
        self.near_out(0).start()

    def second(self):
        for k in self.evens[1:]:
            self.far_in(k).wait_recv()
            self.near_out(k).start()

    def hop(self, sems, source, target):
        here = self.held.at[:, :, self.lanes(source)]
        return push(here, here, sems[0].at[0], sems[1].at[0], seq=target)

    def third(self):
        self.own().wait()
        for k in self.evens:
            self.near_in(k).wait_recv()
        self.hop(self.core, self.seq, self.sibling).start()
        if self.four:
            self.hop(self.chip, self.seq, self.beside).start()

    def fourth(self):
        self.hop(self.chip, self.beside, self.beside).wait_recv()
        self.hop(self.onward, self.beside, self.sibling).start()

    def finish(self):
        self.hop(self.core, self.sibling, self.sibling).wait_recv()
        self.hop(self.core, self.seq, self.sibling).wait_send()
        if self.four:
            self.hop(self.onward, lax.rem(self.sibling + 2, 4), self.sibling).wait_recv()
            self.hop(self.chip, self.seq, self.beside).wait_send()
            self.hop(self.onward, self.beside, self.sibling).wait_send()

    def core_out(self, k):
        return self.over(self.core, k, seq=self.sibling)

    def core_in(self, k):
        here = self.part(k, self.sibling)
        return push(here, here, self.core[0].at[k], self.core[1].at[k], seq=self.sibling)

    def at_once(self, between):
        self.start()
        self.core_out(0).start()
        for k in self.evens[1:]:
            self.far_in(k).wait_recv()
            self.near_out(k).start()
            self.core_out(k).start()
        between()
        for k in self.evens:
            self.near_in(k).wait_recv()
            self.core_out(k ^ 1).start()
        self.own().wait()
        for k in range(self.count):
            self.core_in(k).wait_recv()

    def drain(self, each=False):
        for k in self.evens:
            self.near_out(k).wait_send()
            if k:
                self.far_out(k).wait_send()
        if each:
            for k in range(self.count):
                self.core_out(k).wait_send()


def gather_sems(count, each):
    n = count if each else 1
    pair = lambda size: [pltpu.SemaphoreType.DMA((size,)), pltpu.SemaphoreType.DMA((size,))]
    return pair(count) + pair(count) + pair(n) + pair(1) + pair(1) + [pltpu.SemaphoreType.DMA]


def bundle(refs):
    return [(refs[2 * n], refs[2 * n + 1]) for n in range(5)] + [refs[10]]


class States:
    def __init__(self, big, small, sems):
        self.refs, self.sems = (big, small), sems
        self.seq, _, self.sibling, self.beside = places()

    def hop(self, n, source, target):
        out = []
        for m, ref in enumerate(self.refs):
            here = ref.at[source]
            out.append(push(here, here, self.sems[0].at[n, m], self.sems[1].at[n, m], seq=target))
        return out

    def start(self):
        for copy in self.hop(0, self.seq, self.sibling) + self.hop(1, self.seq, self.beside):
            copy.start()

    def finish(self):
        for copy in self.hop(1, self.beside, self.beside):
            copy.wait_recv()
        for copy in self.hop(2, self.beside, self.sibling):
            copy.start()
        for copy in self.hop(0, self.sibling, self.sibling):
            copy.wait_recv()
        for copy in self.hop(2, lax.rem(self.sibling + 2, 4), self.sibling):
            copy.wait_recv()

    def drain(self):
        for copy in (
            self.hop(0, self.seq, self.sibling)
            + self.hop(1, self.seq, self.beside)
            + self.hop(2, self.beside, self.sibling)
        ):
            copy.wait_send()


def doc_parts(doc_ref, col_ref, edge_ref):
    here = lax.broadcasted_iota(jnp.int32, (C, C), 0)
    there = lax.broadcasted_iota(jnp.int32, (C, C), 1)
    eye = jnp.where(here == there, 1.0, 0.0).astype(BF16)
    for n in range(doc_ref.shape[1] // C):
        row = doc_ref[:, n * C : (n + 1) * C].astype(F32)
        col_ref[n * C : (n + 1) * C] = dot_nt(eye, jnp.broadcast_to(row, (128, C)).astype(BF16))
        low = jnp.min(row, axis=1, keepdims=True)
        high = jnp.max(row, axis=1, keepdims=True)
        edge_ref[n : n + 1] = jnp.broadcast_to(low, (1, D))
        edge_ref[n + 8 : n + 9] = jnp.broadcast_to(high, (1, D))


def spread_small(vec_refs, bias_ref, out_ref):
    def repeat(values):
        width = values.shape[1]
        rows = lax.broadcasted_iota(jnp.int32, (width, 128), 0)
        lanes = lax.broadcasted_iota(jnp.int32, (width, 128), 1)
        pick = jnp.where(lax.rem(lanes, width) == rows, 1.0, 0.0).astype(BF16)
        return dot(jnp.broadcast_to(values, (8, width)).astype(BF16), pick)[0:1]

    out_ref[...] = jnp.zeros_like(out_ref)
    for n, ref in enumerate(vec_refs):
        out_ref[n : n + 1] = repeat(ref[...])
    for b in range(max(bias_ref.shape[1] // 128, 1)):
        out_ref[5 + b : 6 + b] = repeat(bias_ref[:, b * 128 : (b + 1) * 128])


def join_small(count, part, gathered, vec_ref, bias_ref):
    lanes = lax.broadcasted_iota(jnp.int32, (8, D), 1)
    total = jnp.zeros((8, D), F32)
    for f in range(count):
        total = jnp.where(lanes // part == f, wide(gathered[f], 4), total)
    vec_ref[...] = total
    size = 4 * part
    for r in range(4):
        at = lanes[0:1] + r * D
        row = jnp.zeros((1, D), F32)
        for f in range(r * D // size, -(-(r + 1) * D // size)):
            for b in range(max(size // 128, 1)):
                use = (at // size == f) & (lax.rem(at, size) // 128 == b)
                row = jnp.where(use, wide(gathered[f, 5 + b : 6 + b], 4), row)
        bias_ref[0:1, r * D : (r + 1) * D] = row


def front_kernel(
    count, x_ref, doc_ref, wq_ref, wk_ref, wv_ref, ws_ref, wo_ref, wh_ref, wr_ref,
    v0, v1, v2, v3, v4, bias_in,
    qkvf_out, o_ref, p_ref, s_ref, z_ref, kept_ref, w_out, wo_out, wh_out, wr_out, vec_out, bias_out,
    qkvf, hidden, w_all, mine, mine_o, mine_h, mine_r, spread, smalls, col_ref, edge_ref, state,
    tail, tails, tail_rows, *sems,
):
    step = pl.program_id(0)
    seq, at, _, _ = places()
    link = mine.dtype
    groups_of_sems = []
    for _ in range(5):
        groups_of_sems.append(bundle(sems[:11]))
        sems = sems[11:]
    small_send, small_recv, state_send, state_recv, out_sem = sems
    main = Gather(count, mine, w_all, D, 3 * D, False, groups_of_sems[0])
    q_piece = Gather(count, mine, w_all, 0, D, False, groups_of_sems[1])
    o_piece = Gather(count, mine_o, wo_out, 0, D, True, groups_of_sems[2])
    h_piece = Gather(count, mine_h, wh_out, 0, FF, True, groups_of_sems[3])
    r_piece = Gather(count, mine_r, wr_out, 0, D, False, groups_of_sems[4])
    later = (q_piece, o_piece, h_piece, r_piece)
    states = States(tails, tail_rows, (state_send, state_recv))

    def small_copy(k, owner):
        return push(
            spread, smalls.at[owner], small_send.at[k], small_recv.at[k], fsdp=at ^ k
        )

    def save():
        return (
            pltpu.make_async_copy(qkvf, qkvf_out, out_sem.at[0]),
            pltpu.make_async_copy(w_all, w_out, out_sem.at[1]),
        )

    @pl.when(step == 0)
    def _():
        greet(count)
        for n, ref in enumerate((wq_ref, wk_ref, wv_ref, ws_ref)):
            mine[:, n * D : (n + 1) * D] = ref[...].astype(BF16).astype(link)
        spread_small((v0, v1, v2, v3, v4), bias_in, spread)
        for k in range(1, count):
            small_copy(k, at).start()

        def between():
            mine_o[...] = wo_ref[...].astype(BF16).astype(link)
            mine_h[...] = wh_ref[...].astype(BF16).astype(link)
            mine_r[...] = wr_ref[...].astype(BF16).astype(link)
            doc_parts(doc_ref, col_ref, edge_ref)
            tail[...] = jnp.zeros_like(tail)
            smalls[at] = spread[...]
            for k in range(1, count):
                small_copy(k, at ^ k).wait_recv()
            join_small(count, v0.shape[1], smalls, vec_out, bias_out)
            q_piece.start()
            o_piece.start()

            @pl.loop(0, 8)
            def _(n):
                here = pl.ds(pl.multiple_of(n * C, C), C)
                unit, _ = norm_parts(x_ref[here].astype(F32))
                hidden[here] = (unit * vec_out[0:1] + vec_out[1:2]).astype(BF16)

        main.at_once(between)
        h_piece.start()
        r_piece.start()

    @pl.when(step < FRONT)
    def _():
        size = 8 // FRONT * C
        here = pl.ds(pl.multiple_of(step * size, size), size)
        weights = w_all[:, :, D:].reshape(D, 3 * D).astype(BF16)
        rows = dot(hidden[here], weights).astype(BF16)
        qkvf[here, D:] = rows
        slots = wide(flag(col_ref[here], edge_ref[15:16]), 4) * jnp.exp(rows[:, 2 * D :].astype(F32))
        slots = slots.astype(BF16)
        keys, values = state_terms(slots, rows[:, 0:D], rows[:, D : 2 * D])
        tail[0:64] += keys
        tail[64:128] += values
        tail[128:129] += jnp.sum(slots.astype(F32), axis=0, keepdims=True)

    @pl.when(step == 1)
    def _():
        q_piece.second()
        o_piece.second()

    @pl.when(step == FRONT - 1)
    def _():
        tails[seq] = tail[0:128].astype(link)
        tail_rows[seq, 0:1] = tail[128:129]
        tail_rows[seq, 1:2] = edge_ref[15:16]
        tail_rows[seq, 2:8] = jnp.zeros((6, D), F32)
        states.start()
        q_piece.third()
        q_piece.finish()

        @pl.loop(0, FRONT)
        def _(n):
            size = 8 // FRONT * C
            here = pl.ds(pl.multiple_of(n * size, size), size)
            weights = w_all[:, :, 0:D].reshape(D, D).astype(BF16)
            qkvf[here, 0:D] = dot(hidden[here], weights).astype(BF16)

        for copy in save():
            copy.start()
        o_piece.third()
        states.finish()
        first = edge_ref[0:1]
        state[...] = jnp.zeros_like(state)
        for n in range(4):
            use = jnp.where(tail_rows[n, 1:2] == first, 1.0, 0.0) * (n < seq).astype(F32)
            state[0:128] += use * tails[n].astype(F32)
            state[128:129] += use * tail_rows[n, 0:1]
        h_piece.second()

    per = 8 // FRONT
    for u in range(per):

        @pl.when(step >= FRONT)
        def _(u=u):
            n = (step - FRONT) * per + u
            here = pl.ds(pl.multiple_of(n * C, C), C)
            block = pl.ds(u * C, C)
            attend_body(
                n, qkvf.at[here], col_ref[here], doc_ref[:, here].astype(F32), edge_ref, state,
                o_ref.at[block], p_ref.at[block], s_ref.at[block], z_ref.at[block],
                kept_ref.at[pl.ds(u, 1)],
            )

        if u == 0:

            @pl.when(step == FRONT)
            def _():
                o_piece.fourth()

            @pl.when(step == FRONT + 1)
            def _():
                r_piece.second()
                h_piece.third()

            @pl.when(step == FRONT + 3)
            def _():
                r_piece.third()
                h_piece.fourth()

    @pl.when(step == 2 * FRONT - 1)
    def _():
        for piece in (o_piece, h_piece, r_piece):
            piece.finish()
        for piece in later:
            piece.drain()
        main.drain(True)
        states.drain()
        for k in range(1, count):
            small_copy(k, at).wait_send()
        for copy in save():
            copy.wait()


def front(count, tokens, doc_ids, weights, vectors, bias):
    rows = tokens.shape[0]
    part = weights[0].shape[0]
    link = BF16 if part % 16 == 0 else F32
    once = lambda a: pl.BlockSpec(a.shape, lambda i: (0,) * a.ndim)
    late = lambda i: jnp.maximum(i - FRONT, 0)
    per = 8 // FRONT
    tall = pl.BlockSpec((per * C, D), lambda i: (late(i), 0))
    anywhere = pl.BlockSpec(memory_space=pl.ANY)
    vmem = pltpu.VMEM
    return pl.pallas_call(
        functools.partial(front_kernel, count),
        grid=(2 * FRONT,),
        in_specs=[once(tokens), once(doc_ids)] + [once(a) for a in (*weights, *vectors, bias)],
        out_specs=[anywhere]
        + [tall] * 4
        + [pl.BlockSpec((per, 128, D), lambda i: (late(i), 0, 0))]
        + [anywhere] * 4
        + [whole(8, D), whole(1, FF)],
        out_shape=[shape_of((rows, 4 * D), BF16), shape_of((rows, D), BF16)]
        + [shape_of((rows, D), F32)] * 3
        + [
            shape_of((8, 128, D), F32),
            shape_of((count, part, 4 * D), link),
            shape_of((count, part, D), link),
            shape_of((count, part, FF), link),
            shape_of((count, 4 * part, D), link),
            shape_of((8, D), F32),
            shape_of((1, FF), F32),
        ],
        scratch_shapes=[
            vmem((rows, 4 * D), BF16),
            vmem((rows, D), BF16),
            vmem((count, part, 4 * D), link),
            vmem((part, 4 * D), link),
            vmem((part, D), link),
            vmem((part, FF), link),
            vmem((4 * part, D), link),
            vmem((8, 128), F32),
            vmem((count, 8, 128), F32),
            vmem((rows, 128), F32),
            vmem((16, D), F32),
            vmem((136, D), F32),
            vmem((136, D), F32),
            vmem((4, 128, D), link),
            vmem((4, 8, D), F32),
        ]
        + gather_sems(count, True)
        + gather_sems(count, False) * 4
        + [
            pltpu.SemaphoreType.DMA((count,)),
            pltpu.SemaphoreType.DMA((count,)),
            pltpu.SemaphoreType.DMA((3, 2)),
            pltpu.SemaphoreType.DMA((3, 2)),
            pltpu.SemaphoreType.DMA((2,)),
        ],
        compiler_params=pltpu.CompilerParams(
            vmem_limit_bytes=62 * MIB, collective_id=1, has_side_effects=True
        ),
        name="front",
    )(tokens, doc_ids, *weights, *vectors, bias)


ROOT = 0.7978845608028654
CUBE = 0.044715


def gelu_both(u):
    square = u * u
    bent = jnp.tanh(ROOT * u * (1.0 + CUBE * square))
    half = 0.5 * (1.0 + bent)
    slope = half + 0.5 * u * (1.0 - bent * bent) * (ROOT * (1.0 + 3.0 * CUBE * square))
    return u * half, slope


def forward_kernel(
    x_ref, o_ref, g_ref, small_ref, bias_ref, wo_ref, wh_ref, wr_ref,
    y_ref, dy_ref, do_ref, pack_ref, pack_r_ref, gsmall_ref, gwo_ref, gwh_ref, gwr_ref,
):
    step = pl.program_id(0)

    @pl.when(step == 0)
    def _():
        for ref in (gwo_ref, gwh_ref, gwr_ref, gsmall_ref):
            ref[...] = jnp.zeros_like(ref)

    attended, cot = o_ref[...], g_ref[...]
    middle = x_ref[...].astype(F32) + dot(attended, wo_ref[...])
    unit, scale = norm_parts(middle)
    hidden = (unit * small_ref[2:3] + small_ref[3:4]).astype(BF16)
    out = middle + small_ref[4:5]
    grad_hidden = jnp.zeros((x_ref.shape[0], D), F32)
    cot32 = cot.astype(F32)
    tiles = FF // FEED_LANES

    def into(j):
        cols = slice(j * FEED_LANES, (j + 1) * FEED_LANES)
        inner = dot(hidden, wh_ref[:, cols]) + bias_ref[0:1, cols]
        return inner, dot_nt(cot, wr_ref[cols, :])

    def bend(inner, grad):
        gated, slope = gelu_both(inner)
        return gated.astype(BF16), (grad * slope).astype(BF16)

    def outof(j, active, low):
        cols = slice(j * FEED_LANES, (j + 1) * FEED_LANES)
        there = slice(cols.start % D, cols.start % D + FEED_LANES)
        row = 8 + cols.start // D
        gwr_ref[:, cols] += dot_tn(cot, active)
        gsmall_ref[row : row + 1, there] += jnp.sum(low.astype(F32), axis=0, keepdims=True)
        gwh_ref[:, cols] += dot_tn(hidden, low)
        return dot(active, wr_ref[cols, :]), dot_nt(low, wh_ref[:, cols])

    coming = into(0)
    for j in range(tiles):
        bent = bend(*coming)
        if j + 1 < tiles:
            coming = into(j + 1)
        to_out, to_hidden = outof(j, *bent)
        out = out + to_out
        grad_hidden = grad_hidden + to_hidden
    y_ref[...] = out.astype(BF16)
    gsmall_ref[2:3] += jnp.sum(grad_hidden * unit, axis=0, keepdims=True)
    gsmall_ref[3:4] += jnp.sum(grad_hidden, axis=0, keepdims=True)
    gsmall_ref[4:5] += jnp.sum(cot32, axis=0, keepdims=True)
    grad_middle = cot32 + norm_back(unit, scale, small_ref[2:3], grad_hidden)
    dy_ref[...] = grad_middle
    branch = grad_middle.astype(BF16)
    gwo_ref[...] += dot_tn(attended, branch)
    do_ref[...] = dot_nt(branch, wo_ref[...]).astype(BF16)

    @pl.when(step == pl.num_programs(0) - 1)
    def _():
        half, part = pack_ref.shape[3], pack_ref.shape[4]
        kind = pack_ref.dtype
        for q in range(4):
            x, c = q // 2, q % 2
            hidden_part = gwh_ref[:, q * 512 : (q + 1) * 512].reshape(half, 2, part, 512)
            out_part = gwo_ref[:, q * 128 : (q + 1) * 128].reshape(half, 2, part, 128)
            turned = gwr_ref[q * 128 : (q + 1) * 128].T.reshape(half, 2, 4, part, 128)
            for y in range(2):
                pack_ref[c, x, y, :, :, 0:512] = hidden_part[:, y].astype(kind)
                pack_ref[c, x, y, :, :, 512:640] = out_part[:, y].astype(kind)
                for j in range(4):
                    pack_r_ref[c, y, :, x, :, j * 128 : (j + 1) * 128] = turned[:, y, j].astype(kind)


def row_body(
    n, qkvf_ref, do_ref, p_ref, s_ref, z_ref, kept_ref, col, row, edge_ref,
    r_ref, dn_ref, dz_ref, head_ref, aside,
):
    first = edge_ref[pl.ds(0, 1)]
    before = edge_ref[pl.ds(8 + jnp.maximum(n - 1, 0), 1)]
    last = jnp.where(n == 0, first, before)
    vis = visible(col, row)
    carried = wide(flag(col, last), 2)
    slots = jnp.exp(qkvf_ref[:, 3 * D :].astype(F32)).astype(BF16)
    own = wide(flag(col, first), 2)
    states = [expand(kept_ref[0, 64:128, lanes_of(g)]).astype(BF16) for g in range(2)]

    def mixing(g):
        return masked(dot_nt(stacked(do_ref[:, lanes_of(g)]), part_of(qkvf_ref, 2, g)), vis)

    def to_reading(g, back_mix):
        lanes = lanes_of(g)
        back = select(dot(back_mix, slots[:, lanes]))
        return back + carried * dot_nt(do_ref[:, lanes], states[g])

    def to_scores(g, back_reading):
        lanes = lanes_of(g)
        probs, score, inverse = p_ref[:, lanes], s_ref[:, lanes], z_ref[:, lanes]
        shared = back_reading * inverse * probs
        back_score = shared - probs * head_sums(shared)
        back_numer = back_score * inverse * SCALE
        back_total = -(shared + back_score * score) * inverse
        reading = (probs * inverse).astype(BF16)
        r_ref[:, lanes] = reading
        dn_ref[:, lanes] = back_numer
        dz_ref[:, lanes] = back_total
        return back_numer, back_total, reading

    def to_state(g, back_numer, back_total, reading):
        lanes = lanes_of(g)
        head_ref[0:64, lanes] += compacted(
            dot_tn((own * back_numer).astype(BF16), part_of(qkvf_ref, 0, g))
        )
        head_ref[64:128, lanes] += compacted(
            dot_tn((own * reading.astype(F32)).astype(BF16), do_ref[:, lanes])
        )
        head_ref[128:129, lanes] += jnp.sum(own * back_total, axis=0, keepdims=True)

    back_mix = mixing(0)
    back_mix_two = mixing(1)
    aside()
    back_reading = to_reading(0, back_mix)
    back_reading_two = to_reading(1, back_mix_two)
    parts = to_scores(0, back_reading)
    to_state(0, *parts)
    parts = to_scores(1, back_reading_two)
    to_state(1, *parts)


def query_body(n, qkvf_ref, kept_ref, col, row, edge_ref, dn_ref, dq_ref):
    first = edge_ref[pl.ds(0, 1)]
    before = edge_ref[pl.ds(8 + jnp.maximum(n - 1, 0), 1)]
    last = jnp.where(n == 0, first, before)
    vis = visible(col, row)
    carried = wide(flag(col, last), 2)
    slots = jnp.exp(qkvf_ref[:, 3 * D :].astype(F32)).astype(BF16)
    lows = [dn_ref[:, lanes_of(g)].astype(BF16) for g in range(2)]
    states = [expand(kept_ref[0, 0:64, lanes_of(g)]).astype(BF16) for g in range(2)]

    def affine(g):
        return masked(dot_nt(stacked(lows[g]), slots[:, lanes_of(g)]), vis)

    def to_queries(g, back_affinity):
        out = select(dot(back_affinity, part_of(qkvf_ref, 1, g))) + carried * dot(lows[g], states[g])
        dq_ref[:, lanes_of(g)] = out.astype(BF16)

    one, two = affine(0), affine(1)
    to_queries(0, one)
    to_queries(1, two)


def column_body(
    n, qkvf_ref, do_ref, r_ref, dn_ref, dz_ref, col, row, edge_ref, state, snap, snap_rows, d_ref
):
    newest = edge_ref[15:16]
    after = edge_ref[pl.ds(jnp.minimum(n + 1, 7), 1)]
    following = jnp.where(n == 7, newest, after)
    first = edge_ref[pl.ds(n, 1)]
    vis = visible_back(col, row)
    carried = wide(flag(col, following), 2)
    own = wide(flag(col, first), 2)
    kept = jnp.where(following == first, 1.0, 0.0)[:, :GROUP]
    snap[n] = state[0:128].astype(BF16)
    snap_rows[pl.ds(n, 1)] = state[128:129]
    key_states = [expand(state[0:64, lanes_of(g)]).astype(BF16) for g in range(2)]
    value_states = [expand(state[64:128, lanes_of(g)]).astype(BF16) for g in range(2)]
    slots = jnp.exp(qkvf_ref[:, 3 * D :].astype(F32)).astype(BF16)
    numers = [dn_ref[:, lanes_of(g)] for g in range(2)]

    def mixing(g, apart):
        return masked(dot_nt(apart, r_ref[:, lanes_of(g)]), vis)

    def affine(g, apart):
        return masked(dot_nt(apart, numers[g].astype(BF16)), vis)

    def to_values(g, mix):
        lanes = lanes_of(g)
        out = select(dot(mix, do_ref[:, lanes])) + carried * dot(slots[:, lanes], value_states[g])
        d_ref[:, 2 * D + g * GROUP : 2 * D + (g + 1) * GROUP] = out.astype(BF16)

    def to_keys(g, back_affinity):
        lanes = lanes_of(g)
        out = select(dot(back_affinity, part_of(qkvf_ref, 0, g)))
        out = out + carried * dot(slots[:, lanes], key_states[g])
        d_ref[:, D + g * GROUP : D + (g + 1) * GROUP] = out.astype(BF16)

    def to_state(g):
        lanes = lanes_of(g)
        state[0:64, lanes] = kept * state[0:64, lanes] + compacted(
            dot_tn((own * numers[g]).astype(BF16), part_of(qkvf_ref, 0, g))
        )
        state[64:128, lanes] = kept * state[64:128, lanes] + compacted(
            dot_tn((own * r_ref[:, lanes].astype(F32)).astype(BF16), do_ref[:, lanes])
        )
        state[128:129, lanes] = kept * state[128:129, lanes] + jnp.sum(
            own * dz_ref[:, lanes], axis=0, keepdims=True
        )

    apart = stacked(slots[:, lanes_of(0)])
    mix = mixing(0, apart)
    back_affinity = affine(0, apart)
    apart = stacked(slots[:, lanes_of(1)])
    mix_two = mixing(1, apart)
    to_values(0, mix)
    affinity_two = affine(1, apart)
    to_keys(0, back_affinity)
    to_state(0)
    to_values(1, mix_two)
    to_keys(1, affinity_two)
    to_state(1)


def slot_body(n, qkvf_ref, do_ref, r_ref, dn_ref, dz_ref, col, row, edge_ref, snap, snap_rows, d_ref):
    newest = edge_ref[15:16]
    after = edge_ref[pl.ds(jnp.minimum(n + 1, 7), 1)]
    following = jnp.where(n == 7, newest, after)
    vis = visible_back(col, row)
    carried = wide(flag(col, following), 2)
    left = lane_heads(C, 128) == 0
    norm_state = snap_rows[pl.ds(n, 1)]
    key_states = [expand(snap[n, 0:64, lanes_of(g)]) for g in range(2)]
    value_states = [expand(snap[n, 64:128, lanes_of(g)]) for g in range(2)]

    def mixing(g):
        return masked(dot_nt(stacked(part_of(qkvf_ref, 2, g)), do_ref[:, lanes_of(g)]), vis)

    def affine(g):
        return masked(dot_nt(stacked(part_of(qkvf_ref, 1, g)), part_of(qkvf_ref, 0, g)), vis)

    def from_mix(g, back_mix):
        return select(dot(back_mix, r_ref[:, lanes_of(g)]))

    def from_affinity(g, affinity):
        high, low = split(dn_ref[:, lanes_of(g)])
        parts = []
        for p in range(2):
            pair = slice(p * 128, (p + 1) * 128)
            both = dot(
                affinity[p * 512 : (p + 1) * 512],
                jnp.concatenate([high[:, pair], low[:, pair]], axis=1),
            )
            both = both[:, :128] + both[:, 128:]
            parts.append(jnp.where(left, both[:C], both[C:]))
        return jnp.concatenate(parts, axis=1)

    def from_totals():
        high, low = split(dz_ref[...])
        return dot(vis, high) + dot(vis, low)

    def from_state(g):
        return carried * (
            dot_nt(part_of(qkvf_ref, 1, g), key_states[g])
            + dot_nt(part_of(qkvf_ref, 2, g), value_states[g])
            + norm_state[:, lanes_of(g)]
        )

    def to_slots(g, back_slots):
        written = jnp.exp(part_of(qkvf_ref, 3, g).astype(F32))
        d_ref[:, 3 * D + g * GROUP : 3 * D + (g + 1) * GROUP] = (back_slots * written).astype(BF16)

    norm = from_totals()
    mix = mixing(0)
    affinity = affine(0)
    mix_two = mixing(1)
    total = from_mix(0, mix)
    affinity_two = affine(1)
    total = total + from_affinity(0, affinity)
    total_two = from_mix(1, mix_two)
    to_slots(0, total + norm[:, lanes_of(0)] + from_state(0))
    total_two = total_two + from_affinity(1, affinity_two)
    to_slots(1, total_two + norm[:, lanes_of(1)] + from_state(1))


class Scatter:
    def __init__(self, count, source, own, axes, direct, out, buffers):
        self.axes, self.direct, self.out = axes, direct, out
        self.seq, self.at, self.sibling, self.beside = places()
        self.source, self.own = source, own
        self.core = lax.rem(self.seq, 2)
        self.total, self.local, self.last, self.done = buffers[:4]
        self.stages = []
        size = source.shape[0]
        base = 0
        for n, axis in enumerate(axes):
            ways = {"core": 2, "x": 2, "y": 2, "z": count // 2, "all": count}[axis]
            size = size // ways
            me = {
                "core": self.core, "x": self.seq // 2, "y": lax.rem(self.at, 2), "z": self.at // 2,
                "all": self.at,
            }[axis]
            held = source
            if own is not None and n > 0:
                held = own
            come, sems = buffers[4 + 2 * n], buffers[5 + 2 * n]
            self.stages.append((axis, ways, size, base, me, held, come, sems))
            if own is None or n > 0:
                base = base + me * size

    def copies(self, n):
        axis, ways, size, base, me, held, come, sems = self.stages[n]
        for k in range(1, ways):
            if axis in ("core", "x"):
                device = {"seq": self.sibling if axis == "core" else self.beside}
            else:
                device = {"fsdp": self.at ^ (2 * k if axis == "z" else k)}
            yield push(
                held.at[pl.ds(base + (me ^ k) * size, size)], come.at[k - 1],
                sems.at[0, k - 1], sems.at[1, k - 1], **device,
            )

    def copy_own(self):
        size = self.source.shape[0] // 2
        return pltpu.make_async_copy(
            self.source.at[pl.ds(self.core * size, size)], self.own, self.local
        )

    def start(self):
        for copy in self.copies(0):
            copy.start()
        if self.own is not None:
            self.copy_own().start()

    def advance(self, n):
        axis, ways, size, base, me, held, come, sems = self.stages[n]
        for copy in self.copies(n):
            copy.wait_recv()
        mine = held
        first = base + me * size
        if n == 0 and self.own is not None:
            self.copy_own().wait()
            mine, first = self.own, 0

        def added(slab):
            total = mine[first + slab].astype(F32)
            for k in range(1, ways):
                total = total + come[k - 1, slab].astype(F32)
            return total

        if n + 1 == len(self.stages):
            self.total[...] = added(0)
            self.copy_done().start()
            for copy in self.sent():
                copy.start()
            return

        @pl.loop(0, size)
        def _(slab):
            mine[first + slab] = added(slab).astype(mine.dtype)

        for copy in self.copies(n + 1):
            copy.start()

    def copy_done(self):
        return pltpu.make_async_copy(self.total, self.out.at[self.seq], self.done)

    def sent(self):
        other = lax.rem(self.sibling + 2, 4)
        for n, target in enumerate((self.sibling, self.beside, other)[: 3 if self.direct else 2]):
            yield push(
                self.total, self.out.at[self.seq], self.last.at[0, n], self.last.at[1, n], seq=target
            )

    def forwarded(self, source):
        here = self.out.at[source]
        return push(here, here, self.last.at[0, 2], self.last.at[1, 2], seq=self.sibling)

    def come_in(self, n, source):
        here = self.out.at[source]
        return push(here, here, self.last.at[0, n], self.last.at[1, n], seq=source)

    def forward(self):
        self.come_in(1, self.beside).wait_recv()
        self.forwarded(self.beside).start()

    def finish(self):
        other = lax.rem(self.sibling + 2, 4)
        self.come_in(0, self.sibling).wait_recv()
        if self.direct:
            self.come_in(1, self.beside).wait_recv()
        else:
            self.forwarded(self.beside).wait_send()
        self.forwarded(other).wait_recv()
        self.copy_done().wait()
        for copy in self.sent():
            copy.wait_send()
        for n in range(len(self.stages)):
            for copy in self.copies(n):
                copy.wait_send()


def scatter_scratch(count, part, lanes, link, axes, hbm):
    vmem, dma = pltpu.VMEM, pltpu.SemaphoreType.DMA
    size = 2 * 4 * count // 2
    out = [vmem((size // 2, part, lanes), link)] if hbm else []
    out += [vmem((part, lanes), F32), dma, dma((2, 3)), dma]
    for axis in axes:
        ways = {"core": 2, "x": 2, "y": 2, "z": count // 2, "all": count}[axis]
        size = size // ways
        out += [vmem((ways - 1, size, part, lanes), link), dma((2, ways - 1))]
    return out


OVER_X = ("core", "x", "y", "z")
OVER_Y = ("core", "y", "z", "x")
SHORT = ("core", "x", "all")


class SmallSum:
    def __init__(self, count, mine, from_seq, half, from_fsdp, sems):
        self.count, self.mine, self.from_seq = count, mine, from_seq
        self.half, self.from_fsdp, self.sems = half, from_fsdp, sems
        self.seq, self.at, _, _ = places()

    def over_seq(self, k, slot):
        return push(
            self.mine, self.from_seq.at[slot], self.sems[0].at[0, k], self.sems[0].at[1, k],
            seq=self.seq ^ k,
        )

    def over_fsdp(self, k, slot):
        return push(
            self.half, self.from_fsdp.at[slot], self.sems[1].at[0, k], self.sems[1].at[1, k],
            fsdp=self.at ^ k,
        )

    def start(self):
        for k in range(1, 4):
            self.over_seq(k, self.seq).start()
        self.from_seq[self.seq] = self.mine[...]

    def second(self):
        for k in range(1, 4):
            self.over_seq(k, self.seq ^ k).wait_recv()
        total = self.from_seq[0]
        for n in range(1, 4):
            total = total + self.from_seq[n]
        self.half[...] = total
        for k in range(1, self.count):
            self.over_fsdp(k, self.at).start()
        self.from_fsdp[self.at] = total

    def finish(self, out_ref):
        for k in range(1, self.count):
            self.over_fsdp(k, self.at ^ k).wait_recv()
        total = self.from_fsdp[0]
        for n in range(1, self.count):
            total = total + self.from_fsdp[n]
        out_ref[...] = total
        for k in range(1, 4):
            self.over_seq(k, self.seq).wait_send()
        for k in range(1, self.count):
            self.over_fsdp(k, self.at).wait_send()


def small_scratch(count, rows):
    vmem, dma = pltpu.VMEM, pltpu.SemaphoreType.DMA
    return [
        vmem((4, rows, D), F32), vmem((rows, D), F32), vmem((count, rows, D), F32),
        dma((2, 4)), dma((2, count)),
    ]


QUERY, COLUMN, SLOT, INPUT = 8, 16, 24, 32


def back_kernel(
    count, per, x_ref, xs_ref, qkvf_ref, do_ref, p_ref, s_ref, z_ref, kept_ref, dy_ref, doc_ref,
    small_ref, w_ref, ffg_ref, ffr_ref, ffs_ref,
    gi_ref, ff_out, fr_out, q_out, kv_out, f_out, s1_out, s2_out,
    d_all, h_turned, reading, numer, total, col_ref, edge_ref, head, state, heads, head_rows,
    snap, snap_rows, w_held, w_sem, q_piece, kv_piece, f_piece, last_small, *rest,
):
    step = pl.program_id(0)
    seq, at, _, _ = places()
    link = q_piece.dtype

    def take(size):
        nonlocal rest
        out, rest = rest[:size], rest[size:]
        return out

    (own,) = take(1)
    ff = Scatter(count, ffg_ref, own, OVER_X, False, ff_out, take(12))
    (own,) = take(1)
    fr = Scatter(count, ffr_ref, own, OVER_Y, False, fr_out, take(12))
    for_q = Scatter(count, q_piece, None, OVER_X, False, q_out, take(12))
    for_kv = Scatter(count, kv_piece, None, OVER_X, False, kv_out, take(12))
    for_f = Scatter(count, f_piece, None, SHORT, True, f_out, take(10))
    small_one = SmallSum(count, ffs_ref, *take(3), take(2))
    small_two = SmallSum(count, last_small, *take(3), take(2))
    states = States(heads, head_rows, take(2))

    def chunk(u, first, turned=False):
        n = step * per + u - first
        n = 7 - n if turned else n
        here = pl.ds(pl.multiple_of(n * C, C), C)
        block = pl.ds((per - 1 - u if turned else u) * C, C)
        return n, here, block, col_ref[here], doc_ref[:, here].astype(F32)

    def fetch():
        return pltpu.make_async_copy(w_ref, w_held, w_sem)

    def weight_grad(piece, d_lanes, lanes, short=False):
        grad = dot(h_turned[...], d_all[:, d_lanes])
        half, part = count // 2, piece.shape[1]
        for q in range(4):
            x, c = q // 2, q % 2
            share = grad[:, q * 128 : (q + 1) * 128].reshape(half, 2, part, 128).astype(link)
            if short:
                first = (c * 2 + x) * count
                piece[first : first + count, :, lanes] = share.reshape(count, part, 128)
                continue
            for y in range(2):
                first = ((c * 2 + x) * 2 + y) * half
                piece[first : first + half, :, lanes] = share[:, y]

    @pl.when(step == 0)
    def _():
        greet(count)
        fetch().start()
        ff.start()
        small_one.start()
        doc_parts(doc_ref, col_ref, edge_ref)
        head[...] = jnp.zeros_like(head)
        last_small[...] = jnp.zeros_like(last_small)

    def turn():
        weight_grad(q_piece, slice(0, D), slice(0, 128))
        for_q.start()
        states.finish()
        newest = edge_ref[15:16]
        state[...] = jnp.zeros_like(state)
        for n in range(4):
            use = jnp.where(head_rows[n, 1:2] == newest, 1.0, 0.0) * (n > seq).astype(F32)
            state[0:128] += use * heads[n].astype(F32)
            state[128:129] += use * head_rows[n, 0:1]

    def send_states():
        heads[seq] = head[0:128].astype(link)
        head_rows[seq, 0:1] = head[128:129]
        head_rows[seq, 1:2] = edge_ref[0:1]
        head_rows[seq, 2:8] = jnp.zeros((6, D), F32)
        states.start()

    def key_value_grads():
        weight_grad(kv_piece, slice(D, 2 * D), slice(0, 128))
        weight_grad(kv_piece, slice(2 * D, 3 * D), slice(128, 256))
        for_kv.start()

    def slot_grads():
        weight_grad(f_piece, slice(3 * D, 4 * D), slice(0, 128), True)
        for_f.start()

    def last():
        small_two.start()
        for_f.advance(2)
        small_two.second()
        for_kv.forward()
        for piece in (ff, fr, for_q):
            piece.finish()
        states.drain()
        small_two.finish(s2_out)
        for_kv.finish()
        for_f.finish()

    schedule = {
        0: [fr.start],
        2: [lambda: ff.advance(0), small_one.second],
        4: [lambda: fr.advance(0)],
        QUERY - 1: [send_states],
        QUERY + 7: [turn],
        COLUMN: [lambda: ff.advance(1)],
        COLUMN + 1: [lambda: fr.advance(1), lambda: for_q.advance(0)],
        COLUMN + 4: [lambda: for_q.advance(1)],
        COLUMN + 5: [lambda: ff.advance(2)],
        COLUMN + 7: [key_value_grads, lambda: for_q.advance(2)],
        SLOT: [lambda: fr.advance(2)],
        SLOT + 1: [lambda: for_kv.advance(0)],
        SLOT + 2: [lambda: ff.advance(3)],
        SLOT + 4: [lambda: fr.advance(3), lambda: for_q.advance(3)],
        SLOT + 6: [lambda: for_kv.advance(1)],
        SLOT + 7: [slot_grads],
        INPUT + 1: [lambda: for_f.advance(0), lambda: for_kv.advance(2)],
        INPUT + 3: [ff.forward, for_q.forward, fr.forward, lambda: small_one.finish(s1_out)],
        INPUT + 5: [lambda: for_f.advance(1), lambda: for_kv.advance(3)],
        INPUT + 7: [last],
    }

    for u in range(per):

        @pl.when(step < QUERY // per)
        def _(u=u):
            n, here, block, col, row = chunk(u, 0)

            def aside():
                unit, _ = norm_parts(x_ref[block].astype(F32))
                h_turned[:, here] = (unit * small_ref[0:1] + small_ref[1:2]).astype(BF16).T

            row_body(
                n, qkvf_ref.at[block], do_ref.at[block], p_ref.at[block], s_ref.at[block],
                z_ref.at[block], kept_ref.at[pl.ds(u, 1)], col, row, edge_ref,
                reading.at[here], numer.at[here], total.at[here], head, aside,
            )

        @pl.when((step >= QUERY // per) & (step < COLUMN // per))
        def _(u=u):
            n, here, block, col, row = chunk(u, QUERY)
            query_body(
                n, qkvf_ref.at[block], kept_ref.at[pl.ds(u, 1)], col, row, edge_ref,
                numer.at[here], d_all.at[here, 0:D],
            )

        @pl.when((step >= COLUMN // per) & (step < SLOT // per))
        def _(u=u):
            n, here, block, col, row = chunk(u, COLUMN, True)
            column_body(
                n, qkvf_ref.at[block], do_ref.at[block], reading.at[here], numer.at[here],
                total.at[here], col, row, edge_ref, state, snap, snap_rows, d_all.at[here],
            )

        @pl.when((step >= SLOT // per) & (step < INPUT // per))
        def _(u=u):
            n, here, block, col, row = chunk(u, SLOT, True)
            slot_body(
                n, qkvf_ref.at[block], do_ref.at[block], reading.at[here], numer.at[here],
                total.at[here], col, row, edge_ref, snap, snap_rows, d_all.at[here],
            )

        if u == 0:

            @pl.when(step == INPUT // per)
            def _():
                fetch().wait()

            @pl.when(step >= INPUT // per)
            def _():
                size = xs_ref.shape[0]
                here = pl.ds(pl.multiple_of((step - INPUT // per) * size, size), size)
                grad = dot_nt(d_all[here], w_held[...])
                unit, scale = norm_parts(xs_ref[...].astype(F32))
                last_small[0:1] += jnp.sum(grad * unit, axis=0, keepdims=True)
                last_small[1:2] += jnp.sum(grad, axis=0, keepdims=True)
                gi_ref[...] = dy_ref[...] + norm_back(unit, scale, small_ref[0:1], grad)

        for when, actions in schedule.items():
            if when % per == u:

                @pl.when(step == when // per)
                def _(actions=actions):
                    for action in actions:
                        action()


def back(
    count, tokens, qkvf, do, probs, score, inverse, kept, dy, doc_ids, small, w_all, ffg, ffr, ffs
):
    rows = tokens.shape[0]
    part, link = ffg.shape[1], ffg.dtype
    per = 2 if link == BF16 else 1
    size = per * C
    blocks = 8 // per
    once = lambda a: pl.BlockSpec(a.shape, lambda i: (0,) * a.ndim)
    anywhere = pl.BlockSpec(memory_space=pl.ANY)
    vmem, dma = pltpu.VMEM, pltpu.SemaphoreType.DMA

    def early(i):
        return jnp.minimum(i, blocks - 1)

    def twice(i):
        return jnp.where(i < blocks, i, jnp.clip(i - blocks, 0, blocks - 1))

    def turned(i):
        return blocks - 1 - lax.rem(jnp.clip(i - 2 * blocks, 0, 2 * blocks - 1), blocks)

    def always(i):
        return jnp.where(i < 2 * blocks, twice(i), turned(i))

    def both(i):
        return jnp.where(i < blocks, i, turned(i))

    late = lambda i: (jnp.maximum(i - 4 * blocks, 0), 0)
    tall = pl.BlockSpec((size, D), late)
    some = lambda lanes, order: pl.BlockSpec((size, lanes), lambda i: (order(i), 0))
    slabs = 4 * count
    return pl.pallas_call(
        functools.partial(back_kernel, count, per),
        grid=(5 * blocks,),
        in_specs=[some(D, early), tall, some(4 * D, always), some(D, both)]
        + [some(D, early)] * 3
        + [pl.BlockSpec((per, 128, D), lambda i: (twice(i), 0, 0)), tall]
        + [once(doc_ids), once(small), anywhere, anywhere, anywhere, once(ffs)],
        out_specs=[tall] + [anywhere] * 5 + [whole(16, D), whole(8, D)],
        out_shape=[
            shape_of((rows, D), F32),
            shape_of((4, part, 640), F32),
            shape_of((4, part, D), F32),
            shape_of((4, part, 128), F32),
            shape_of((4, part, 256), F32),
            shape_of((4, part, 128), F32),
            shape_of((16, D), F32),
            shape_of((8, D), F32),
        ],
        scratch_shapes=[
            vmem((rows, 4 * D), BF16),
            vmem((D, rows), BF16),
            vmem((rows, D), BF16),
            vmem((rows, D), F32),
            vmem((rows, D), F32),
            vmem((rows, 128), F32),
            vmem((16, D), F32),
            vmem((136, D), F32),
            vmem((136, D), F32),
            vmem((4, 128, D), link),
            vmem((4, 8, D), F32),
            vmem((8, 128, D), BF16),
            vmem((8, D), F32),
            vmem(w_all.shape, BF16),
            dma,
            vmem((slabs, part, 128), link),
            vmem((slabs, part, 256), link),
            vmem((slabs, part, 128), link),
            vmem((8, D), F32),
        ]
        + scatter_scratch(count, part, 640, link, OVER_X, True)
        + scatter_scratch(count, part, D, link, OVER_Y, True)
        + scatter_scratch(count, part, 128, link, OVER_X, False)
        + scatter_scratch(count, part, 256, link, OVER_X, False)
        + scatter_scratch(count, part, 128, link, SHORT, False)
        + small_scratch(count, 16)
        + small_scratch(count, 8)
        + [dma((3, 2)), dma((3, 2))],
        compiler_params=pltpu.CompilerParams(
            vmem_limit_bytes=(62 if link == BF16 else 63) * MIB, collective_id=2, has_side_effects=True
        ),
        name="back",
    )(
        tokens, tokens, qkvf, do, probs, score, inverse, kept, dy, doc_ids, small, w_all, ffg, ffr,
        ffs,
    )


def finish_kernel(
    count, part, gi_ref, ff_ref, fr_ref, q_ref, kv_ref, f_ref, s1_ref, s2_ref, gi_out, *rest
):
    at = lax.axis_index("fsdp")
    *outs, held, sems = rest
    size = held.shape[0] // 8

    def move(n, out):
        here = pl.ds(n * size, size)
        if out:
            return pltpu.make_async_copy(held.at[here], gi_out.at[here], sems.at[1, n])
        return pltpu.make_async_copy(gi_ref.at[here], held.at[here], sems.at[0, n])

    def pick(row, size):
        out = row(0, size)
        for f in range(1, count):
            out = jnp.where(at == f, row(f * size, size), out)
        return out

    def bias(start, size):
        r = start // D
        return s1_ref[8 + r : 9 + r, start - r * D : start - r * D + size]

    def row_of_sums(ref, n):
        return lambda start, size: ref[n : n + 1, start : start + size]

    for n in range(8):
        move(n, False).start()
    for n in range(4):
        lanes = slice(n * 128, (n + 1) * 128)
        outs[0][:, lanes] = q_ref[n]
        outs[1][:, lanes] = kv_ref[n, :, 0:128]
        outs[2][:, lanes] = kv_ref[n, :, 128:256]
        outs[3][:, lanes] = f_ref[n]
        outs[4][:, lanes] = ff_ref[n, :, 512:640]
        outs[5][:, n * 512 : (n + 1) * 512] = ff_ref[n, :, 0:512]
        for j in range(4):
            outs[6][j * part : (j + 1) * part, lanes] = fr_ref[n, :, j * 128 : (j + 1) * 128]
    for n in range(8):
        move(n, False).wait()
        move(n, True).start()
    outs[7][...] = pick(row_of_sums(s2_ref, 0), part)
    outs[8][...] = pick(row_of_sums(s2_ref, 1), part)
    outs[9][...] = pick(row_of_sums(s1_ref, 2), part)
    outs[10][...] = pick(row_of_sums(s1_ref, 3), part)
    outs[11][...] = pick(bias, 4 * part)
    outs[12][...] = pick(row_of_sums(s1_ref, 4), part)
    for n in range(8):
        move(n, True).wait()


def finish(count, part, grad_input, *sums):
    once = lambda shape: pl.BlockSpec(shape, lambda: (0,) * len(shape))
    anywhere = pl.BlockSpec(memory_space=pl.ANY)
    shapes = [(part, D)] * 5 + [(part, FF), (4 * part, D)]
    shapes += [(1, part)] * 4 + [(1, 4 * part), (1, part)]
    return pl.pallas_call(
        functools.partial(finish_kernel, count, part),
        in_specs=[anywhere] + [once(a.shape) for a in sums],
        out_specs=[anywhere] + [once(s) for s in shapes],
        out_shape=[shape_of(s, F32) for s in (grad_input.shape, *shapes)],
        scratch_shapes=[
            pltpu.VMEM(grad_input.shape, F32),
            pltpu.SemaphoreType.DMA((2, 8)),
        ],
        compiler_params=PARAMS,
        name="finish",
    )(grad_input, *sums)


def rows_of(lanes, order=lambda i: i):
    return pl.BlockSpec((C, lanes), lambda i: (order(i), 0))


def whole(*shape):
    return pl.BlockSpec(shape, lambda i: (0,) * len(shape))


def row_of(order=lambda i: i):
    return pl.BlockSpec((1, C), lambda i: (0, order(i)))


def shape_of(shape, kind):
    return jax.ShapeDtypeStruct(shape, kind)


PARAMS = pltpu.CompilerParams(vmem_limit_bytes=62 * MIB)


def on_device(
    tokens, doc_ids, w_query, w_key, w_value, w_slots, w_output, w_hidden, w_return,
    gain_first, shift_first, gain_second, shift_second, bias_hidden, bias_return, cotangent,
):
    rows = tokens.shape[0]
    count = lax.axis_size("fsdp")
    part = gain_first.shape[0]
    flat = lambda a: a.reshape(1, a.shape[0])
    qkvf, attended, probs, score, inverse, kept, w_qkvf, w_o, w_h, w_r, small, bias = front(
        count, tokens, doc_ids,
        (w_query, w_key, w_value, w_slots, w_output, w_hidden, w_return),
        [flat(a) for a in (gain_first, shift_first, gain_second, shift_second, bias_return)],
        flat(bias_hidden),
    )
    link = w_qkvf.dtype
    w_qkvf, w_o, w_h, w_r = (
        a.reshape(-1, a.shape[2]).astype(BF16) for a in (w_qkvf, w_o, w_h, w_r)
    )
    tall = pl.BlockSpec((FEED_ROWS, D), lambda i: (i, 0))
    half = count // 2
    out, grad_middle, grad_attended, pack, pack_r, ff_small = pl.pallas_call(
        forward_kernel,
        grid=(rows // FEED_ROWS,),
        in_specs=[tall] * 3
        + [whole(8, D), whole(1, FF), whole(D, D), whole(D, FF), whole(FF, D)],
        out_specs=[tall] * 3
        + [whole(2, 2, 2, half, part, 640), whole(2, 2, half, 2, part, D), whole(16, D)],
        out_shape=[
            shape_of((rows, D), BF16),
            shape_of((rows, D), F32),
            shape_of((rows, D), BF16),
            shape_of((2, 2, 2, half, part, 640), link),
            shape_of((2, 2, half, 2, part, D), link),
            shape_of((16, D), F32),
        ],
        scratch_shapes=[
            pltpu.VMEM((D, D), F32),
            pltpu.VMEM((D, FF), F32),
            pltpu.VMEM((D, FF), F32),
        ],
        compiler_params=PARAMS,
        name="feed",
    )(tokens, attended, cotangent, small, bias, w_o, w_h, w_r)

    grad_input, *sums = back(
        count, tokens, qkvf, grad_attended, probs, score, inverse, kept, grad_middle, doc_ids,
        small, w_qkvf, pack.reshape(-1, part, 640), pack_r.reshape(-1, part, D), ff_small,
    )
    grad_input, *grads = finish(count, part, grad_input, *sums)
    return (out, grad_input, *grads[:7], *(a.reshape(-1) for a in grads[7:]))


def solution(mesh):
    tall, flat, one = P(("fsdp", "seq"), None), P("fsdp", None), P("fsdp")
    return jax.shard_map(
        on_device,
        mesh=mesh,
        in_specs=(tall, P("fsdp", "seq")) + (flat,) * 7 + (one,) * 6 + (tall,),
        out_specs=(tall, tall) + (flat,) * 7 + (one,) * 6,
        check_vma=False,
    )
```

```python
import functools
import types

import jax
import jax.numpy as jnp
from jax import lax
from jax.experimental import pallas as pl
from jax.experimental.pallas import tpu as pltpu
from jax.sharding import PartitionSpec as P

D = 512
H = 8
M = 64
FF = 2048
C = 256
GROUP = 256
EPS = 1e-05
SCALE = 0.125
F32 = jnp.float32
BF16 = jnp.bfloat16
FEED_ROWS = 512
FEED_LANES = 256
FRONT = 4
MIB = 1024 * 1024


def dot(a, b):
    return lax.dot_general(a, b, (((1,), (0,)), ((), ())), preferred_element_type=F32)


def dot_nt(a, b):
    return lax.dot_general(a, b, (((1,), (1,)), ((), ())), preferred_element_type=F32)


def dot_tn(a, b):
    return lax.dot_general(a, b, (((0,), (0,)), ((), ())), preferred_element_type=F32)


def lane_heads(rows, lanes):
    return lax.broadcasted_iota(jnp.int32, (rows, lanes), 1) // M


def stacked(values):
    heads = lane_heads(C, GROUP)
    zero = jnp.zeros_like(values)
    return jnp.concatenate([jnp.where(heads == h, values, zero) for h in range(4)], axis=0)


def select(values):
    heads = lane_heads(C, GROUP)
    out = values[3 * C :]
    for h in (2, 1, 0):
        out = jnp.where(heads == h, values[h * C : (h + 1) * C], out)
    return out


def masked(values, mask):
    return jnp.concatenate(
        [values[h * C : (h + 1) * C].astype(BF16) * mask for h in range(4)], axis=0
    )


def expand(compact):
    rows = lax.broadcasted_iota(jnp.int32, (GROUP, GROUP), 0) // M
    full = jnp.concatenate([compact] * 4, axis=0)
    return jnp.where(rows == lane_heads(GROUP, GROUP), full, jnp.zeros_like(full))


def compacted(full):
    heads = lane_heads(M, GROUP)
    out = full[3 * M :]
    for h in (2, 1, 0):
        out = jnp.where(heads == h, full[h * M : (h + 1) * M], out)
    return out


def split(values):
    high = values.astype(BF16)
    return high, (values - high.astype(F32)).astype(BF16)


def ones_block():
    rows = lax.broadcasted_iota(jnp.int32, (GROUP, GROUP), 0) // M
    return (rows == lane_heads(GROUP, GROUP)).astype(BF16)


def head_sums(values):
    high, low = split(values)
    ones = ones_block()
    return dot(high, ones) + dot(low, ones)


def head_max(values):
    left = lane_heads(C, 128) == 0
    out = []
    for p in range(2):
        pair = values[:, p * 128 : (p + 1) * 128]
        one = jnp.max(jnp.where(left, pair, -jnp.inf), axis=1, keepdims=True)
        two = jnp.max(jnp.where(left, -jnp.inf, pair), axis=1, keepdims=True)
        out.append(jnp.where(left, one, two))
    return jnp.concatenate(out, axis=1)


def wide(values, times):
    return jnp.concatenate([values] * times, axis=1)


def visible(doc_col, doc_row):
    same = wide(doc_col, 2) == doc_row
    here = lax.broadcasted_iota(jnp.int32, (C, C), 0)
    there = lax.broadcasted_iota(jnp.int32, (C, C), 1)
    return jnp.where(same & (here >= there), 1.0, 0.0).astype(BF16)


def visible_back(doc_col, doc_row):
    same = wide(doc_col, 2) == doc_row
    here = lax.broadcasted_iota(jnp.int32, (C, C), 0)
    there = lax.broadcasted_iota(jnp.int32, (C, C), 1)
    return jnp.where(same & (there >= here), 1.0, 0.0).astype(BF16)


def flag(doc_col, doc):
    return jnp.where(doc_col == doc[:, :128], 1.0, 0.0)


def norm_parts(values):
    centre = jnp.mean(values, axis=-1, keepdims=True)
    centred = values - centre
    spread = jnp.mean(centred * centred, axis=-1, keepdims=True)
    scale = lax.rsqrt(spread + EPS)
    return centred * scale, scale


def norm_back(unit, scale, gain, grad):
    inner = grad * gain
    return scale * (
        inner
        - jnp.mean(inner, axis=-1, keepdims=True)
        - unit * jnp.mean(inner * unit, axis=-1, keepdims=True)
    )


def groups(values):
    return values[:, :GROUP], values[:, GROUP:]


def state_terms(slots, left, right):
    one, two = [], []
    for g in range(2):
        lanes = slice(g * GROUP, (g + 1) * GROUP)
        both = dot_tn(slots[:, lanes], jnp.concatenate([left[:, lanes], right[:, lanes]], axis=1))
        one.append(compacted(both[:, :GROUP]))
        two.append(compacted(both[:, GROUP:]))
    return jnp.concatenate(one, axis=1), jnp.concatenate(two, axis=1)


def lanes_of(g):
    return slice(g * GROUP, (g + 1) * GROUP)


def part_of(ref, part, g):
    return ref[:, part * D + g * GROUP : part * D + (g + 1) * GROUP]


def attend_body(
    n, qkvf_ref, slots, vis, col, edge_ref, state, o_ref, p_ref, s_ref, z_ref, kept_ref
):
    kept_ref[0] = state[0:128]
    first = edge_ref[pl.ds(0, 1)]
    before = edge_ref[pl.ds(8 + jnp.maximum(n - 1, 0), 1)]
    last = jnp.where(n == 0, first, before)
    newest = edge_ref[pl.ds(8 + n, 1)]
    carried = wide(flag(col, last), 2)
    norm = dot(vis, slots)
    key_states = [expand(state[0:64, lanes_of(g)]).astype(BF16) for g in range(2)]
    value_states = [expand(state[64:128, lanes_of(g)]).astype(BF16) for g in range(2)]
    norm_state = state[128:129]

    def affine(g):
        return masked(dot_nt(stacked(part_of(qkvf_ref, 0, g)), part_of(qkvf_ref, 1, g)), vis)

    def scores(g, affinity):
        lanes = lanes_of(g)
        numer = select(dot(affinity, slots[:, lanes]))
        numer = numer + carried * dot_nt(part_of(qkvf_ref, 0, g), key_states[g])
        inverse = 1.0 / (norm[:, lanes] + carried * norm_state[:, lanes])
        return numer * inverse * SCALE, inverse

    def grow(score):
        return jnp.exp(score - head_max(score))

    def read(g, score, inverse, grown):
        lanes = lanes_of(g)
        probs = grown / head_sums(grown)
        p_ref[:, lanes] = probs
        s_ref[:, lanes] = score
        z_ref[:, lanes] = inverse
        return (probs * inverse).astype(BF16)

    def mixing(g, reading):
        return masked(dot_nt(stacked(reading), slots[:, lanes_of(g)]), vis)

    def mixed(g, reading, mix):
        out = select(dot(mix, part_of(qkvf_ref, 2, g))) + carried * dot(reading, value_states[g])
        o_ref[:, lanes_of(g)] = out.astype(BF16)

    affinity = affine(0)
    score, inverse = scores(0, affinity)
    affinity = affine(1)
    grown = grow(score)
    score_two, inverse_two = scores(1, affinity)
    reading = read(0, score, inverse, grown)
    tail = wide(flag(col, newest), 4).astype(BF16) * slots
    new_keys, new_values = state_terms(tail, qkvf_ref[:, D : 2 * D], qkvf_ref[:, 2 * D : 3 * D])
    same = jnp.where(last == newest, 1.0, 0.0)
    state[0:64] = same * state[0:64] + new_keys
    state[64:128] = same * state[64:128] + new_values
    state[128:129] = same * state[128:129] + jnp.sum(tail.astype(F32), axis=0, keepdims=True)
    grown = grow(score_two)
    mix = mixing(0, reading)
    reading_two = read(1, score_two, inverse_two, grown)
    mixed(0, reading, mix)
    mix = mixing(1, reading_two)
    mixed(1, reading_two, mix)


MESH_ID = pl.DeviceIdType.MESH


def places():
    seq, at = lax.axis_index("seq"), lax.axis_index("fsdp")
    core = lax.rem(seq, 2)
    return seq, at, seq + 1 - 2 * core, lax.rem(seq + 2, 4)


def push(src, dst, send, recv, **device):
    return pltpu.make_async_remote_copy(
        src_ref=src, dst_ref=dst, send_sem=send, recv_sem=recv,
        device_id=device, device_id_type=MESH_ID,
    )


def greet(count):
    seq, at, _, _ = places()
    barrier = pltpu.get_barrier_semaphore()
    for k in range(1, count):
        pl.semaphore_signal(barrier, inc=1, device_id={"fsdp": at ^ k}, device_id_type=MESH_ID)
    for k in range(1, 4):
        pl.semaphore_signal(barrier, inc=1, device_id={"seq": seq ^ k}, device_id_type=MESH_ID)
    pl.semaphore_wait(barrier, count - 1 + 3)


class Gather:
    def __init__(self, count, mine, held, base, width, four, sems):
        self.count, self.mine, self.held, self.four = count, mine, held, four
        self.far, self.near, self.core, self.chip, self.onward, self.local = sems
        self.seq, self.at, self.sibling, self.beside = places()
        self.base, self.share = base, width // (4 if four else 2)
        self.evens = range(0, count, 2)

    def lanes(self, seq):
        place = seq if self.four else lax.rem(seq, 2)
        return pl.ds(pl.multiple_of(self.base + place * self.share, 128), self.share)

    def part(self, k, seq):
        return self.held.at[self.at ^ k, :, self.lanes(seq)]

    def source(self, k):
        if k:
            return self.part(k, self.seq)
        return self.mine.at[:, self.lanes(self.seq)]

    def own(self):
        return pltpu.make_async_copy(self.source(0), self.part(0, self.seq), self.local)

    def over(self, sems, k, **device):
        return push(self.source(k), self.part(k, self.seq), sems[0].at[k], sems[1].at[k], **device)

    def come(self, sems, k, owner):
        here = self.part(owner, self.seq)
        return push(here, here, sems[0].at[k], sems[1].at[k], seq=self.sibling)

    def far_out(self, k):
        return push(
            self.source(0), self.part(0, self.seq), self.far[0].at[k], self.far[1].at[k],
            fsdp=self.at ^ k,
        )

    def far_in(self, k):
        return self.come(self.far, k, k)

    def near_out(self, k):
        return self.over(self.near, k, fsdp=self.at ^ 1)

    def near_in(self, k):
        return self.come(self.near, k, k ^ 1)

    def start(self):
        self.own().start()
        for k in self.evens[1:]:
            self.far_out(k).start()
        self.near_out(0).start()

    def second(self):
        for k in self.evens[1:]:
            self.far_in(k).wait_recv()
            self.near_out(k).start()

    def hop(self, sems, source, target):
        here = self.held.at[:, :, self.lanes(source)]
        return push(here, here, sems[0].at[0], sems[1].at[0], seq=target)

    def third(self):
        self.own().wait()
        for k in self.evens:
            self.near_in(k).wait_recv()
        self.hop(self.core, self.seq, self.sibling).start()
        if self.four:
            self.hop(self.chip, self.seq, self.beside).start()

    def fourth(self):
        self.hop(self.chip, self.beside, self.beside).wait_recv()
        self.hop(self.onward, self.beside, self.sibling).start()

    def finish(self):
        self.hop(self.core, self.sibling, self.sibling).wait_recv()
        self.hop(self.core, self.seq, self.sibling).wait_send()
        if self.four:
            self.hop(self.onward, lax.rem(self.sibling + 2, 4), self.sibling).wait_recv()
            self.hop(self.chip, self.seq, self.beside).wait_send()
            self.hop(self.onward, self.beside, self.sibling).wait_send()

    def core_out(self, k):
        return self.over(self.core, k, seq=self.sibling)

    def core_in(self, k):
        here = self.part(k, self.sibling)
        return push(here, here, self.core[0].at[k], self.core[1].at[k], seq=self.sibling)

    def at_once(self, between):
        self.start()
        self.core_out(0).start()
        for k in self.evens[1:]:
            self.far_in(k).wait_recv()
            self.near_out(k).start()
            self.core_out(k).start()
        between()
        for k in self.evens:
            self.near_in(k).wait_recv()
            self.core_out(k ^ 1).start()
        self.own().wait()
        for k in range(self.count):
            self.core_in(k).wait_recv()

    def drain(self, each=False):
        for k in self.evens:
            self.near_out(k).wait_send()
            if k:
                self.far_out(k).wait_send()
        if each:
            for k in range(self.count):
                self.core_out(k).wait_send()


def gather_sems(count, each):
    n = count if each else 1
    pair = lambda size: [pltpu.SemaphoreType.DMA((size,)), pltpu.SemaphoreType.DMA((size,))]
    return pair(count) + pair(count) + pair(n) + pair(1) + pair(1) + [pltpu.SemaphoreType.DMA]


def bundle(refs):
    return [(refs[2 * n], refs[2 * n + 1]) for n in range(5)] + [refs[10]]


class States:
    def __init__(self, big, small, sems):
        self.refs, self.sems = (big, small), sems
        self.seq, _, self.sibling, self.beside = places()

    def hop(self, n, source, target):
        out = []
        for m, ref in enumerate(self.refs):
            here = ref.at[source]
            out.append(push(here, here, self.sems[0].at[n, m], self.sems[1].at[n, m], seq=target))
        return out

    def start(self):
        for copy in self.hop(0, self.seq, self.sibling) + self.hop(1, self.seq, self.beside):
            copy.start()

    def finish(self):
        for copy in self.hop(1, self.beside, self.beside):
            copy.wait_recv()
        for copy in self.hop(2, self.beside, self.sibling):
            copy.start()
        for copy in self.hop(0, self.sibling, self.sibling):
            copy.wait_recv()
        for copy in self.hop(2, lax.rem(self.sibling + 2, 4), self.sibling):
            copy.wait_recv()

    def drain(self):
        for copy in (
            self.hop(0, self.seq, self.sibling)
            + self.hop(1, self.seq, self.beside)
            + self.hop(2, self.beside, self.sibling)
        ):
            copy.wait_send()


def doc_parts(doc_ref, col_ref, edge_ref):
    here = lax.broadcasted_iota(jnp.int32, (C, C), 0)
    there = lax.broadcasted_iota(jnp.int32, (C, C), 1)
    eye = jnp.where(here == there, 1.0, 0.0).astype(BF16)
    for n in range(doc_ref.shape[1] // C):
        row = doc_ref[:, n * C : (n + 1) * C].astype(F32)
        col_ref[n * C : (n + 1) * C] = dot_nt(eye, jnp.broadcast_to(row, (128, C)).astype(BF16))
        low = jnp.min(row, axis=1, keepdims=True)
        high = jnp.max(row, axis=1, keepdims=True)
        edge_ref[n : n + 1] = jnp.broadcast_to(low, (1, D))
        edge_ref[n + 8 : n + 9] = jnp.broadcast_to(high, (1, D))


def spread_small(vec_refs, bias_ref, out_ref):
    def repeat(values):
        width = values.shape[1]
        rows = lax.broadcasted_iota(jnp.int32, (width, 128), 0)
        lanes = lax.broadcasted_iota(jnp.int32, (width, 128), 1)
        pick = jnp.where(lax.rem(lanes, width) == rows, 1.0, 0.0).astype(BF16)
        return dot(jnp.broadcast_to(values, (8, width)).astype(BF16), pick)[0:1]

    out_ref[...] = jnp.zeros_like(out_ref)
    for n, ref in enumerate(vec_refs):
        out_ref[n : n + 1] = repeat(ref[...])
    for b in range(max(bias_ref.shape[1] // 128, 1)):
        out_ref[5 + b : 6 + b] = repeat(bias_ref[:, b * 128 : (b + 1) * 128])


def join_small(count, part, gathered, vec_ref, bias_ref):
    lanes = lax.broadcasted_iota(jnp.int32, (8, D), 1)
    total = jnp.zeros((8, D), F32)
    for f in range(count):
        total = jnp.where(lanes // part == f, wide(gathered[f], 4), total)
    vec_ref[...] = total
    size = 4 * part
    for r in range(4):
        at = lanes[0:1] + r * D
        row = jnp.zeros((1, D), F32)
        for f in range(r * D // size, -(-(r + 1) * D // size)):
            for b in range(max(size // 128, 1)):
                use = (at // size == f) & (lax.rem(at, size) // 128 == b)
                row = jnp.where(use, wide(gathered[f, 5 + b : 6 + b], 4), row)
        bias_ref[0:1, r * D : (r + 1) * D] = row


ROOT = 0.7978845608028654
CUBE = 0.044715


def gelu_both(u):
    square = u * u
    bent = jnp.tanh(ROOT * u * (1.0 + CUBE * square))
    half = 0.5 * (1.0 + bent)
    slope = half + 0.5 * u * (1.0 - bent * bent) * (ROOT * (1.0 + 3.0 * CUBE * square))
    return u * half, slope


def feed_body(
    values, attended, cot, vec_ref, bias_ref, w_out, w_hidden, w_return, ready,
    y_ref, dy_ref, do_ref, gsmall_ref, gwo_ref, gwh_ref, gwr_ref,
):
    middle = values.astype(F32) + dot(attended, w_out())
    unit, scale = norm_parts(middle)
    hidden = (unit * vec_ref[2:3] + vec_ref[3:4]).astype(BF16)
    out = middle + vec_ref[4:5]
    grad_hidden = jnp.zeros_like(middle)
    cot32 = cot.astype(F32)
    tiles = FF // FEED_LANES
    ready()

    def into(j):
        cols = slice(j * FEED_LANES, (j + 1) * FEED_LANES)
        inner = dot(hidden, w_hidden(j)) + bias_ref[0:1, cols]
        return inner, dot_nt(cot, w_return(j))

    def bend(inner, grad):
        gated, slope = gelu_both(inner)
        return gated.astype(BF16), (grad * slope).astype(BF16)

    def outof(j, active, low):
        cols = slice(j * FEED_LANES, (j + 1) * FEED_LANES)
        there = slice(cols.start % D, cols.start % D + FEED_LANES)
        row = 8 + cols.start // D
        gwr_ref[:, cols] += dot_tn(cot, active)
        gsmall_ref[row : row + 1, there] += jnp.sum(low.astype(F32), axis=0, keepdims=True)
        gwh_ref[:, cols] += dot_tn(hidden, low)
        return dot(active, w_return(j)), dot_nt(low, w_hidden(j))

    coming = into(0)
    for j in range(tiles):
        bent = bend(*coming)
        if j + 1 < tiles:
            coming = into(j + 1)
        to_out, to_hidden = outof(j, *bent)
        out = out + to_out
        grad_hidden = grad_hidden + to_hidden
    y_ref[...] = out.astype(BF16)
    gsmall_ref[2:3] += jnp.sum(grad_hidden * unit, axis=0, keepdims=True)
    gsmall_ref[3:4] += jnp.sum(grad_hidden, axis=0, keepdims=True)
    gsmall_ref[4:5] += jnp.sum(cot32, axis=0, keepdims=True)
    grad_middle = cot32 + norm_back(unit, scale, vec_ref[2:3], grad_hidden)
    dy_ref[...] = grad_middle
    branch = grad_middle.astype(BF16)
    gwo_ref[...] += dot_tn(attended, branch)
    do_ref[...] = dot_nt(branch, w_out()).astype(BF16)


def pack_grads(count, part, gwo_ref, gwh_ref, gwr_ref, put):
    half = count // 2
    for q in range(4):
        x, c = q // 2, q % 2
        hidden_part = gwh_ref[:, q * 512 : (q + 1) * 512].reshape(half, 2, part, 512)
        out_part = gwo_ref[:, q * 128 : (q + 1) * 128].reshape(half, 2, part, 128)
        turned = gwr_ref[q * 128 : (q + 1) * 128].T.reshape(half, 2, 4, part, 128)
        for y in range(2):
            over_x, over_y = ((c * 2 + x) * 2 + y) * half, ((c * 2 + y) * 2 + x) * half
            put(0, over_x, slice(0, 512), hidden_part[:, y])
            put(0, over_x, slice(512, 640), out_part[:, y])
            for j in range(4):
                put(1, over_y, slice(j * 128, (j + 1) * 128), turned[:, y, j])


def feed_kernel(
    x_ref, o_ref, g_ref, small_ref, bias_ref, wo_ref, wh_ref, wr_ref,
    y_ref, dy_ref, do_ref, pack_ref, pack_r_ref, gsmall_ref, gwo_ref, gwh_ref, gwr_ref,
):
    step = pl.program_id(0)
    count, part = wh_ref.shape[0], wh_ref.shape[1]

    @pl.when(step == 0)
    def _():
        for ref in (gwo_ref, gwh_ref, gwr_ref, gsmall_ref):
            ref[...] = jnp.zeros_like(ref)

    feed_body(
        x_ref[...], o_ref[...], g_ref[...], small_ref, bias_ref, *weight_views(wo_ref, wh_ref, wr_ref),
        lambda: None, y_ref, dy_ref, do_ref, gsmall_ref, gwo_ref, gwh_ref, gwr_ref,
    )

    @pl.when(step == pl.num_programs(0) - 1)
    def _():
        def put(which, slab, lanes, values):
            ref = (pack_ref, pack_r_ref)[which]
            n = values.shape[0] * part
            ref[slab * part : slab * part + n, lanes] = values.reshape(n, -1).astype(ref.dtype)

        pack_grads(count, part, gwo_ref, gwh_ref, gwr_ref, put)


def weight_views(wo_ref, wh_ref, wr_ref):
    def w_out():
        return wo_ref[...].reshape(D, D).astype(BF16)

    def w_hidden(j):
        cols = slice(j * FEED_LANES, (j + 1) * FEED_LANES)
        return wh_ref[:, :, cols].reshape(D, FEED_LANES).astype(BF16)

    def w_return(j):
        n = FEED_LANES // wr_ref.shape[1]
        return wr_ref[j * n : (j + 1) * n].reshape(FEED_LANES, D).astype(BF16)

    return w_out, w_hidden, w_return


def front_kernel(count, joined, names, *refs):
    r = types.SimpleNamespace(**dict(zip(names, refs)))
    sems = refs[len(names) :]
    x_ref, doc_ref, vec_out, bias_out = r.x, r.doc, r.vec, r.bias
    qkvf, hidden, w_all, mine = r.qkvf, r.hidden, r.w_all, r.mine
    mine_o, mine_h, mine_r, spread, smalls = r.mine_o, r.mine_h, r.mine_r, r.spread, r.smalls
    col_ref, edge_ref, state, tail = r.col, r.edge, r.state, r.tail
    tails, tail_rows = r.tails, r.tail_rows
    step = pl.program_id(0)
    seq, at, _, _ = places()
    link = mine.dtype
    groups_of_sems = []
    for _ in range(5):
        groups_of_sems.append(bundle(sems[:11]))
        sems = sems[11:]
    small_send, small_recv, state_send, state_recv, out_sem, stage_sem, fed_sem = sems
    main = Gather(count, mine, w_all, D, 3 * D, False, groups_of_sems[0])
    q_piece = Gather(count, mine, w_all, 0, D, False, groups_of_sems[1])
    o_piece = Gather(count, mine_o, r.wo_all, 0, D, True, groups_of_sems[2])
    h_piece = Gather(count, mine_h, r.wh_all, 0, FF, True, groups_of_sems[3])
    r_piece = Gather(count, mine_r, r.wr_all, 0, D, False, groups_of_sems[4])
    later = (q_piece, o_piece, h_piece, r_piece)
    states = States(tails, tail_rows, (state_send, state_recv))

    def small_copy(k, owner):
        return push(
            spread, smalls.at[owner], small_send.at[k], small_recv.at[k], fsdp=at ^ k
        )

    def save():
        return (
            pltpu.make_async_copy(qkvf, r.qkvf_out, out_sem.at[0]),
            pltpu.make_async_copy(w_all, r.w_out, out_sem.at[1]),
        )

    @pl.when(step == 0)
    def _():
        greet(count)
        for n, ref in enumerate((r.w0, r.w1, r.w2, r.w3)):
            mine[:, n * D : (n + 1) * D] = ref[...].astype(BF16).astype(link)
        spread_small((r.v0, r.v1, r.v2, r.v3, r.v4), r.bias_in, spread)
        for k in range(1, count):
            small_copy(k, at).start()

        def between():
            mine_o[...] = r.w4[...].astype(BF16).astype(link)
            mine_h[...] = r.w5[...].astype(BF16).astype(link)
            mine_r[...] = r.w6[...].astype(BF16).astype(link)
            doc_parts(doc_ref, col_ref, edge_ref)
            tail[...] = jnp.zeros_like(tail)
            smalls[at] = spread[...]
            for k in range(1, count):
                small_copy(k, at ^ k).wait_recv()
            join_small(count, r.v0.shape[1], smalls, vec_out, bias_out)
            q_piece.start()
            o_piece.start()

            @pl.loop(0, 8)
            def _(n):
                here = pl.ds(pl.multiple_of(n * C, C), C)
                unit, _ = norm_parts(x_ref[here].astype(F32))
                hidden[here] = (unit * vec_out[0:1] + vec_out[1:2]).astype(BF16)

        main.at_once(between)
        h_piece.start()
        r_piece.start()

    @pl.when(step < FRONT)
    def _():
        size = 8 // FRONT * C
        here = pl.ds(pl.multiple_of(step * size, size), size)
        weights = w_all[:, :, D:].reshape(D, 3 * D).astype(BF16)
        rows = dot(hidden[here], weights).astype(BF16)
        qkvf[here, D:] = rows
        slots = wide(flag(col_ref[here], edge_ref[15:16]), 4) * jnp.exp(rows[:, 2 * D :].astype(F32))
        slots = slots.astype(BF16)
        keys, values = state_terms(slots, rows[:, 0:D], rows[:, D : 2 * D])
        tail[0:64] += keys
        tail[64:128] += values
        tail[128:129] += jnp.sum(slots.astype(F32), axis=0, keepdims=True)

    @pl.when(step == 1)
    def _():
        q_piece.second()
        o_piece.second()

    @pl.when(step == FRONT - 1)
    def _():
        tails[seq] = tail[0:128].astype(link)
        tail_rows[seq, 0:1] = tail[128:129]
        tail_rows[seq, 1:2] = edge_ref[15:16]
        tail_rows[seq, 2:8] = jnp.zeros((6, D), F32)
        states.start()
        q_piece.third()
        q_piece.finish()

        @pl.loop(0, FRONT)
        def _(n):
            size = 8 // FRONT * C
            here = pl.ds(pl.multiple_of(n * size, size), size)
            weights = w_all[:, :, 0:D].reshape(D, D).astype(BF16)
            qkvf[here, 0:D] = dot(hidden[here], weights).astype(BF16)

        for copy in save():
            copy.start()
        o_piece.third()

        @pl.loop(0, 8)
        def _(n):
            here = pl.ds(pl.multiple_of(n * C, C), C)
            hidden[here] = jnp.exp(qkvf[here, 3 * D :].astype(F32)).astype(BF16)
            r.seen[n] = visible(col_ref[here], doc_ref[:, here].astype(F32))

        states.finish()
        first = edge_ref[0:1]
        state[...] = jnp.zeros_like(state)
        for n in range(4):
            use = jnp.where(tail_rows[n, 1:2] == first, 1.0, 0.0) * (n < seq).astype(F32)
            state[0:128] += use * tails[n].astype(F32)
            state[128:129] += use * tail_rows[n, 0:1]
        h_piece.second()

    per = 8 // FRONT

    def kept_copies(n):
        here = pl.ds(pl.multiple_of(n * per * C, per * C), per * C)
        slot = lax.rem(n, 2)
        return [
            pltpu.make_async_copy(r.stage.at[slot, k], out.at[here], stage_sem.at[slot, k])
            for k, out in enumerate((r.p, r.s, r.z))
        ]

    @pl.when((step >= FRONT + 2) & (step < 2 * FRONT))
    def _():
        for copy in kept_copies(step - FRONT - 2):
            copy.wait()

    for u in range(per):

        @pl.when((step >= FRONT) & (step < 2 * FRONT))
        def _(u=u):
            n = (step - FRONT) * per + u
            here = pl.ds(pl.multiple_of(n * C, C), C)
            block = pl.ds(u * C, C)
            slot = lax.rem(step - FRONT, 2)
            attend_body(
                n, qkvf.at[here], hidden[here], r.seen[n], col_ref[here], edge_ref, state,
                r.o.at[here if joined else block], *(r.stage.at[slot, k, block] for k in range(3)),
                r.kept.at[pl.ds(u, 1)],
            )

        if u == 0:

            @pl.when(step == FRONT)
            def _():
                o_piece.fourth()

            @pl.when(step == FRONT + 1)
            def _():
                h_piece.third()

    @pl.when(step == FRONT)
    def _():
        r_piece.second()

    @pl.when((step >= FRONT) & (step < 2 * FRONT))
    def _():
        for copy in kept_copies(step - FRONT):
            copy.start()

    @pl.when(step == 2 * FRONT - 1)
    def _():
        r_piece.third()
        h_piece.fourth()
        o_piece.finish()
        for copy in save():
            copy.wait()

    def complete():
        h_piece.finish()
        r_piece.finish()
        for piece in later:
            piece.drain()
        main.drain(True)
        states.drain()
        for k in range(1, count):
            small_copy(k, at).wait_send()
        for n in (FRONT - 2, FRONT - 1):
            for copy in kept_copies(n):
                copy.wait()

    if not joined:
        pl.when(step == 2 * FRONT - 1)(complete)
        return

    @pl.when(step == 2 * FRONT)
    def _():
        for ref in (r.gwo, r.gwh, r.gwr, r.gsmall):
            ref[...] = jnp.zeros_like(ref)

    fed = step - 2 * FRONT

    def fed_copies(n):
        here = pl.ds(pl.multiple_of(n * FEED_ROWS, FEED_ROWS), FEED_ROWS)
        slot = lax.rem(n, 2)
        pairs = ((r.held_y, r.y), (r.held_dy, r.dy), (r.held_do, r.do))
        return [
            pltpu.make_async_copy(held.at[slot], out.at[here], fed_sem.at[slot, k])
            for k, (held, out) in enumerate(pairs)
        ]

    @pl.when(fed >= 2)
    def _():
        for copy in fed_copies(fed - 2):
            copy.wait()

    @pl.when(fed >= 0)
    def _():
        here = pl.ds(pl.multiple_of(fed * FEED_ROWS, FEED_ROWS), FEED_ROWS)
        slot = lax.rem(fed, 2)
        feed_body(
            x_ref[here], r.o[here], r.g[...], vec_out, bias_out,
            *weight_views(r.wo_all, r.wh_all, r.wr_all),
            lambda: pl.when(step == 2 * FRONT)(complete),
            r.held_y.at[slot], r.held_dy.at[slot], r.held_do.at[slot], r.gsmall, r.gwo, r.gwh, r.gwr,
        )
        for copy in fed_copies(fed):
            copy.start()

    @pl.when(step == pl.num_programs(0) - 1)
    def _():
        part = mine.shape[0]

        def put(which, slab, lanes, values):
            n = values.shape[0] * part
            at_lane = 640 * which + lanes.start
            qkvf[slab * part : slab * part + n, at_lane : at_lane + values.shape[2]] = (
                values.reshape(n, -1).astype(BF16)
            )

        pack_grads(count, part, r.gwo, r.gwh, r.gwr, put)
        copies = [
            pltpu.make_async_copy(qkvf.at[:, 0:640], r.pack, out_sem.at[0]),
            pltpu.make_async_copy(qkvf.at[:, 640:1152], r.pack_r, out_sem.at[1]),
        ]
        for copy in copies:
            copy.start()
        last = x_ref.shape[0] // FEED_ROWS - 1
        for copy in (*fed_copies(last - 1), *fed_copies(last), *copies):
            copy.wait()


def front(count, tokens, doc_ids, weights, vectors, bias, cotangent):
    rows = tokens.shape[0]
    part = weights[0].shape[0]
    link = BF16 if part % 16 == 0 else F32
    joined = link == BF16
    per = 8 // FRONT
    once = lambda a: pl.BlockSpec(a.shape, lambda i: (0,) * a.ndim)
    late = lambda i: jnp.clip(i - FRONT, 0, FRONT - 1)
    tall = pl.BlockSpec((per * C, D), lambda i: (late(i), 0))
    fed = pl.BlockSpec((FEED_ROWS, D), lambda i: (jnp.maximum(i - 2 * FRONT, 0), 0))
    anywhere = pl.BlockSpec(memory_space=pl.ANY)
    vmem, dma = pltpu.VMEM, pltpu.SemaphoreType.DMA
    ins = {"x": (tokens, once(tokens)), "doc": (doc_ids, once(doc_ids))}
    ins |= {f"w{n}": (a, once(a)) for n, a in enumerate(weights)}
    ins |= {f"v{n}": (a, once(a)) for n, a in enumerate(vectors)}
    ins["bias_in"] = (bias, once(bias))
    wide_rows, slabs = shape_of((rows, D), F32), 4 * count
    outs = {
        "qkvf_out": (shape_of((rows, 4 * D), BF16), anywhere),
        "p": (wide_rows, anywhere),
        "s": (wide_rows, anywhere),
        "z": (wide_rows, anywhere),
        "kept": (
            shape_of((8, 128, D), F32), pl.BlockSpec((per, 128, D), lambda i: (late(i), 0, 0)),
        ),
        "w_out": (shape_of((count, part, 4 * D), link), anywhere),
        "vec": (shape_of((8, D), F32), whole(8, D)),
    }
    scratch = {
        "qkvf": vmem((rows, 4 * D), BF16),
        "hidden": vmem((rows, D), BF16),
        "w_all": vmem((count, part, 4 * D), link),
        "mine": vmem((part, 4 * D), link),
        "mine_o": vmem((part, D), link),
        "mine_h": vmem((part, FF), link),
        "mine_r": vmem((4 * part, D), link),
        "spread": vmem((8, 128), F32),
        "smalls": vmem((count, 8, 128), F32),
        "col": vmem((rows, 128), F32),
        "edge": vmem((16, D), F32),
        "state": vmem((136, D), F32),
        "tail": vmem((136, D), F32),
        "tails": vmem((4, 128, D), link),
        "tail_rows": vmem((4, 8, D), F32),
        "stage": vmem((2, 3, per * C, D), F32),
        "seen": vmem((8, C, C), BF16),
    }
    gathered = {
        "wo_all": (count, part, D), "wh_all": (count, part, FF), "wr_all": (count, 4 * part, D),
    }
    if joined:
        ins["g"] = (cotangent, fed)
        outs |= {
            "y": (shape_of((rows, D), BF16), anywhere),
            "dy": (wide_rows, anywhere),
            "do": (shape_of((rows, D), BF16), anywhere),
            "pack": (shape_of((slabs * part, 640), BF16), anywhere),
            "pack_r": (shape_of((slabs * part, D), BF16), anywhere),
            "gsmall": (shape_of((16, D), F32), whole(16, D)),
        }
        scratch |= {name: vmem(shape, link) for name, shape in gathered.items()}
        scratch |= {
            "held_y": vmem((2, FEED_ROWS, D), BF16), "held_dy": vmem((2, FEED_ROWS, D), F32),
            "held_do": vmem((2, FEED_ROWS, D), BF16),
            "o": vmem((rows, D), BF16), "bias": vmem((1, FF), F32), "gwo": vmem((D, D), F32),
            "gwh": vmem((D, FF), F32), "gwr": vmem((D, FF), F32),
        }
    else:
        outs |= {name: (shape_of(shape, link), anywhere) for name, shape in gathered.items()}
        outs |= {
            "o": (shape_of((rows, D), BF16), tall), "bias": (shape_of((1, FF), F32), whole(1, FF)),
        }
    found = pl.pallas_call(
        functools.partial(front_kernel, count, joined, (*ins, *outs, *scratch)),
        grid=(2 * FRONT + (rows // FEED_ROWS if joined else 0),),
        in_specs=[spec for _, spec in ins.values()],
        out_specs=[spec for _, spec in outs.values()],
        out_shape=[shape for shape, _ in outs.values()],
        scratch_shapes=list(scratch.values())
        + gather_sems(count, True)
        + gather_sems(count, False) * 4
        + [dma((count,)), dma((count,)), dma((3, 2)), dma((3, 2)), dma((2,)), dma((2, 3)), dma((2, 3))],
        compiler_params=pltpu.CompilerParams(
            vmem_limit_bytes=62 * MIB, collective_id=1, has_side_effects=True
        ),
        name="front",
    )(*(a for a, _ in ins.values()))
    found = dict(zip(outs, found))
    if not joined:
        found |= feed(count, part, tokens, found, cotangent, link)
    return found


def feed(count, part, tokens, found, cotangent, link):
    rows, slabs = tokens.shape[0], 4 * count
    tall = pl.BlockSpec((256, D), lambda i: (i, 0))
    weights = [found[name] for name in ("wo_all", "wh_all", "wr_all")]
    names = ("y", "dy", "do", "pack", "pack_r", "gsmall")
    return dict(
        zip(
            names,
            pl.pallas_call(
                feed_kernel,
                grid=(rows // 256,),
                in_specs=[tall] * 3
                + [whole(8, D), whole(1, FF)]
                + [whole(*a.shape) for a in weights],
                out_specs=[tall] * 3
                + [whole(slabs * part, 640), whole(slabs * part, D), whole(16, D)],
                out_shape=[
                    shape_of((rows, D), BF16),
                    shape_of((rows, D), F32),
                    shape_of((rows, D), BF16),
                    shape_of((slabs * part, 640), link),
                    shape_of((slabs * part, D), link),
                    shape_of((16, D), F32),
                ],
                scratch_shapes=[
                    pltpu.VMEM((D, D), F32), pltpu.VMEM((D, FF), F32), pltpu.VMEM((D, FF), F32),
                ],
                compiler_params=PARAMS,
                name="feed",
            )(tokens, found["o"], cotangent, found["vec"], found["bias"], *weights),
        )
    )


def row_body(
    n, qkvf_ref, do_ref, p_ref, s_ref, z_ref, kept_ref, col, row, edge_ref,
    r_ref, dn_ref, dz_ref, head_ref, aside,
):
    first = edge_ref[pl.ds(0, 1)]
    before = edge_ref[pl.ds(8 + jnp.maximum(n - 1, 0), 1)]
    last = jnp.where(n == 0, first, before)
    vis = visible(col, row)
    carried = wide(flag(col, last), 2)
    slots = jnp.exp(qkvf_ref[:, 3 * D :].astype(F32)).astype(BF16)
    own = wide(flag(col, first), 2)
    states = [expand(kept_ref[0, 64:128, lanes_of(g)]).astype(BF16) for g in range(2)]

    def mixing(g):
        return masked(dot_nt(stacked(do_ref[:, lanes_of(g)]), part_of(qkvf_ref, 2, g)), vis)

    def to_reading(g, back_mix):
        lanes = lanes_of(g)
        back = select(dot(back_mix, slots[:, lanes]))
        return back + carried * dot_nt(do_ref[:, lanes], states[g])

    def to_scores(g, back_reading):
        lanes = lanes_of(g)
        probs, score, inverse = p_ref[:, lanes], s_ref[:, lanes], z_ref[:, lanes]
        shared = back_reading * inverse * probs
        back_score = shared - probs * head_sums(shared)
        back_numer = back_score * inverse * SCALE
        back_total = -(shared + back_score * score) * inverse
        reading = (probs * inverse).astype(BF16)
        r_ref[:, lanes] = reading
        dn_ref[:, lanes] = back_numer
        dz_ref[:, lanes] = back_total
        return back_numer, back_total, reading

    def to_state(g, back_numer, back_total, reading):
        lanes = lanes_of(g)
        head_ref[0:64, lanes] += compacted(
            dot_tn((own * back_numer).astype(BF16), part_of(qkvf_ref, 0, g))
        )
        head_ref[64:128, lanes] += compacted(
            dot_tn((own * reading.astype(F32)).astype(BF16), do_ref[:, lanes])
        )
        head_ref[128:129, lanes] += jnp.sum(own * back_total, axis=0, keepdims=True)

    back_mix = mixing(0)
    back_mix_two = mixing(1)
    aside()
    back_reading = to_reading(0, back_mix)
    back_reading_two = to_reading(1, back_mix_two)
    parts = to_scores(0, back_reading)
    to_state(0, *parts)
    parts = to_scores(1, back_reading_two)
    to_state(1, *parts)


def query_body(n, qkvf_ref, kept_ref, col, row, edge_ref, dn_ref, dq_ref):
    first = edge_ref[pl.ds(0, 1)]
    before = edge_ref[pl.ds(8 + jnp.maximum(n - 1, 0), 1)]
    last = jnp.where(n == 0, first, before)
    vis = visible(col, row)
    carried = wide(flag(col, last), 2)
    slots = jnp.exp(qkvf_ref[:, 3 * D :].astype(F32)).astype(BF16)
    lows = [dn_ref[:, lanes_of(g)].astype(BF16) for g in range(2)]
    states = [expand(kept_ref[0, 0:64, lanes_of(g)]).astype(BF16) for g in range(2)]

    def affine(g):
        return masked(dot_nt(stacked(lows[g]), slots[:, lanes_of(g)]), vis)

    def to_queries(g, back_affinity):
        out = select(dot(back_affinity, part_of(qkvf_ref, 1, g))) + carried * dot(lows[g], states[g])
        dq_ref[:, lanes_of(g)] = out.astype(BF16)

    one, two = affine(0), affine(1)
    to_queries(0, one)
    to_queries(1, two)


def column_body(
    n, qkvf_ref, do_ref, r_ref, dn_ref, dz_ref, col, row, edge_ref, state, snap, snap_rows, d_ref
):
    newest = edge_ref[15:16]
    after = edge_ref[pl.ds(jnp.minimum(n + 1, 7), 1)]
    following = jnp.where(n == 7, newest, after)
    first = edge_ref[pl.ds(n, 1)]
    vis = visible_back(col, row)
    carried = wide(flag(col, following), 2)
    own = wide(flag(col, first), 2)
    kept = jnp.where(following == first, 1.0, 0.0)[:, :GROUP]
    snap[n] = state[0:128].astype(BF16)
    snap_rows[pl.ds(n, 1)] = state[128:129]
    key_states = [expand(state[0:64, lanes_of(g)]).astype(BF16) for g in range(2)]
    value_states = [expand(state[64:128, lanes_of(g)]).astype(BF16) for g in range(2)]
    slots = jnp.exp(qkvf_ref[:, 3 * D :].astype(F32)).astype(BF16)
    numers = [dn_ref[:, lanes_of(g)] for g in range(2)]

    def mixing(g, apart):
        return masked(dot_nt(apart, r_ref[:, lanes_of(g)]), vis)

    def affine(g, apart):
        return masked(dot_nt(apart, numers[g].astype(BF16)), vis)

    def to_values(g, mix):
        lanes = lanes_of(g)
        out = select(dot(mix, do_ref[:, lanes])) + carried * dot(slots[:, lanes], value_states[g])
        d_ref[:, 2 * D + g * GROUP : 2 * D + (g + 1) * GROUP] = out.astype(BF16)

    def to_keys(g, back_affinity):
        lanes = lanes_of(g)
        out = select(dot(back_affinity, part_of(qkvf_ref, 0, g)))
        out = out + carried * dot(slots[:, lanes], key_states[g])
        d_ref[:, D + g * GROUP : D + (g + 1) * GROUP] = out.astype(BF16)

    def to_state(g):
        lanes = lanes_of(g)
        state[0:64, lanes] = kept * state[0:64, lanes] + compacted(
            dot_tn((own * numers[g]).astype(BF16), part_of(qkvf_ref, 0, g))
        )
        state[64:128, lanes] = kept * state[64:128, lanes] + compacted(
            dot_tn((own * r_ref[:, lanes].astype(F32)).astype(BF16), do_ref[:, lanes])
        )
        state[128:129, lanes] = kept * state[128:129, lanes] + jnp.sum(
            own * dz_ref[:, lanes], axis=0, keepdims=True
        )

    apart = stacked(slots[:, lanes_of(0)])
    mix = mixing(0, apart)
    back_affinity = affine(0, apart)
    apart = stacked(slots[:, lanes_of(1)])
    mix_two = mixing(1, apart)
    to_values(0, mix)
    affinity_two = affine(1, apart)
    to_keys(0, back_affinity)
    to_state(0)
    to_values(1, mix_two)
    to_keys(1, affinity_two)
    to_state(1)


def slot_body(n, qkvf_ref, do_ref, r_ref, dn_ref, dz_ref, col, row, edge_ref, snap, snap_rows, d_ref):
    newest = edge_ref[15:16]
    after = edge_ref[pl.ds(jnp.minimum(n + 1, 7), 1)]
    following = jnp.where(n == 7, newest, after)
    vis = visible_back(col, row)
    carried = wide(flag(col, following), 2)
    left = lane_heads(C, 128) == 0
    norm_state = snap_rows[pl.ds(n, 1)]
    key_states = [expand(snap[n, 0:64, lanes_of(g)]) for g in range(2)]
    value_states = [expand(snap[n, 64:128, lanes_of(g)]) for g in range(2)]

    def mixing(g):
        return masked(dot_nt(stacked(part_of(qkvf_ref, 2, g)), do_ref[:, lanes_of(g)]), vis)

    def affine(g):
        return masked(dot_nt(stacked(part_of(qkvf_ref, 1, g)), part_of(qkvf_ref, 0, g)), vis)

    def from_mix(g, back_mix):
        return select(dot(back_mix, r_ref[:, lanes_of(g)]))

    def from_affinity(g, affinity):
        high, low = split(dn_ref[:, lanes_of(g)])
        parts = []
        for p in range(2):
            pair = slice(p * 128, (p + 1) * 128)
            both = dot(
                affinity[p * 512 : (p + 1) * 512],
                jnp.concatenate([high[:, pair], low[:, pair]], axis=1),
            )
            both = both[:, :128] + both[:, 128:]
            parts.append(jnp.where(left, both[:C], both[C:]))
        return jnp.concatenate(parts, axis=1)

    def from_totals():
        high, low = split(dz_ref[...])
        return dot(vis, high) + dot(vis, low)

    def from_state(g):
        return carried * (
            dot_nt(part_of(qkvf_ref, 1, g), key_states[g])
            + dot_nt(part_of(qkvf_ref, 2, g), value_states[g])
            + norm_state[:, lanes_of(g)]
        )

    def to_slots(g, back_slots):
        written = jnp.exp(part_of(qkvf_ref, 3, g).astype(F32))
        d_ref[:, 3 * D + g * GROUP : 3 * D + (g + 1) * GROUP] = (back_slots * written).astype(BF16)

    norm = from_totals()
    mix = mixing(0)
    affinity = affine(0)
    mix_two = mixing(1)
    total = from_mix(0, mix)
    affinity_two = affine(1)
    total = total + from_affinity(0, affinity)
    total_two = from_mix(1, mix_two)
    to_slots(0, total + norm[:, lanes_of(0)] + from_state(0))
    total_two = total_two + from_affinity(1, affinity_two)
    to_slots(1, total_two + norm[:, lanes_of(1)] + from_state(1))


class Scatter:
    def __init__(self, count, source, own, axes, direct, out, buffers):
        self.axes, self.direct, self.out = axes, direct, out
        self.seq, self.at, self.sibling, self.beside = places()
        self.source, self.own = source, own
        self.core = lax.rem(self.seq, 2)
        self.total, self.local, self.last, self.done = buffers[:4]
        self.stages = []
        size = source.shape[0]
        base = 0
        for n, axis in enumerate(axes):
            ways = {"core": 2, "x": 2, "y": 2, "z": count // 2, "all": count}[axis]
            size = size // ways
            me = {
                "core": self.core, "x": self.seq // 2, "y": lax.rem(self.at, 2), "z": self.at // 2,
                "all": self.at,
            }[axis]
            held = source
            if own is not None and n > 0:
                held = own
            come, sems = buffers[4 + 2 * n], buffers[5 + 2 * n]
            self.stages.append((axis, ways, size, base, me, held, come, sems))
            if own is None or n > 0:
                base = base + me * size

    def copies(self, n):
        axis, ways, size, base, me, held, come, sems = self.stages[n]
        for k in range(1, ways):
            if axis in ("core", "x"):
                device = {"seq": self.sibling if axis == "core" else self.beside}
            else:
                device = {"fsdp": self.at ^ (2 * k if axis == "z" else k)}
            yield push(
                held.at[pl.ds(base + (me ^ k) * size, size)], come.at[k - 1],
                sems.at[0, k - 1], sems.at[1, k - 1], **device,
            )

    def copy_own(self):
        size = self.source.shape[0] // 2
        return pltpu.make_async_copy(
            self.source.at[pl.ds(self.core * size, size)], self.own, self.local
        )

    def start(self):
        for copy in self.copies(0):
            copy.start()
        if self.own is not None:
            self.copy_own().start()

    def advance(self, n):
        axis, ways, size, base, me, held, come, sems = self.stages[n]
        for copy in self.copies(n):
            copy.wait_recv()
        mine = held
        first = base + me * size
        if n == 0 and self.own is not None:
            self.copy_own().wait()
            mine, first = self.own, 0

        def added(slab):
            total = mine[first + slab].astype(F32)
            for k in range(1, ways):
                total = total + come[k - 1, slab].astype(F32)
            return total

        if n + 1 == len(self.stages):
            self.total[...] = added(0)
            self.copy_done().start()
            for copy in self.sent():
                copy.start()
            return

        @pl.loop(0, size)
        def _(slab):
            mine[first + slab] = added(slab).astype(mine.dtype)

        for copy in self.copies(n + 1):
            copy.start()

    def copy_done(self):
        return pltpu.make_async_copy(self.total, self.out.at[self.seq], self.done)

    def sent(self):
        other = lax.rem(self.sibling + 2, 4)
        for n, target in enumerate((self.sibling, self.beside, other)[: 3 if self.direct else 2]):
            yield push(
                self.total, self.out.at[self.seq], self.last.at[0, n], self.last.at[1, n], seq=target
            )

    def forwarded(self, source):
        here = self.out.at[source]
        return push(here, here, self.last.at[0, 2], self.last.at[1, 2], seq=self.sibling)

    def come_in(self, n, source):
        here = self.out.at[source]
        return push(here, here, self.last.at[0, n], self.last.at[1, n], seq=source)

    def forward(self):
        self.come_in(1, self.beside).wait_recv()
        self.forwarded(self.beside).start()

    def finish(self):
        other = lax.rem(self.sibling + 2, 4)
        self.come_in(0, self.sibling).wait_recv()
        if self.direct:
            self.come_in(1, self.beside).wait_recv()
        else:
            self.forwarded(self.beside).wait_send()
        self.forwarded(other).wait_recv()
        self.copy_done().wait()
        for copy in self.sent():
            copy.wait_send()
        for n in range(len(self.stages)):
            for copy in self.copies(n):
                copy.wait_send()


def scatter_scratch(count, part, lanes, link, axes, hbm):
    vmem, dma = pltpu.VMEM, pltpu.SemaphoreType.DMA
    size = 2 * 4 * count // 2
    out = [vmem((size // 2, part, lanes), link)] if hbm else []
    out += [vmem((part, lanes), F32), dma, dma((2, 3)), dma]
    for axis in axes:
        ways = {"core": 2, "x": 2, "y": 2, "z": count // 2, "all": count}[axis]
        size = size // ways
        out += [vmem((ways - 1, size, part, lanes), link), dma((2, ways - 1))]
    return out


OVER_X = ("core", "x", "y", "z")
OVER_Y = ("core", "y", "x", "z")
SHORT = ("core", "x", "all")


class SmallSum:
    def __init__(self, count, mine, from_seq, half, from_fsdp, sems):
        self.count, self.mine, self.from_seq = count, mine, from_seq
        self.half, self.from_fsdp, self.sems = half, from_fsdp, sems
        self.seq, self.at, _, _ = places()

    def lanes(self, owner):
        if self.from_fsdp.shape[2] == D:
            return pl.ds(0, D)
        first = owner * (D // self.count) // 128 * 128
        return pl.ds(pl.multiple_of(first, 128), 128)

    def over_seq(self, k, slot):
        return push(
            self.mine, self.from_seq.at[slot], self.sems[0].at[0, k], self.sems[0].at[1, k],
            seq=self.seq ^ k,
        )

    def over_fsdp(self, k):
        return push(
            self.half.at[:, self.lanes(self.at ^ k)], self.from_fsdp.at[self.at],
            self.sems[1].at[0, k], self.sems[1].at[1, k], fsdp=self.at ^ k,
        )

    def fsdp_in(self, k):
        here = self.from_fsdp.at[self.at ^ k]
        return push(here, here, self.sems[1].at[0, k], self.sems[1].at[1, k], fsdp=self.at ^ k)

    def start(self):
        for k in range(1, 4):
            self.over_seq(k, self.seq).start()
        self.from_seq[self.seq] = self.mine[...]

    def second(self):
        for k in range(1, 4):
            self.over_seq(k, self.seq ^ k).wait_recv()
        total = self.from_seq[0]
        for n in range(1, 4):
            total = total + self.from_seq[n]
        self.half[...] = total
        for k in range(1, self.count):
            self.over_fsdp(k).start()
        self.from_fsdp[self.at] = self.half[:, self.lanes(self.at)]

    def finish(self, out_ref):
        for k in range(1, self.count):
            self.fsdp_in(k).wait_recv()
        total = self.from_fsdp[0]
        for n in range(1, self.count):
            total = total + self.from_fsdp[n]
        out_ref[...] = total
        for k in range(1, 4):
            self.over_seq(k, self.seq).wait_send()
        for k in range(1, self.count):
            self.over_fsdp(k).wait_send()


def small_scratch(count, rows, lanes):
    vmem, dma = pltpu.VMEM, pltpu.SemaphoreType.DMA
    return [
        vmem((4, rows, D), F32), vmem((rows, D), F32), vmem((count, rows, lanes), F32),
        dma((2, 4)), dma((2, count)),
    ]


QUERY, COLUMN, SLOT, INPUT = 8, 16, 24, 32


def back_kernel(
    count, per, x_ref, xs_ref, qkvf_ref, do_ref, p_ref, s_ref, z_ref, kept_ref, dy_ref, doc_ref,
    small_ref, w_ref, ffg_ref, ffr_ref, ffs_ref,
    gi_ref, ff_out, fr_out, q_out, kv_out, f_out, s1_out, s2_out,
    gi_held, gi_sem, scores, scores_sem, d_all, h_turned, reading, numer, total, col_ref, edge_ref, head, state, heads, head_rows,
    snap, snap_rows, w_held, w_sem, q_piece, kv_piece, f_piece, last_small, *rest,
):
    step = pl.program_id(0)
    seq, at, _, _ = places()
    link = q_piece.dtype

    def take(size):
        nonlocal rest
        out, rest = rest[:size], rest[size:]
        return out

    (own,) = take(1)
    ff = Scatter(count, ffg_ref, own, OVER_X, False, ff_out, take(12))
    (own,) = take(1)
    fr = Scatter(count, ffr_ref, own, OVER_Y, False, fr_out, take(12))
    for_q = Scatter(count, q_piece, None, OVER_X, False, q_out, take(12))
    for_kv = Scatter(count, kv_piece, None, OVER_X, False, kv_out, take(12))
    for_f = Scatter(count, f_piece, None, SHORT, True, f_out, take(10))
    small_one = SmallSum(count, ffs_ref, *take(3), take(2))
    small_two = SmallSum(count, last_small, *take(3), take(2))
    states = States(heads, head_rows, take(2))

    def chunk(u, first, turned=False):
        n = step * per + u - first
        n = 7 - n if turned else n
        here = pl.ds(pl.multiple_of(n * C, C), C)
        block = pl.ds((per - 1 - u if turned else u) * C, C)
        return n, here, block, col_ref[here], doc_ref[:, here].astype(F32)

    def fetch():
        return pltpu.make_async_copy(w_ref, w_held, w_sem)

    def fetch_scores(n):
        slot, here = lax.rem(n, 2), pl.ds(pl.multiple_of(n * per * C, per * C), per * C)
        return [
            pltpu.make_async_copy(ref.at[here], scores.at[slot, k], scores_sem.at[slot, k])
            for k, ref in enumerate((p_ref, s_ref, z_ref))
        ]

    def give(n):
        here = pl.ds(pl.multiple_of(n * per * C, per * C), per * C)
        slot = lax.rem(n, 2)
        return pltpu.make_async_copy(gi_held.at[slot], gi_ref.at[here], gi_sem.at[slot])

    def weight_grad(piece, d_lanes, lanes, short=False):
        grad = dot(h_turned[...], d_all[:, d_lanes])
        half, part = count // 2, piece.shape[1]
        for q in range(4):
            x, c = q // 2, q % 2
            share = grad[:, q * 128 : (q + 1) * 128].reshape(half, 2, part, 128).astype(link)
            if short:
                first = (c * 2 + x) * count
                piece[first : first + count, :, lanes] = share.reshape(count, part, 128)
                continue
            for y in range(2):
                first = ((c * 2 + x) * 2 + y) * half
                piece[first : first + half, :, lanes] = share[:, y]

    @pl.when(step == 0)
    def _():
        for n in range(2):
            for copy in fetch_scores(n):
                copy.start()
        fetch().start()
        greet(count)
        ff.start()
        small_one.start()
        doc_parts(doc_ref, col_ref, edge_ref)
        head[...] = jnp.zeros_like(head)
        last_small[...] = jnp.zeros_like(last_small)

    def turn():
        weight_grad(q_piece, slice(0, D), slice(0, 128))
        for_q.start()
        states.finish()
        newest = edge_ref[15:16]
        state[...] = jnp.zeros_like(state)
        for n in range(4):
            use = jnp.where(head_rows[n, 1:2] == newest, 1.0, 0.0) * (n > seq).astype(F32)
            state[0:128] += use * heads[n].astype(F32)
            state[128:129] += use * head_rows[n, 0:1]

    def send_states():
        heads[seq] = head[0:128].astype(link)
        head_rows[seq, 0:1] = head[128:129]
        head_rows[seq, 1:2] = edge_ref[0:1]
        head_rows[seq, 2:8] = jnp.zeros((6, D), F32)
        states.start()

    def key_value_grads():
        weight_grad(kv_piece, slice(D, 2 * D), slice(0, 128))
        weight_grad(kv_piece, slice(2 * D, 3 * D), slice(128, 256))
        for_kv.start()

    def slot_grads():
        weight_grad(f_piece, slice(3 * D, 4 * D), slice(0, 128), True)
        for_f.start()

    def last():
        small_two.start()
        for_f.advance(1)
        small_two.second()
        for_kv.advance(3)
        fr.forward()
        for_f.advance(2)
        for_kv.forward()
        for piece in (ff, fr, for_q):
            piece.finish()
        states.drain()
        small_two.finish(s2_out)
        for_kv.finish()
        for_f.finish()
        for n in (8 // per - 2, 8 // per - 1):
            give(n).wait()

    schedule = {
        0: [fr.start],
        2: [lambda: ff.advance(0), small_one.second],
        4: [lambda: fr.advance(0)],
        QUERY - 1: [send_states],
        QUERY + 7: [turn],
        COLUMN: [lambda: ff.advance(1), lambda: fr.advance(1)],
        COLUMN + 1: [lambda: for_q.advance(0)],
        COLUMN + 5: [lambda: fr.advance(2)],
        COLUMN + 6: [lambda: ff.advance(2)],
        COLUMN + 7: [key_value_grads, lambda: for_q.advance(1)],
        SLOT + 1: [lambda: for_kv.advance(0), lambda: for_q.advance(2)],
        SLOT + 4: [lambda: ff.advance(3)],
        SLOT + 6: [lambda: for_kv.advance(1), lambda: fr.advance(3)],
        SLOT + 7: [slot_grads, lambda: for_q.advance(3)],
        INPUT + 1: [lambda: for_f.advance(0), lambda: for_kv.advance(2)],
        INPUT + 3: [ff.forward, for_q.forward, lambda: small_one.finish(s1_out)],
        INPUT + 7: [last],
    }

    @pl.when(step < QUERY // per)
    def _():
        for copy in fetch_scores(step):
            copy.wait()

    for u in range(per):

        @pl.when(step < QUERY // per)
        def _(u=u):
            n, here, block, col, row = chunk(u, 0)
            kept_scores = [scores.at[lax.rem(step, 2), k, block] for k in range(3)]

            def aside():
                unit, _ = norm_parts(x_ref[block].astype(F32))
                h_turned[:, here] = (unit * small_ref[0:1] + small_ref[1:2]).astype(BF16).T

            row_body(
                n, qkvf_ref.at[block], do_ref.at[block], *kept_scores, kept_ref.at[pl.ds(u, 1)],
                col, row, edge_ref,
                reading.at[here], numer.at[here], total.at[here], head, aside,
            )

        @pl.when((step >= QUERY // per) & (step < COLUMN // per))
        def _(u=u):
            n, here, block, col, row = chunk(u, QUERY)
            query_body(
                n, qkvf_ref.at[block], kept_ref.at[pl.ds(u, 1)], col, row, edge_ref,
                numer.at[here], d_all.at[here, 0:D],
            )

        @pl.when((step >= COLUMN // per) & (step < SLOT // per))
        def _(u=u):
            n, here, block, col, row = chunk(u, COLUMN, True)
            column_body(
                n, qkvf_ref.at[block], do_ref.at[block], reading.at[here], numer.at[here],
                total.at[here], col, row, edge_ref, state, snap, snap_rows, d_all.at[here],
            )

        @pl.when((step >= SLOT // per) & (step < INPUT // per))
        def _(u=u):
            n, here, block, col, row = chunk(u, SLOT, True)
            slot_body(
                n, qkvf_ref.at[block], do_ref.at[block], reading.at[here], numer.at[here],
                total.at[here], col, row, edge_ref, snap, snap_rows, d_all.at[here],
            )

        if u == per - 1:

            @pl.when(step + 2 < QUERY // per)
            def _():
                for copy in fetch_scores(step + 2):
                    copy.start()

        if u == 0:

            @pl.when(step >= INPUT // per + 2)
            def _():
                give(step - INPUT // per - 2).wait()

            @pl.when(step == INPUT // per)
            def _():
                fetch().wait()

            @pl.when(step >= INPUT // per)
            def _():
                size = xs_ref.shape[0]
                here = pl.ds(pl.multiple_of((step - INPUT // per) * size, size), size)
                grad = dot_nt(d_all[here], w_held[...])
                unit, scale = norm_parts(xs_ref[...].astype(F32))
                last_small[0:1] += jnp.sum(grad * unit, axis=0, keepdims=True)
                last_small[1:2] += jnp.sum(grad, axis=0, keepdims=True)
                gi_held[lax.rem(step - INPUT // per, 2)] = dy_ref[...] + norm_back(
                    unit, scale, small_ref[0:1], grad
                )
                give(step - INPUT // per).start()

        for when, actions in schedule.items():
            if when % per == u:

                @pl.when(step == when // per)
                def _(actions=actions):
                    for action in actions:
                        action()


def back(
    count, tokens, qkvf, do, probs, score, inverse, kept, dy, doc_ids, small, w_all, ffg, ffr, ffs
):
    rows = tokens.shape[0]
    part, link = ffg.shape[1], ffg.dtype
    per = 2 if link == BF16 else 1
    size = per * C
    blocks = 8 // per
    once = lambda a: pl.BlockSpec(a.shape, lambda i: (0,) * a.ndim)
    anywhere = pl.BlockSpec(memory_space=pl.ANY)
    vmem, dma = pltpu.VMEM, pltpu.SemaphoreType.DMA

    def early(i):
        return jnp.minimum(i, blocks - 1)

    def twice(i):
        return jnp.where(i < blocks, i, jnp.clip(i - blocks, 0, blocks - 1))

    def turned(i):
        return blocks - 1 - lax.rem(jnp.clip(i - 2 * blocks, 0, 2 * blocks - 1), blocks)

    def always(i):
        return jnp.where(i < 2 * blocks, twice(i), turned(i))

    def both(i):
        return jnp.where(i < blocks, i, turned(i))

    late = lambda i: (jnp.maximum(i - 4 * blocks, 0), 0)
    tall = pl.BlockSpec((size, D), late)
    some = lambda lanes, order: pl.BlockSpec((size, lanes), lambda i: (order(i), 0))
    slabs = 4 * count
    return pl.pallas_call(
        functools.partial(back_kernel, count, per),
        grid=(5 * blocks,),
        in_specs=[some(D, early), tall, some(4 * D, always), some(D, both)]
        + [anywhere] * 3
        + [pl.BlockSpec((per, 128, D), lambda i: (twice(i), 0, 0)), tall]
        + [once(doc_ids), once(small), anywhere, anywhere, anywhere, once(ffs)],
        out_specs=[anywhere] * 6 + [whole(16, D), whole(8, 128)],
        out_shape=[
            shape_of((rows, D), F32),
            shape_of((4, part, 640), F32),
            shape_of((4, part, D), F32),
            shape_of((4, part, 128), F32),
            shape_of((4, part, 256), F32),
            shape_of((4, part, 128), F32),
            shape_of((16, D), F32),
            shape_of((8, 128), F32),
        ],
        scratch_shapes=[
            vmem((2, size, D), F32),
            dma((2,)),
            vmem((2, 3, size, D), F32),
            dma((2, 3)),
            vmem((rows, 4 * D), BF16),
            vmem((D, rows), BF16),
            vmem((rows, D), BF16),
            vmem((rows, D), F32),
            vmem((rows, D), F32),
            vmem((rows, 128), F32),
            vmem((16, D), F32),
            vmem((136, D), F32),
            vmem((136, D), F32),
            vmem((4, 128, D), link),
            vmem((4, 8, D), F32),
            vmem((8, 128, D), BF16),
            vmem((8, D), F32),
            vmem(w_all.shape, BF16),
            dma,
            vmem((slabs, part, 128), link),
            vmem((slabs, part, 256), link),
            vmem((slabs, part, 128), link),
            vmem((8, D), F32),
        ]
        + scatter_scratch(count, part, 640, link, OVER_X, True)
        + scatter_scratch(count, part, D, link, OVER_Y, True)
        + scatter_scratch(count, part, 128, link, OVER_X, False)
        + scatter_scratch(count, part, 256, link, OVER_X, False)
        + scatter_scratch(count, part, 128, link, SHORT, False)
        + small_scratch(count, 16, D)
        + small_scratch(count, 8, 128)
        + [dma((3, 2)), dma((3, 2))],
        compiler_params=pltpu.CompilerParams(
            vmem_limit_bytes=(62 if link == BF16 else 63) * MIB, collective_id=2, has_side_effects=True
        ),
        name="back",
    )(
        tokens, tokens, qkvf, do, probs, score, inverse, kept, dy, doc_ids, small, w_all, ffg, ffr,
        ffs,
    )


def finish_kernel(
    count, part, y_ref, gi_ref, ff_ref, fr_ref, q_ref, kv_ref, f_ref, s1_ref, s2_ref, y_out, gi_out,
    *rest,
):
    at = lax.axis_index("fsdp")
    *outs, held_y, held, sems = rest

    def move(n, out):
        source, through, target, here = gi_ref, held, gi_out, pl.ds(n * 512, 512)
        if n >= 4:
            source, through, target, here = y_ref, held_y, y_out, pl.ds((n - 4) * 1024, 1024)
        if out:
            return pltpu.make_async_copy(through.at[here], target.at[here], sems.at[1, n])
        return pltpu.make_async_copy(source.at[here], through.at[here], sems.at[0, n])

    def pick(row, size):
        out = row(0, size)
        for f in range(1, count):
            out = jnp.where(at == f, row(f * size, size), out)
        return out

    def bias(start, size):
        r = start // D
        return s1_ref[8 + r : 9 + r, start - r * D : start - r * D + size]

    def row_of_sums(ref, n):
        return lambda start, size: ref[
            n : n + 1, start % ref.shape[1] : start % ref.shape[1] + size
        ]

    for n in range(6):
        move(n, False).start()
    for n in range(4):
        lanes = slice(n * 128, (n + 1) * 128)
        outs[0][:, lanes] = q_ref[n]
        outs[1][:, lanes] = kv_ref[n, :, 0:128]
        outs[2][:, lanes] = kv_ref[n, :, 128:256]
        outs[3][:, lanes] = f_ref[n]
        outs[4][:, lanes] = ff_ref[n, :, 512:640]
        outs[5][:, n * 512 : (n + 1) * 512] = ff_ref[n, :, 0:512]
        for j in range(4):
            outs[6][j * part : (j + 1) * part, lanes] = fr_ref[n, :, j * 128 : (j + 1) * 128]
    for n in range(6):
        move(n, False).wait()
        move(n, True).start()
    outs[7][...] = pick(row_of_sums(s2_ref, 0), part)
    outs[8][...] = pick(row_of_sums(s2_ref, 1), part)
    outs[9][...] = pick(row_of_sums(s1_ref, 2), part)
    outs[10][...] = pick(row_of_sums(s1_ref, 3), part)
    outs[11][...] = pick(bias, 4 * part)
    outs[12][...] = pick(row_of_sums(s1_ref, 4), part)
    for n in range(6):
        move(n, True).wait()


def finish(count, part, out, grad_input, *sums):
    once = lambda shape: pl.BlockSpec(shape, lambda: (0,) * len(shape))
    anywhere = pl.BlockSpec(memory_space=pl.ANY)
    shapes = [(part, D)] * 5 + [(part, FF), (4 * part, D)]
    shapes += [(1, part)] * 4 + [(1, 4 * part), (1, part)]
    return pl.pallas_call(
        functools.partial(finish_kernel, count, part),
        in_specs=[anywhere] * 2 + [once(a.shape) for a in sums],
        out_specs=[anywhere] * 2 + [once(s) for s in shapes],
        out_shape=[shape_of(out.shape, BF16)]
        + [shape_of(s, F32) for s in (grad_input.shape, *shapes)],
        scratch_shapes=[
            pltpu.VMEM(out.shape, BF16),
            pltpu.VMEM(grad_input.shape, F32),
            pltpu.SemaphoreType.DMA((2, 6)),
        ],
        compiler_params=PARAMS,
        name="finish",
    )(out, grad_input, *sums)


def rows_of(lanes, order=lambda i: i):
    return pl.BlockSpec((C, lanes), lambda i: (order(i), 0))


def whole(*shape):
    return pl.BlockSpec(shape, lambda i: (0,) * len(shape))


def row_of(order=lambda i: i):
    return pl.BlockSpec((1, C), lambda i: (0, order(i)))


def shape_of(shape, kind):
    return jax.ShapeDtypeStruct(shape, kind)


PARAMS = pltpu.CompilerParams(vmem_limit_bytes=62 * MIB)


def on_device(
    tokens, doc_ids, w_query, w_key, w_value, w_slots, w_output, w_hidden, w_return,
    gain_first, shift_first, gain_second, shift_second, bias_hidden, bias_return, cotangent,
):
    rows = tokens.shape[0]
    count = lax.axis_size("fsdp")
    part = gain_first.shape[0]
    flat = lambda a: a.reshape(1, a.shape[0])
    found = front(
        count, tokens, doc_ids,
        (w_query, w_key, w_value, w_slots, w_output, w_hidden, w_return),
        [flat(a) for a in (gain_first, shift_first, gain_second, shift_second, bias_return)],
        flat(bias_hidden), cotangent,
    )
    grad_input, *sums = back(
        count, tokens, *(found[name] for name in ("qkvf_out", "do", "p", "s", "z", "kept", "dy")),
        doc_ids, found["vec"], found["w_out"].reshape(D, 4 * D).astype(BF16),
        found["pack"].reshape(-1, part, 640), found["pack_r"].reshape(-1, part, D), found["gsmall"],
    )
    out, grad_input, *grads = finish(count, part, found["y"], grad_input, *sums)
    return (out, grad_input, *grads[:7], *(a.reshape(-1) for a in grads[7:]))


def solution(mesh):
    tall, flat, one = P(("fsdp", "seq"), None), P("fsdp", None), P("fsdp")
    return jax.shard_map(
        on_device,
        mesh=mesh,
        in_specs=(tall, P("fsdp", "seq")) + (flat,) * 7 + (one,) * 6 + (tall,),
        out_specs=(tall, tall) + (flat,) * 7 + (one,) * 6,
        check_vma=False,
    )
```

```python
import functools
import types

import jax
import jax.numpy as jnp
from jax import lax
from jax.experimental import pallas as pl
from jax.experimental.pallas import tpu as pltpu
from jax.sharding import PartitionSpec as P

D = 512
H = 8
M = 64
FF = 2048
C = 256
GROUP = 256
EPS = 1e-05
SCALE = 0.125
F32 = jnp.float32
BF16 = jnp.bfloat16
FEED_ROWS = 512
FEED_LANES = 256
FRONT = 4
MIB = 1024 * 1024


def dot(a, b):
    return lax.dot_general(a, b, (((1,), (0,)), ((), ())), preferred_element_type=F32)


def dot_nt(a, b):
    return lax.dot_general(a, b, (((1,), (1,)), ((), ())), preferred_element_type=F32)


def dot_tn(a, b):
    return lax.dot_general(a, b, (((0,), (0,)), ((), ())), preferred_element_type=F32)


def lane_heads(rows, lanes):
    return lax.broadcasted_iota(jnp.int32, (rows, lanes), 1) // M


def stacked(values):
    heads = lane_heads(C, GROUP)
    zero = jnp.zeros_like(values)
    return jnp.concatenate([jnp.where(heads == h, values, zero) for h in range(4)], axis=0)


def select(values):
    heads = lane_heads(C, GROUP)
    out = values[3 * C :]
    for h in (2, 1, 0):
        out = jnp.where(heads == h, values[h * C : (h + 1) * C], out)
    return out


def masked(values, mask):
    return jnp.concatenate(
        [values[h * C : (h + 1) * C].astype(BF16) * mask for h in range(4)], axis=0
    )


def expand(compact):
    rows = lax.broadcasted_iota(jnp.int32, (GROUP, GROUP), 0) // M
    full = jnp.concatenate([compact] * 4, axis=0)
    return jnp.where(rows == lane_heads(GROUP, GROUP), full, jnp.zeros_like(full))


def compacted(full):
    heads = lane_heads(M, GROUP)
    out = full[3 * M :]
    for h in (2, 1, 0):
        out = jnp.where(heads == h, full[h * M : (h + 1) * M], out)
    return out


def split(values):
    high = values.astype(BF16)
    return high, (values - high.astype(F32)).astype(BF16)


def ones_block():
    rows = lax.broadcasted_iota(jnp.int32, (GROUP, GROUP), 0) // M
    return (rows == lane_heads(GROUP, GROUP)).astype(BF16)


def head_sums(values):
    high, low = split(values)
    ones = ones_block()
    return dot(high, ones) + dot(low, ones)


def head_max(values):
    left = lane_heads(C, 128) == 0
    out = []
    for p in range(2):
        pair = values[:, p * 128 : (p + 1) * 128]
        one = jnp.max(jnp.where(left, pair, -jnp.inf), axis=1, keepdims=True)
        two = jnp.max(jnp.where(left, -jnp.inf, pair), axis=1, keepdims=True)
        out.append(jnp.where(left, one, two))
    return jnp.concatenate(out, axis=1)


def wide(values, times):
    return jnp.concatenate([values] * times, axis=1)


def visible(doc_col, doc_row):
    same = wide(doc_col, 2) == doc_row
    here = lax.broadcasted_iota(jnp.int32, (C, C), 0)
    there = lax.broadcasted_iota(jnp.int32, (C, C), 1)
    return jnp.where(same & (here >= there), 1.0, 0.0).astype(BF16)


def visible_back(doc_col, doc_row):
    same = wide(doc_col, 2) == doc_row
    here = lax.broadcasted_iota(jnp.int32, (C, C), 0)
    there = lax.broadcasted_iota(jnp.int32, (C, C), 1)
    return jnp.where(same & (there >= here), 1.0, 0.0).astype(BF16)


def flag(doc_col, doc):
    return jnp.where(doc_col == doc[:, :128], 1.0, 0.0)


def norm_parts(values):
    centre = jnp.mean(values, axis=-1, keepdims=True)
    centred = values - centre
    spread = jnp.mean(centred * centred, axis=-1, keepdims=True)
    scale = lax.rsqrt(spread + EPS)
    return centred * scale, scale


def norm_back(unit, scale, gain, grad):
    inner = grad * gain
    return scale * (
        inner
        - jnp.mean(inner, axis=-1, keepdims=True)
        - unit * jnp.mean(inner * unit, axis=-1, keepdims=True)
    )


def groups(values):
    return values[:, :GROUP], values[:, GROUP:]


def state_terms(slots, left, right):
    one, two = [], []
    for g in range(2):
        lanes = slice(g * GROUP, (g + 1) * GROUP)
        both = dot_tn(slots[:, lanes], jnp.concatenate([left[:, lanes], right[:, lanes]], axis=1))
        one.append(compacted(both[:, :GROUP]))
        two.append(compacted(both[:, GROUP:]))
    return jnp.concatenate(one, axis=1), jnp.concatenate(two, axis=1)


def lanes_of(g):
    return slice(g * GROUP, (g + 1) * GROUP)


def part_of(ref, part, g):
    return ref[:, part * D + g * GROUP : part * D + (g + 1) * GROUP]


def attend_body(
    n, qkvf_ref, slots, vis, col, edge_ref, state, o_ref, p_ref, s_ref, z_ref, kept_ref
):
    kept_ref[0] = state[0:128]
    first = edge_ref[pl.ds(0, 1)]
    before = edge_ref[pl.ds(8 + jnp.maximum(n - 1, 0), 1)]
    last = jnp.where(n == 0, first, before)
    newest = edge_ref[pl.ds(8 + n, 1)]
    carried = wide(flag(col, last), 2)
    norm = dot(vis, slots)
    key_states = [expand(state[0:64, lanes_of(g)]).astype(BF16) for g in range(2)]
    value_states = [expand(state[64:128, lanes_of(g)]).astype(BF16) for g in range(2)]
    norm_state = state[128:129]

    def affine(g):
        return masked(dot_nt(stacked(part_of(qkvf_ref, 0, g)), part_of(qkvf_ref, 1, g)), vis)

    def scores(g, affinity):
        lanes = lanes_of(g)
        numer = select(dot(affinity, slots[:, lanes]))
        numer = numer + carried * dot_nt(part_of(qkvf_ref, 0, g), key_states[g])
        inverse = 1.0 / (norm[:, lanes] + carried * norm_state[:, lanes])
        return numer * inverse * SCALE, inverse

    def grow(score):
        return jnp.exp(score - head_max(score))

    def read(g, score, inverse, grown):
        lanes = lanes_of(g)
        probs = grown / head_sums(grown)
        p_ref[:, lanes] = probs
        s_ref[:, lanes] = score
        z_ref[:, lanes] = inverse
        return (probs * inverse).astype(BF16)

    def mixing(g, reading):
        return masked(dot_nt(stacked(reading), slots[:, lanes_of(g)]), vis)

    def mixed(g, reading, mix):
        out = select(dot(mix, part_of(qkvf_ref, 2, g))) + carried * dot(reading, value_states[g])
        o_ref[:, lanes_of(g)] = out.astype(BF16)

    affinity = affine(0)
    score, inverse = scores(0, affinity)
    affinity = affine(1)
    grown = grow(score)
    score_two, inverse_two = scores(1, affinity)
    reading = read(0, score, inverse, grown)
    tail = wide(flag(col, newest), 4).astype(BF16) * slots
    new_keys, new_values = state_terms(tail, qkvf_ref[:, D : 2 * D], qkvf_ref[:, 2 * D : 3 * D])
    same = jnp.where(last == newest, 1.0, 0.0)
    state[0:64] = same * state[0:64] + new_keys
    state[64:128] = same * state[64:128] + new_values
    state[128:129] = same * state[128:129] + jnp.sum(tail.astype(F32), axis=0, keepdims=True)
    grown = grow(score_two)
    mix = mixing(0, reading)
    reading_two = read(1, score_two, inverse_two, grown)
    mixed(0, reading, mix)
    mix = mixing(1, reading_two)
    mixed(1, reading_two, mix)


MESH_ID = pl.DeviceIdType.MESH


def places():
    seq, at = lax.axis_index("seq"), lax.axis_index("fsdp")
    core = lax.rem(seq, 2)
    return seq, at, seq + 1 - 2 * core, lax.rem(seq + 2, 4)


def push(src, dst, send, recv, **device):
    return pltpu.make_async_remote_copy(
        src_ref=src, dst_ref=dst, send_sem=send, recv_sem=recv,
        device_id=device, device_id_type=MESH_ID,
    )


def greet(count):
    seq, at, _, _ = places()
    barrier = pltpu.get_barrier_semaphore()
    for k in range(1, count):
        pl.semaphore_signal(barrier, inc=1, device_id={"fsdp": at ^ k}, device_id_type=MESH_ID)
    for k in range(1, 4):
        pl.semaphore_signal(barrier, inc=1, device_id={"seq": seq ^ k}, device_id_type=MESH_ID)


def met(count):
    pl.semaphore_wait(pltpu.get_barrier_semaphore(), count - 1 + 3)


class Gather:
    def __init__(self, count, mine, held, base, width, four, sems):
        self.count, self.mine, self.held, self.four = count, mine, held, four
        self.far, self.near, self.core, self.chip, self.onward, self.local = sems
        self.seq, self.at, self.sibling, self.beside = places()
        self.base, self.share = base, width // (4 if four else 2)
        self.evens = range(0, count, 2)

    def lanes(self, seq):
        place = seq if self.four else lax.rem(seq, 2)
        return pl.ds(pl.multiple_of(self.base + place * self.share, 128), self.share)

    def part(self, k, seq):
        return self.held.at[self.at ^ k, :, self.lanes(seq)]

    def source(self, k):
        if k:
            return self.part(k, self.seq)
        return self.mine.at[:, self.lanes(self.seq)]

    def own(self):
        return pltpu.make_async_copy(self.source(0), self.part(0, self.seq), self.local)

    def over(self, sems, k, **device):
        return push(self.source(k), self.part(k, self.seq), sems[0].at[k], sems[1].at[k], **device)

    def come(self, sems, k, owner):
        here = self.part(owner, self.seq)
        return push(here, here, sems[0].at[k], sems[1].at[k], seq=self.sibling)

    def far_out(self, k):
        return push(
            self.source(0), self.part(0, self.seq), self.far[0].at[k], self.far[1].at[k],
            fsdp=self.at ^ k,
        )

    def far_in(self, k):
        return self.come(self.far, k, k)

    def near_out(self, k):
        return self.over(self.near, k, fsdp=self.at ^ 1)

    def near_in(self, k):
        return self.come(self.near, k, k ^ 1)

    def start(self):
        self.own().start()
        for k in self.evens[1:]:
            self.far_out(k).start()
        self.near_out(0).start()

    def second(self):
        for k in self.evens[1:]:
            self.far_in(k).wait_recv()
            self.near_out(k).start()

    def hop(self, sems, source, target):
        here = self.held.at[:, :, self.lanes(source)]
        return push(here, here, sems[0].at[0], sems[1].at[0], seq=target)

    def third(self):
        self.own().wait()
        for k in self.evens:
            self.near_in(k).wait_recv()
        self.hop(self.core, self.seq, self.sibling).start()
        if self.four:
            self.hop(self.chip, self.seq, self.beside).start()

    def fourth(self):
        self.hop(self.chip, self.beside, self.beside).wait_recv()
        self.hop(self.onward, self.beside, self.sibling).start()

    def finish(self):
        self.hop(self.core, self.sibling, self.sibling).wait_recv()
        self.hop(self.core, self.seq, self.sibling).wait_send()
        if self.four:
            self.hop(self.onward, lax.rem(self.sibling + 2, 4), self.sibling).wait_recv()
            self.hop(self.chip, self.seq, self.beside).wait_send()
            self.hop(self.onward, self.beside, self.sibling).wait_send()

    def core_out(self, k):
        return self.over(self.core, k, seq=self.sibling)

    def core_in(self, k):
        here = self.part(k, self.sibling)
        return push(here, here, self.core[0].at[k], self.core[1].at[k], seq=self.sibling)

    def at_once(self, between):
        self.start()
        self.core_out(0).start()
        for k in self.evens[1:]:
            self.far_in(k).wait_recv()
            self.near_out(k).start()
            self.core_out(k).start()
        between()
        for k in self.evens:
            self.near_in(k).wait_recv()
            self.core_out(k ^ 1).start()
        self.own().wait()
        for k in range(self.count):
            self.core_in(k).wait_recv()

    def drain(self, each=False):
        for k in self.evens:
            self.near_out(k).wait_send()
            if k:
                self.far_out(k).wait_send()
        if each:
            for k in range(self.count):
                self.core_out(k).wait_send()


def gather_sems(count, each):
    n = count if each else 1
    pair = lambda size: [pltpu.SemaphoreType.DMA((size,)), pltpu.SemaphoreType.DMA((size,))]
    return pair(count) + pair(count) + pair(n) + pair(1) + pair(1) + [pltpu.SemaphoreType.DMA]


def bundle(refs):
    return [(refs[2 * n], refs[2 * n + 1]) for n in range(5)] + [refs[10]]


class States:
    def __init__(self, big, small, sems):
        self.refs, self.sems = (big, small), sems
        self.seq, _, self.sibling, self.beside = places()

    def hop(self, n, source, target):
        out = []
        for m, ref in enumerate(self.refs):
            here = ref.at[source]
            out.append(push(here, here, self.sems[0].at[n, m], self.sems[1].at[n, m], seq=target))
        return out

    def start(self):
        for copy in self.hop(0, self.seq, self.sibling) + self.hop(1, self.seq, self.beside):
            copy.start()

    def finish(self):
        for copy in self.hop(1, self.beside, self.beside):
            copy.wait_recv()
        for copy in self.hop(2, self.beside, self.sibling):
            copy.start()
        for copy in self.hop(0, self.sibling, self.sibling):
            copy.wait_recv()
        for copy in self.hop(2, lax.rem(self.sibling + 2, 4), self.sibling):
            copy.wait_recv()

    def drain(self):
        for copy in (
            self.hop(0, self.seq, self.sibling)
            + self.hop(1, self.seq, self.beside)
            + self.hop(2, self.beside, self.sibling)
        ):
            copy.wait_send()


def doc_parts(doc_ref, col_ref, edge_ref):
    here = lax.broadcasted_iota(jnp.int32, (C, C), 0)
    there = lax.broadcasted_iota(jnp.int32, (C, C), 1)
    eye = jnp.where(here == there, 1.0, 0.0).astype(BF16)
    for n in range(doc_ref.shape[1] // C):
        row = doc_ref[:, n * C : (n + 1) * C].astype(F32)
        col_ref[n * C : (n + 1) * C] = dot_nt(eye, jnp.broadcast_to(row, (128, C)).astype(BF16))
        low = jnp.min(row, axis=1, keepdims=True)
        high = jnp.max(row, axis=1, keepdims=True)
        edge_ref[n : n + 1] = jnp.broadcast_to(low, (1, D))
        edge_ref[n + 8 : n + 9] = jnp.broadcast_to(high, (1, D))


def spread_small(vec_refs, bias_ref, out_ref):
    def repeat(values):
        width = values.shape[1]
        rows = lax.broadcasted_iota(jnp.int32, (width, 128), 0)
        lanes = lax.broadcasted_iota(jnp.int32, (width, 128), 1)
        pick = jnp.where(lax.rem(lanes, width) == rows, 1.0, 0.0).astype(BF16)
        return dot(jnp.broadcast_to(values, (8, width)).astype(BF16), pick)[0:1]

    out_ref[...] = jnp.zeros_like(out_ref)
    for n, ref in enumerate(vec_refs):
        out_ref[n : n + 1] = repeat(ref[...])
    for b in range(max(bias_ref.shape[1] // 128, 1)):
        out_ref[5 + b : 6 + b] = repeat(bias_ref[:, b * 128 : (b + 1) * 128])


def join_small(count, part, gathered, vec_ref, bias_ref):
    lanes = lax.broadcasted_iota(jnp.int32, (8, D), 1)
    total = jnp.zeros((8, D), F32)
    for f in range(count):
        total = jnp.where(lanes // part == f, wide(gathered[f], 4), total)
    vec_ref[...] = total
    size = 4 * part
    for r in range(4):
        at = lanes[0:1] + r * D
        row = jnp.zeros((1, D), F32)
        for f in range(r * D // size, -(-(r + 1) * D // size)):
            for b in range(max(size // 128, 1)):
                use = (at // size == f) & (lax.rem(at, size) // 128 == b)
                row = jnp.where(use, wide(gathered[f, 5 + b : 6 + b], 4), row)
        bias_ref[0:1, r * D : (r + 1) * D] = row


ROOT = 0.7978845608028654
CUBE = 0.044715


def gelu_both(u):
    square = u * u
    bent = jnp.tanh(ROOT * u * (1.0 + CUBE * square))
    half = 0.5 * (1.0 + bent)
    slope = half + 0.5 * u * (1.0 - bent * bent) * (ROOT * (1.0 + 3.0 * CUBE * square))
    return u * half, slope


def feed_body(
    values, attended, cot, vec_ref, bias_ref, w_out, w_hidden, w_return, ready,
    y_ref, dy_ref, do_ref, gsmall_ref, gwo_ref, gwh_ref, gwr_ref,
):
    middle = values.astype(F32) + dot(attended, w_out())
    unit, scale = norm_parts(middle)
    hidden = (unit * vec_ref[2:3] + vec_ref[3:4]).astype(BF16)
    out = middle + vec_ref[4:5]
    grad_hidden = jnp.zeros_like(middle)
    cot32 = cot.astype(F32)
    tiles = FF // FEED_LANES
    ready()

    def into(j):
        cols = slice(j * FEED_LANES, (j + 1) * FEED_LANES)
        inner = dot(hidden, w_hidden(j)) + bias_ref[0:1, cols]
        return inner, dot_nt(cot, w_return(j))

    def bend(inner, grad):
        gated, slope = gelu_both(inner)
        return gated.astype(BF16), (grad * slope).astype(BF16)

    def outof(j, active, low):
        cols = slice(j * FEED_LANES, (j + 1) * FEED_LANES)
        there = slice(cols.start % D, cols.start % D + FEED_LANES)
        row = 8 + cols.start // D
        gwr_ref[:, cols] += dot_tn(cot, active)
        gsmall_ref[row : row + 1, there] += jnp.sum(low.astype(F32), axis=0, keepdims=True)
        gwh_ref[:, cols] += dot_tn(hidden, low)
        return dot(active, w_return(j)), dot_nt(low, w_hidden(j))

    coming = into(0)
    for j in range(tiles):
        bent = bend(*coming)
        if j + 1 < tiles:
            coming = into(j + 1)
        to_out, to_hidden = outof(j, *bent)
        out = out + to_out
        grad_hidden = grad_hidden + to_hidden
    y_ref[...] = out.astype(BF16)
    gsmall_ref[2:3] += jnp.sum(grad_hidden * unit, axis=0, keepdims=True)
    gsmall_ref[3:4] += jnp.sum(grad_hidden, axis=0, keepdims=True)
    gsmall_ref[4:5] += jnp.sum(cot32, axis=0, keepdims=True)
    grad_middle = cot32 + norm_back(unit, scale, vec_ref[2:3], grad_hidden)
    dy_ref[...] = grad_middle
    branch = grad_middle.astype(BF16)
    gwo_ref[...] += dot_tn(attended, branch)
    do_ref[...] = dot_nt(branch, w_out()).astype(BF16)


def pack_grads(count, part, gwo_ref, gwh_ref, gwr_ref, put):
    half = count // 2
    for q in range(4):
        x, c = q // 2, q % 2
        hidden_part = gwh_ref[:, q * 512 : (q + 1) * 512].reshape(half, 2, part, 512)
        out_part = gwo_ref[:, q * 128 : (q + 1) * 128].reshape(half, 2, part, 128)
        turned = gwr_ref[q * 128 : (q + 1) * 128].T.reshape(half, 2, 4, part, 128)
        for y in range(2):
            over_x, over_y = ((c * 2 + x) * 2 + y) * half, ((c * 2 + y) * 2 + x) * half
            put(0, over_x, slice(0, 512), hidden_part[:, y])
            put(0, over_x, slice(512, 640), out_part[:, y])
            for j in range(4):
                put(1, over_y, slice(j * 128, (j + 1) * 128), turned[:, y, j])


def feed_kernel(
    x_ref, o_ref, g_ref, small_ref, bias_ref, wo_ref, wh_ref, wr_ref,
    y_ref, dy_ref, do_ref, pack_ref, pack_r_ref, gsmall_ref, gwo_ref, gwh_ref, gwr_ref,
):
    step = pl.program_id(0)
    count, part = wh_ref.shape[0], wh_ref.shape[1]

    @pl.when(step == 0)
    def _():
        for ref in (gwo_ref, gwh_ref, gwr_ref, gsmall_ref):
            ref[...] = jnp.zeros_like(ref)

    feed_body(
        x_ref[...], o_ref[...], g_ref[...], small_ref, bias_ref, *weight_views(wo_ref, wh_ref, wr_ref),
        lambda: None, y_ref, dy_ref, do_ref, gsmall_ref, gwo_ref, gwh_ref, gwr_ref,
    )

    @pl.when(step == pl.num_programs(0) - 1)
    def _():
        def put(which, slab, lanes, values):
            ref = (pack_ref, pack_r_ref)[which]
            n = values.shape[0] * part
            ref[slab * part : slab * part + n, lanes] = values.reshape(n, -1).astype(ref.dtype)

        pack_grads(count, part, gwo_ref, gwh_ref, gwr_ref, put)


def weight_views(wo_ref, wh_ref, wr_ref):
    def w_out():
        return wo_ref[...].reshape(D, D).astype(BF16)

    def w_hidden(j):
        cols = slice(j * FEED_LANES, (j + 1) * FEED_LANES)
        return wh_ref[:, :, cols].reshape(D, FEED_LANES).astype(BF16)

    def w_return(j):
        n = FEED_LANES // wr_ref.shape[1]
        return wr_ref[j * n : (j + 1) * n].reshape(FEED_LANES, D).astype(BF16)

    return w_out, w_hidden, w_return


def front_kernel(count, joined, names, *refs):
    r = types.SimpleNamespace(**dict(zip(names, refs)))
    sems = refs[len(names) :]
    x_ref, doc_ref, vec_out, bias_out = r.x, r.doc, r.vec, r.bias
    qkvf, hidden, w_all, mine = r.qkvf, r.hidden, r.w_all, r.mine
    mine_o, mine_h, mine_r, spread, smalls = r.mine_o, r.mine_h, r.mine_r, r.spread, r.smalls
    col_ref, edge_ref, state, tail = r.col, r.edge, r.state, r.tail
    tails, tail_rows = r.tails, r.tail_rows
    step = pl.program_id(0)
    seq, at, _, _ = places()
    link = mine.dtype
    groups_of_sems = []
    for _ in range(5):
        groups_of_sems.append(bundle(sems[:11]))
        sems = sems[11:]
    small_send, small_recv, state_send, state_recv, out_sem, stage_sem, fed_sem = sems
    main = Gather(count, mine, w_all, D, 3 * D, False, groups_of_sems[0])
    q_piece = Gather(count, mine, w_all, 0, D, False, groups_of_sems[1])
    o_piece = Gather(count, mine_o, r.wo_all, 0, D, True, groups_of_sems[2])
    h_piece = Gather(count, mine_h, r.wh_all, 0, FF, True, groups_of_sems[3])
    r_piece = Gather(count, mine_r, r.wr_all, 0, D, False, groups_of_sems[4])
    later = (q_piece, o_piece, h_piece, r_piece)
    states = States(tails, tail_rows, (state_send, state_recv))

    def small_copy(k, owner):
        return push(
            spread, smalls.at[owner], small_send.at[k], small_recv.at[k], fsdp=at ^ k
        )

    def save():
        return (
            pltpu.make_async_copy(qkvf, r.qkvf_out, out_sem.at[0]),
            pltpu.make_async_copy(w_all, r.w_out, out_sem.at[1]),
        )

    @pl.when(step == 0)
    def _():
        greet(count)
        for n, ref in enumerate((r.w0, r.w1, r.w2, r.w3)):
            mine[:, n * D : (n + 1) * D] = ref[...].astype(BF16).astype(link)
        spread_small((r.v0, r.v1, r.v2, r.v3, r.v4), r.bias_in, spread)
        doc_parts(doc_ref, col_ref, edge_ref)
        tail[...] = jnp.zeros_like(tail)
        met(count)
        for k in range(1, count):
            small_copy(k, at).start()

        def between():
            mine_o[...] = r.w4[...].astype(BF16).astype(link)
            mine_h[...] = r.w5[...].astype(BF16).astype(link)
            mine_r[...] = r.w6[...].astype(BF16).astype(link)
            smalls[at] = spread[...]
            for k in range(1, count):
                small_copy(k, at ^ k).wait_recv()
            join_small(count, r.v0.shape[1], smalls, vec_out, bias_out)
            q_piece.start()
            o_piece.start()

            @pl.loop(0, 8)
            def _(n):
                here = pl.ds(pl.multiple_of(n * C, C), C)
                unit, _ = norm_parts(x_ref[here].astype(F32))
                hidden[here] = (unit * vec_out[0:1] + vec_out[1:2]).astype(BF16)

        main.at_once(between)
        h_piece.start()
        r_piece.start()

    @pl.when(step < FRONT)
    def _():
        size = 8 // FRONT * C
        here = pl.ds(pl.multiple_of(step * size, size), size)
        weights = w_all[:, :, D:].reshape(D, 3 * D).astype(BF16)
        rows = dot(hidden[here], weights).astype(BF16)
        qkvf[here, D:] = rows
        slots = wide(flag(col_ref[here], edge_ref[15:16]), 4) * jnp.exp(rows[:, 2 * D :].astype(F32))
        slots = slots.astype(BF16)
        keys, values = state_terms(slots, rows[:, 0:D], rows[:, D : 2 * D])
        tail[0:64] += keys
        tail[64:128] += values
        tail[128:129] += jnp.sum(slots.astype(F32), axis=0, keepdims=True)

    @pl.when(step == 1)
    def _():
        q_piece.second()
        o_piece.second()

    @pl.when(step == FRONT - 1)
    def _():
        tails[seq] = tail[0:128].astype(link)
        tail_rows[seq, 0:1] = tail[128:129]
        tail_rows[seq, 1:2] = edge_ref[15:16]
        tail_rows[seq, 2:8] = jnp.zeros((6, D), F32)
        states.start()
        q_piece.third()
        q_piece.finish()

        @pl.loop(0, FRONT)
        def _(n):
            size = 8 // FRONT * C
            here = pl.ds(pl.multiple_of(n * size, size), size)
            weights = w_all[:, :, 0:D].reshape(D, D).astype(BF16)
            qkvf[here, 0:D] = dot(hidden[here], weights).astype(BF16)

        for copy in save():
            copy.start()
        o_piece.third()

        @pl.loop(0, 8)
        def _(n):
            here = pl.ds(pl.multiple_of(n * C, C), C)
            hidden[here] = jnp.exp(qkvf[here, 3 * D :].astype(F32)).astype(BF16)
            r.seen[n] = visible(col_ref[here], doc_ref[:, here].astype(F32))

        states.finish()
        first = edge_ref[0:1]
        state[...] = jnp.zeros_like(state)
        for n in range(4):
            use = jnp.where(tail_rows[n, 1:2] == first, 1.0, 0.0) * (n < seq).astype(F32)
            state[0:128] += use * tails[n].astype(F32)
            state[128:129] += use * tail_rows[n, 0:1]
        h_piece.second()

    per = 8 // FRONT

    def kept_copies(n):
        here = pl.ds(pl.multiple_of(n * per * C, per * C), per * C)
        slot = lax.rem(n, 2)
        return [
            pltpu.make_async_copy(r.stage.at[slot, k], out.at[here], stage_sem.at[slot, k])
            for k, out in enumerate((r.p, r.s, r.z))
        ]

    @pl.when((step >= FRONT + 2) & (step < 2 * FRONT))
    def _():
        for copy in kept_copies(step - FRONT - 2):
            copy.wait()

    @pl.when((step >= FRONT) & (step < 2 * FRONT))
    def _():
        slot = lax.rem(step - FRONT, 2)

        @pl.loop(0, per)
        def _(u):
            n = (step - FRONT) * per + u
            here = pl.ds(pl.multiple_of(n * C, C), C)
            block = pl.ds(pl.multiple_of(u * C, C), C)
            attend_body(
                n, qkvf.at[here], hidden[here], r.seen[n], col_ref[here], edge_ref, state,
                r.o.at[here if joined else block], *(r.stage.at[slot, k, block] for k in range(3)),
                r.kept.at[pl.ds(u, 1)],
            )

            @pl.when(n == 0)
            def _():
                o_piece.fourth()

            @pl.when(n == per - 1)
            def _():
                r_piece.second()

            @pl.when(n == per)
            def _():
                h_piece.third()

    @pl.when((step >= FRONT) & (step < 2 * FRONT))
    def _():
        for copy in kept_copies(step - FRONT):
            copy.start()

    @pl.when(step == 2 * FRONT - 1)
    def _():
        r_piece.third()
        h_piece.fourth()
        o_piece.finish()
        for copy in save():
            copy.wait()

    def complete():
        h_piece.finish()
        r_piece.finish()
        for piece in later:
            piece.drain()
        main.drain(True)
        states.drain()
        for k in range(1, count):
            small_copy(k, at).wait_send()
        for n in (FRONT - 2, FRONT - 1):
            for copy in kept_copies(n):
                copy.wait()

    if not joined:
        pl.when(step == 2 * FRONT - 1)(complete)
        return

    @pl.when(step == 2 * FRONT)
    def _():
        for ref in (r.gwo, r.gwh, r.gwr, r.gsmall):
            ref[...] = jnp.zeros_like(ref)

    fed = step - 2 * FRONT

    def fed_copies(n):
        here = pl.ds(pl.multiple_of(n * FEED_ROWS, FEED_ROWS), FEED_ROWS)
        slot = lax.rem(n, 2)
        pairs = ((r.held_y, r.y), (r.held_dy, r.dy), (r.held_do, r.do))
        return [
            pltpu.make_async_copy(held.at[slot], out.at[here], fed_sem.at[slot, k])
            for k, (held, out) in enumerate(pairs)
        ]

    @pl.when(fed >= 2)
    def _():
        for copy in fed_copies(fed - 2):
            copy.wait()

    @pl.when(fed >= 0)
    def _():
        here = pl.ds(pl.multiple_of(fed * FEED_ROWS, FEED_ROWS), FEED_ROWS)
        slot = lax.rem(fed, 2)
        feed_body(
            x_ref[here], r.o[here], r.g[...], vec_out, bias_out,
            *weight_views(r.wo_all, r.wh_all, r.wr_all),
            lambda: pl.when(step == 2 * FRONT)(complete),
            r.held_y.at[slot], r.held_dy.at[slot], r.held_do.at[slot], r.gsmall, r.gwo, r.gwh, r.gwr,
        )
        for copy in fed_copies(fed):
            copy.start()

    @pl.when(step == pl.num_programs(0) - 1)
    def _():
        part = mine.shape[0]

        def put(which, slab, lanes, values):
            n = values.shape[0] * part
            at_lane = 640 * which + lanes.start
            qkvf[slab * part : slab * part + n, at_lane : at_lane + values.shape[2]] = (
                values.reshape(n, -1).astype(BF16)
            )

        pack_grads(count, part, r.gwo, r.gwh, r.gwr, put)
        copies = [
            pltpu.make_async_copy(qkvf.at[:, 0:640], r.pack, out_sem.at[0]),
            pltpu.make_async_copy(qkvf.at[:, 640:1152], r.pack_r, out_sem.at[1]),
        ]
        for copy in copies:
            copy.start()
        last = x_ref.shape[0] // FEED_ROWS - 1
        for copy in (*fed_copies(last - 1), *fed_copies(last), *copies):
            copy.wait()


def front(count, tokens, doc_ids, weights, vectors, bias, cotangent):
    rows = tokens.shape[0]
    part = weights[0].shape[0]
    link = BF16 if part % 16 == 0 else F32
    joined = link == BF16
    per = 8 // FRONT
    once = lambda a: pl.BlockSpec(a.shape, lambda i: (0,) * a.ndim)
    late = lambda i: jnp.clip(i - FRONT, 0, FRONT - 1)
    tall = pl.BlockSpec((per * C, D), lambda i: (late(i), 0))
    fed = pl.BlockSpec((FEED_ROWS, D), lambda i: (jnp.maximum(i - 2 * FRONT, 0), 0))
    anywhere = pl.BlockSpec(memory_space=pl.ANY)
    vmem, dma = pltpu.VMEM, pltpu.SemaphoreType.DMA
    ins = {"x": (tokens, once(tokens)), "doc": (doc_ids, once(doc_ids))}
    ins |= {f"w{n}": (a, once(a)) for n, a in enumerate(weights)}
    ins |= {f"v{n}": (a, once(a)) for n, a in enumerate(vectors)}
    ins["bias_in"] = (bias, once(bias))
    wide_rows, slabs = shape_of((rows, D), F32), 4 * count
    outs = {
        "qkvf_out": (shape_of((rows, 4 * D), BF16), anywhere),
        "p": (wide_rows, anywhere),
        "s": (wide_rows, anywhere),
        "z": (wide_rows, anywhere),
        "kept": (
            shape_of((8, 128, D), F32), pl.BlockSpec((per, 128, D), lambda i: (late(i), 0, 0)),
        ),
        "w_out": (shape_of((count, part, 4 * D), link), anywhere),
        "vec": (shape_of((8, D), F32), whole(8, D)),
    }
    scratch = {
        "qkvf": vmem((rows, 4 * D), BF16),
        "hidden": vmem((rows, D), BF16),
        "w_all": vmem((count, part, 4 * D), link),
        "mine": vmem((part, 4 * D), link),
        "mine_o": vmem((part, D), link),
        "mine_h": vmem((part, FF), link),
        "mine_r": vmem((4 * part, D), link),
        "spread": vmem((8, 128), F32),
        "smalls": vmem((count, 8, 128), F32),
        "col": vmem((rows, 128), F32),
        "edge": vmem((16, D), F32),
        "state": vmem((136, D), F32),
        "tail": vmem((136, D), F32),
        "tails": vmem((4, 128, D), link),
        "tail_rows": vmem((4, 8, D), F32),
        "stage": vmem((2, 3, per * C, D), F32),
        "seen": vmem((8, C, C), BF16),
    }
    gathered = {
        "wo_all": (count, part, D), "wh_all": (count, part, FF), "wr_all": (count, 4 * part, D),
    }
    if joined:
        ins["g"] = (cotangent, fed)
        outs |= {
            "y": (shape_of((rows, D), BF16), anywhere),
            "dy": (wide_rows, anywhere),
            "do": (shape_of((rows, D), BF16), anywhere),
            "pack": (shape_of((slabs * part, 640), BF16), anywhere),
            "pack_r": (shape_of((slabs * part, D), BF16), anywhere),
            "gsmall": (shape_of((16, D), F32), whole(16, D)),
        }
        scratch |= {name: vmem(shape, link) for name, shape in gathered.items()}
        scratch |= {
            "held_y": vmem((2, FEED_ROWS, D), BF16), "held_dy": vmem((2, FEED_ROWS, D), F32),
            "held_do": vmem((2, FEED_ROWS, D), BF16),
            "o": vmem((rows, D), BF16), "bias": vmem((1, FF), F32), "gwo": vmem((D, D), F32),
            "gwh": vmem((D, FF), F32), "gwr": vmem((D, FF), F32),
        }
    else:
        outs |= {name: (shape_of(shape, link), anywhere) for name, shape in gathered.items()}
        outs |= {
            "o": (shape_of((rows, D), BF16), tall), "bias": (shape_of((1, FF), F32), whole(1, FF)),
        }
    found = pl.pallas_call(
        functools.partial(front_kernel, count, joined, (*ins, *outs, *scratch)),
        grid=(2 * FRONT + (rows // FEED_ROWS if joined else 0),),
        in_specs=[spec for _, spec in ins.values()],
        out_specs=[spec for _, spec in outs.values()],
        out_shape=[shape for shape, _ in outs.values()],
        scratch_shapes=list(scratch.values())
        + gather_sems(count, True)
        + gather_sems(count, False) * 4
        + [dma((count,)), dma((count,)), dma((3, 2)), dma((3, 2)), dma((2,)), dma((2, 3)), dma((2, 3))],
        compiler_params=pltpu.CompilerParams(
            vmem_limit_bytes=62 * MIB, collective_id=1, has_side_effects=True
        ),
        name="front",
    )(*(a for a, _ in ins.values()))
    found = dict(zip(outs, found))
    if not joined:
        found |= feed(count, part, tokens, found, cotangent, link)
    return found


def feed(count, part, tokens, found, cotangent, link):
    rows, slabs = tokens.shape[0], 4 * count
    tall = pl.BlockSpec((256, D), lambda i: (i, 0))
    weights = [found[name] for name in ("wo_all", "wh_all", "wr_all")]
    names = ("y", "dy", "do", "pack", "pack_r", "gsmall")
    return dict(
        zip(
            names,
            pl.pallas_call(
                feed_kernel,
                grid=(rows // 256,),
                in_specs=[tall] * 3
                + [whole(8, D), whole(1, FF)]
                + [whole(*a.shape) for a in weights],
                out_specs=[tall] * 3
                + [whole(slabs * part, 640), whole(slabs * part, D), whole(16, D)],
                out_shape=[
                    shape_of((rows, D), BF16),
                    shape_of((rows, D), F32),
                    shape_of((rows, D), BF16),
                    shape_of((slabs * part, 640), link),
                    shape_of((slabs * part, D), link),
                    shape_of((16, D), F32),
                ],
                scratch_shapes=[
                    pltpu.VMEM((D, D), F32), pltpu.VMEM((D, FF), F32), pltpu.VMEM((D, FF), F32),
                ],
                compiler_params=PARAMS,
                name="feed",
            )(tokens, found["o"], cotangent, found["vec"], found["bias"], *weights),
        )
    )


def row_body(
    n, qkvf_ref, do_ref, p_ref, s_ref, z_ref, kept_ref, col, row, edge_ref,
    r_ref, dn_ref, dz_ref, head_ref, aside,
):
    first = edge_ref[pl.ds(0, 1)]
    before = edge_ref[pl.ds(8 + jnp.maximum(n - 1, 0), 1)]
    last = jnp.where(n == 0, first, before)
    vis = visible(col, row)
    carried = wide(flag(col, last), 2)
    slots = jnp.exp(qkvf_ref[:, 3 * D :].astype(F32)).astype(BF16)
    own = wide(flag(col, first), 2)
    states = [expand(kept_ref[0, 64:128, lanes_of(g)]).astype(BF16) for g in range(2)]

    def mixing(g):
        return masked(dot_nt(stacked(do_ref[:, lanes_of(g)]), part_of(qkvf_ref, 2, g)), vis)

    def to_reading(g, back_mix):
        lanes = lanes_of(g)
        back = select(dot(back_mix, slots[:, lanes]))
        return back + carried * dot_nt(do_ref[:, lanes], states[g])

    def to_scores(g, back_reading):
        lanes = lanes_of(g)
        probs, score, inverse = p_ref[:, lanes], s_ref[:, lanes], z_ref[:, lanes]
        shared = back_reading * inverse * probs
        back_score = shared - probs * head_sums(shared)
        back_numer = back_score * inverse * SCALE
        back_total = -(shared + back_score * score) * inverse
        reading = (probs * inverse).astype(BF16)
        r_ref[:, lanes] = reading
        dn_ref[:, lanes] = back_numer
        dz_ref[:, lanes] = back_total
        return back_numer, back_total, reading

    def to_state(g, back_numer, back_total, reading):
        lanes = lanes_of(g)
        head_ref[0:64, lanes] += compacted(
            dot_tn((own * back_numer).astype(BF16), part_of(qkvf_ref, 0, g))
        )
        head_ref[64:128, lanes] += compacted(
            dot_tn((own * reading.astype(F32)).astype(BF16), do_ref[:, lanes])
        )
        head_ref[128:129, lanes] += jnp.sum(own * back_total, axis=0, keepdims=True)

    back_mix = mixing(0)
    back_mix_two = mixing(1)
    aside()
    back_reading = to_reading(0, back_mix)
    back_reading_two = to_reading(1, back_mix_two)
    parts = to_scores(0, back_reading)
    to_state(0, *parts)
    parts = to_scores(1, back_reading_two)
    to_state(1, *parts)


def query_body(n, qkvf_ref, kept_ref, col, row, edge_ref, dn_ref, dq_ref):
    first = edge_ref[pl.ds(0, 1)]
    before = edge_ref[pl.ds(8 + jnp.maximum(n - 1, 0), 1)]
    last = jnp.where(n == 0, first, before)
    vis = visible(col, row)
    carried = wide(flag(col, last), 2)
    slots = jnp.exp(qkvf_ref[:, 3 * D :].astype(F32)).astype(BF16)
    lows = [dn_ref[:, lanes_of(g)].astype(BF16) for g in range(2)]
    states = [expand(kept_ref[0, 0:64, lanes_of(g)]).astype(BF16) for g in range(2)]

    def affine(g):
        return masked(dot_nt(stacked(lows[g]), slots[:, lanes_of(g)]), vis)

    def to_queries(g, back_affinity):
        out = select(dot(back_affinity, part_of(qkvf_ref, 1, g))) + carried * dot(lows[g], states[g])
        dq_ref[:, lanes_of(g)] = out.astype(BF16)

    one, two = affine(0), affine(1)
    to_queries(0, one)
    to_queries(1, two)


def column_body(
    n, qkvf_ref, do_ref, r_ref, dn_ref, dz_ref, col, row, edge_ref, state, snap, snap_rows, d_ref
):
    newest = edge_ref[15:16]
    after = edge_ref[pl.ds(jnp.minimum(n + 1, 7), 1)]
    following = jnp.where(n == 7, newest, after)
    first = edge_ref[pl.ds(n, 1)]
    vis = visible_back(col, row)
    carried = wide(flag(col, following), 2)
    own = wide(flag(col, first), 2)
    kept = jnp.where(following == first, 1.0, 0.0)[:, :GROUP]
    snap[n] = state[0:128].astype(BF16)
    snap_rows[pl.ds(n, 1)] = state[128:129]
    key_states = [expand(state[0:64, lanes_of(g)]).astype(BF16) for g in range(2)]
    value_states = [expand(state[64:128, lanes_of(g)]).astype(BF16) for g in range(2)]
    slots = jnp.exp(qkvf_ref[:, 3 * D :].astype(F32)).astype(BF16)
    numers = [dn_ref[:, lanes_of(g)] for g in range(2)]

    def mixing(g, apart):
        return masked(dot_nt(apart, r_ref[:, lanes_of(g)]), vis)

    def affine(g, apart):
        return masked(dot_nt(apart, numers[g].astype(BF16)), vis)

    def to_values(g, mix):
        lanes = lanes_of(g)
        out = select(dot(mix, do_ref[:, lanes])) + carried * dot(slots[:, lanes], value_states[g])
        d_ref[:, 2 * D + g * GROUP : 2 * D + (g + 1) * GROUP] = out.astype(BF16)

    def to_keys(g, back_affinity):
        lanes = lanes_of(g)
        out = select(dot(back_affinity, part_of(qkvf_ref, 0, g)))
        out = out + carried * dot(slots[:, lanes], key_states[g])
        d_ref[:, D + g * GROUP : D + (g + 1) * GROUP] = out.astype(BF16)

    def to_state(g):
        lanes = lanes_of(g)
        state[0:64, lanes] = kept * state[0:64, lanes] + compacted(
            dot_tn((own * numers[g]).astype(BF16), part_of(qkvf_ref, 0, g))
        )
        state[64:128, lanes] = kept * state[64:128, lanes] + compacted(
            dot_tn((own * r_ref[:, lanes].astype(F32)).astype(BF16), do_ref[:, lanes])
        )
        state[128:129, lanes] = kept * state[128:129, lanes] + jnp.sum(
            own * dz_ref[:, lanes], axis=0, keepdims=True
        )

    apart = stacked(slots[:, lanes_of(0)])
    mix = mixing(0, apart)
    back_affinity = affine(0, apart)
    apart = stacked(slots[:, lanes_of(1)])
    mix_two = mixing(1, apart)
    to_values(0, mix)
    affinity_two = affine(1, apart)
    to_keys(0, back_affinity)
    to_state(0)
    to_values(1, mix_two)
    to_keys(1, affinity_two)
    to_state(1)


def slot_body(n, qkvf_ref, do_ref, r_ref, dn_ref, dz_ref, col, row, edge_ref, snap, snap_rows, d_ref):
    newest = edge_ref[15:16]
    after = edge_ref[pl.ds(jnp.minimum(n + 1, 7), 1)]
    following = jnp.where(n == 7, newest, after)
    vis = visible_back(col, row)
    carried = wide(flag(col, following), 2)
    left = lane_heads(C, 128) == 0
    norm_state = snap_rows[pl.ds(n, 1)]
    key_states = [expand(snap[n, 0:64, lanes_of(g)]) for g in range(2)]
    value_states = [expand(snap[n, 64:128, lanes_of(g)]) for g in range(2)]

    def mixing(g):
        return masked(dot_nt(stacked(part_of(qkvf_ref, 2, g)), do_ref[:, lanes_of(g)]), vis)

    def affine(g):
        return masked(dot_nt(stacked(part_of(qkvf_ref, 1, g)), part_of(qkvf_ref, 0, g)), vis)

    def from_mix(g, back_mix):
        return select(dot(back_mix, r_ref[:, lanes_of(g)]))

    def from_affinity(g, affinity):
        high, low = split(dn_ref[:, lanes_of(g)])
        parts = []
        for p in range(2):
            pair = slice(p * 128, (p + 1) * 128)
            both = dot(
                affinity[p * 512 : (p + 1) * 512],
                jnp.concatenate([high[:, pair], low[:, pair]], axis=1),
            )
            both = both[:, :128] + both[:, 128:]
            parts.append(jnp.where(left, both[:C], both[C:]))
        return jnp.concatenate(parts, axis=1)

    def from_totals():
        high, low = split(dz_ref[...])
        return dot(vis, high) + dot(vis, low)

    def from_state(g):
        return carried * (
            dot_nt(part_of(qkvf_ref, 1, g), key_states[g])
            + dot_nt(part_of(qkvf_ref, 2, g), value_states[g])
            + norm_state[:, lanes_of(g)]
        )

    def to_slots(g, back_slots):
        written = jnp.exp(part_of(qkvf_ref, 3, g).astype(F32))
        d_ref[:, 3 * D + g * GROUP : 3 * D + (g + 1) * GROUP] = (back_slots * written).astype(BF16)

    norm = from_totals()
    mix = mixing(0)
    affinity = affine(0)
    mix_two = mixing(1)
    total = from_mix(0, mix)
    affinity_two = affine(1)
    total = total + from_affinity(0, affinity)
    total_two = from_mix(1, mix_two)
    to_slots(0, total + norm[:, lanes_of(0)] + from_state(0))
    total_two = total_two + from_affinity(1, affinity_two)
    to_slots(1, total_two + norm[:, lanes_of(1)] + from_state(1))


class Scatter:
    def __init__(self, count, source, own, axes, direct, out, buffers):
        self.axes, self.direct, self.out = axes, direct, out
        self.seq, self.at, self.sibling, self.beside = places()
        self.source, self.own = source, own
        self.core = lax.rem(self.seq, 2)
        self.total, self.local, self.last, self.done = buffers[:4]
        self.stages = []
        size = source.shape[0]
        base = 0
        for n, axis in enumerate(axes):
            ways = {"core": 2, "x": 2, "y": 2, "z": count // 2, "all": count}[axis]
            size = size // ways
            me = {
                "core": self.core, "x": self.seq // 2, "y": lax.rem(self.at, 2), "z": self.at // 2,
                "all": self.at,
            }[axis]
            held = source
            if own is not None and n > 0:
                held = own
            come, sems = buffers[4 + 2 * n], buffers[5 + 2 * n]
            self.stages.append((axis, ways, size, base, me, held, come, sems))
            if own is None or n > 0:
                base = base + me * size

    def copies(self, n):
        axis, ways, size, base, me, held, come, sems = self.stages[n]
        for k in range(1, ways):
            if axis in ("core", "x"):
                device = {"seq": self.sibling if axis == "core" else self.beside}
            else:
                device = {"fsdp": self.at ^ (2 * k if axis == "z" else k)}
            yield push(
                held.at[pl.ds(base + (me ^ k) * size, size)], come.at[k - 1],
                sems.at[0, k - 1], sems.at[1, k - 1], **device,
            )

    def copy_own(self):
        size = self.source.shape[0] // 2
        return pltpu.make_async_copy(
            self.source.at[pl.ds(self.core * size, size)], self.own, self.local
        )

    def start(self):
        for copy in self.copies(0):
            copy.start()
        if self.own is not None:
            self.copy_own().start()

    def advance(self, n):
        axis, ways, size, base, me, held, come, sems = self.stages[n]
        for copy in self.copies(n):
            copy.wait_recv()
        mine = held
        first = base + me * size
        if n == 0 and self.own is not None:
            self.copy_own().wait()
            mine, first = self.own, 0

        def added(slab):
            total = mine[first + slab].astype(F32)
            for k in range(1, ways):
                total = total + come[k - 1, slab].astype(F32)
            return total

        if n + 1 == len(self.stages):
            self.total[...] = added(0)
            self.copy_done().start()
            for copy in self.sent():
                copy.start()
            return

        @pl.loop(0, size)
        def _(slab):
            mine[first + slab] = added(slab).astype(mine.dtype)

        for copy in self.copies(n + 1):
            copy.start()

    def copy_done(self):
        return pltpu.make_async_copy(self.total, self.out.at[self.seq], self.done)

    def sent(self):
        other = lax.rem(self.sibling + 2, 4)
        for n, target in enumerate((self.sibling, self.beside, other)[: 3 if self.direct else 2]):
            yield push(
                self.total, self.out.at[self.seq], self.last.at[0, n], self.last.at[1, n], seq=target
            )

    def forwarded(self, source):
        here = self.out.at[source]
        return push(here, here, self.last.at[0, 2], self.last.at[1, 2], seq=self.sibling)

    def come_in(self, n, source):
        here = self.out.at[source]
        return push(here, here, self.last.at[0, n], self.last.at[1, n], seq=source)

    def forward(self):
        self.come_in(1, self.beside).wait_recv()
        self.forwarded(self.beside).start()

    def finish(self):
        other = lax.rem(self.sibling + 2, 4)
        self.come_in(0, self.sibling).wait_recv()
        if self.direct:
            self.come_in(1, self.beside).wait_recv()
        else:
            self.forwarded(self.beside).wait_send()
        self.forwarded(other).wait_recv()
        self.copy_done().wait()
        for copy in self.sent():
            copy.wait_send()
        for n in range(len(self.stages)):
            for copy in self.copies(n):
                copy.wait_send()


def scatter_scratch(count, part, lanes, link, axes, hbm):
    vmem, dma = pltpu.VMEM, pltpu.SemaphoreType.DMA
    size = 2 * 4 * count // 2
    out = [vmem((size // 2, part, lanes), link)] if hbm else []
    out += [vmem((part, lanes), F32), dma, dma((2, 3)), dma]
    for axis in axes:
        ways = {"core": 2, "x": 2, "y": 2, "z": count // 2, "all": count}[axis]
        size = size // ways
        out += [vmem((ways - 1, size, part, lanes), link), dma((2, ways - 1))]
    return out


OVER_X = ("core", "x", "y", "z")
OVER_Y = ("core", "y", "x", "z")
SHORT = ("core", "x", "all")


class SmallSum:
    def __init__(self, count, mine, from_seq, half, from_fsdp, sems):
        self.count, self.mine, self.from_seq = count, mine, from_seq
        self.half, self.from_fsdp, self.sems = half, from_fsdp, sems
        self.seq, self.at, _, _ = places()

    def lanes(self, owner):
        if self.from_fsdp.shape[2] == D:
            return pl.ds(0, D)
        first = owner * (D // self.count) // 128 * 128
        return pl.ds(pl.multiple_of(first, 128), 128)

    def over_seq(self, k, slot):
        return push(
            self.mine, self.from_seq.at[slot], self.sems[0].at[0, k], self.sems[0].at[1, k],
            seq=self.seq ^ k,
        )

    def over_fsdp(self, k):
        return push(
            self.half.at[:, self.lanes(self.at ^ k)], self.from_fsdp.at[self.at],
            self.sems[1].at[0, k], self.sems[1].at[1, k], fsdp=self.at ^ k,
        )

    def fsdp_in(self, k):
        here = self.from_fsdp.at[self.at ^ k]
        return push(here, here, self.sems[1].at[0, k], self.sems[1].at[1, k], fsdp=self.at ^ k)

    def start(self):
        for k in range(1, 4):
            self.over_seq(k, self.seq).start()
        self.from_seq[self.seq] = self.mine[...]

    def second(self):
        for k in range(1, 4):
            self.over_seq(k, self.seq ^ k).wait_recv()
        total = self.from_seq[0]
        for n in range(1, 4):
            total = total + self.from_seq[n]
        self.half[...] = total
        for k in range(1, self.count):
            self.over_fsdp(k).start()
        self.from_fsdp[self.at] = self.half[:, self.lanes(self.at)]

    def finish(self, out_ref):
        for k in range(1, self.count):
            self.fsdp_in(k).wait_recv()
        total = self.from_fsdp[0]
        for n in range(1, self.count):
            total = total + self.from_fsdp[n]
        out_ref[...] = total
        for k in range(1, 4):
            self.over_seq(k, self.seq).wait_send()
        for k in range(1, self.count):
            self.over_fsdp(k).wait_send()


def small_scratch(count, rows, lanes):
    vmem, dma = pltpu.VMEM, pltpu.SemaphoreType.DMA
    return [
        vmem((4, rows, D), F32), vmem((rows, D), F32), vmem((count, rows, lanes), F32),
        dma((2, 4)), dma((2, count)),
    ]


QUERY, COLUMN, SLOT, INPUT = 8, 16, 24, 32


def back_kernel(
    count, per, x_ref, xs_ref, qkvf_ref, do_ref, p_ref, s_ref, z_ref, kept_ref, dy_ref, doc_ref,
    small_ref, w_ref, ffg_ref, ffr_ref, ffs_ref,
    gi_ref, ff_out, fr_out, q_out, kv_out, f_out, s1_out, s2_out,
    gi_held, gi_sem, scores, scores_sem, d_all, h_turned, reading, numer, total, col_ref, edge_ref, head, state, heads, head_rows,
    snap, snap_rows, w_held, w_sem, q_piece, kv_piece, f_piece, last_small, *rest,
):
    step = pl.program_id(0)
    seq, at, _, _ = places()
    link = q_piece.dtype

    def take(size):
        nonlocal rest
        out, rest = rest[:size], rest[size:]
        return out

    (own,) = take(1)
    ff = Scatter(count, ffg_ref, own, OVER_X, False, ff_out, take(12))
    (own,) = take(1)
    fr = Scatter(count, ffr_ref, own, OVER_Y, False, fr_out, take(12))
    for_q = Scatter(count, q_piece, None, OVER_X, False, q_out, take(12))
    for_kv = Scatter(count, kv_piece, None, OVER_X, False, kv_out, take(12))
    for_f = Scatter(count, f_piece, None, SHORT, True, f_out, take(10))
    small_one = SmallSum(count, ffs_ref, *take(3), take(2))
    small_two = SmallSum(count, last_small, *take(3), take(2))
    states = States(heads, head_rows, take(2))

    def chunk(u, first, turned=False):
        n = step * per + u - first
        n = 7 - n if turned else n
        here = pl.ds(pl.multiple_of(n * C, C), C)
        block = pl.ds(pl.multiple_of((per - 1 - u if turned else u) * C, C), C)
        return n, here, block, col_ref[here], doc_ref[:, here].astype(F32)

    def fetch():
        return pltpu.make_async_copy(w_ref, w_held, w_sem)

    def fetch_scores(n):
        slot, here = lax.rem(n, 2), pl.ds(pl.multiple_of(n * per * C, per * C), per * C)
        return [
            pltpu.make_async_copy(ref.at[here], scores.at[slot, k], scores_sem.at[slot, k])
            for k, ref in enumerate((p_ref, s_ref, z_ref))
        ]

    def give(n):
        here = pl.ds(pl.multiple_of(n * per * C, per * C), per * C)
        slot = lax.rem(n, 2)
        return pltpu.make_async_copy(gi_held.at[slot], gi_ref.at[here], gi_sem.at[slot])

    def weight_grad(piece, d_lanes, lanes, short=False):
        grad = dot(h_turned[...], d_all[:, d_lanes])
        half, part = count // 2, piece.shape[1]
        for q in range(4):
            x, c = q // 2, q % 2
            share = grad[:, q * 128 : (q + 1) * 128].reshape(half, 2, part, 128).astype(link)
            if short:
                first = (c * 2 + x) * count
                piece[first : first + count, :, lanes] = share.reshape(count, part, 128)
                continue
            for y in range(2):
                first = ((c * 2 + x) * 2 + y) * half
                piece[first : first + half, :, lanes] = share[:, y]

    @pl.when(step == 0)
    def _():
        greet(count)
        for n in range(2):
            for copy in fetch_scores(n):
                copy.start()
        fetch().start()
        doc_parts(doc_ref, col_ref, edge_ref)
        head[...] = jnp.zeros_like(head)
        last_small[...] = jnp.zeros_like(last_small)

    def turn():
        weight_grad(q_piece, slice(0, D), slice(0, 128))
        for_q.start()
        states.finish()
        newest = edge_ref[15:16]
        state[...] = jnp.zeros_like(state)
        for n in range(4):
            use = jnp.where(head_rows[n, 1:2] == newest, 1.0, 0.0) * (n > seq).astype(F32)
            state[0:128] += use * heads[n].astype(F32)
            state[128:129] += use * head_rows[n, 0:1]

    def send_states():
        heads[seq] = head[0:128].astype(link)
        head_rows[seq, 0:1] = head[128:129]
        head_rows[seq, 1:2] = edge_ref[0:1]
        head_rows[seq, 2:8] = jnp.zeros((6, D), F32)
        states.start()

    def key_value_grads():
        weight_grad(kv_piece, slice(D, 2 * D), slice(0, 128))
        weight_grad(kv_piece, slice(2 * D, 3 * D), slice(128, 256))
        for_kv.start()

    def slot_grads():
        weight_grad(f_piece, slice(3 * D, 4 * D), slice(0, 128), True)
        for_f.start()

    def last():
        small_two.start()
        fr.forward()
        for_kv.forward()
        for_f.advance(2)
        small_two.second()
        for piece in (ff, fr, for_q):
            piece.finish()
        states.drain()
        small_two.finish(s2_out)
        for_kv.finish()
        for_f.finish()
        for n in (8 // per - 2, 8 // per - 1):
            give(n).wait()

    def begin():
        met(count)
        ff.start()
        small_one.start()

    schedule = {
        0: [begin],
        1: [fr.start],
        3: [lambda: ff.advance(0), small_one.second],
        5: [lambda: fr.advance(0)],
        QUERY - 1: [send_states],
        QUERY + 7: [turn],
        COLUMN: [lambda: ff.advance(1), lambda: fr.advance(1)],
        COLUMN + 1: [lambda: for_q.advance(0)],
        COLUMN + 5: [lambda: fr.advance(2)],
        COLUMN + 6: [lambda: ff.advance(2)],
        COLUMN + 7: [key_value_grads, lambda: for_q.advance(1)],
        SLOT + 1: [lambda: for_kv.advance(0), lambda: for_q.advance(2)],
        SLOT + 4: [lambda: ff.advance(3)],
        SLOT + 6: [lambda: for_kv.advance(1), lambda: fr.advance(3)],
        SLOT + 7: [slot_grads, lambda: for_q.advance(3)],
        INPUT + 1: [lambda: for_f.advance(0), lambda: for_kv.advance(2)],
        INPUT + 3: [ff.forward, for_q.forward, lambda: small_one.finish(s1_out)],
        INPUT + 5: [lambda: for_f.advance(1), lambda: for_kv.advance(3)],
        INPUT + 7: [last],
    }

    @pl.when(step < QUERY // per)
    def _():
        for copy in fetch_scores(step):
            copy.wait()

    @pl.loop(0, per)
    def _(u):
        at_chunk = step * per + u

        @pl.when(at_chunk < QUERY)
        def _():
            n, here, block, col, row = chunk(u, 0)
            kept_scores = [scores.at[lax.rem(step, 2), k, block] for k in range(3)]

            def aside():
                unit, _ = norm_parts(x_ref[block].astype(F32))
                h_turned[:, here] = (unit * small_ref[0:1] + small_ref[1:2]).astype(BF16).T

            row_body(
                n, qkvf_ref.at[block], do_ref.at[block], *kept_scores, kept_ref.at[pl.ds(u, 1)],
                col, row, edge_ref,
                reading.at[here], numer.at[here], total.at[here], head, aside,
            )

        @pl.when((at_chunk >= QUERY) & (at_chunk < COLUMN))
        def _():
            n, here, block, col, row = chunk(u, QUERY)
            query_body(
                n, qkvf_ref.at[block], kept_ref.at[pl.ds(u, 1)], col, row, edge_ref,
                numer.at[here], d_all.at[here, 0:D],
            )

        @pl.when((at_chunk >= COLUMN) & (at_chunk < SLOT))
        def _():
            n, here, block, col, row = chunk(u, COLUMN, True)
            column_body(
                n, qkvf_ref.at[block], do_ref.at[block], reading.at[here], numer.at[here],
                total.at[here], col, row, edge_ref, state, snap, snap_rows, d_all.at[here],
            )

        @pl.when((at_chunk >= SLOT) & (at_chunk < INPUT))
        def _():
            n, here, block, col, row = chunk(u, SLOT, True)
            slot_body(
                n, qkvf_ref.at[block], do_ref.at[block], reading.at[here], numer.at[here],
                total.at[here], col, row, edge_ref, snap, snap_rows, d_all.at[here],
            )

        @pl.when((at_chunk >= INPUT) & (u == 0))
        def _():
            nth = step - INPUT // per

            @pl.when(nth >= 2)
            def _():
                give(nth - 2).wait()

            @pl.when(nth == 0)
            def _():
                fetch().wait()

            size = xs_ref.shape[0]
            here = pl.ds(pl.multiple_of(nth * size, size), size)
            grad = dot_nt(d_all[here], w_held[...])
            unit, scale = norm_parts(xs_ref[...].astype(F32))
            last_small[0:1] += jnp.sum(grad * unit, axis=0, keepdims=True)
            last_small[1:2] += jnp.sum(grad, axis=0, keepdims=True)
            gi_held[lax.rem(nth, 2)] = dy_ref[...] + norm_back(unit, scale, small_ref[0:1], grad)
            give(nth).start()

        for when, actions in schedule.items():

            @pl.when(at_chunk == when)
            def _(actions=actions):
                for action in actions:
                    action()

    @pl.when(step + 2 < QUERY // per)
    def _():
        for copy in fetch_scores(step + 2):
            copy.start()


def back(
    count, tokens, qkvf, do, probs, score, inverse, kept, dy, doc_ids, small, w_all, ffg, ffr, ffs
):
    rows = tokens.shape[0]
    part, link = ffg.shape[1], ffg.dtype
    per = 2 if link == BF16 else 1
    size = per * C
    blocks = 8 // per
    once = lambda a: pl.BlockSpec(a.shape, lambda i: (0,) * a.ndim)
    anywhere = pl.BlockSpec(memory_space=pl.ANY)
    vmem, dma = pltpu.VMEM, pltpu.SemaphoreType.DMA

    def early(i):
        return jnp.minimum(i, blocks - 1)

    def twice(i):
        return jnp.where(i < blocks, i, jnp.clip(i - blocks, 0, blocks - 1))

    def turned(i):
        return blocks - 1 - lax.rem(jnp.clip(i - 2 * blocks, 0, 2 * blocks - 1), blocks)

    def always(i):
        return jnp.where(i < 2 * blocks, twice(i), turned(i))

    def both(i):
        return jnp.where(i < blocks, i, turned(i))

    late = lambda i: (jnp.maximum(i - 4 * blocks, 0), 0)
    tall = pl.BlockSpec((size, D), late)
    some = lambda lanes, order: pl.BlockSpec((size, lanes), lambda i: (order(i), 0))
    slabs = 4 * count
    return pl.pallas_call(
        functools.partial(back_kernel, count, per),
        grid=(5 * blocks,),
        in_specs=[some(D, early), tall, some(4 * D, always), some(D, both)]
        + [anywhere] * 3
        + [pl.BlockSpec((per, 128, D), lambda i: (twice(i), 0, 0)), tall]
        + [once(doc_ids), once(small), anywhere, anywhere, anywhere, once(ffs)],
        out_specs=[anywhere] * 6 + [whole(16, D), whole(8, 128)],
        out_shape=[
            shape_of((rows, D), F32),
            shape_of((4, part, 640), F32),
            shape_of((4, part, D), F32),
            shape_of((4, part, 128), F32),
            shape_of((4, part, 256), F32),
            shape_of((4, part, 128), F32),
            shape_of((16, D), F32),
            shape_of((8, 128), F32),
        ],
        scratch_shapes=[
            vmem((2, size, D), F32),
            dma((2,)),
            vmem((2, 3, size, D), F32),
            dma((2, 3)),
            vmem((rows, 4 * D), BF16),
            vmem((D, rows), BF16),
            vmem((rows, D), BF16),
            vmem((rows, D), F32),
            vmem((rows, D), F32),
            vmem((rows, 128), F32),
            vmem((16, D), F32),
            vmem((136, D), F32),
            vmem((136, D), F32),
            vmem((4, 128, D), link),
            vmem((4, 8, D), F32),
            vmem((8, 128, D), BF16),
            vmem((8, D), F32),
            vmem(w_all.shape, BF16),
            dma,
            vmem((slabs, part, 128), link),
            vmem((slabs, part, 256), link),
            vmem((slabs, part, 128), link),
            vmem((8, D), F32),
        ]
        + scatter_scratch(count, part, 640, link, OVER_X, True)
        + scatter_scratch(count, part, D, link, OVER_Y, True)
        + scatter_scratch(count, part, 128, link, OVER_X, False)
        + scatter_scratch(count, part, 256, link, OVER_X, False)
        + scatter_scratch(count, part, 128, link, SHORT, False)
        + small_scratch(count, 16, D)
        + small_scratch(count, 8, 128)
        + [dma((3, 2)), dma((3, 2))],
        compiler_params=pltpu.CompilerParams(
            vmem_limit_bytes=(62 if link == BF16 else 63) * MIB, collective_id=2, has_side_effects=True
        ),
        name="back",
    )(
        tokens, tokens, qkvf, do, probs, score, inverse, kept, dy, doc_ids, small, w_all, ffg, ffr,
        ffs,
    )


def finish_kernel(
    count, part, y_ref, gi_ref, ff_ref, fr_ref, q_ref, kv_ref, f_ref, s1_ref, s2_ref, y_out, gi_out,
    *rest,
):
    at = lax.axis_index("fsdp")
    *outs, held_y, held, sems = rest

    def move(n, out):
        source, through, target, here = gi_ref, held, gi_out, pl.ds(n * 512, 512)
        if n >= 4:
            source, through, target, here = y_ref, held_y, y_out, pl.ds((n - 4) * 1024, 1024)
        if out:
            return pltpu.make_async_copy(through.at[here], target.at[here], sems.at[1, n])
        return pltpu.make_async_copy(source.at[here], through.at[here], sems.at[0, n])

    def pick(row, size):
        out = row(0, size)
        for f in range(1, count):
            out = jnp.where(at == f, row(f * size, size), out)
        return out

    def bias(start, size):
        r = start // D
        return s1_ref[8 + r : 9 + r, start - r * D : start - r * D + size]

    def row_of_sums(ref, n):
        return lambda start, size: ref[
            n : n + 1, start % ref.shape[1] : start % ref.shape[1] + size
        ]

    for n in range(6):
        move(n, False).start()
    for n in range(4):
        lanes = slice(n * 128, (n + 1) * 128)
        outs[0][:, lanes] = q_ref[n]
        outs[1][:, lanes] = kv_ref[n, :, 0:128]
        outs[2][:, lanes] = kv_ref[n, :, 128:256]
        outs[3][:, lanes] = f_ref[n]
        outs[4][:, lanes] = ff_ref[n, :, 512:640]
        outs[5][:, n * 512 : (n + 1) * 512] = ff_ref[n, :, 0:512]
        for j in range(4):
            outs[6][j * part : (j + 1) * part, lanes] = fr_ref[n, :, j * 128 : (j + 1) * 128]
    for n in range(6):
        move(n, False).wait()
        move(n, True).start()
    outs[7][...] = pick(row_of_sums(s2_ref, 0), part)
    outs[8][...] = pick(row_of_sums(s2_ref, 1), part)
    outs[9][...] = pick(row_of_sums(s1_ref, 2), part)
    outs[10][...] = pick(row_of_sums(s1_ref, 3), part)
    outs[11][...] = pick(bias, 4 * part)
    outs[12][...] = pick(row_of_sums(s1_ref, 4), part)
    for n in range(6):
        move(n, True).wait()


def finish(count, part, out, grad_input, *sums):
    once = lambda shape: pl.BlockSpec(shape, lambda: (0,) * len(shape))
    anywhere = pl.BlockSpec(memory_space=pl.ANY)
    shapes = [(part, D)] * 5 + [(part, FF), (4 * part, D)]
    shapes += [(1, part)] * 4 + [(1, 4 * part), (1, part)]
    return pl.pallas_call(
        functools.partial(finish_kernel, count, part),
        in_specs=[anywhere] * 2 + [once(a.shape) for a in sums],
        out_specs=[anywhere] * 2 + [once(s) for s in shapes],
        out_shape=[shape_of(out.shape, BF16)]
        + [shape_of(s, F32) for s in (grad_input.shape, *shapes)],
        scratch_shapes=[
            pltpu.VMEM(out.shape, BF16),
            pltpu.VMEM(grad_input.shape, F32),
            pltpu.SemaphoreType.DMA((2, 6)),
        ],
        compiler_params=PARAMS,
        name="finish",
    )(out, grad_input, *sums)


def rows_of(lanes, order=lambda i: i):
    return pl.BlockSpec((C, lanes), lambda i: (order(i), 0))


def whole(*shape):
    return pl.BlockSpec(shape, lambda i: (0,) * len(shape))


def row_of(order=lambda i: i):
    return pl.BlockSpec((1, C), lambda i: (0, order(i)))


def shape_of(shape, kind):
    return jax.ShapeDtypeStruct(shape, kind)


PARAMS = pltpu.CompilerParams(vmem_limit_bytes=62 * MIB)


def on_device(
    tokens, doc_ids, w_query, w_key, w_value, w_slots, w_output, w_hidden, w_return,
    gain_first, shift_first, gain_second, shift_second, bias_hidden, bias_return, cotangent,
):
    rows = tokens.shape[0]
    count = lax.axis_size("fsdp")
    part = gain_first.shape[0]
    flat = lambda a: a.reshape(1, a.shape[0])
    found = front(
        count, tokens, doc_ids,
        (w_query, w_key, w_value, w_slots, w_output, w_hidden, w_return),
        [flat(a) for a in (gain_first, shift_first, gain_second, shift_second, bias_return)],
        flat(bias_hidden), cotangent,
    )
    grad_input, *sums = back(
        count, tokens, *(found[name] for name in ("qkvf_out", "do", "p", "s", "z", "kept", "dy")),
        doc_ids, found["vec"], found["w_out"].reshape(D, 4 * D).astype(BF16),
        found["pack"].reshape(-1, part, 640), found["pack_r"].reshape(-1, part, D), found["gsmall"],
    )
    out, grad_input, *grads = finish(count, part, found["y"], grad_input, *sums)
    return (out, grad_input, *grads[:7], *(a.reshape(-1) for a in grads[7:]))


def solution(mesh):
    tall, flat, one = P(("fsdp", "seq"), None), P("fsdp", None), P("fsdp")
    return jax.shard_map(
        on_device,
        mesh=mesh,
        in_specs=(tall, P("fsdp", "seq")) + (flat,) * 7 + (one,) * 6 + (tall,),
        out_specs=(tall, tall) + (flat,) * 7 + (one,) * 6,
        check_vma=False,
    )
```

```python
import functools
import types

import jax
import jax.numpy as jnp
from jax import lax
from jax.experimental import pallas as pl
from jax.experimental.pallas import tpu as pltpu
from jax.sharding import PartitionSpec as P

D = 512
H = 8
M = 64
FF = 2048
C = 256
GROUP = 256
EPS = 1e-05
SCALE = 0.125
F32 = jnp.float32
BF16 = jnp.bfloat16
FEED_ROWS = 512
FEED_LANES = 256
FRONT = 4
MIB = 1024 * 1024


def dot(a, b):
    return lax.dot_general(a, b, (((1,), (0,)), ((), ())), preferred_element_type=F32)


def dot_nt(a, b):
    return lax.dot_general(a, b, (((1,), (1,)), ((), ())), preferred_element_type=F32)


def dot_tn(a, b):
    return lax.dot_general(a, b, (((0,), (0,)), ((), ())), preferred_element_type=F32)


def lane_heads(rows, lanes):
    return lax.broadcasted_iota(jnp.int32, (rows, lanes), 1) // M


def stacked(values):
    heads = lane_heads(C, GROUP)
    zero = jnp.zeros_like(values)
    return jnp.concatenate([jnp.where(heads == h, values, zero) for h in range(4)], axis=0)


def select(values):
    heads = lane_heads(C, GROUP)
    out = values[3 * C :]
    for h in (2, 1, 0):
        out = jnp.where(heads == h, values[h * C : (h + 1) * C], out)
    return out


def masked(values, mask):
    return jnp.concatenate(
        [values[h * C : (h + 1) * C].astype(BF16) * mask for h in range(4)], axis=0
    )


def expand(compact):
    rows = lax.broadcasted_iota(jnp.int32, (GROUP, GROUP), 0) // M
    full = jnp.concatenate([compact] * 4, axis=0)
    return jnp.where(rows == lane_heads(GROUP, GROUP), full, jnp.zeros_like(full))


def compacted(full):
    heads = lane_heads(M, GROUP)
    out = full[3 * M :]
    for h in (2, 1, 0):
        out = jnp.where(heads == h, full[h * M : (h + 1) * M], out)
    return out


def split(values):
    high = values.astype(BF16)
    return high, (values - high.astype(F32)).astype(BF16)


def ones_block():
    rows = lax.broadcasted_iota(jnp.int32, (GROUP, GROUP), 0) // M
    return (rows == lane_heads(GROUP, GROUP)).astype(BF16)


def head_sums(values):
    high, low = split(values)
    ones = ones_block()
    return dot(high, ones) + dot(low, ones)


def head_max(values):
    left = lane_heads(C, 128) == 0
    out = []
    for p in range(2):
        pair = values[:, p * 128 : (p + 1) * 128]
        one = jnp.max(jnp.where(left, pair, -jnp.inf), axis=1, keepdims=True)
        two = jnp.max(jnp.where(left, -jnp.inf, pair), axis=1, keepdims=True)
        out.append(jnp.where(left, one, two))
    return jnp.concatenate(out, axis=1)


def wide(values, times):
    return jnp.concatenate([values] * times, axis=1)


def visible(doc_col, doc_row):
    same = wide(doc_col, 2) == doc_row
    here = lax.broadcasted_iota(jnp.int32, (C, C), 0)
    there = lax.broadcasted_iota(jnp.int32, (C, C), 1)
    return jnp.where(same & (here >= there), 1.0, 0.0).astype(BF16)


def visible_back(doc_col, doc_row):
    same = wide(doc_col, 2) == doc_row
    here = lax.broadcasted_iota(jnp.int32, (C, C), 0)
    there = lax.broadcasted_iota(jnp.int32, (C, C), 1)
    return jnp.where(same & (there >= here), 1.0, 0.0).astype(BF16)


def flag(doc_col, doc):
    return jnp.where(doc_col == doc[:, :128], 1.0, 0.0)


def norm_parts(values):
    centre = jnp.mean(values, axis=-1, keepdims=True)
    centred = values - centre
    spread = jnp.mean(centred * centred, axis=-1, keepdims=True)
    scale = lax.rsqrt(spread + EPS)
    return centred * scale, scale


def norm_back(unit, scale, gain, grad):
    inner = grad * gain
    return scale * (
        inner
        - jnp.mean(inner, axis=-1, keepdims=True)
        - unit * jnp.mean(inner * unit, axis=-1, keepdims=True)
    )


def groups(values):
    return values[:, :GROUP], values[:, GROUP:]


def state_terms(slots, left, right):
    one, two = [], []
    for g in range(2):
        lanes = slice(g * GROUP, (g + 1) * GROUP)
        both = dot_tn(slots[:, lanes], jnp.concatenate([left[:, lanes], right[:, lanes]], axis=1))
        one.append(compacted(both[:, :GROUP]))
        two.append(compacted(both[:, GROUP:]))
    return jnp.concatenate(one, axis=1), jnp.concatenate(two, axis=1)


def lanes_of(g):
    return slice(g * GROUP, (g + 1) * GROUP)


def part_of(ref, part, g):
    return ref[:, part * D + g * GROUP : part * D + (g + 1) * GROUP]


def affinities(qkvf_ref, g, vis):
    return masked(dot_nt(stacked(part_of(qkvf_ref, 0, g)), part_of(qkvf_ref, 1, g)), vis)


def attend_body(
    n, qkvf_ref, slots, vis, affine_ref, col, edge_ref, state, o_ref, p_ref, s_ref, z_ref, kept_ref
):
    kept_ref[0] = state[0:128]
    first = edge_ref[pl.ds(0, 1)]
    before = edge_ref[pl.ds(8 + jnp.maximum(n - 1, 0), 1)]
    last = jnp.where(n == 0, first, before)
    newest = edge_ref[pl.ds(8 + n, 1)]
    carried = wide(flag(col, last), 2)
    norm = dot(vis, slots)
    key_states = [expand(state[0:64, lanes_of(g)]).astype(BF16) for g in range(2)]
    value_states = [expand(state[64:128, lanes_of(g)]).astype(BF16) for g in range(2)]
    norm_state = state[128:129]

    def scores(g, affinity):
        lanes = lanes_of(g)
        numer = select(dot(affinity, slots[:, lanes]))
        numer = numer + carried * dot_nt(part_of(qkvf_ref, 0, g), key_states[g])
        inverse = 1.0 / (norm[:, lanes] + carried * norm_state[:, lanes])
        return numer * inverse * SCALE, inverse

    def grow(score):
        return jnp.exp(score - head_max(score))

    def read(g, score, inverse, grown):
        lanes = lanes_of(g)
        probs = grown / head_sums(grown)
        p_ref[:, lanes] = probs
        s_ref[:, lanes] = score
        z_ref[:, lanes] = inverse
        return (probs * inverse).astype(BF16)

    def mixing(g, reading):
        return masked(dot_nt(stacked(reading), slots[:, lanes_of(g)]), vis)

    def mixed(g, reading, mix):
        out = select(dot(mix, part_of(qkvf_ref, 2, g))) + carried * dot(reading, value_states[g])
        o_ref[:, lanes_of(g)] = out.astype(BF16)

    score, inverse = scores(0, affine_ref[...])
    affinity = affinities(qkvf_ref, 1, vis)
    grown = grow(score)
    score_two, inverse_two = scores(1, affinity)
    reading = read(0, score, inverse, grown)
    tail = wide(flag(col, newest), 4).astype(BF16) * slots
    new_keys, new_values = state_terms(tail, qkvf_ref[:, D : 2 * D], qkvf_ref[:, 2 * D : 3 * D])
    same = jnp.where(last == newest, 1.0, 0.0)
    state[0:64] = same * state[0:64] + new_keys
    state[64:128] = same * state[64:128] + new_values
    state[128:129] = same * state[128:129] + jnp.sum(tail.astype(F32), axis=0, keepdims=True)
    grown = grow(score_two)
    mix = mixing(0, reading)
    reading_two = read(1, score_two, inverse_two, grown)
    mixed(0, reading, mix)
    mix = mixing(1, reading_two)
    mixed(1, reading_two, mix)


MESH_ID = pl.DeviceIdType.MESH


def places():
    seq, at = lax.axis_index("seq"), lax.axis_index("fsdp")
    core = lax.rem(seq, 2)
    return seq, at, seq + 1 - 2 * core, lax.rem(seq + 2, 4)


def push(src, dst, send, recv, **device):
    return pltpu.make_async_remote_copy(
        src_ref=src, dst_ref=dst, send_sem=send, recv_sem=recv,
        device_id=device, device_id_type=MESH_ID,
    )


def greet(count):
    seq, at, _, _ = places()
    barrier = pltpu.get_barrier_semaphore()
    for k in range(1, count):
        pl.semaphore_signal(barrier, inc=1, device_id={"fsdp": at ^ k}, device_id_type=MESH_ID)
    for k in range(1, 4):
        pl.semaphore_signal(barrier, inc=1, device_id={"seq": seq ^ k}, device_id_type=MESH_ID)


def met(count):
    pl.semaphore_wait(pltpu.get_barrier_semaphore(), count - 1 + 3)


class Gather:
    def __init__(self, count, mine, held, base, width, four, sems):
        self.count, self.mine, self.held, self.four = count, mine, held, four
        self.far, self.near, self.core, self.chip, self.onward, self.local = sems
        self.seq, self.at, self.sibling, self.beside = places()
        self.base, self.share = base, width // (4 if four else 2)
        self.evens = range(0, count, 2)

    def lanes(self, seq):
        place = seq if self.four else lax.rem(seq, 2)
        return pl.ds(pl.multiple_of(self.base + place * self.share, 128), self.share)

    def part(self, k, seq):
        return self.held.at[self.at ^ k, :, self.lanes(seq)]

    def source(self, k):
        if k:
            return self.part(k, self.seq)
        return self.mine.at[:, self.lanes(self.seq)]

    def own(self):
        return pltpu.make_async_copy(self.source(0), self.part(0, self.seq), self.local)

    def over(self, sems, k, **device):
        return push(self.source(k), self.part(k, self.seq), sems[0].at[k], sems[1].at[k], **device)

    def come(self, sems, k, owner):
        here = self.part(owner, self.seq)
        return push(here, here, sems[0].at[k], sems[1].at[k], seq=self.sibling)

    def far_out(self, k):
        return push(
            self.source(0), self.part(0, self.seq), self.far[0].at[k], self.far[1].at[k],
            fsdp=self.at ^ k,
        )

    def far_in(self, k):
        return self.come(self.far, k, k)

    def near_out(self, k):
        return self.over(self.near, k, fsdp=self.at ^ 1)

    def near_in(self, k):
        return self.come(self.near, k, k ^ 1)

    def start(self):
        self.own().start()
        for k in self.evens[1:]:
            self.far_out(k).start()
        self.near_out(0).start()

    def second(self):
        for k in self.evens[1:]:
            self.far_in(k).wait_recv()
            self.near_out(k).start()

    def hop(self, sems, source, target):
        here = self.held.at[:, :, self.lanes(source)]
        return push(here, here, sems[0].at[0], sems[1].at[0], seq=target)

    def third(self):
        self.own().wait()
        for k in self.evens:
            self.near_in(k).wait_recv()
        self.hop(self.core, self.seq, self.sibling).start()
        if self.four:
            self.hop(self.chip, self.seq, self.beside).start()

    def fourth(self):
        self.hop(self.chip, self.beside, self.beside).wait_recv()
        self.hop(self.onward, self.beside, self.sibling).start()

    def finish(self):
        self.hop(self.core, self.sibling, self.sibling).wait_recv()
        self.hop(self.core, self.seq, self.sibling).wait_send()
        if self.four:
            self.hop(self.onward, lax.rem(self.sibling + 2, 4), self.sibling).wait_recv()
            self.hop(self.chip, self.seq, self.beside).wait_send()
            self.hop(self.onward, self.beside, self.sibling).wait_send()

    def core_out(self, k):
        return self.over(self.core, k, seq=self.sibling)

    def core_in(self, k):
        here = self.part(k, self.sibling)
        return push(here, here, self.core[0].at[k], self.core[1].at[k], seq=self.sibling)

    def at_once(self, between):
        self.start()
        self.core_out(0).start()
        for k in self.evens[1:]:
            self.far_in(k).wait_recv()
            self.near_out(k).start()
            self.core_out(k).start()
        between()
        for k in self.evens:
            self.near_in(k).wait_recv()
            self.core_out(k ^ 1).start()
        self.own().wait()
        for k in range(self.count):
            self.core_in(k).wait_recv()

    def drain(self, each=False):
        for k in self.evens:
            self.near_out(k).wait_send()
            if k:
                self.far_out(k).wait_send()
        if each:
            for k in range(self.count):
                self.core_out(k).wait_send()


def gather_sems(count, each):
    n = count if each else 1
    pair = lambda size: [pltpu.SemaphoreType.DMA((size,)), pltpu.SemaphoreType.DMA((size,))]
    return pair(count) + pair(count) + pair(n) + pair(1) + pair(1) + [pltpu.SemaphoreType.DMA]


def bundle(refs):
    return [(refs[2 * n], refs[2 * n + 1]) for n in range(5)] + [refs[10]]


class States:
    def __init__(self, big, small, sems):
        self.refs, self.sems = (big, small), sems
        self.seq, _, self.sibling, self.beside = places()

    def hop(self, n, source, target):
        out = []
        for m, ref in enumerate(self.refs):
            here = ref.at[source]
            out.append(push(here, here, self.sems[0].at[n, m], self.sems[1].at[n, m], seq=target))
        return out

    def start(self):
        for copy in self.hop(0, self.seq, self.sibling) + self.hop(1, self.seq, self.beside):
            copy.start()

    def forward(self):
        for copy in self.hop(1, self.beside, self.beside):
            copy.wait_recv()
        for copy in self.hop(2, self.beside, self.sibling):
            copy.start()

    def finish(self):
        for copy in self.hop(0, self.sibling, self.sibling):
            copy.wait_recv()
        for copy in self.hop(2, lax.rem(self.sibling + 2, 4), self.sibling):
            copy.wait_recv()

    def drain(self):
        for copy in (
            self.hop(0, self.seq, self.sibling)
            + self.hop(1, self.seq, self.beside)
            + self.hop(2, self.beside, self.sibling)
        ):
            copy.wait_send()


def doc_parts(doc_ref, col_ref, edge_ref):
    here = lax.broadcasted_iota(jnp.int32, (C, C), 0)
    there = lax.broadcasted_iota(jnp.int32, (C, C), 1)
    eye = jnp.where(here == there, 1.0, 0.0).astype(BF16)
    for n in range(doc_ref.shape[1] // C):
        row = doc_ref[:, n * C : (n + 1) * C].astype(F32)
        col_ref[n * C : (n + 1) * C] = dot_nt(eye, jnp.broadcast_to(row, (128, C)).astype(BF16))
        low = jnp.min(row, axis=1, keepdims=True)
        high = jnp.max(row, axis=1, keepdims=True)
        edge_ref[n : n + 1] = jnp.broadcast_to(low, (1, D))
        edge_ref[n + 8 : n + 9] = jnp.broadcast_to(high, (1, D))


def spread_small(vec_refs, bias_ref, out_ref):
    def repeat(values):
        width = values.shape[1]
        rows = lax.broadcasted_iota(jnp.int32, (width, 128), 0)
        lanes = lax.broadcasted_iota(jnp.int32, (width, 128), 1)
        pick = jnp.where(lax.rem(lanes, width) == rows, 1.0, 0.0).astype(BF16)
        return dot(jnp.broadcast_to(values, (8, width)).astype(BF16), pick)[0:1]

    out_ref[...] = jnp.zeros_like(out_ref)
    for n, ref in enumerate(vec_refs):
        out_ref[n : n + 1] = repeat(ref[...])
    for b in range(max(bias_ref.shape[1] // 128, 1)):
        out_ref[5 + b : 6 + b] = repeat(bias_ref[:, b * 128 : (b + 1) * 128])


def join_small(count, part, gathered, vec_ref, bias_ref):
    lanes = lax.broadcasted_iota(jnp.int32, (8, D), 1)
    total = jnp.zeros((8, D), F32)
    for f in range(count):
        total = jnp.where(lanes // part == f, wide(gathered[f], 4), total)
    vec_ref[...] = total
    size = 4 * part
    for r in range(4):
        at = lanes[0:1] + r * D
        row = jnp.zeros((1, D), F32)
        for f in range(r * D // size, -(-(r + 1) * D // size)):
            for b in range(max(size // 128, 1)):
                use = (at // size == f) & (lax.rem(at, size) // 128 == b)
                row = jnp.where(use, wide(gathered[f, 5 + b : 6 + b], 4), row)
        bias_ref[0:1, r * D : (r + 1) * D] = row


ROOT = 0.7978845608028654
CUBE = 0.044715


def gelu_both(u):
    square = u * u
    bent = jnp.tanh(ROOT * u * (1.0 + CUBE * square))
    half = 0.5 * (1.0 + bent)
    slope = half + 0.5 * u * (1.0 - bent * bent) * (ROOT * (1.0 + 3.0 * CUBE * square))
    return u * half, slope


def feed_start(values, attended, vec_ref, w_out):
    middle = values.astype(F32) + dot(attended, w_out())
    unit, _ = norm_parts(middle)
    return middle, (unit * vec_ref[2:3] + vec_ref[3:4]).astype(BF16)


def feed_body(
    middle, hidden, attended, cot, vec_ref, bias_ref, w_out, w_hidden, w_return,
    y_ref, dy_ref, do_ref, gsmall_ref, gwo_ref, gwh_ref, gwr_ref,
):
    out = middle + vec_ref[4:5]
    grad_hidden = jnp.zeros_like(middle)
    cot32 = cot.astype(F32)
    tiles = FF // FEED_LANES

    def into(j):
        cols = slice(j * FEED_LANES, (j + 1) * FEED_LANES)
        inner = dot(hidden, w_hidden(j)) + bias_ref[0:1, cols]
        return inner, dot_nt(cot, w_return(j))

    def bend(inner, grad):
        gated, slope = gelu_both(inner)
        return gated.astype(BF16), (grad * slope).astype(BF16)

    def outof(j, active, low):
        cols = slice(j * FEED_LANES, (j + 1) * FEED_LANES)
        there = slice(cols.start % D, cols.start % D + FEED_LANES)
        row = 8 + cols.start // D
        gwr_ref[:, cols] += dot_tn(cot, active)
        gsmall_ref[row : row + 1, there] += jnp.sum(low.astype(F32), axis=0, keepdims=True)
        gwh_ref[:, cols] += dot_tn(hidden, low)
        return dot(active, w_return(j)), dot_nt(low, w_hidden(j))

    coming = into(0)
    for j in range(tiles):
        bent = bend(*coming)
        if j + 1 < tiles:
            coming = into(j + 1)
        to_out, to_hidden = outof(j, *bent)
        out = out + to_out
        grad_hidden = grad_hidden + to_hidden
        if j == tiles // 2:
            unit, scale = norm_parts(middle)
    y_ref[...] = out.astype(BF16)
    gsmall_ref[2:3] += jnp.sum(grad_hidden * unit, axis=0, keepdims=True)
    gsmall_ref[3:4] += jnp.sum(grad_hidden, axis=0, keepdims=True)
    gsmall_ref[4:5] += jnp.sum(cot32, axis=0, keepdims=True)
    grad_middle = cot32 + norm_back(unit, scale, vec_ref[2:3], grad_hidden)
    dy_ref[...] = grad_middle
    branch = grad_middle.astype(BF16)
    gwo_ref[...] += dot_tn(attended, branch)
    do_ref[...] = dot_nt(branch, w_out()).astype(BF16)


def pack_grads(count, part, gwo_ref, gwh_ref, gwr_ref, put):
    half = count // 2
    for q in range(4):
        x, c = q // 2, q % 2
        hidden_part = gwh_ref[:, q * 512 : (q + 1) * 512].reshape(half, 2, part, 512)
        out_part = gwo_ref[:, q * 128 : (q + 1) * 128].reshape(half, 2, part, 128)
        turned = gwr_ref[q * 128 : (q + 1) * 128].T.reshape(half, 2, 4, part, 128)
        for y in range(2):
            over_x, over_y = ((c * 2 + x) * 2 + y) * half, ((c * 2 + y) * 2 + x) * half
            put(0, over_x, slice(0, 512), hidden_part[:, y])
            put(1, over_y, slice(512, 640), out_part[:, y])
            for j in range(4):
                put(1, over_y, slice(j * 128, (j + 1) * 128), turned[:, y, j])


def feed_kernel(
    x_ref, o_ref, g_ref, small_ref, bias_ref, wo_ref, wh_ref, wr_ref,
    y_ref, dy_ref, do_ref, pack_ref, pack_r_ref, gsmall_ref, gwo_ref, gwh_ref, gwr_ref,
):
    step = pl.program_id(0)
    count, part = wh_ref.shape[0], wh_ref.shape[1]

    @pl.when(step == 0)
    def _():
        for ref in (gwo_ref, gwh_ref, gwr_ref, gsmall_ref):
            ref[...] = jnp.zeros_like(ref)

    views = weight_views(wo_ref, wh_ref, wr_ref)
    feed_body(
        *feed_start(x_ref[...], o_ref[...], small_ref, views[0]), o_ref[...], g_ref[...], small_ref,
        bias_ref, *views, y_ref, dy_ref, do_ref, gsmall_ref, gwo_ref, gwh_ref, gwr_ref,
    )

    @pl.when(step == pl.num_programs(0) - 1)
    def _():
        def put(which, slab, lanes, values):
            ref = (pack_ref, pack_r_ref)[which]
            n = values.shape[0] * part
            ref[slab * part : slab * part + n, lanes] = values.reshape(n, -1).astype(ref.dtype)

        pack_grads(count, part, gwo_ref, gwh_ref, gwr_ref, put)


def weight_views(wo_ref, wh_ref, wr_ref):
    def w_out():
        return wo_ref[...].reshape(D, D).astype(BF16)

    def w_hidden(j):
        cols = slice(j * FEED_LANES, (j + 1) * FEED_LANES)
        return wh_ref[:, :, cols].reshape(D, FEED_LANES).astype(BF16)

    def w_return(j):
        n = FEED_LANES // wr_ref.shape[1]
        return wr_ref[j * n : (j + 1) * n].reshape(FEED_LANES, D).astype(BF16)

    return w_out, w_hidden, w_return


def front_kernel(count, joined, names, *refs):
    r = types.SimpleNamespace(**dict(zip(names, refs)))
    sems = refs[len(names) :]
    x_ref, doc_ref, vec_out, bias_out = r.x, r.doc, r.vec, r.bias
    qkvf, hidden, w_all, mine = r.qkvf, r.hidden, r.w_all, r.mine
    mine_o, mine_h, mine_r, spread, smalls = r.mine_o, r.mine_h, r.mine_r, r.spread, r.smalls
    col_ref, edge_ref, state, tail = r.col, r.edge, r.state, r.tail
    tails, tail_rows = r.tails, r.tail_rows
    slots = r.o if joined else r.slots
    step = pl.program_id(0)
    seq, at, _, _ = places()
    link = mine.dtype
    groups_of_sems = []
    for _ in range(5):
        groups_of_sems.append(bundle(sems[:11]))
        sems = sems[11:]
    small_send, small_recv, state_send, state_recv, out_sem, stage_sem, fed_sem = sems
    main = Gather(count, mine, w_all, D, 3 * D, False, groups_of_sems[0])
    q_piece = Gather(count, mine, w_all, 0, D, False, groups_of_sems[1])
    o_piece = Gather(count, mine_o, r.wo_all, 0, D, True, groups_of_sems[2])
    h_piece = Gather(count, mine_h, r.wh_all, 0, FF, True, groups_of_sems[3])
    r_piece = Gather(count, mine_r, r.wr_all, 0, D, False, groups_of_sems[4])
    later = (q_piece, o_piece, h_piece, r_piece)
    states = States(tails, tail_rows, (state_send, state_recv))

    def small_copy(k, owner):
        return push(
            spread, smalls.at[owner], small_send.at[k], small_recv.at[k], fsdp=at ^ k
        )

    def save():
        return (
            pltpu.make_async_copy(qkvf, r.qkvf_out, out_sem.at[0]),
            pltpu.make_async_copy(w_all, r.w_out, out_sem.at[1]),
        )

    @pl.when(step == 0)
    def _():
        greet(count)
        for n, ref in enumerate((r.w0, r.w1, r.w2, r.w3)):
            mine[:, n * D : (n + 1) * D] = ref[...].astype(BF16).astype(link)
        spread_small((r.v0, r.v1, r.v2, r.v3, r.v4), r.bias_in, spread)
        doc_parts(doc_ref, col_ref, edge_ref)
        tail[...] = jnp.zeros_like(tail)
        met(count)
        for k in range(1, count):
            small_copy(k, at).start()

        def between():
            mine_o[...] = r.w4[...].astype(BF16).astype(link)
            mine_h[...] = r.w5[...].astype(BF16).astype(link)
            mine_r[...] = r.w6[...].astype(BF16).astype(link)
            smalls[at] = spread[...]
            for k in range(1, count):
                small_copy(k, at ^ k).wait_recv()
            join_small(count, r.v0.shape[1], smalls, vec_out, bias_out)
            q_piece.start()
            o_piece.start()

            @pl.loop(0, 8)
            def _(n):
                here = pl.ds(pl.multiple_of(n * C, C), C)
                unit, _ = norm_parts(x_ref[here].astype(F32))
                hidden[here] = (unit * vec_out[0:1] + vec_out[1:2]).astype(BF16)

        main.at_once(between)
        q_piece.second()
        h_piece.start()

    @pl.when(step < FRONT)
    def _():
        size = 8 // FRONT * C
        here = pl.ds(pl.multiple_of(step * size, size), size)
        weights = w_all[:, :, D:].reshape(D, 3 * D).astype(BF16)
        rows = dot(hidden[here], weights).astype(BF16)
        qkvf[here, D:] = rows
        slots = wide(flag(col_ref[here], edge_ref[15:16]), 4) * jnp.exp(rows[:, 2 * D :].astype(F32))
        slots = slots.astype(BF16)
        keys, values = state_terms(slots, rows[:, 0:D], rows[:, D : 2 * D])
        tail[0:64] += keys
        tail[64:128] += values
        tail[128:129] += jnp.sum(slots.astype(F32), axis=0, keepdims=True)

    @pl.when(step == 1)
    def _():
        o_piece.second()
        r_piece.start()

    @pl.when(step == FRONT - 2)
    def _():
        q_piece.third()

    @pl.when(step == FRONT - 1)
    def _():
        tails[seq] = tail[0:128].astype(link)
        tail_rows[seq, 0:1] = tail[128:129]
        tail_rows[seq, 1:2] = edge_ref[15:16]
        tail_rows[seq, 2:8] = jnp.zeros((6, D), F32)
        states.start()

        @pl.loop(0, 8)
        def _(n):
            here = pl.ds(pl.multiple_of(n * C, C), C)
            slots[here] = jnp.exp(qkvf[here, 3 * D :].astype(F32)).astype(BF16)
            r.seen[n] = visible(col_ref[here], doc_ref[:, here].astype(F32))

        q_piece.finish()
        h_piece.second()

        @pl.loop(0, FRONT)
        def _(n):
            size = 8 // FRONT * C
            here = pl.ds(pl.multiple_of(n * size, size), size)
            weights = w_all[:, :, 0:D].reshape(D, D).astype(BF16)
            qkvf[here, 0:D] = dot(hidden[here], weights).astype(BF16)

        for copy in save():
            copy.start()
        o_piece.third()

        @pl.loop(0, 8)
        def _(n):
            rows = qkvf.at[pl.ds(pl.multiple_of(n * C, C), C)]
            r.affine[n] = affinities(rows, 0, r.seen[n])

        states.forward()
        states.finish()
        first = edge_ref[0:1]
        state[...] = jnp.zeros_like(state)
        for n in range(4):
            use = jnp.where(tail_rows[n, 1:2] == first, 1.0, 0.0) * (n < seq).astype(F32)
            state[0:128] += use * tails[n].astype(F32)
            state[128:129] += use * tail_rows[n, 0:1]
        h_piece.third()

    per = 8 // FRONT

    def kept_copies(n):
        here = pl.ds(pl.multiple_of(n * C, C), C)
        slot = lax.rem(n, 2)
        return [
            pltpu.make_async_copy(r.stage.at[slot, k], out.at[here], stage_sem.at[slot, k])
            for k, out in enumerate((r.p, r.s, r.z))
        ]

    @pl.when((step >= FRONT) & (step < 2 * FRONT))
    def _():
        @pl.loop(0, per, unroll=True)
        def _(u):
            n = (step - FRONT) * per + u
            slot = lax.rem(n, 2)

            @pl.when(n >= 2)
            def _():
                for copy in kept_copies(n - 2):
                    copy.wait()

            here = pl.ds(pl.multiple_of(n * C, C), C)
            block = pl.ds(pl.multiple_of(u * C, C), C)
            attend_body(
                n, qkvf.at[here], slots[here], r.seen[n], r.affine.at[n], col_ref[here], edge_ref, state,
                r.o.at[here if joined else block], *(r.stage.at[slot, k] for k in range(3)),
                r.kept.at[pl.ds(u, 1)],
            )
            for copy in kept_copies(n):
                copy.start()

            @pl.when(n == 0)
            def _():
                o_piece.fourth()

            @pl.when(n == per - 1)
            def _():
                r_piece.second()

            @pl.when(n == 6)
            def _():
                h_piece.fourth()

    @pl.when(step == 2 * FRONT - 1)
    def _():
        r_piece.third()
        o_piece.finish()
        for copy in save():
            copy.wait()

    def complete():
        h_piece.finish()
        r_piece.finish()
        for piece in later:
            piece.drain()
        main.drain(True)
        states.drain()
        for k in range(1, count):
            small_copy(k, at).wait_send()
        for n in (6, 7):
            for copy in kept_copies(n):
                copy.wait()

    if not joined:
        pl.when(step == 2 * FRONT - 1)(complete)
        return

    views = weight_views(r.wo_all, r.wh_all, r.wr_all)

    @pl.when(step == 2 * FRONT - 1)
    def _():
        for ref in (r.gwo, r.gwh, r.gwr, r.gsmall):
            ref[...] = jnp.zeros_like(ref)

        @pl.loop(0, x_ref.shape[0] // FEED_ROWS)
        def _(n):
            here = pl.ds(pl.multiple_of(n * FEED_ROWS, FEED_ROWS), FEED_ROWS)
            r.middle[here], hidden[here] = feed_start(x_ref[here], r.o[here], vec_out, views[0])

        complete()

    fed = step - 2 * FRONT

    def fed_copies(n):
        here = pl.ds(pl.multiple_of(n * FEED_ROWS, FEED_ROWS), FEED_ROWS)
        slot = lax.rem(n, 2)
        pairs = ((r.held_y, r.y), (r.held_dy, r.dy), (r.held_do, r.do))
        return [
            pltpu.make_async_copy(held.at[slot], out.at[here], fed_sem.at[slot, k])
            for k, (held, out) in enumerate(pairs)
        ]

    @pl.when(fed >= 2)
    def _():
        for copy in fed_copies(fed - 2):
            copy.wait()

    @pl.when(fed >= 0)
    def _():
        here = pl.ds(pl.multiple_of(fed * FEED_ROWS, FEED_ROWS), FEED_ROWS)
        slot = lax.rem(fed, 2)
        feed_body(
            r.middle[here], hidden[here], r.o[here], r.g[...], vec_out, bias_out, *views,
            r.held_y.at[slot], r.held_dy.at[slot], r.held_do.at[slot], r.gsmall, r.gwo, r.gwh, r.gwr,
        )
        for copy in fed_copies(fed):
            copy.start()

    @pl.when(step == pl.num_programs(0) - 1)
    def _():
        part = mine.shape[0]

        def put(which, slab, lanes, values):
            n = values.shape[0] * part
            at_lane = D * which + lanes.start
            qkvf[slab * part : slab * part + n, at_lane : at_lane + values.shape[2]] = (
                values.reshape(n, -1).astype(BF16)
            )

        pack_grads(count, part, r.gwo, r.gwh, r.gwr, put)
        copies = [
            pltpu.make_async_copy(qkvf.at[:, 0:D], r.pack, out_sem.at[0]),
            pltpu.make_async_copy(qkvf.at[:, D:1152], r.pack_r, out_sem.at[1]),
        ]
        for copy in copies:
            copy.start()
        last = x_ref.shape[0] // FEED_ROWS - 1
        for copy in (*fed_copies(last - 1), *fed_copies(last), *copies):
            copy.wait()


def front(count, tokens, doc_ids, weights, vectors, bias, cotangent):
    rows = tokens.shape[0]
    part = weights[0].shape[0]
    link = BF16 if part % 16 == 0 else F32
    joined = link == BF16
    per = 8 // FRONT
    once = lambda a: pl.BlockSpec(a.shape, lambda i: (0,) * a.ndim)
    late = lambda i: jnp.clip(i - FRONT, 0, FRONT - 1)
    tall = pl.BlockSpec((per * C, D), lambda i: (late(i), 0))
    fed = pl.BlockSpec((FEED_ROWS, D), lambda i: (jnp.maximum(i - 2 * FRONT, 0), 0))
    anywhere = pl.BlockSpec(memory_space=pl.ANY)
    vmem, dma = pltpu.VMEM, pltpu.SemaphoreType.DMA
    ins = {"x": (tokens, once(tokens)), "doc": (doc_ids, once(doc_ids))}
    ins |= {f"w{n}": (a, once(a)) for n, a in enumerate(weights)}
    ins |= {f"v{n}": (a, once(a)) for n, a in enumerate(vectors)}
    ins["bias_in"] = (bias, once(bias))
    wide_rows, slabs = shape_of((rows, D), F32), 4 * count
    outs = {
        "qkvf_out": (shape_of((rows, 4 * D), BF16), anywhere),
        "p": (wide_rows, anywhere),
        "s": (wide_rows, anywhere),
        "z": (wide_rows, anywhere),
        "kept": (
            shape_of((8, 128, D), F32), pl.BlockSpec((per, 128, D), lambda i: (late(i), 0, 0)),
        ),
        "w_out": (shape_of((count, part, 4 * D), link), anywhere),
        "vec": (shape_of((8, D), F32), whole(8, D)),
    }
    scratch = {
        "qkvf": vmem((rows, 4 * D), BF16),
        "hidden": vmem((rows, D), BF16),
        "w_all": vmem((count, part, 4 * D), link),
        "mine": vmem((part, 4 * D), link),
        "mine_o": vmem((part, D), link),
        "mine_h": vmem((part, FF), link),
        "mine_r": vmem((4 * part, D), link),
        "spread": vmem((8, 128), F32),
        "smalls": vmem((count, 8, 128), F32),
        "col": vmem((rows, 128), F32),
        "edge": vmem((16, D), F32),
        "state": vmem((136, D), F32),
        "tail": vmem((136, D), F32),
        "tails": vmem((4, 128, D), link),
        "tail_rows": vmem((4, 8, D), F32),
        "stage": vmem((2, 3, C, D), F32),
        "seen": vmem((8, C, C), BF16),
        "affine": vmem((8, 4 * C, C), BF16),
    }
    gathered = {
        "wo_all": (count, part, D), "wh_all": (count, part, FF), "wr_all": (count, 4 * part, D),
    }
    if joined:
        ins["g"] = (cotangent, fed)
        outs |= {
            "y": (shape_of((rows, D), BF16), anywhere),
            "dy": (wide_rows, anywhere),
            "do": (shape_of((rows, D), BF16), anywhere),
            "pack": (shape_of((slabs * part, D), BF16), anywhere),
            "pack_r": (shape_of((slabs * part, 640), BF16), anywhere),
            "gsmall": (shape_of((16, D), F32), whole(16, D)),
        }
        scratch |= {name: vmem(shape, link) for name, shape in gathered.items()}
        scratch |= {
            "held_y": vmem((2, FEED_ROWS, D), BF16), "held_dy": vmem((2, FEED_ROWS, D), F32),
            "held_do": vmem((2, FEED_ROWS, D), BF16),
            "middle": vmem((rows, D), F32),
            "o": vmem((rows, D), BF16), "bias": vmem((1, FF), F32), "gwo": vmem((D, D), F32),
            "gwh": vmem((D, FF), F32), "gwr": vmem((D, FF), F32),
        }
    else:
        outs |= {name: (shape_of(shape, link), anywhere) for name, shape in gathered.items()}
        outs |= {
            "o": (shape_of((rows, D), BF16), tall), "bias": (shape_of((1, FF), F32), whole(1, FF)),
        }
        scratch["slots"] = vmem((rows, D), BF16)
    found = pl.pallas_call(
        functools.partial(front_kernel, count, joined, (*ins, *outs, *scratch)),
        grid=(2 * FRONT + (rows // FEED_ROWS if joined else 0),),
        in_specs=[spec for _, spec in ins.values()],
        out_specs=[spec for _, spec in outs.values()],
        out_shape=[shape for shape, _ in outs.values()],
        scratch_shapes=list(scratch.values())
        + gather_sems(count, True)
        + gather_sems(count, False) * 4
        + [dma((count,)), dma((count,)), dma((3, 2)), dma((3, 2)), dma((2,)), dma((2, 3)), dma((2, 3))],
        compiler_params=pltpu.CompilerParams(
            vmem_limit_bytes=62 * MIB, collective_id=1, has_side_effects=True
        ),
        name="front",
    )(*(a for a, _ in ins.values()))
    found = dict(zip(outs, found))
    if not joined:
        found |= feed(count, part, tokens, found, cotangent, link)
    return found


def feed(count, part, tokens, found, cotangent, link):
    rows, slabs = tokens.shape[0], 4 * count
    tall = pl.BlockSpec((256, D), lambda i: (i, 0))
    weights = [found[name] for name in ("wo_all", "wh_all", "wr_all")]
    names = ("y", "dy", "do", "pack", "pack_r", "gsmall")
    return dict(
        zip(
            names,
            pl.pallas_call(
                feed_kernel,
                grid=(rows // 256,),
                in_specs=[tall] * 3
                + [whole(8, D), whole(1, FF)]
                + [whole(*a.shape) for a in weights],
                out_specs=[tall] * 3
                + [whole(slabs * part, D), whole(slabs * part, 640), whole(16, D)],
                out_shape=[
                    shape_of((rows, D), BF16),
                    shape_of((rows, D), F32),
                    shape_of((rows, D), BF16),
                    shape_of((slabs * part, D), link),
                    shape_of((slabs * part, 640), link),
                    shape_of((16, D), F32),
                ],
                scratch_shapes=[
                    pltpu.VMEM((D, D), F32), pltpu.VMEM((D, FF), F32), pltpu.VMEM((D, FF), F32),
                ],
                compiler_params=PARAMS,
                name="feed",
            )(tokens, found["o"], cotangent, found["vec"], found["bias"], *weights),
        )
    )


def row_body(
    n, qkvf_ref, do_ref, p_ref, s_ref, z_ref, kept_ref, col, row, edge_ref,
    r_ref, dn_ref, dz_ref, head_ref, aside,
):
    first = edge_ref[pl.ds(0, 1)]
    before = edge_ref[pl.ds(8 + jnp.maximum(n - 1, 0), 1)]
    last = jnp.where(n == 0, first, before)
    vis = visible(col, row)
    carried = wide(flag(col, last), 2)
    slots = jnp.exp(qkvf_ref[:, 3 * D :].astype(F32)).astype(BF16)
    own = wide(flag(col, first), 2)
    states = [expand(kept_ref[0, 64:128, lanes_of(g)]).astype(BF16) for g in range(2)]

    def mixing(g):
        return masked(dot_nt(stacked(do_ref[:, lanes_of(g)]), part_of(qkvf_ref, 2, g)), vis)

    def to_reading(g, back_mix):
        lanes = lanes_of(g)
        back = select(dot(back_mix, slots[:, lanes]))
        return back + carried * dot_nt(do_ref[:, lanes], states[g])

    def to_scores(g, back_reading):
        lanes = lanes_of(g)
        probs, score, inverse = p_ref[:, lanes], s_ref[:, lanes], z_ref[:, lanes]
        shared = back_reading * inverse * probs
        back_score = shared - probs * head_sums(shared)
        back_numer = back_score * inverse * SCALE
        back_total = -(shared + back_score * score) * inverse
        reading = (probs * inverse).astype(BF16)
        r_ref[:, lanes] = reading
        dn_ref[:, lanes] = back_numer
        dz_ref[:, lanes] = back_total
        return back_numer, back_total, reading

    def to_state(g, back_numer, back_total, reading):
        lanes = lanes_of(g)
        head_ref[0:64, lanes] += compacted(
            dot_tn((own * back_numer).astype(BF16), part_of(qkvf_ref, 0, g))
        )
        head_ref[64:128, lanes] += compacted(
            dot_tn((own * reading.astype(F32)).astype(BF16), do_ref[:, lanes])
        )
        head_ref[128:129, lanes] += jnp.sum(own * back_total, axis=0, keepdims=True)

    back_mix = mixing(0)
    back_mix_two = mixing(1)
    aside()
    back_reading = to_reading(0, back_mix)
    back_reading_two = to_reading(1, back_mix_two)
    parts = to_scores(0, back_reading)
    to_state(0, *parts)
    parts = to_scores(1, back_reading_two)
    to_state(1, *parts)


def query_body(n, qkvf_ref, kept_ref, col, row, edge_ref, dn_ref, dq_ref):
    first = edge_ref[pl.ds(0, 1)]
    before = edge_ref[pl.ds(8 + jnp.maximum(n - 1, 0), 1)]
    last = jnp.where(n == 0, first, before)
    vis = visible(col, row)
    carried = wide(flag(col, last), 2)
    slots = jnp.exp(qkvf_ref[:, 3 * D :].astype(F32)).astype(BF16)
    lows = [dn_ref[:, lanes_of(g)].astype(BF16) for g in range(2)]
    states = [expand(kept_ref[0, 0:64, lanes_of(g)]).astype(BF16) for g in range(2)]

    def affine(g):
        return masked(dot_nt(stacked(lows[g]), slots[:, lanes_of(g)]), vis)

    def to_queries(g, back_affinity):
        out = select(dot(back_affinity, part_of(qkvf_ref, 1, g))) + carried * dot(lows[g], states[g])
        dq_ref[:, lanes_of(g)] = out.astype(BF16)

    one, two = affine(0), affine(1)
    to_queries(0, one)
    to_queries(1, two)


def column_body(
    n, qkvf_ref, do_ref, r_ref, dn_ref, dz_ref, col, row, edge_ref, state, snap, snap_rows, d_ref
):
    newest = edge_ref[15:16]
    after = edge_ref[pl.ds(jnp.minimum(n + 1, 7), 1)]
    following = jnp.where(n == 7, newest, after)
    first = edge_ref[pl.ds(n, 1)]
    vis = visible_back(col, row)
    carried = wide(flag(col, following), 2)
    own = wide(flag(col, first), 2)
    kept = jnp.where(following == first, 1.0, 0.0)[:, :GROUP]
    snap[n] = state[0:128].astype(BF16)
    snap_rows[pl.ds(n, 1)] = state[128:129]
    key_states = [expand(state[0:64, lanes_of(g)]).astype(BF16) for g in range(2)]
    value_states = [expand(state[64:128, lanes_of(g)]).astype(BF16) for g in range(2)]
    slots = jnp.exp(qkvf_ref[:, 3 * D :].astype(F32)).astype(BF16)
    numers = [dn_ref[:, lanes_of(g)] for g in range(2)]

    def mixing(g, apart):
        return masked(dot_nt(apart, r_ref[:, lanes_of(g)]), vis)

    def affine(g, apart):
        return masked(dot_nt(apart, numers[g].astype(BF16)), vis)

    def to_values(g, mix):
        lanes = lanes_of(g)
        out = select(dot(mix, do_ref[:, lanes])) + carried * dot(slots[:, lanes], value_states[g])
        d_ref[:, 2 * D + g * GROUP : 2 * D + (g + 1) * GROUP] = out.astype(BF16)

    def to_keys(g, back_affinity):
        lanes = lanes_of(g)
        out = select(dot(back_affinity, part_of(qkvf_ref, 0, g)))
        out = out + carried * dot(slots[:, lanes], key_states[g])
        d_ref[:, D + g * GROUP : D + (g + 1) * GROUP] = out.astype(BF16)

    def to_state(g):
        lanes = lanes_of(g)
        state[0:64, lanes] = kept * state[0:64, lanes] + compacted(
            dot_tn((own * numers[g]).astype(BF16), part_of(qkvf_ref, 0, g))
        )
        state[64:128, lanes] = kept * state[64:128, lanes] + compacted(
            dot_tn((own * r_ref[:, lanes].astype(F32)).astype(BF16), do_ref[:, lanes])
        )
        state[128:129, lanes] = kept * state[128:129, lanes] + jnp.sum(
            own * dz_ref[:, lanes], axis=0, keepdims=True
        )

    apart = stacked(slots[:, lanes_of(0)])
    mix = mixing(0, apart)
    back_affinity = affine(0, apart)
    apart = stacked(slots[:, lanes_of(1)])
    mix_two = mixing(1, apart)
    to_values(0, mix)
    affinity_two = affine(1, apart)
    to_keys(0, back_affinity)
    to_state(0)
    to_values(1, mix_two)
    to_keys(1, affinity_two)
    to_state(1)


def slot_body(n, qkvf_ref, do_ref, r_ref, dn_ref, dz_ref, col, row, edge_ref, snap, snap_rows, d_ref):
    newest = edge_ref[15:16]
    after = edge_ref[pl.ds(jnp.minimum(n + 1, 7), 1)]
    following = jnp.where(n == 7, newest, after)
    vis = visible_back(col, row)
    carried = wide(flag(col, following), 2)
    left = lane_heads(C, 128) == 0
    norm_state = snap_rows[pl.ds(n, 1)]
    key_states = [expand(snap[n, 0:64, lanes_of(g)]) for g in range(2)]
    value_states = [expand(snap[n, 64:128, lanes_of(g)]) for g in range(2)]

    def mixing(g):
        return masked(dot_nt(stacked(part_of(qkvf_ref, 2, g)), do_ref[:, lanes_of(g)]), vis)

    def affine(g):
        return masked(dot_nt(stacked(part_of(qkvf_ref, 1, g)), part_of(qkvf_ref, 0, g)), vis)

    def from_mix(g, back_mix):
        return select(dot(back_mix, r_ref[:, lanes_of(g)]))

    def from_affinity(g, affinity):
        high, low = split(dn_ref[:, lanes_of(g)])
        parts = []
        for p in range(2):
            pair = slice(p * 128, (p + 1) * 128)
            both = dot(
                affinity[p * 512 : (p + 1) * 512],
                jnp.concatenate([high[:, pair], low[:, pair]], axis=1),
            )
            both = both[:, :128] + both[:, 128:]
            parts.append(jnp.where(left, both[:C], both[C:]))
        return jnp.concatenate(parts, axis=1)

    def from_totals():
        high, low = split(dz_ref[...])
        return dot(vis, high) + dot(vis, low)

    def from_state(g):
        return carried * (
            dot_nt(part_of(qkvf_ref, 1, g), key_states[g])
            + dot_nt(part_of(qkvf_ref, 2, g), value_states[g])
            + norm_state[:, lanes_of(g)]
        )

    def to_slots(g, back_slots):
        written = jnp.exp(part_of(qkvf_ref, 3, g).astype(F32))
        d_ref[:, 3 * D + g * GROUP : 3 * D + (g + 1) * GROUP] = (back_slots * written).astype(BF16)

    norm = from_totals()
    mix = mixing(0)
    affinity = affine(0)
    mix_two = mixing(1)
    total = from_mix(0, mix)
    affinity_two = affine(1)
    total = total + from_affinity(0, affinity)
    total_two = from_mix(1, mix_two)
    to_slots(0, total + norm[:, lanes_of(0)] + from_state(0))
    total_two = total_two + from_affinity(1, affinity_two)
    to_slots(1, total_two + norm[:, lanes_of(1)] + from_state(1))


class Scatter:
    def __init__(self, count, source, own, axes, direct, out, buffers):
        self.axes, self.direct, self.out = axes, direct, out
        self.seq, self.at, self.sibling, self.beside = places()
        self.source, self.own = source, own
        self.core = lax.rem(self.seq, 2)
        self.total, self.local, self.last, self.done = buffers[:4]
        self.stages = []
        size = source.shape[0]
        base = 0
        for n, axis in enumerate(axes):
            ways = {"core": 2, "x": 2, "y": 2, "z": count // 2, "all": count}[axis]
            size = size // ways
            me = {
                "core": self.core, "x": self.seq // 2, "y": lax.rem(self.at, 2), "z": self.at // 2,
                "all": self.at,
            }[axis]
            held = source
            if own is not None and n > 0:
                held = own
            come, sems = buffers[4 + 2 * n], buffers[5 + 2 * n]
            self.stages.append((axis, ways, size, base, me, held, come, sems))
            if own is None or n > 0:
                base = base + me * size

    def copies(self, n, halves=(0, 1)):
        axis, ways, size, base, me, held, come, sems = self.stages[n]
        if axis == "x":
            for half in halves:
                first, some = half * (size // 2), size // 2
                yield push(
                    held.at[pl.ds(base + (me ^ 1) * size + first, some)],
                    come.at[0, pl.ds(first, some)],
                    sems.at[0, half], sems.at[1, half], seq=self.beside,
                )
            return
        for k in range(1, ways):
            if axis == "core":
                device = {"seq": self.sibling}
            else:
                device = {"fsdp": self.at ^ (2 * k if axis == "z" else k)}
            yield push(
                held.at[pl.ds(base + (me ^ k) * size, size)], come.at[k - 1],
                sems.at[0, k - 1], sems.at[1, k - 1], **device,
            )

    def copy_own(self):
        size = self.source.shape[0] // 2
        return pltpu.make_async_copy(
            self.source.at[pl.ds(self.core * size, size)], self.own, self.local
        )

    def start(self):
        for copy in self.copies(0):
            copy.start()
        if self.own is not None:
            self.copy_own().start()

    def advance(self, n, halves=(0, 1)):
        axis, ways, size, base, me, held, come, sems = self.stages[n]
        for copy in self.copies(n):
            copy.wait_recv()
        mine = held
        first = base + me * size
        if n == 0 and self.own is not None:
            self.copy_own().wait()
            mine, first = self.own, 0

        def added(slab):
            total = mine[first + slab].astype(F32)
            for k in range(1, ways):
                total = total + come[k - 1, slab].astype(F32)
            return total

        if n + 1 == len(self.stages):
            self.total[...] = added(0)
            self.copy_done().start()
            for copy in self.sent():
                copy.start()
            return

        @pl.loop(0, size)
        def _(slab):
            mine[first + slab] = added(slab).astype(mine.dtype)

        for copy in self.copies(n + 1, halves):
            copy.start()

    def copy_done(self):
        return pltpu.make_async_copy(self.total, self.out.at[self.seq], self.done)

    def sent(self):
        other = lax.rem(self.sibling + 2, 4)
        for n, target in enumerate((self.sibling, self.beside, other)[: 3 if self.direct else 2]):
            yield push(
                self.total, self.out.at[self.seq], self.last.at[0, n], self.last.at[1, n], seq=target
            )

    def forwarded(self, source):
        here = self.out.at[source]
        return push(here, here, self.last.at[0, 2], self.last.at[1, 2], seq=self.sibling)

    def come_in(self, n, source):
        here = self.out.at[source]
        return push(here, here, self.last.at[0, n], self.last.at[1, n], seq=source)

    def forward(self):
        self.come_in(1, self.beside).wait_recv()
        self.forwarded(self.beside).start()

    def finish(self):
        other = lax.rem(self.sibling + 2, 4)
        self.come_in(0, self.sibling).wait_recv()
        if self.direct:
            self.come_in(1, self.beside).wait_recv()
        else:
            self.forwarded(self.beside).wait_send()
        self.forwarded(other).wait_recv()
        self.copy_done().wait()
        for copy in self.sent():
            copy.wait_send()
        for n in range(len(self.stages)):
            for copy in self.copies(n):
                copy.wait_send()


def scatter_scratch(count, part, lanes, link, axes, hbm):
    vmem, dma = pltpu.VMEM, pltpu.SemaphoreType.DMA
    size = 2 * 4 * count // 2
    out = [vmem((size // 2, part, lanes), link)] if hbm else []
    out += [vmem((part, lanes), F32), dma, dma((2, 3)), dma]
    for axis in axes:
        ways = {"core": 2, "x": 2, "y": 2, "z": count // 2, "all": count}[axis]
        size = size // ways
        out += [vmem((ways - 1, size, part, lanes), link), dma((2, max(ways - 1, 2)))]
    return out


OVER_X = ("core", "x", "y", "z")
OVER_Y = ("core", "y", "x", "z")
SHORT = ("core", "x", "all")


class SmallSum:
    def __init__(self, count, mine, from_seq, half, from_fsdp, sems):
        self.count, self.mine, self.from_seq = count, mine, from_seq
        self.half, self.from_fsdp, self.sems = half, from_fsdp, sems
        self.seq, self.at, _, _ = places()

    def lanes(self, owner):
        if self.from_fsdp.shape[2] == D:
            return pl.ds(0, D)
        first = owner * (D // self.count) // 128 * 128
        return pl.ds(pl.multiple_of(first, 128), 128)

    def over_seq(self, k, slot):
        return push(
            self.mine, self.from_seq.at[slot], self.sems[0].at[0, k], self.sems[0].at[1, k],
            seq=self.seq ^ k,
        )

    def over_fsdp(self, k):
        return push(
            self.half.at[:, self.lanes(self.at ^ k)], self.from_fsdp.at[self.at],
            self.sems[1].at[0, k], self.sems[1].at[1, k], fsdp=self.at ^ k,
        )

    def fsdp_in(self, k):
        here = self.from_fsdp.at[self.at ^ k]
        return push(here, here, self.sems[1].at[0, k], self.sems[1].at[1, k], fsdp=self.at ^ k)

    def start(self):
        for k in range(1, 4):
            self.over_seq(k, self.seq).start()
        self.from_seq[self.seq] = self.mine[...]

    def second(self):
        for k in range(1, 4):
            self.over_seq(k, self.seq ^ k).wait_recv()
        total = self.from_seq[0]
        for n in range(1, 4):
            total = total + self.from_seq[n]
        self.half[...] = total
        for k in range(1, self.count):
            self.over_fsdp(k).start()
        self.from_fsdp[self.at] = self.half[:, self.lanes(self.at)]

    def finish(self, out_ref):
        for k in range(1, self.count):
            self.fsdp_in(k).wait_recv()
        total = self.from_fsdp[0]
        for n in range(1, self.count):
            total = total + self.from_fsdp[n]
        out_ref[...] = total
        for k in range(1, 4):
            self.over_seq(k, self.seq).wait_send()
        for k in range(1, self.count):
            self.over_fsdp(k).wait_send()


def small_scratch(count, rows, lanes):
    vmem, dma = pltpu.VMEM, pltpu.SemaphoreType.DMA
    return [
        vmem((4, rows, D), F32), vmem((rows, D), F32), vmem((count, rows, lanes), F32),
        dma((2, 4)), dma((2, count)),
    ]


QUERY, COLUMN, SLOT, INPUT = 8, 16, 24, 32


def back_kernel(
    count, per, x_ref, xs_ref, qkvf_ref, do_ref, p_ref, s_ref, z_ref, kept_ref, dy_ref, doc_ref,
    small_ref, w_ref, ffg_ref, ffr_ref, ffs_ref,
    gi_ref, ff_out, fr_out, q_out, kv_out, f_out, s1_out, s2_out,
    gi_held, gi_sem, scores, scores_sem, d_all, h_turned, reading, numer, total, col_ref, edge_ref, head, state, heads, head_rows,
    snap, snap_rows, w_held, w_sem, q_piece, kv_piece, f_piece, last_small, *rest,
):
    step = pl.program_id(0)
    seq, at, _, _ = places()
    link = q_piece.dtype

    def take(size):
        nonlocal rest
        out, rest = rest[:size], rest[size:]
        return out

    (own,) = take(1)
    ff = Scatter(count, ffg_ref, own, OVER_X, False, ff_out, take(12))
    (own,) = take(1)
    fr = Scatter(count, ffr_ref, own, OVER_Y, False, fr_out, take(12))
    for_q = Scatter(count, q_piece, None, OVER_X, False, q_out, take(12))
    for_kv = Scatter(count, kv_piece, None, OVER_X, False, kv_out, take(12))
    for_f = Scatter(count, f_piece, None, SHORT, True, f_out, take(10))
    small_one = SmallSum(count, ffs_ref, *take(3), take(2))
    small_two = SmallSum(count, last_small, *take(3), take(2))
    states = States(heads, head_rows, take(2))

    def chunk(u, first, turned=False):
        n = step * per + u - first
        n = 7 - n if turned else n
        here = pl.ds(pl.multiple_of(n * C, C), C)
        block = pl.ds(pl.multiple_of((per - 1 - u if turned else u) * C, C), C)
        return n, here, block, col_ref[here], doc_ref[:, here].astype(F32)

    def fetch():
        return pltpu.make_async_copy(w_ref, w_held, w_sem)

    def fetch_scores(n):
        slot, here = lax.rem(n, 2), pl.ds(pl.multiple_of(n * per * C, per * C), per * C)
        return [
            pltpu.make_async_copy(ref.at[here], scores.at[slot, k], scores_sem.at[slot, k])
            for k, ref in enumerate((p_ref, s_ref, z_ref))
        ]

    def give(n):
        here = pl.ds(pl.multiple_of(n * per * C, per * C), per * C)
        slot = lax.rem(n, 2)
        return pltpu.make_async_copy(gi_held.at[slot], gi_ref.at[here], gi_sem.at[slot])

    def weight_grad(piece, d_lanes, lanes, short=False):
        grad = dot(h_turned[...], d_all[:, d_lanes])
        half, part = count // 2, piece.shape[1]
        for q in range(4):
            x, c = q // 2, q % 2
            share = grad[:, q * 128 : (q + 1) * 128].reshape(half, 2, part, 128).astype(link)
            if short:
                first = (c * 2 + x) * count
                piece[first : first + count, :, lanes] = share.reshape(count, part, 128)
                continue
            for y in range(2):
                first = ((c * 2 + x) * 2 + y) * half
                piece[first : first + half, :, lanes] = share[:, y]

    @pl.when(step == 0)
    def _():
        greet(count)
        for n in range(2):
            for copy in fetch_scores(n):
                copy.start()
        fetch().start()
        doc_parts(doc_ref, col_ref, edge_ref)
        head[...] = jnp.zeros_like(head)
        last_small[...] = jnp.zeros_like(last_small)

    def turn():
        weight_grad(q_piece, slice(0, D), slice(0, 128))
        for_q.start()
        states.finish()
        newest = edge_ref[15:16]
        state[...] = jnp.zeros_like(state)
        for n in range(4):
            use = jnp.where(head_rows[n, 1:2] == newest, 1.0, 0.0) * (n > seq).astype(F32)
            state[0:128] += use * heads[n].astype(F32)
            state[128:129] += use * head_rows[n, 0:1]

    def send_states():
        heads[seq] = head[0:128].astype(link)
        head_rows[seq, 0:1] = head[128:129]
        head_rows[seq, 1:2] = edge_ref[0:1]
        head_rows[seq, 2:8] = jnp.zeros((6, D), F32)
        states.start()

    def key_value_grads():
        weight_grad(kv_piece, slice(D, 2 * D), slice(0, 128))
        weight_grad(kv_piece, slice(2 * D, 3 * D), slice(128, 256))
        for_kv.start()

    def slot_grads():
        weight_grad(f_piece, slice(3 * D, 4 * D), slice(0, 128), True)
        for_f.start()

    def last():
        small_two.start()
        for piece in (fr, ff, for_q, for_kv):
            piece.forward()
        for_f.advance(2)
        small_two.second()
        for piece in (ff, fr, for_q):
            piece.finish()
        states.drain()
        small_two.finish(s2_out)
        for_kv.finish()
        for_f.finish()
        for n in (8 // per - 2, 8 // per - 1):
            give(n).wait()

    def rest_of_ff():
        for copy in ff.copies(1, (1,)):
            copy.start()

    def begin():
        met(count)
        ff.start()
        small_one.start()

    schedule = {
        0: [begin],
        1: [fr.start],
        3: [lambda: ff.advance(0, (0,)), small_one.second],
        5: [lambda: fr.advance(0)],
        QUERY - 1: [send_states],
        QUERY + 5: [states.forward, rest_of_ff],
        QUERY + 7: [turn],
        COLUMN + 1: [lambda: fr.advance(1), lambda: for_q.advance(0)],
        COLUMN + 2: [lambda: ff.advance(1)],
        COLUMN + 6: [lambda: fr.advance(2)],
        SLOT: [lambda: ff.advance(2)],
        COLUMN + 7: [key_value_grads, lambda: for_q.advance(1)],
        SLOT + 1: [lambda: for_kv.advance(0), lambda: for_q.advance(2)],
        SLOT + 6: [lambda: for_kv.advance(1), lambda: fr.advance(3)],
        SLOT + 7: [slot_grads, lambda: ff.advance(3), lambda: for_q.advance(3)],
        INPUT + 1: [lambda: for_f.advance(0), lambda: for_kv.advance(2)],
        INPUT + 3: [lambda: small_one.finish(s1_out)],
        INPUT + 5: [lambda: for_f.advance(1), lambda: for_kv.advance(3)],
        INPUT + 7: [last],
    }

    @pl.when(step < QUERY // per)
    def _():
        for copy in fetch_scores(step):
            copy.wait()

    @pl.loop(0, per)
    def _(u):
        at_chunk = step * per + u

        @pl.when(at_chunk < QUERY)
        def _():
            n, here, block, col, row = chunk(u, 0)
            kept_scores = [scores.at[lax.rem(step, 2), k, block] for k in range(3)]

            def aside():
                unit, _ = norm_parts(x_ref[block].astype(F32))
                h_turned[:, here] = (unit * small_ref[0:1] + small_ref[1:2]).astype(BF16).T

            row_body(
                n, qkvf_ref.at[block], do_ref.at[block], *kept_scores, kept_ref.at[pl.ds(u, 1)],
                col, row, edge_ref,
                reading.at[here], numer.at[here], total.at[here], head, aside,
            )

        @pl.when((at_chunk >= QUERY) & (at_chunk < COLUMN))
        def _():
            n, here, block, col, row = chunk(u, QUERY)
            query_body(
                n, qkvf_ref.at[block], kept_ref.at[pl.ds(u, 1)], col, row, edge_ref,
                numer.at[here], d_all.at[here, 0:D],
            )

        @pl.when((at_chunk >= COLUMN) & (at_chunk < SLOT))
        def _():
            n, here, block, col, row = chunk(u, COLUMN, True)
            column_body(
                n, qkvf_ref.at[block], do_ref.at[block], reading.at[here], numer.at[here],
                total.at[here], col, row, edge_ref, state, snap, snap_rows, d_all.at[here],
            )

        @pl.when((at_chunk >= SLOT) & (at_chunk < INPUT))
        def _():
            n, here, block, col, row = chunk(u, SLOT, True)
            slot_body(
                n, qkvf_ref.at[block], do_ref.at[block], reading.at[here], numer.at[here],
                total.at[here], col, row, edge_ref, snap, snap_rows, d_all.at[here],
            )

        @pl.when((at_chunk >= INPUT) & (u == 0))
        def _():
            nth = step - INPUT // per

            @pl.when(nth >= 2)
            def _():
                give(nth - 2).wait()

            @pl.when(nth == 0)
            def _():
                fetch().wait()

            size = xs_ref.shape[0]
            here = pl.ds(pl.multiple_of(nth * size, size), size)
            grad = dot_nt(d_all[here], w_held[...])
            unit, scale = norm_parts(xs_ref[...].astype(F32))
            last_small[0:1] += jnp.sum(grad * unit, axis=0, keepdims=True)
            last_small[1:2] += jnp.sum(grad, axis=0, keepdims=True)
            gi_held[lax.rem(nth, 2)] = dy_ref[...] + norm_back(unit, scale, small_ref[0:1], grad)
            give(nth).start()

        for when, actions in schedule.items():

            @pl.when(at_chunk == when)
            def _(actions=actions):
                for action in actions:
                    action()

    @pl.when(step + 2 < QUERY // per)
    def _():
        for copy in fetch_scores(step + 2):
            copy.start()


def back(
    count, tokens, qkvf, do, probs, score, inverse, kept, dy, doc_ids, small, w_all, ffg, ffr, ffs
):
    rows = tokens.shape[0]
    part, link = ffg.shape[1], ffg.dtype
    per = 2 if link == BF16 else 1
    size = per * C
    blocks = 8 // per
    once = lambda a: pl.BlockSpec(a.shape, lambda i: (0,) * a.ndim)
    anywhere = pl.BlockSpec(memory_space=pl.ANY)
    vmem, dma = pltpu.VMEM, pltpu.SemaphoreType.DMA

    def early(i):
        return jnp.minimum(i, blocks - 1)

    def twice(i):
        return jnp.where(i < blocks, i, jnp.clip(i - blocks, 0, blocks - 1))

    def turned(i):
        return blocks - 1 - lax.rem(jnp.clip(i - 2 * blocks, 0, 2 * blocks - 1), blocks)

    def always(i):
        return jnp.where(i < 2 * blocks, twice(i), turned(i))

    def both(i):
        return jnp.where(i < blocks, i, turned(i))

    late = lambda i: (jnp.maximum(i - 4 * blocks, 0), 0)
    tall = pl.BlockSpec((size, D), late)
    some = lambda lanes, order: pl.BlockSpec((size, lanes), lambda i: (order(i), 0))
    slabs = 4 * count
    return pl.pallas_call(
        functools.partial(back_kernel, count, per),
        grid=(5 * blocks,),
        in_specs=[some(D, early), tall, some(4 * D, always), some(D, both)]
        + [anywhere] * 3
        + [pl.BlockSpec((per, 128, D), lambda i: (twice(i), 0, 0)), tall]
        + [once(doc_ids), once(small), anywhere, anywhere, anywhere, once(ffs)],
        out_specs=[anywhere] * 6 + [whole(16, D), whole(8, 128)],
        out_shape=[
            shape_of((rows, D), F32),
            shape_of((4, part, D), F32),
            shape_of((4, part, 640), F32),
            shape_of((4, part, 128), F32),
            shape_of((4, part, 256), F32),
            shape_of((4, part, 128), F32),
            shape_of((16, D), F32),
            shape_of((8, 128), F32),
        ],
        scratch_shapes=[
            vmem((2, size, D), F32),
            dma((2,)),
            vmem((2, 3, size, D), F32),
            dma((2, 3)),
            vmem((rows, 4 * D), BF16),
            vmem((D, rows), BF16),
            vmem((rows, D), BF16),
            vmem((rows, D), F32),
            vmem((rows, D), F32),
            vmem((rows, 128), F32),
            vmem((16, D), F32),
            vmem((136, D), F32),
            vmem((136, D), F32),
            vmem((4, 128, D), link),
            vmem((4, 8, D), F32),
            vmem((8, 128, D), BF16),
            vmem((8, D), F32),
            vmem(w_all.shape, BF16),
            dma,
            vmem((slabs, part, 128), link),
            vmem((slabs, part, 256), link),
            vmem((slabs, part, 128), link),
            vmem((8, D), F32),
        ]
        + scatter_scratch(count, part, D, link, OVER_X, True)
        + scatter_scratch(count, part, 640, link, OVER_Y, True)
        + scatter_scratch(count, part, 128, link, OVER_X, False)
        + scatter_scratch(count, part, 256, link, OVER_X, False)
        + scatter_scratch(count, part, 128, link, SHORT, False)
        + small_scratch(count, 16, D)
        + small_scratch(count, 8, 128)
        + [dma((3, 2)), dma((3, 2))],
        compiler_params=pltpu.CompilerParams(
            vmem_limit_bytes=(62 if link == BF16 else 63) * MIB, collective_id=2, has_side_effects=True
        ),
        name="back",
    )(
        tokens, tokens, qkvf, do, probs, score, inverse, kept, dy, doc_ids, small, w_all, ffg, ffr,
        ffs,
    )


def finish_kernel(
    count, part, y_ref, gi_ref, ff_ref, fr_ref, q_ref, kv_ref, f_ref, s1_ref, s2_ref, y_out, gi_out,
    *rest,
):
    at = lax.axis_index("fsdp")
    *outs, held_y, held, sems = rest

    def move(n, out):
        source, through, target, here = gi_ref, held, gi_out, pl.ds(n * 512, 512)
        if n >= 4:
            source, through, target, here = y_ref, held_y, y_out, pl.ds((n - 4) * 1024, 1024)
        if out:
            return pltpu.make_async_copy(through.at[here], target.at[here], sems.at[1, n])
        return pltpu.make_async_copy(source.at[here], through.at[here], sems.at[0, n])

    def pick(row, size):
        out = row(0, size)
        for f in range(1, count):
            out = jnp.where(at == f, row(f * size, size), out)
        return out

    def bias(start, size):
        r = start // D
        return s1_ref[8 + r : 9 + r, start - r * D : start - r * D + size]

    def row_of_sums(ref, n):
        return lambda start, size: ref[
            n : n + 1, start % ref.shape[1] : start % ref.shape[1] + size
        ]

    for n in range(6):
        move(n, False).start()
    for n in range(4):
        lanes = slice(n * 128, (n + 1) * 128)
        outs[0][:, lanes] = q_ref[n]
        outs[1][:, lanes] = kv_ref[n, :, 0:128]
        outs[2][:, lanes] = kv_ref[n, :, 128:256]
        outs[3][:, lanes] = f_ref[n]
        outs[4][:, lanes] = fr_ref[n, :, 512:640]
        outs[5][:, n * 512 : (n + 1) * 512] = ff_ref[n]
        for j in range(4):
            outs[6][j * part : (j + 1) * part, lanes] = fr_ref[n, :, j * 128 : (j + 1) * 128]
    for n in range(6):
        move(n, False).wait()
        move(n, True).start()
    outs[7][...] = pick(row_of_sums(s2_ref, 0), part)
    outs[8][...] = pick(row_of_sums(s2_ref, 1), part)
    outs[9][...] = pick(row_of_sums(s1_ref, 2), part)
    outs[10][...] = pick(row_of_sums(s1_ref, 3), part)
    outs[11][...] = pick(bias, 4 * part)
    outs[12][...] = pick(row_of_sums(s1_ref, 4), part)
    for n in range(6):
        move(n, True).wait()


def finish(count, part, out, grad_input, *sums):
    once = lambda shape: pl.BlockSpec(shape, lambda: (0,) * len(shape))
    anywhere = pl.BlockSpec(memory_space=pl.ANY)
    shapes = [(part, D)] * 5 + [(part, FF), (4 * part, D)]
    shapes += [(1, part)] * 4 + [(1, 4 * part), (1, part)]
    return pl.pallas_call(
        functools.partial(finish_kernel, count, part),
        in_specs=[anywhere] * 2 + [once(a.shape) for a in sums],
        out_specs=[anywhere] * 2 + [once(s) for s in shapes],
        out_shape=[shape_of(out.shape, BF16)]
        + [shape_of(s, F32) for s in (grad_input.shape, *shapes)],
        scratch_shapes=[
            pltpu.VMEM(out.shape, BF16),
            pltpu.VMEM(grad_input.shape, F32),
            pltpu.SemaphoreType.DMA((2, 6)),
        ],
        compiler_params=PARAMS,
        name="finish",
    )(out, grad_input, *sums)


def rows_of(lanes, order=lambda i: i):
    return pl.BlockSpec((C, lanes), lambda i: (order(i), 0))


def whole(*shape):
    return pl.BlockSpec(shape, lambda i: (0,) * len(shape))


def row_of(order=lambda i: i):
    return pl.BlockSpec((1, C), lambda i: (0, order(i)))


def shape_of(shape, kind):
    return jax.ShapeDtypeStruct(shape, kind)


PARAMS = pltpu.CompilerParams(vmem_limit_bytes=62 * MIB)


def on_device(
    tokens, doc_ids, w_query, w_key, w_value, w_slots, w_output, w_hidden, w_return,
    gain_first, shift_first, gain_second, shift_second, bias_hidden, bias_return, cotangent,
):
    rows = tokens.shape[0]
    count = lax.axis_size("fsdp")
    part = gain_first.shape[0]
    flat = lambda a: a.reshape(1, a.shape[0])
    found = front(
        count, tokens, doc_ids,
        (w_query, w_key, w_value, w_slots, w_output, w_hidden, w_return),
        [flat(a) for a in (gain_first, shift_first, gain_second, shift_second, bias_return)],
        flat(bias_hidden), cotangent,
    )
    grad_input, *sums = back(
        count, tokens, *(found[name] for name in ("qkvf_out", "do", "p", "s", "z", "kept", "dy")),
        doc_ids, found["vec"], found["w_out"].reshape(D, 4 * D).astype(BF16),
        found["pack"].reshape(-1, part, D), found["pack_r"].reshape(-1, part, 640), found["gsmall"],
    )
    out, grad_input, *grads = finish(count, part, found["y"], grad_input, *sums)
    return (out, grad_input, *grads[:7], *(a.reshape(-1) for a in grads[7:]))


def solution(mesh):
    tall, flat, one = P(("fsdp", "seq"), None), P("fsdp", None), P("fsdp")
    return jax.shard_map(
        on_device,
        mesh=mesh,
        in_specs=(tall, P("fsdp", "seq")) + (flat,) * 7 + (one,) * 6 + (tall,),
        out_specs=(tall, tall) + (flat,) * 7 + (one,) * 6,
        check_vma=False,
    )
```

```python
import functools
import types

import jax
import jax.numpy as jnp
from jax import lax
from jax.experimental import pallas as pl
from jax.experimental.pallas import tpu as pltpu
from jax.sharding import PartitionSpec as P

D = 512
H = 8
M = 64
FF = 2048
C = 256
GROUP = 256
EPS = 1e-05
SCALE = 0.125
F32 = jnp.float32
BF16 = jnp.bfloat16
FEED_ROWS = 512
FEED_LANES = 256
FRONT = 4
MIB = 1024 * 1024


def dot(a, b):
    return lax.dot_general(a, b, (((1,), (0,)), ((), ())), preferred_element_type=F32)


def dot_nt(a, b):
    return lax.dot_general(a, b, (((1,), (1,)), ((), ())), preferred_element_type=F32)


def dot_tn(a, b):
    return lax.dot_general(a, b, (((0,), (0,)), ((), ())), preferred_element_type=F32)


def lane_heads(rows, lanes):
    return lax.broadcasted_iota(jnp.int32, (rows, lanes), 1) // M


def stacked(values):
    heads = lane_heads(C, GROUP)
    zero = jnp.zeros_like(values)
    return jnp.concatenate([jnp.where(heads == h, values, zero) for h in range(4)], axis=0)


def select(values):
    heads = lane_heads(C, GROUP)
    out = values[3 * C :]
    for h in (2, 1, 0):
        out = jnp.where(heads == h, values[h * C : (h + 1) * C], out)
    return out


def masked(values, mask):
    return jnp.concatenate(
        [values[h * C : (h + 1) * C].astype(BF16) * mask for h in range(4)], axis=0
    )


def expand(compact):
    rows = lax.broadcasted_iota(jnp.int32, (GROUP, GROUP), 0) // M
    full = jnp.concatenate([compact] * 4, axis=0)
    return jnp.where(rows == lane_heads(GROUP, GROUP), full, jnp.zeros_like(full))


def compacted(full):
    heads = lane_heads(M, GROUP)
    out = full[3 * M :]
    for h in (2, 1, 0):
        out = jnp.where(heads == h, full[h * M : (h + 1) * M], out)
    return out


def split(values):
    high = values.astype(BF16)
    return high, (values - high.astype(F32)).astype(BF16)


def ones_block():
    rows = lax.broadcasted_iota(jnp.int32, (GROUP, GROUP), 0) // M
    return (rows == lane_heads(GROUP, GROUP)).astype(BF16)


def head_sums(values):
    high, low = split(values)
    ones = ones_block()
    return dot(high, ones) + dot(low, ones)


def head_max(values):
    left = lane_heads(C, 128) == 0
    out = []
    for p in range(2):
        pair = values[:, p * 128 : (p + 1) * 128]
        one = jnp.max(jnp.where(left, pair, -jnp.inf), axis=1, keepdims=True)
        two = jnp.max(jnp.where(left, -jnp.inf, pair), axis=1, keepdims=True)
        out.append(jnp.where(left, one, two))
    return jnp.concatenate(out, axis=1)


def wide(values, times):
    return jnp.concatenate([values] * times, axis=1)


def visible(doc_col, doc_row):
    same = wide(doc_col, 2) == doc_row
    here = lax.broadcasted_iota(jnp.int32, (C, C), 0)
    there = lax.broadcasted_iota(jnp.int32, (C, C), 1)
    return jnp.where(same & (here >= there), 1.0, 0.0).astype(BF16)


def visible_back(doc_col, doc_row):
    same = wide(doc_col, 2) == doc_row
    here = lax.broadcasted_iota(jnp.int32, (C, C), 0)
    there = lax.broadcasted_iota(jnp.int32, (C, C), 1)
    return jnp.where(same & (there >= here), 1.0, 0.0).astype(BF16)


def flag(doc_col, doc):
    return jnp.where(doc_col == doc[:, :128], 1.0, 0.0)


def norm_parts(values):
    centre = jnp.mean(values, axis=-1, keepdims=True)
    centred = values - centre
    spread = jnp.mean(centred * centred, axis=-1, keepdims=True)
    scale = lax.rsqrt(spread + EPS)
    return centred * scale, scale


def norm_back(unit, scale, gain, grad):
    inner = grad * gain
    return scale * (
        inner
        - jnp.mean(inner, axis=-1, keepdims=True)
        - unit * jnp.mean(inner * unit, axis=-1, keepdims=True)
    )


def groups(values):
    return values[:, :GROUP], values[:, GROUP:]


def state_terms(slots, left, right):
    one, two = [], []
    for g in range(2):
        lanes = slice(g * GROUP, (g + 1) * GROUP)
        both = dot_tn(slots[:, lanes], jnp.concatenate([left[:, lanes], right[:, lanes]], axis=1))
        one.append(compacted(both[:, :GROUP]))
        two.append(compacted(both[:, GROUP:]))
    return jnp.concatenate(one, axis=1), jnp.concatenate(two, axis=1)


def lanes_of(g):
    return slice(g * GROUP, (g + 1) * GROUP)


def part_of(ref, part, g):
    return ref[:, part * D + g * GROUP : part * D + (g + 1) * GROUP]


def affinities(qkvf_ref, g, vis):
    return masked(dot_nt(stacked(part_of(qkvf_ref, 0, g)), part_of(qkvf_ref, 1, g)), vis)


def attend_body(
    n, qkvf_ref, slots, vis, affine_ref, col, edge_ref, state, o_ref, p_ref, s_ref, z_ref, kept_ref
):
    kept_ref[0] = state[0:128]
    first = edge_ref[pl.ds(0, 1)]
    before = edge_ref[pl.ds(8 + jnp.maximum(n - 1, 0), 1)]
    last = jnp.where(n == 0, first, before)
    newest = edge_ref[pl.ds(8 + n, 1)]
    carried = wide(flag(col, last), 2)
    norm = dot(vis, slots)
    key_states = [expand(state[0:64, lanes_of(g)]).astype(BF16) for g in range(2)]
    value_states = [expand(state[64:128, lanes_of(g)]).astype(BF16) for g in range(2)]
    norm_state = state[128:129]

    def scores(g, affinity):
        lanes = lanes_of(g)
        numer = select(dot(affinity, slots[:, lanes]))
        numer = numer + carried * dot_nt(part_of(qkvf_ref, 0, g), key_states[g])
        inverse = 1.0 / (norm[:, lanes] + carried * norm_state[:, lanes])
        return numer * inverse * SCALE, inverse

    def grow(score):
        return jnp.exp(score - head_max(score))

    def read(g, score, inverse, grown):
        lanes = lanes_of(g)
        probs = grown / head_sums(grown)
        p_ref[:, lanes] = probs
        s_ref[:, lanes] = score
        z_ref[:, lanes] = inverse
        return (probs * inverse).astype(BF16)

    def mixing(g, reading):
        return masked(dot_nt(stacked(reading), slots[:, lanes_of(g)]), vis)

    def mixed(g, reading, mix):
        out = select(dot(mix, part_of(qkvf_ref, 2, g))) + carried * dot(reading, value_states[g])
        o_ref[:, lanes_of(g)] = out.astype(BF16)

    score, inverse = scores(0, affine_ref[...])
    affinity = affinities(qkvf_ref, 1, vis)
    grown = grow(score)
    score_two, inverse_two = scores(1, affinity)
    reading = read(0, score, inverse, grown)
    tail = wide(flag(col, newest), 4).astype(BF16) * slots
    new_keys, new_values = state_terms(tail, qkvf_ref[:, D : 2 * D], qkvf_ref[:, 2 * D : 3 * D])
    same = jnp.where(last == newest, 1.0, 0.0)
    state[0:64] = same * state[0:64] + new_keys
    state[64:128] = same * state[64:128] + new_values
    state[128:129] = same * state[128:129] + jnp.sum(tail.astype(F32), axis=0, keepdims=True)
    grown = grow(score_two)
    mix = mixing(0, reading)
    reading_two = read(1, score_two, inverse_two, grown)
    mixed(0, reading, mix)
    mix = mixing(1, reading_two)
    mixed(1, reading_two, mix)


MESH_ID = pl.DeviceIdType.MESH


def places():
    seq, at = lax.axis_index("seq"), lax.axis_index("fsdp")
    core = lax.rem(seq, 2)
    return seq, at, seq + 1 - 2 * core, lax.rem(seq + 2, 4)


def push(src, dst, send, recv, **device):
    return pltpu.make_async_remote_copy(
        src_ref=src, dst_ref=dst, send_sem=send, recv_sem=recv,
        device_id=device, device_id_type=MESH_ID,
    )


def greet(count):
    seq, at, _, _ = places()
    barrier = pltpu.get_barrier_semaphore()
    for k in range(1, count):
        pl.semaphore_signal(barrier, inc=1, device_id={"fsdp": at ^ k}, device_id_type=MESH_ID)
    for k in range(1, 4):
        pl.semaphore_signal(barrier, inc=1, device_id={"seq": seq ^ k}, device_id_type=MESH_ID)


def met(count):
    pl.semaphore_wait(pltpu.get_barrier_semaphore(), count - 1 + 3)


class Gather:
    def __init__(self, count, mine, held, base, width, four, sems):
        self.count, self.mine, self.held, self.four = count, mine, held, four
        self.far, self.near, self.core, self.chip, self.onward, self.local = sems
        self.seq, self.at, self.sibling, self.beside = places()
        self.base, self.share = base, width // (4 if four else 2)
        self.evens = range(0, count, 2)

    def lanes(self, seq):
        place = seq if self.four else lax.rem(seq, 2)
        return pl.ds(pl.multiple_of(self.base + place * self.share, 128), self.share)

    def part(self, k, seq):
        return self.held.at[self.at ^ k, :, self.lanes(seq)]

    def source(self, k):
        if k:
            return self.part(k, self.seq)
        return self.mine.at[:, self.lanes(self.seq)]

    def own(self):
        return pltpu.make_async_copy(self.source(0), self.part(0, self.seq), self.local)

    def over(self, sems, k, **device):
        return push(self.source(k), self.part(k, self.seq), sems[0].at[k], sems[1].at[k], **device)

    def come(self, sems, k, owner):
        here = self.part(owner, self.seq)
        return push(here, here, sems[0].at[k], sems[1].at[k], seq=self.sibling)

    def far_out(self, k):
        return push(
            self.source(0), self.part(0, self.seq), self.far[0].at[k], self.far[1].at[k],
            fsdp=self.at ^ k,
        )

    def far_in(self, k):
        return self.come(self.far, k, k)

    def near_out(self, k):
        return self.over(self.near, k, fsdp=self.at ^ 1)

    def near_in(self, k):
        return self.come(self.near, k, k ^ 1)

    def start(self):
        self.own().start()
        for k in self.evens[1:]:
            self.far_out(k).start()
        self.near_out(0).start()

    def second(self):
        for k in self.evens[1:]:
            self.far_in(k).wait_recv()
            self.near_out(k).start()

    def hop(self, sems, source, target):
        here = self.held.at[:, :, self.lanes(source)]
        return push(here, here, sems[0].at[0], sems[1].at[0], seq=target)

    def third(self):
        self.own().wait()
        for k in self.evens:
            self.near_in(k).wait_recv()
        self.hop(self.core, self.seq, self.sibling).start()
        if self.four:
            self.hop(self.chip, self.seq, self.beside).start()

    def fourth(self):
        self.hop(self.chip, self.beside, self.beside).wait_recv()
        self.hop(self.onward, self.beside, self.sibling).start()

    def finish(self):
        self.hop(self.core, self.sibling, self.sibling).wait_recv()
        self.hop(self.core, self.seq, self.sibling).wait_send()
        if self.four:
            self.hop(self.onward, lax.rem(self.sibling + 2, 4), self.sibling).wait_recv()
            self.hop(self.chip, self.seq, self.beside).wait_send()
            self.hop(self.onward, self.beside, self.sibling).wait_send()

    def core_out(self, k):
        return self.over(self.core, k, seq=self.sibling)

    def core_in(self, k):
        here = self.part(k, self.sibling)
        return push(here, here, self.core[0].at[k], self.core[1].at[k], seq=self.sibling)

    def at_once(self, between):
        self.start()
        self.core_out(0).start()
        for k in self.evens[1:]:
            self.far_in(k).wait_recv()
            self.near_out(k).start()
            self.core_out(k).start()
        between()
        for k in self.evens:
            self.near_in(k).wait_recv()
            self.core_out(k ^ 1).start()
        self.own().wait()
        for k in range(self.count):
            self.core_in(k).wait_recv()

    def drain(self, each=False):
        for k in self.evens:
            self.near_out(k).wait_send()
            if k:
                self.far_out(k).wait_send()
        if each:
            for k in range(self.count):
                self.core_out(k).wait_send()


def gather_sems(count, each):
    n = count if each else 1
    pair = lambda size: [pltpu.SemaphoreType.DMA((size,)), pltpu.SemaphoreType.DMA((size,))]
    return pair(count) + pair(count) + pair(n) + pair(1) + pair(1) + [pltpu.SemaphoreType.DMA]


def bundle(refs):
    return [(refs[2 * n], refs[2 * n + 1]) for n in range(5)] + [refs[10]]


class States:
    def __init__(self, big, small, sems):
        self.refs, self.sems = (big, small), sems
        self.seq, _, self.sibling, self.beside = places()

    def hop(self, n, source, target):
        out = []
        for m, ref in enumerate(self.refs):
            here = ref.at[source]
            out.append(push(here, here, self.sems[0].at[n, m], self.sems[1].at[n, m], seq=target))
        return out

    def start(self):
        for copy in self.hop(0, self.seq, self.sibling) + self.hop(1, self.seq, self.beside):
            copy.start()

    def forward(self):
        for copy in self.hop(1, self.beside, self.beside):
            copy.wait_recv()
        for copy in self.hop(2, self.beside, self.sibling):
            copy.start()

    def finish(self):
        for copy in self.hop(0, self.sibling, self.sibling):
            copy.wait_recv()
        for copy in self.hop(2, lax.rem(self.sibling + 2, 4), self.sibling):
            copy.wait_recv()

    def drain(self):
        for copy in (
            self.hop(0, self.seq, self.sibling)
            + self.hop(1, self.seq, self.beside)
            + self.hop(2, self.beside, self.sibling)
        ):
            copy.wait_send()


def doc_parts(doc_ref, col_ref, edge_ref):
    here = lax.broadcasted_iota(jnp.int32, (C, C), 0)
    there = lax.broadcasted_iota(jnp.int32, (C, C), 1)
    eye = jnp.where(here == there, 1.0, 0.0).astype(BF16)
    for n in range(doc_ref.shape[1] // C):
        row = doc_ref[:, n * C : (n + 1) * C].astype(F32)
        col_ref[n * C : (n + 1) * C] = dot_nt(eye, jnp.broadcast_to(row, (128, C)).astype(BF16))
        low = jnp.min(row, axis=1, keepdims=True)
        high = jnp.max(row, axis=1, keepdims=True)
        edge_ref[n : n + 1] = jnp.broadcast_to(low, (1, D))
        edge_ref[n + 8 : n + 9] = jnp.broadcast_to(high, (1, D))


def spread_small(vec_refs, bias_ref, out_ref):
    def repeat(values):
        width = values.shape[1]
        rows = lax.broadcasted_iota(jnp.int32, (width, 128), 0)
        lanes = lax.broadcasted_iota(jnp.int32, (width, 128), 1)
        pick = jnp.where(lax.rem(lanes, width) == rows, 1.0, 0.0).astype(BF16)
        return dot(jnp.broadcast_to(values, (8, width)).astype(BF16), pick)[0:1]

    out_ref[...] = jnp.zeros_like(out_ref)
    for n, ref in enumerate(vec_refs):
        out_ref[n : n + 1] = repeat(ref[...])
    for b in range(max(bias_ref.shape[1] // 128, 1)):
        out_ref[5 + b : 6 + b] = repeat(bias_ref[:, b * 128 : (b + 1) * 128])


def join_small(count, part, gathered, vec_ref, bias_ref):
    lanes = lax.broadcasted_iota(jnp.int32, (8, D), 1)
    total = jnp.zeros((8, D), F32)
    for f in range(count):
        total = jnp.where(lanes // part == f, wide(gathered[f], 4), total)
    vec_ref[...] = total
    size = 4 * part
    for r in range(4):
        at = lanes[0:1] + r * D
        row = jnp.zeros((1, D), F32)
        for f in range(r * D // size, -(-(r + 1) * D // size)):
            for b in range(max(size // 128, 1)):
                use = (at // size == f) & (lax.rem(at, size) // 128 == b)
                row = jnp.where(use, wide(gathered[f, 5 + b : 6 + b], 4), row)
        bias_ref[0:1, r * D : (r + 1) * D] = row


ROOT = 0.7978845608028654
CUBE = 0.044715


def gelu_both(u):
    square = u * u
    bent = jnp.tanh(ROOT * u * (1.0 + CUBE * square))
    half = 0.5 * (1.0 + bent)
    slope = half + 0.5 * u * (1.0 - bent * bent) * (ROOT * (1.0 + 3.0 * CUBE * square))
    return u * half, slope


def feed_start(values, attended, vec_ref, w_out):
    middle = values.astype(F32) + dot(attended, w_out())
    unit, _ = norm_parts(middle)
    return middle, (unit * vec_ref[2:3] + vec_ref[3:4]).astype(BF16)


def feed_body(
    middle, hidden, attended, cot, vec_ref, bias_ref, w_out, w_hidden, w_return,
    y_ref, dy_ref, do_ref, gsmall_ref, gwo_ref, gwh_ref, gwr_ref,
):
    out = middle + vec_ref[4:5]
    grad_hidden = jnp.zeros_like(middle)
    cot32 = cot.astype(F32)
    tiles = FF // FEED_LANES

    def into(j):
        cols = slice(j * FEED_LANES, (j + 1) * FEED_LANES)
        inner = dot(hidden, w_hidden(j)) + bias_ref[0:1, cols]
        return inner, dot_nt(cot, w_return(j))

    def bend(inner, grad):
        gated, slope = gelu_both(inner)
        return gated.astype(BF16), (grad * slope).astype(BF16)

    def outof(j, active, low):
        cols = slice(j * FEED_LANES, (j + 1) * FEED_LANES)
        there = slice(cols.start % D, cols.start % D + FEED_LANES)
        row = 8 + cols.start // D
        gwr_ref[:, cols] += dot_tn(cot, active)
        gsmall_ref[row : row + 1, there] += jnp.sum(low.astype(F32), axis=0, keepdims=True)
        gwh_ref[:, cols] += dot_tn(hidden, low)
        return dot(active, w_return(j)), dot_nt(low, w_hidden(j))

    coming = into(0)
    for j in range(tiles):
        bent = bend(*coming)
        if j + 1 < tiles:
            coming = into(j + 1)
        to_out, to_hidden = outof(j, *bent)
        out = out + to_out
        grad_hidden = grad_hidden + to_hidden
        if j == tiles // 2:
            unit, scale = norm_parts(middle)
    y_ref[...] = out.astype(BF16)
    gsmall_ref[2:3] += jnp.sum(grad_hidden * unit, axis=0, keepdims=True)
    gsmall_ref[3:4] += jnp.sum(grad_hidden, axis=0, keepdims=True)
    gsmall_ref[4:5] += jnp.sum(cot32, axis=0, keepdims=True)
    grad_middle = cot32 + norm_back(unit, scale, vec_ref[2:3], grad_hidden)
    dy_ref[...] = grad_middle
    branch = grad_middle.astype(BF16)
    gwo_ref[...] += dot_tn(attended, branch)
    do_ref[...] = dot_nt(branch, w_out()).astype(BF16)


def pack_grads(count, part, gwo_ref, gwh_ref, gwr_ref, put):
    half = count // 2
    for q in range(4):
        x, c = q // 2, q % 2
        hidden_part = gwh_ref[:, q * 512 : (q + 1) * 512].reshape(half, 2, part, 512)
        out_part = gwo_ref[:, q * 128 : (q + 1) * 128].reshape(half, 2, part, 128)
        turned = gwr_ref[q * 128 : (q + 1) * 128].T.reshape(half, 2, 4, part, 128)
        for y in range(2):
            over_x, over_y = ((c * 2 + x) * 2 + y) * half, ((c * 2 + y) * 2 + x) * half
            put(0, over_x, slice(0, 512), hidden_part[:, y])
            put(1, over_y, slice(512, 640), out_part[:, y])
            for j in range(4):
                put(1, over_y, slice(j * 128, (j + 1) * 128), turned[:, y, j])


def feed_kernel(
    x_ref, o_ref, g_ref, small_ref, bias_ref, wo_ref, wh_ref, wr_ref,
    y_ref, dy_ref, do_ref, pack_ref, pack_r_ref, gsmall_ref, gwo_ref, gwh_ref, gwr_ref,
):
    step = pl.program_id(0)
    count, part = wh_ref.shape[0], wh_ref.shape[1]

    @pl.when(step == 0)
    def _():
        for ref in (gwo_ref, gwh_ref, gwr_ref, gsmall_ref):
            ref[...] = jnp.zeros_like(ref)

    views = weight_views(wo_ref, wh_ref, wr_ref)
    feed_body(
        *feed_start(x_ref[...], o_ref[...], small_ref, views[0]), o_ref[...], g_ref[...], small_ref,
        bias_ref, *views, y_ref, dy_ref, do_ref, gsmall_ref, gwo_ref, gwh_ref, gwr_ref,
    )

    @pl.when(step == pl.num_programs(0) - 1)
    def _():
        def put(which, slab, lanes, values):
            ref = (pack_ref, pack_r_ref)[which]
            n = values.shape[0] * part
            ref[slab * part : slab * part + n, lanes] = values.reshape(n, -1).astype(ref.dtype)

        pack_grads(count, part, gwo_ref, gwh_ref, gwr_ref, put)


def weight_views(wo_ref, wh_ref, wr_ref):
    def w_out():
        return wo_ref[...].reshape(D, D).astype(BF16)

    def w_hidden(j):
        cols = slice(j * FEED_LANES, (j + 1) * FEED_LANES)
        return wh_ref[:, :, cols].reshape(D, FEED_LANES).astype(BF16)

    def w_return(j):
        n = FEED_LANES // wr_ref.shape[1]
        return wr_ref[j * n : (j + 1) * n].reshape(FEED_LANES, D).astype(BF16)

    return w_out, w_hidden, w_return


def front_kernel(count, joined, names, *refs):
    r = types.SimpleNamespace(**dict(zip(names, refs)))
    sems = refs[len(names) :]
    x_ref, doc_ref, vec_out, bias_out = r.x, r.doc, r.vec, r.bias
    qkvf, hidden, w_all, mine = r.qkvf, r.hidden, r.w_all, r.mine
    mine_o, mine_h, mine_r, spread, smalls = r.mine_o, r.mine_h, r.mine_r, r.spread, r.smalls
    col_ref, edge_ref, state, tail = r.col, r.edge, r.state, r.tail
    tails, tail_rows = r.tails, r.tail_rows
    slots = r.o if joined else r.slots
    step = pl.program_id(0)
    seq, at, _, _ = places()
    link = mine.dtype
    groups_of_sems = []
    for _ in range(5):
        groups_of_sems.append(bundle(sems[:11]))
        sems = sems[11:]
    small_send, small_recv, state_send, state_recv, out_sem, stage_sem, fed_sem = sems
    main = Gather(count, mine, w_all, D, 3 * D, False, groups_of_sems[0])
    q_piece = Gather(count, mine, w_all, 0, D, False, groups_of_sems[1])
    o_piece = Gather(count, mine_o, r.wo_all, 0, D, True, groups_of_sems[2])
    h_piece = Gather(count, mine_h, r.wh_all, 0, FF, True, groups_of_sems[3])
    r_piece = Gather(count, mine_r, r.wr_all, 0, D, False, groups_of_sems[4])
    later = (q_piece, o_piece, h_piece, r_piece)
    states = States(tails, tail_rows, (state_send, state_recv))

    def small_copy(k, owner):
        return push(
            spread, smalls.at[owner], small_send.at[k], small_recv.at[k], fsdp=at ^ k
        )

    def save():
        return (
            pltpu.make_async_copy(qkvf, r.qkvf_out, out_sem.at[0]),
            pltpu.make_async_copy(w_all, r.w_out, out_sem.at[1]),
        )

    @pl.when(step == 0)
    def _():
        greet(count)
        for n, ref in enumerate((r.w0, r.w1, r.w2, r.w3)):
            mine[:, n * D : (n + 1) * D] = ref[...].astype(BF16).astype(link)
        spread_small((r.v0, r.v1, r.v2, r.v3, r.v4), r.bias_in, spread)
        doc_parts(doc_ref, col_ref, edge_ref)
        tail[...] = jnp.zeros_like(tail)
        met(count)
        for k in range(1, count):
            small_copy(k, at).start()

        def between():
            mine_o[...] = r.w4[...].astype(BF16).astype(link)
            mine_h[...] = r.w5[...].astype(BF16).astype(link)
            mine_r[...] = r.w6[...].astype(BF16).astype(link)
            smalls[at] = spread[...]
            for k in range(1, count):
                small_copy(k, at ^ k).wait_recv()
            join_small(count, r.v0.shape[1], smalls, vec_out, bias_out)
            q_piece.start()
            o_piece.start()

            @pl.loop(0, 8)
            def _(n):
                here = pl.ds(pl.multiple_of(n * C, C), C)
                unit, _ = norm_parts(x_ref[here].astype(F32))
                hidden[here] = (unit * vec_out[0:1] + vec_out[1:2]).astype(BF16)
                r.seen[n] = visible(col_ref[here], doc_ref[:, here].astype(F32))

            if joined:
                for ref in (r.gwo, r.gwh, r.gwr, r.gsmall):
                    ref[...] = jnp.zeros_like(ref)

        main.at_once(between)
        q_piece.second()
        h_piece.start()

    @pl.when(step < FRONT)
    def _():
        size = 8 // FRONT * C
        here = pl.ds(pl.multiple_of(step * size, size), size)
        weights = w_all[:, :, D:].reshape(D, 3 * D).astype(BF16)
        rows = dot(hidden[here], weights).astype(BF16)
        qkvf[here, D:] = rows
        slots = wide(flag(col_ref[here], edge_ref[15:16]), 4) * jnp.exp(rows[:, 2 * D :].astype(F32))
        slots = slots.astype(BF16)
        keys, values = state_terms(slots, rows[:, 0:D], rows[:, D : 2 * D])
        tail[0:64] += keys
        tail[64:128] += values
        tail[128:129] += jnp.sum(slots.astype(F32), axis=0, keepdims=True)

    @pl.when(step == 1)
    def _():
        o_piece.second()
        r_piece.start()

    @pl.when(step == FRONT - 2)
    def _():
        q_piece.third()

    @pl.when(step == FRONT - 1)
    def _():
        tails[seq] = tail[0:128].astype(link)
        tail_rows[seq, 0:1] = tail[128:129]
        tail_rows[seq, 1:2] = edge_ref[15:16]
        tail_rows[seq, 2:8] = jnp.zeros((6, D), F32)
        states.start()

        @pl.loop(0, 8)
        def _(n):
            here = pl.ds(pl.multiple_of(n * C, C), C)
            slots[here] = jnp.exp(qkvf[here, 3 * D :].astype(F32)).astype(BF16)

        q_piece.finish()
        h_piece.second()

        @pl.loop(0, FRONT)
        def _(n):
            size = 8 // FRONT * C
            here = pl.ds(pl.multiple_of(n * size, size), size)
            weights = w_all[:, :, 0:D].reshape(D, D).astype(BF16)
            qkvf[here, 0:D] = dot(hidden[here], weights).astype(BF16)

        for copy in save():
            copy.start()
        o_piece.third()

        @pl.loop(0, 8)
        def _(n):
            rows = qkvf.at[pl.ds(pl.multiple_of(n * C, C), C)]
            r.affine[n] = affinities(rows, 0, r.seen[n])

        states.forward()
        states.finish()
        first = edge_ref[0:1]
        state[...] = jnp.zeros_like(state)
        for n in range(4):
            use = jnp.where(tail_rows[n, 1:2] == first, 1.0, 0.0) * (n < seq).astype(F32)
            state[0:128] += use * tails[n].astype(F32)
            state[128:129] += use * tail_rows[n, 0:1]
        h_piece.third()

    per = 8 // FRONT

    def kept_copies(n):
        here = pl.ds(pl.multiple_of(n * C, C), C)
        slot = lax.rem(n, 2)
        return [
            pltpu.make_async_copy(r.stage.at[slot, k], out.at[here], stage_sem.at[slot, k])
            for k, out in enumerate((r.p, r.s, r.z))
        ]

    @pl.when((step >= FRONT) & (step < 2 * FRONT))
    def _():
        @pl.loop(0, per, unroll=True)
        def _(u):
            n = (step - FRONT) * per + u
            slot = lax.rem(n, 2)

            @pl.when(n >= 2)
            def _():
                for copy in kept_copies(n - 2):
                    copy.wait()

            here = pl.ds(pl.multiple_of(n * C, C), C)
            block = pl.ds(pl.multiple_of(u * C, C), C)
            attend_body(
                n, qkvf.at[here], slots[here], r.seen[n], r.affine.at[n], col_ref[here], edge_ref, state,
                r.o.at[here if joined else block], *(r.stage.at[slot, k] for k in range(3)),
                r.kept.at[pl.ds(u, 1)],
            )
            for copy in kept_copies(n):
                copy.start()

            @pl.when(n == 0)
            def _():
                o_piece.fourth()

            @pl.when(n == per - 1)
            def _():
                r_piece.second()

            @pl.when(n == 6)
            def _():
                h_piece.fourth()

    @pl.when(step == 2 * FRONT - 1)
    def _():
        r_piece.third()
        o_piece.finish()
        for copy in save():
            copy.wait()

    def complete():
        h_piece.finish()
        r_piece.finish()
        for piece in later:
            piece.drain()
        main.drain(True)
        states.drain()
        for k in range(1, count):
            small_copy(k, at).wait_send()
        for n in (6, 7):
            for copy in kept_copies(n):
                copy.wait()

    if not joined:
        pl.when(step == 2 * FRONT - 1)(complete)
        return

    views = weight_views(r.wo_all, r.wh_all, r.wr_all)

    @pl.when(step == 2 * FRONT - 1)
    def _():
        @pl.loop(0, x_ref.shape[0] // FEED_ROWS)
        def _(n):
            here = pl.ds(pl.multiple_of(n * FEED_ROWS, FEED_ROWS), FEED_ROWS)
            r.middle[here], hidden[here] = feed_start(x_ref[here], r.o[here], vec_out, views[0])

        complete()

    fed = step - 2 * FRONT

    def fed_copies(n):
        here = pl.ds(pl.multiple_of(n * FEED_ROWS, FEED_ROWS), FEED_ROWS)
        slot = lax.rem(n, 2)
        pairs = ((r.held_y, r.y), (r.held_dy, r.dy), (r.held_do, r.do))
        return [
            pltpu.make_async_copy(held.at[slot], out.at[here], fed_sem.at[slot, k])
            for k, (held, out) in enumerate(pairs)
        ]

    @pl.when(fed >= 2)
    def _():
        for copy in fed_copies(fed - 2):
            copy.wait()

    @pl.when(fed >= 0)
    def _():
        here = pl.ds(pl.multiple_of(fed * FEED_ROWS, FEED_ROWS), FEED_ROWS)
        slot = lax.rem(fed, 2)
        feed_body(
            r.middle[here], hidden[here], r.o[here], r.g[...], vec_out, bias_out, *views,
            r.held_y.at[slot], r.held_dy.at[slot], r.held_do.at[slot], r.gsmall, r.gwo, r.gwh, r.gwr,
        )
        for copy in fed_copies(fed):
            copy.start()

    @pl.when(step == pl.num_programs(0) - 1)
    def _():
        part = mine.shape[0]

        def put(which, slab, lanes, values):
            n = values.shape[0] * part
            at_lane = D * which + lanes.start
            qkvf[slab * part : slab * part + n, at_lane : at_lane + values.shape[2]] = (
                values.reshape(n, -1).astype(BF16)
            )

        pack_grads(count, part, r.gwo, r.gwh, r.gwr, put)
        copies = [
            pltpu.make_async_copy(qkvf.at[:, 0:D], r.pack, out_sem.at[0]),
            pltpu.make_async_copy(qkvf.at[:, D:1152], r.pack_r, out_sem.at[1]),
        ]
        for copy in copies:
            copy.start()
        last = x_ref.shape[0] // FEED_ROWS - 1
        for copy in (*fed_copies(last - 1), *fed_copies(last), *copies):
            copy.wait()


def front(count, tokens, doc_ids, weights, vectors, bias, cotangent):
    rows = tokens.shape[0]
    part = weights[0].shape[0]
    link = BF16 if part % 16 == 0 else F32
    joined = link == BF16
    per = 8 // FRONT
    once = lambda a: pl.BlockSpec(a.shape, lambda i: (0,) * a.ndim)
    late = lambda i: jnp.clip(i - FRONT, 0, FRONT - 1)
    tall = pl.BlockSpec((per * C, D), lambda i: (late(i), 0))
    fed = pl.BlockSpec((FEED_ROWS, D), lambda i: (jnp.maximum(i - 2 * FRONT, 0), 0))
    anywhere = pl.BlockSpec(memory_space=pl.ANY)
    vmem, dma = pltpu.VMEM, pltpu.SemaphoreType.DMA
    ins = {"x": (tokens, once(tokens)), "doc": (doc_ids, once(doc_ids))}
    ins |= {f"w{n}": (a, once(a)) for n, a in enumerate(weights)}
    ins |= {f"v{n}": (a, once(a)) for n, a in enumerate(vectors)}
    ins["bias_in"] = (bias, once(bias))
    wide_rows, slabs = shape_of((rows, D), F32), 4 * count
    outs = {
        "qkvf_out": (shape_of((rows, 4 * D), BF16), anywhere),
        "p": (wide_rows, anywhere),
        "s": (wide_rows, anywhere),
        "z": (wide_rows, anywhere),
        "kept": (
            shape_of((8, 128, D), F32), pl.BlockSpec((per, 128, D), lambda i: (late(i), 0, 0)),
        ),
        "w_out": (shape_of((count, part, 4 * D), link), anywhere),
        "vec": (shape_of((8, D), F32), whole(8, D)),
    }
    scratch = {
        "qkvf": vmem((rows, 4 * D), BF16),
        "hidden": vmem((rows, D), BF16),
        "w_all": vmem((count, part, 4 * D), link),
        "mine": vmem((part, 4 * D), link),
        "mine_o": vmem((part, D), link),
        "mine_h": vmem((part, FF), link),
        "mine_r": vmem((4 * part, D), link),
        "spread": vmem((8, 128), F32),
        "smalls": vmem((count, 8, 128), F32),
        "col": vmem((rows, 128), F32),
        "edge": vmem((16, D), F32),
        "state": vmem((136, D), F32),
        "tail": vmem((136, D), F32),
        "tails": vmem((4, 128, D), link),
        "tail_rows": vmem((4, 8, D), F32),
        "stage": vmem((2, 3, C, D), F32),
        "seen": vmem((8, C, C), BF16),
        "affine": vmem((8, 4 * C, C), BF16),
    }
    gathered = {
        "wo_all": (count, part, D), "wh_all": (count, part, FF), "wr_all": (count, 4 * part, D),
    }
    if joined:
        ins["g"] = (cotangent, fed)
        outs |= {
            "y": (shape_of((rows, D), BF16), anywhere),
            "dy": (wide_rows, anywhere),
            "do": (shape_of((rows, D), BF16), anywhere),
            "pack": (shape_of((slabs * part, D), BF16), anywhere),
            "pack_r": (shape_of((slabs * part, 640), BF16), anywhere),
            "gsmall": (shape_of((16, D), F32), whole(16, D)),
        }
        scratch |= {name: vmem(shape, link) for name, shape in gathered.items()}
        scratch |= {
            "held_y": vmem((2, FEED_ROWS, D), BF16), "held_dy": vmem((2, FEED_ROWS, D), F32),
            "held_do": vmem((2, FEED_ROWS, D), BF16),
            "middle": vmem((rows, D), F32),
            "o": vmem((rows, D), BF16), "bias": vmem((1, FF), F32), "gwo": vmem((D, D), F32),
            "gwh": vmem((D, FF), F32), "gwr": vmem((D, FF), F32),
        }
    else:
        outs |= {name: (shape_of(shape, link), anywhere) for name, shape in gathered.items()}
        outs |= {
            "o": (shape_of((rows, D), BF16), tall), "bias": (shape_of((1, FF), F32), whole(1, FF)),
        }
        scratch["slots"] = vmem((rows, D), BF16)
    found = pl.pallas_call(
        functools.partial(front_kernel, count, joined, (*ins, *outs, *scratch)),
        grid=(2 * FRONT + (rows // FEED_ROWS if joined else 0),),
        in_specs=[spec for _, spec in ins.values()],
        out_specs=[spec for _, spec in outs.values()],
        out_shape=[shape for shape, _ in outs.values()],
        scratch_shapes=list(scratch.values())
        + gather_sems(count, True)
        + gather_sems(count, False) * 4
        + [dma((count,)), dma((count,)), dma((3, 2)), dma((3, 2)), dma((2,)), dma((2, 3)), dma((2, 3))],
        compiler_params=pltpu.CompilerParams(
            vmem_limit_bytes=62 * MIB, collective_id=1, has_side_effects=True
        ),
        name="front",
    )(*(a for a, _ in ins.values()))
    found = dict(zip(outs, found))
    if not joined:
        found |= feed(count, part, tokens, found, cotangent, link)
    return found


def feed(count, part, tokens, found, cotangent, link):
    rows, slabs = tokens.shape[0], 4 * count
    tall = pl.BlockSpec((256, D), lambda i: (i, 0))
    weights = [found[name] for name in ("wo_all", "wh_all", "wr_all")]
    names = ("y", "dy", "do", "pack", "pack_r", "gsmall")
    return dict(
        zip(
            names,
            pl.pallas_call(
                feed_kernel,
                grid=(rows // 256,),
                in_specs=[tall] * 3
                + [whole(8, D), whole(1, FF)]
                + [whole(*a.shape) for a in weights],
                out_specs=[tall] * 3
                + [whole(slabs * part, D), whole(slabs * part, 640), whole(16, D)],
                out_shape=[
                    shape_of((rows, D), BF16),
                    shape_of((rows, D), F32),
                    shape_of((rows, D), BF16),
                    shape_of((slabs * part, D), link),
                    shape_of((slabs * part, 640), link),
                    shape_of((16, D), F32),
                ],
                scratch_shapes=[
                    pltpu.VMEM((D, D), F32), pltpu.VMEM((D, FF), F32), pltpu.VMEM((D, FF), F32),
                ],
                compiler_params=PARAMS,
                name="feed",
            )(tokens, found["o"], cotangent, found["vec"], found["bias"], *weights),
        )
    )


def row_body(
    n, qkvf_ref, do_ref, p_ref, s_ref, z_ref, kept_ref, col, row, edge_ref,
    r_ref, dn_ref, dz_ref, head_ref, aside,
):
    first = edge_ref[pl.ds(0, 1)]
    before = edge_ref[pl.ds(8 + jnp.maximum(n - 1, 0), 1)]
    last = jnp.where(n == 0, first, before)
    vis = visible(col, row)
    carried = wide(flag(col, last), 2)
    slots = jnp.exp(qkvf_ref[:, 3 * D :].astype(F32)).astype(BF16)
    own = wide(flag(col, first), 2)
    states = [expand(kept_ref[0, 64:128, lanes_of(g)]).astype(BF16) for g in range(2)]

    def mixing(g):
        return masked(dot_nt(stacked(do_ref[:, lanes_of(g)]), part_of(qkvf_ref, 2, g)), vis)

    def to_reading(g, back_mix):
        lanes = lanes_of(g)
        back = select(dot(back_mix, slots[:, lanes]))
        return back + carried * dot_nt(do_ref[:, lanes], states[g])

    def to_scores(g, back_reading):
        lanes = lanes_of(g)
        probs, score, inverse = p_ref[:, lanes], s_ref[:, lanes], z_ref[:, lanes]
        shared = back_reading * inverse * probs
        back_score = shared - probs * head_sums(shared)
        back_numer = back_score * inverse * SCALE
        back_total = -(shared + back_score * score) * inverse
        reading = (probs * inverse).astype(BF16)
        r_ref[:, lanes] = reading
        dn_ref[:, lanes] = back_numer
        dz_ref[:, lanes] = back_total
        return back_numer, back_total, reading

    def to_state(g, back_numer, back_total, reading):
        lanes = lanes_of(g)
        head_ref[0:64, lanes] += compacted(
            dot_tn((own * back_numer).astype(BF16), part_of(qkvf_ref, 0, g))
        )
        head_ref[64:128, lanes] += compacted(
            dot_tn((own * reading.astype(F32)).astype(BF16), do_ref[:, lanes])
        )
        head_ref[128:129, lanes] += jnp.sum(own * back_total, axis=0, keepdims=True)

    back_mix = mixing(0)
    back_mix_two = mixing(1)
    aside()
    back_reading = to_reading(0, back_mix)
    back_reading_two = to_reading(1, back_mix_two)
    parts = to_scores(0, back_reading)
    to_state(0, *parts)
    parts = to_scores(1, back_reading_two)
    to_state(1, *parts)


def query_body(n, qkvf_ref, kept_ref, col, row, edge_ref, dn_ref, dq_ref):
    first = edge_ref[pl.ds(0, 1)]
    before = edge_ref[pl.ds(8 + jnp.maximum(n - 1, 0), 1)]
    last = jnp.where(n == 0, first, before)
    vis = visible(col, row)
    carried = wide(flag(col, last), 2)
    slots = jnp.exp(qkvf_ref[:, 3 * D :].astype(F32)).astype(BF16)
    lows = [dn_ref[:, lanes_of(g)].astype(BF16) for g in range(2)]
    states = [expand(kept_ref[0, 0:64, lanes_of(g)]).astype(BF16) for g in range(2)]

    def affine(g):
        return masked(dot_nt(stacked(lows[g]), slots[:, lanes_of(g)]), vis)

    def to_queries(g, back_affinity):
        out = select(dot(back_affinity, part_of(qkvf_ref, 1, g))) + carried * dot(lows[g], states[g])
        dq_ref[:, lanes_of(g)] = out.astype(BF16)

    one, two = affine(0), affine(1)
    to_queries(0, one)
    to_queries(1, two)


def column_body(
    n, qkvf_ref, do_ref, r_ref, dn_ref, dz_ref, col, row, edge_ref, state, snap, snap_rows, d_ref
):
    newest = edge_ref[15:16]
    after = edge_ref[pl.ds(jnp.minimum(n + 1, 7), 1)]
    following = jnp.where(n == 7, newest, after)
    first = edge_ref[pl.ds(n, 1)]
    vis = visible_back(col, row)
    carried = wide(flag(col, following), 2)
    own = wide(flag(col, first), 2)
    kept = jnp.where(following == first, 1.0, 0.0)[:, :GROUP]
    snap[n] = state[0:128].astype(BF16)
    snap_rows[pl.ds(n, 1)] = state[128:129]
    key_states = [expand(state[0:64, lanes_of(g)]).astype(BF16) for g in range(2)]
    value_states = [expand(state[64:128, lanes_of(g)]).astype(BF16) for g in range(2)]
    slots = jnp.exp(qkvf_ref[:, 3 * D :].astype(F32)).astype(BF16)
    numers = [dn_ref[:, lanes_of(g)] for g in range(2)]

    def mixing(g, apart):
        return masked(dot_nt(apart, r_ref[:, lanes_of(g)]), vis)

    def affine(g, apart):
        return masked(dot_nt(apart, numers[g].astype(BF16)), vis)

    def to_values(g, mix):
        lanes = lanes_of(g)
        out = select(dot(mix, do_ref[:, lanes])) + carried * dot(slots[:, lanes], value_states[g])
        d_ref[:, 2 * D + g * GROUP : 2 * D + (g + 1) * GROUP] = out.astype(BF16)

    def to_keys(g, back_affinity):
        lanes = lanes_of(g)
        out = select(dot(back_affinity, part_of(qkvf_ref, 0, g)))
        out = out + carried * dot(slots[:, lanes], key_states[g])
        d_ref[:, D + g * GROUP : D + (g + 1) * GROUP] = out.astype(BF16)

    def to_state(g):
        lanes = lanes_of(g)
        state[0:64, lanes] = kept * state[0:64, lanes] + compacted(
            dot_tn((own * numers[g]).astype(BF16), part_of(qkvf_ref, 0, g))
        )
        state[64:128, lanes] = kept * state[64:128, lanes] + compacted(
            dot_tn((own * r_ref[:, lanes].astype(F32)).astype(BF16), do_ref[:, lanes])
        )
        state[128:129, lanes] = kept * state[128:129, lanes] + jnp.sum(
            own * dz_ref[:, lanes], axis=0, keepdims=True
        )

    apart = stacked(slots[:, lanes_of(0)])
    mix = mixing(0, apart)
    back_affinity = affine(0, apart)
    apart = stacked(slots[:, lanes_of(1)])
    mix_two = mixing(1, apart)
    to_values(0, mix)
    affinity_two = affine(1, apart)
    to_keys(0, back_affinity)
    to_state(0)
    to_values(1, mix_two)
    to_keys(1, affinity_two)
    to_state(1)


def slot_body(n, qkvf_ref, do_ref, r_ref, dn_ref, dz_ref, col, row, edge_ref, snap, snap_rows, d_ref):
    newest = edge_ref[15:16]
    after = edge_ref[pl.ds(jnp.minimum(n + 1, 7), 1)]
    following = jnp.where(n == 7, newest, after)
    vis = visible_back(col, row)
    carried = wide(flag(col, following), 2)
    left = lane_heads(C, 128) == 0
    norm_state = snap_rows[pl.ds(n, 1)]
    key_states = [expand(snap[n, 0:64, lanes_of(g)]) for g in range(2)]
    value_states = [expand(snap[n, 64:128, lanes_of(g)]) for g in range(2)]

    def mixing(g):
        return masked(dot_nt(stacked(part_of(qkvf_ref, 2, g)), do_ref[:, lanes_of(g)]), vis)

    def affine(g):
        return masked(dot_nt(stacked(part_of(qkvf_ref, 1, g)), part_of(qkvf_ref, 0, g)), vis)

    def from_mix(g, back_mix):
        return select(dot(back_mix, r_ref[:, lanes_of(g)]))

    def from_affinity(g, affinity):
        high, low = split(dn_ref[:, lanes_of(g)])
        parts = []
        for p in range(2):
            pair = slice(p * 128, (p + 1) * 128)
            both = dot(
                affinity[p * 512 : (p + 1) * 512],
                jnp.concatenate([high[:, pair], low[:, pair]], axis=1),
            )
            both = both[:, :128] + both[:, 128:]
            parts.append(jnp.where(left, both[:C], both[C:]))
        return jnp.concatenate(parts, axis=1)

    def from_totals():
        high, low = split(dz_ref[...])
        return dot(vis, high) + dot(vis, low)

    def from_state(g):
        return carried * (
            dot_nt(part_of(qkvf_ref, 1, g), key_states[g])
            + dot_nt(part_of(qkvf_ref, 2, g), value_states[g])
            + norm_state[:, lanes_of(g)]
        )

    def to_slots(g, back_slots):
        written = jnp.exp(part_of(qkvf_ref, 3, g).astype(F32))
        d_ref[:, 3 * D + g * GROUP : 3 * D + (g + 1) * GROUP] = (back_slots * written).astype(BF16)

    norm = from_totals()
    mix = mixing(0)
    affinity = affine(0)
    mix_two = mixing(1)
    total = from_mix(0, mix)
    affinity_two = affine(1)
    total = total + from_affinity(0, affinity)
    total_two = from_mix(1, mix_two)
    to_slots(0, total + norm[:, lanes_of(0)] + from_state(0))
    total_two = total_two + from_affinity(1, affinity_two)
    to_slots(1, total_two + norm[:, lanes_of(1)] + from_state(1))


class Scatter:
    def __init__(self, count, source, own, axes, direct, out, buffers):
        self.axes, self.direct, self.out = axes, direct, out
        self.seq, self.at, self.sibling, self.beside = places()
        self.source, self.own = source, own
        self.core = lax.rem(self.seq, 2)
        self.total, self.local, self.last, self.done = buffers[:4]
        self.stages = []
        size = source.shape[0]
        base = 0
        for n, axis in enumerate(axes):
            ways = {"core": 2, "x": 2, "y": 2, "z": count // 2, "all": count}[axis]
            size = size // ways
            me = {
                "core": self.core, "x": self.seq // 2, "y": lax.rem(self.at, 2), "z": self.at // 2,
                "all": self.at,
            }[axis]
            held = source
            if own is not None and n > 0:
                held = own
            come, sems = buffers[4 + 2 * n], buffers[5 + 2 * n]
            self.stages.append((axis, ways, size, base, me, held, come, sems))
            if own is None or n > 0:
                base = base + me * size

    def copies(self, n, halves=(0, 1)):
        axis, ways, size, base, me, held, come, sems = self.stages[n]
        if axis == "x":
            for half in halves:
                first, some = half * (size // 2), size // 2
                yield push(
                    held.at[pl.ds(base + (me ^ 1) * size + first, some)],
                    come.at[0, pl.ds(first, some)],
                    sems.at[0, half], sems.at[1, half], seq=self.beside,
                )
            return
        for k in range(1, ways):
            if axis == "core":
                device = {"seq": self.sibling}
            else:
                device = {"fsdp": self.at ^ (2 * k if axis == "z" else k)}
            yield push(
                held.at[pl.ds(base + (me ^ k) * size, size)], come.at[k - 1],
                sems.at[0, k - 1], sems.at[1, k - 1], **device,
            )

    def copy_own(self):
        size = self.source.shape[0] // 2
        return pltpu.make_async_copy(
            self.source.at[pl.ds(self.core * size, size)], self.own, self.local
        )

    def start(self):
        for copy in self.copies(0):
            copy.start()
        if self.own is not None:
            self.copy_own().start()

    def advance(self, n, halves=(0, 1)):
        axis, ways, size, base, me, held, come, sems = self.stages[n]
        for copy in self.copies(n):
            copy.wait_recv()
        mine = held
        first = base + me * size
        if n == 0 and self.own is not None:
            self.copy_own().wait()
            mine, first = self.own, 0

        def added(slab):
            total = mine[first + slab].astype(F32)
            for k in range(1, ways):
                total = total + come[k - 1, slab].astype(F32)
            return total

        if n + 1 == len(self.stages):
            self.total[...] = added(0)
            self.copy_done().start()
            for copy in self.sent():
                copy.start()
            return

        @pl.loop(0, size)
        def _(slab):
            mine[first + slab] = added(slab).astype(mine.dtype)

        for copy in self.copies(n + 1, halves):
            copy.start()

    def copy_done(self):
        return pltpu.make_async_copy(self.total, self.out.at[self.seq], self.done)

    def sent(self):
        other = lax.rem(self.sibling + 2, 4)
        for n, target in enumerate((self.sibling, self.beside, other)[: 3 if self.direct else 2]):
            yield push(
                self.total, self.out.at[self.seq], self.last.at[0, n], self.last.at[1, n], seq=target
            )

    def forwarded(self, source):
        here = self.out.at[source]
        return push(here, here, self.last.at[0, 2], self.last.at[1, 2], seq=self.sibling)

    def come_in(self, n, source):
        here = self.out.at[source]
        return push(here, here, self.last.at[0, n], self.last.at[1, n], seq=source)

    def forward(self):
        self.come_in(1, self.beside).wait_recv()
        self.forwarded(self.beside).start()

    def finish(self):
        other = lax.rem(self.sibling + 2, 4)
        self.come_in(0, self.sibling).wait_recv()
        if self.direct:
            self.come_in(1, self.beside).wait_recv()
        else:
            self.forwarded(self.beside).wait_send()
        self.forwarded(other).wait_recv()
        self.copy_done().wait()
        for copy in self.sent():
            copy.wait_send()
        for n in range(len(self.stages)):
            for copy in self.copies(n):
                copy.wait_send()


def scatter_scratch(count, part, lanes, link, axes, hbm):
    vmem, dma = pltpu.VMEM, pltpu.SemaphoreType.DMA
    size = 2 * 4 * count // 2
    out = [vmem((size // 2, part, lanes), link)] if hbm else []
    out += [vmem((part, lanes), F32), dma, dma((2, 3)), dma]
    for axis in axes:
        ways = {"core": 2, "x": 2, "y": 2, "z": count // 2, "all": count}[axis]
        size = size // ways
        out += [vmem((ways - 1, size, part, lanes), link), dma((2, max(ways - 1, 2)))]
    return out


OVER_X = ("core", "x", "y", "z")
OVER_Y = ("core", "y", "x", "z")
SHORT = ("core", "x", "all")


class SmallSum:
    def __init__(self, count, mine, from_seq, half, from_fsdp, sems):
        self.count, self.mine, self.from_seq = count, mine, from_seq
        self.half, self.from_fsdp, self.sems = half, from_fsdp, sems
        self.seq, self.at, _, _ = places()

    def lanes(self, owner):
        if self.from_fsdp.shape[2] == D:
            return pl.ds(0, D)
        first = owner * (D // self.count) // 128 * 128
        return pl.ds(pl.multiple_of(first, 128), 128)

    def over_seq(self, k, slot):
        return push(
            self.mine, self.from_seq.at[slot], self.sems[0].at[0, k], self.sems[0].at[1, k],
            seq=self.seq ^ k,
        )

    def over_fsdp(self, k):
        return push(
            self.half.at[:, self.lanes(self.at ^ k)], self.from_fsdp.at[self.at],
            self.sems[1].at[0, k], self.sems[1].at[1, k], fsdp=self.at ^ k,
        )

    def fsdp_in(self, k):
        here = self.from_fsdp.at[self.at ^ k]
        return push(here, here, self.sems[1].at[0, k], self.sems[1].at[1, k], fsdp=self.at ^ k)

    def start(self):
        for k in range(1, 4):
            self.over_seq(k, self.seq).start()
        self.from_seq[self.seq] = self.mine[...]

    def second(self):
        for k in range(1, 4):
            self.over_seq(k, self.seq ^ k).wait_recv()
        total = self.from_seq[0]
        for n in range(1, 4):
            total = total + self.from_seq[n]
        self.half[...] = total
        for k in range(1, self.count):
            self.over_fsdp(k).start()
        self.from_fsdp[self.at] = self.half[:, self.lanes(self.at)]

    def finish(self, out_ref):
        for k in range(1, self.count):
            self.fsdp_in(k).wait_recv()
        total = self.from_fsdp[0]
        for n in range(1, self.count):
            total = total + self.from_fsdp[n]
        out_ref[...] = total
        for k in range(1, 4):
            self.over_seq(k, self.seq).wait_send()
        for k in range(1, self.count):
            self.over_fsdp(k).wait_send()


def small_scratch(count, rows, lanes):
    vmem, dma = pltpu.VMEM, pltpu.SemaphoreType.DMA
    return [
        vmem((4, rows, D), F32), vmem((rows, D), F32), vmem((count, rows, lanes), F32),
        dma((2, 4)), dma((2, count)),
    ]


QUERY, COLUMN, SLOT, INPUT = 8, 16, 24, 32


def back_kernel(
    count, per, x_ref, xs_ref, qkvf_ref, do_ref, p_ref, s_ref, z_ref, kept_ref, dy_ref, doc_ref,
    small_ref, w_ref, ffg_ref, ffr_ref, ffs_ref,
    gi_ref, ff_out, fr_out, q_out, kv_out, f_out, s1_out, s2_out,
    gi_held, gi_sem, scores, scores_sem, d_all, h_turned, reading, numer, total, col_ref, edge_ref, head, state, heads, head_rows,
    snap, snap_rows, w_held, w_sem, q_piece, kv_piece, f_piece, last_small, *rest,
):
    step = pl.program_id(0)
    seq, at, _, _ = places()
    link = q_piece.dtype

    def take(size):
        nonlocal rest
        out, rest = rest[:size], rest[size:]
        return out

    (own,) = take(1)
    ff = Scatter(count, ffg_ref, own, OVER_X, False, ff_out, take(12))
    (own,) = take(1)
    fr = Scatter(count, ffr_ref, own, OVER_Y, False, fr_out, take(12))
    for_q = Scatter(count, q_piece, None, OVER_X, False, q_out, take(12))
    for_kv = Scatter(count, kv_piece, None, OVER_X, False, kv_out, take(12))
    for_f = Scatter(count, f_piece, None, SHORT, True, f_out, take(10))
    small_one = SmallSum(count, ffs_ref, *take(3), take(2))
    small_two = SmallSum(count, last_small, *take(3), take(2))
    states = States(heads, head_rows, take(2))

    def chunk(u, first, turned=False):
        n = step * per + u - first
        n = 7 - n if turned else n
        here = pl.ds(pl.multiple_of(n * C, C), C)
        block = pl.ds(pl.multiple_of((per - 1 - u if turned else u) * C, C), C)
        return n, here, block, col_ref[here], doc_ref[:, here].astype(F32)

    def fetch():
        return pltpu.make_async_copy(w_ref, w_held, w_sem)

    def fetch_scores(n):
        slot, here = lax.rem(n, 2), pl.ds(pl.multiple_of(n * per * C, per * C), per * C)
        return [
            pltpu.make_async_copy(ref.at[here], scores.at[slot, k], scores_sem.at[slot, k])
            for k, ref in enumerate((p_ref, s_ref, z_ref))
        ]

    def give(n):
        here = pl.ds(pl.multiple_of(n * per * C, per * C), per * C)
        slot = lax.rem(n, 2)
        return pltpu.make_async_copy(gi_held.at[slot], gi_ref.at[here], gi_sem.at[slot])

    def weight_grad(piece, d_lanes, lanes, short=False):
        grad = dot(h_turned[...], d_all[:, d_lanes])
        half, part = count // 2, piece.shape[1]
        for q in range(4):
            x, c = q // 2, q % 2
            share = grad[:, q * 128 : (q + 1) * 128].reshape(half, 2, part, 128).astype(link)
            if short:
                first = (c * 2 + x) * count
                piece[first : first + count, :, lanes] = share.reshape(count, part, 128)
                continue
            for y in range(2):
                first = ((c * 2 + x) * 2 + y) * half
                piece[first : first + half, :, lanes] = share[:, y]

    @pl.when(step == 0)
    def _():
        greet(count)
        for n in range(2):
            for copy in fetch_scores(n):
                copy.start()
        fetch().start()
        doc_parts(doc_ref, col_ref, edge_ref)
        head[...] = jnp.zeros_like(head)
        last_small[...] = jnp.zeros_like(last_small)

    def turn():
        weight_grad(q_piece, slice(0, D), slice(0, 128))
        for_q.start()
        states.finish()
        newest = edge_ref[15:16]
        state[...] = jnp.zeros_like(state)
        for n in range(4):
            use = jnp.where(head_rows[n, 1:2] == newest, 1.0, 0.0) * (n > seq).astype(F32)
            state[0:128] += use * heads[n].astype(F32)
            state[128:129] += use * head_rows[n, 0:1]

    def send_states():
        heads[seq] = head[0:128].astype(link)
        head_rows[seq, 0:1] = head[128:129]
        head_rows[seq, 1:2] = edge_ref[0:1]
        head_rows[seq, 2:8] = jnp.zeros((6, D), F32)
        states.start()

    def key_value_grads():
        weight_grad(kv_piece, slice(D, 2 * D), slice(0, 128))
        weight_grad(kv_piece, slice(2 * D, 3 * D), slice(128, 256))
        for_kv.start()

    def slot_grads():
        weight_grad(f_piece, slice(3 * D, 4 * D), slice(0, 128), True)
        for_f.start()

    def last():
        small_two.start()
        small_one.finish(s1_out)
        for piece in (ff, for_q):
            piece.forward()
        small_two.second()
        for_f.advance(2)
        for_kv.forward()
        for piece in (ff, fr, for_q):
            piece.finish()
        states.drain()
        small_two.finish(s2_out)
        for_kv.finish()
        for_f.finish()
        for n in (8 // per - 2, 8 // per - 1):
            give(n).wait()

    def rest_of_ff():
        for copy in ff.copies(1, (1,)):
            copy.start()

    def begin():
        met(count)
        ff.start()
        small_one.start()

    schedule = {
        0: [begin],
        1: [fr.start],
        3: [lambda: ff.advance(0, (0,)), small_one.second],
        5: [lambda: fr.advance(0)],
        QUERY - 1: [send_states],
        QUERY + 5: [states.forward, rest_of_ff],
        QUERY + 7: [turn],
        COLUMN + 1: [lambda: fr.advance(1), lambda: for_q.advance(0)],
        COLUMN + 2: [lambda: ff.advance(1)],
        COLUMN + 6: [lambda: fr.advance(2)],
        SLOT: [lambda: ff.advance(2)],
        COLUMN + 7: [key_value_grads, lambda: for_q.advance(1)],
        SLOT + 1: [lambda: for_kv.advance(0), lambda: for_q.advance(2)],
        SLOT + 6: [lambda: for_kv.advance(1), lambda: fr.advance(3)],
        SLOT + 7: [slot_grads],
        INPUT + 1: [lambda: for_f.advance(0), lambda: for_kv.advance(2)],
        INPUT + 3: [lambda: ff.advance(3), lambda: for_q.advance(3), fr.forward],
        INPUT + 5: [lambda: for_f.advance(1), lambda: for_kv.advance(3)],
        INPUT + 7: [last],
    }

    @pl.when(step < QUERY // per)
    def _():
        for copy in fetch_scores(step):
            copy.wait()

    @pl.loop(0, per)
    def _(u):
        at_chunk = step * per + u

        @pl.when(at_chunk < QUERY)
        def _():
            n, here, block, col, row = chunk(u, 0)
            kept_scores = [scores.at[lax.rem(step, 2), k, block] for k in range(3)]

            def aside():
                unit, _ = norm_parts(x_ref[block].astype(F32))
                h_turned[:, here] = (unit * small_ref[0:1] + small_ref[1:2]).astype(BF16).T

            row_body(
                n, qkvf_ref.at[block], do_ref.at[block], *kept_scores, kept_ref.at[pl.ds(u, 1)],
                col, row, edge_ref,
                reading.at[here], numer.at[here], total.at[here], head, aside,
            )

        @pl.when((at_chunk >= QUERY) & (at_chunk < COLUMN))
        def _():
            n, here, block, col, row = chunk(u, QUERY)
            query_body(
                n, qkvf_ref.at[block], kept_ref.at[pl.ds(u, 1)], col, row, edge_ref,
                numer.at[here], d_all.at[here, 0:D],
            )

        @pl.when((at_chunk >= COLUMN) & (at_chunk < SLOT))
        def _():
            n, here, block, col, row = chunk(u, COLUMN, True)
            column_body(
                n, qkvf_ref.at[block], do_ref.at[block], reading.at[here], numer.at[here],
                total.at[here], col, row, edge_ref, state, snap, snap_rows, d_all.at[here],
            )

        @pl.when((at_chunk >= SLOT) & (at_chunk < INPUT))
        def _():
            n, here, block, col, row = chunk(u, SLOT, True)
            slot_body(
                n, qkvf_ref.at[block], do_ref.at[block], reading.at[here], numer.at[here],
                total.at[here], col, row, edge_ref, snap, snap_rows, d_all.at[here],
            )

        @pl.when((at_chunk >= INPUT) & (u == 0))
        def _():
            nth = step - INPUT // per

            @pl.when(nth >= 2)
            def _():
                give(nth - 2).wait()

            @pl.when(nth == 0)
            def _():
                fetch().wait()

            size = xs_ref.shape[0]
            here = pl.ds(pl.multiple_of(nth * size, size), size)
            grad = dot_nt(d_all[here], w_held[...])
            unit, scale = norm_parts(xs_ref[...].astype(F32))
            last_small[0:1] += jnp.sum(grad * unit, axis=0, keepdims=True)
            last_small[1:2] += jnp.sum(grad, axis=0, keepdims=True)
            gi_held[lax.rem(nth, 2)] = dy_ref[...] + norm_back(unit, scale, small_ref[0:1], grad)
            give(nth).start()

        for when, actions in schedule.items():

            @pl.when(at_chunk == when)
            def _(actions=actions):
                for action in actions:
                    action()

    @pl.when(step + 2 < QUERY // per)
    def _():
        for copy in fetch_scores(step + 2):
            copy.start()


def back(
    count, tokens, qkvf, do, probs, score, inverse, kept, dy, doc_ids, small, w_all, ffg, ffr, ffs
):
    rows = tokens.shape[0]
    part, link = ffg.shape[1], ffg.dtype
    per = 2 if link == BF16 else 1
    size = per * C
    blocks = 8 // per
    once = lambda a: pl.BlockSpec(a.shape, lambda i: (0,) * a.ndim)
    anywhere = pl.BlockSpec(memory_space=pl.ANY)
    vmem, dma = pltpu.VMEM, pltpu.SemaphoreType.DMA

    def early(i):
        return jnp.minimum(i, blocks - 1)

    def twice(i):
        return jnp.where(i < blocks, i, jnp.clip(i - blocks, 0, blocks - 1))

    def turned(i):
        return blocks - 1 - lax.rem(jnp.clip(i - 2 * blocks, 0, 2 * blocks - 1), blocks)

    def always(i):
        return jnp.where(i < 2 * blocks, twice(i), turned(i))

    def both(i):
        return jnp.where(i < blocks, i, turned(i))

    late = lambda i: (jnp.maximum(i - 4 * blocks, 0), 0)
    tall = pl.BlockSpec((size, D), late)
    some = lambda lanes, order: pl.BlockSpec((size, lanes), lambda i: (order(i), 0))
    slabs = 4 * count
    return pl.pallas_call(
        functools.partial(back_kernel, count, per),
        grid=(5 * blocks,),
        in_specs=[some(D, early), tall, some(4 * D, always), some(D, both)]
        + [anywhere] * 3
        + [pl.BlockSpec((per, 128, D), lambda i: (twice(i), 0, 0)), tall]
        + [once(doc_ids), once(small), anywhere, anywhere, anywhere, once(ffs)],
        out_specs=[anywhere] * 6 + [whole(16, D), whole(8, 128)],
        out_shape=[
            shape_of((rows, D), F32),
            shape_of((4, part, D), F32),
            shape_of((4, part, 640), F32),
            shape_of((4, part, 128), F32),
            shape_of((4, part, 256), F32),
            shape_of((4, part, 128), F32),
            shape_of((16, D), F32),
            shape_of((8, 128), F32),
        ],
        scratch_shapes=[
            vmem((2, size, D), F32),
            dma((2,)),
            vmem((2, 3, size, D), F32),
            dma((2, 3)),
            vmem((rows, 4 * D), BF16),
            vmem((D, rows), BF16),
            vmem((rows, D), BF16),
            vmem((rows, D), F32),
            vmem((rows, D), F32),
            vmem((rows, 128), F32),
            vmem((16, D), F32),
            vmem((136, D), F32),
            vmem((136, D), F32),
            vmem((4, 128, D), link),
            vmem((4, 8, D), F32),
            vmem((8, 128, D), BF16),
            vmem((8, D), F32),
            vmem(w_all.shape, BF16),
            dma,
            vmem((slabs, part, 128), link),
            vmem((slabs, part, 256), link),
            vmem((slabs, part, 128), link),
            vmem((8, D), F32),
        ]
        + scatter_scratch(count, part, D, link, OVER_X, True)
        + scatter_scratch(count, part, 640, link, OVER_Y, True)
        + scatter_scratch(count, part, 128, link, OVER_X, False)
        + scatter_scratch(count, part, 256, link, OVER_X, False)
        + scatter_scratch(count, part, 128, link, SHORT, False)
        + small_scratch(count, 16, D)
        + small_scratch(count, 8, 128)
        + [dma((3, 2)), dma((3, 2))],
        compiler_params=pltpu.CompilerParams(
            vmem_limit_bytes=(62 if link == BF16 else 63) * MIB, collective_id=2, has_side_effects=True
        ),
        name="back",
    )(
        tokens, tokens, qkvf, do, probs, score, inverse, kept, dy, doc_ids, small, w_all, ffg, ffr,
        ffs,
    )


def finish_kernel(count, part, *refs):
    at = lax.axis_index("fsdp")
    y_ref, gi_ref, *sums = refs[:7]
    s1_ref, s2_ref, y_out, gi_out, *rest = refs[7:]
    outs, (held_y, held, *rest) = rest[:13], rest[13:]
    ff_ref, fr_ref, q_ref, kv_ref, f_ref = rest[:5]
    staged, sems, sum_sems = rest[5:12], rest[12], rest[13]

    def move(n, out):
        source, through, target, here = gi_ref, held, gi_out, pl.ds(n * 512, 512)
        if n >= 4:
            source, through, target, here = y_ref, held_y, y_out, pl.ds((n - 4) * 1024, 1024)
        if out:
            return pltpu.make_async_copy(through.at[here], target.at[here], sems.at[1, n])
        return pltpu.make_async_copy(source.at[here], through.at[here], sems.at[0, n])

    def bring(n):
        return pltpu.make_async_copy(sums[n], rest[n], sum_sems.at[0, n])

    def give(n):
        return pltpu.make_async_copy(staged[n], outs[n], sum_sems.at[1, n])

    def pick(row, size):
        out = row(0, size)
        for f in range(1, count):
            out = jnp.where(at == f, row(f * size, size), out)
        return out

    def bias(start, size):
        r = start // D
        return s1_ref[8 + r : 9 + r, start - r * D : start - r * D + size]

    def row_of_sums(ref, n):
        return lambda start, size: ref[
            n : n + 1, start % ref.shape[1] : start % ref.shape[1] + size
        ]

    for n in range(5):
        bring(n).start()
    for n in range(6):
        move(n, False).start()
    for n in range(5):
        bring(n).wait()
    for n in range(4):
        lanes = slice(n * 128, (n + 1) * 128)
        staged[0][:, lanes] = q_ref[n]
        staged[1][:, lanes] = kv_ref[n, :, 0:128]
        staged[2][:, lanes] = kv_ref[n, :, 128:256]
        staged[3][:, lanes] = f_ref[n]
        staged[4][:, lanes] = fr_ref[n, :, 512:640]
        staged[5][:, n * 512 : (n + 1) * 512] = ff_ref[n]
        for j in range(4):
            staged[6][j * part : (j + 1) * part, lanes] = fr_ref[n, :, j * 128 : (j + 1) * 128]
    for n in range(7):
        give(n).start()
    for n in range(6):
        move(n, False).wait()
        move(n, True).start()
    outs[7][...] = pick(row_of_sums(s2_ref, 0), part)
    outs[8][...] = pick(row_of_sums(s2_ref, 1), part)
    outs[9][...] = pick(row_of_sums(s1_ref, 2), part)
    outs[10][...] = pick(row_of_sums(s1_ref, 3), part)
    outs[11][...] = pick(bias, 4 * part)
    outs[12][...] = pick(row_of_sums(s1_ref, 4), part)
    for n in range(7):
        give(n).wait()
    for n in range(6):
        move(n, True).wait()


def finish(count, part, out, grad_input, *sums):
    once = lambda shape: pl.BlockSpec(shape, lambda: (0,) * len(shape))
    anywhere = pl.BlockSpec(memory_space=pl.ANY)
    vmem, dma = pltpu.VMEM, pltpu.SemaphoreType.DMA
    large = [(part, D)] * 5 + [(part, FF), (4 * part, D)]
    small = [(1, part)] * 4 + [(1, 4 * part), (1, part)]
    return pl.pallas_call(
        functools.partial(finish_kernel, count, part),
        in_specs=[anywhere] * 7 + [once(a.shape) for a in sums[5:]],
        out_specs=[anywhere] * 9 + [once(s) for s in small],
        out_shape=[shape_of(out.shape, BF16)]
        + [shape_of(s, F32) for s in (grad_input.shape, *large, *small)],
        scratch_shapes=[vmem(out.shape, BF16), vmem(grad_input.shape, F32)]
        + [vmem(a.shape, F32) for a in sums[:5]]
        + [vmem(s, F32) for s in large]
        + [dma((2, 6)), dma((2, 7))],
        compiler_params=PARAMS,
        name="finish",
    )(out, grad_input, *sums)


def rows_of(lanes, order=lambda i: i):
    return pl.BlockSpec((C, lanes), lambda i: (order(i), 0))


def whole(*shape):
    return pl.BlockSpec(shape, lambda i: (0,) * len(shape))


def row_of(order=lambda i: i):
    return pl.BlockSpec((1, C), lambda i: (0, order(i)))


def shape_of(shape, kind):
    return jax.ShapeDtypeStruct(shape, kind)


PARAMS = pltpu.CompilerParams(vmem_limit_bytes=62 * MIB)


def on_device(
    tokens, doc_ids, w_query, w_key, w_value, w_slots, w_output, w_hidden, w_return,
    gain_first, shift_first, gain_second, shift_second, bias_hidden, bias_return, cotangent,
):
    rows = tokens.shape[0]
    count = lax.axis_size("fsdp")
    part = gain_first.shape[0]
    flat = lambda a: a.reshape(1, a.shape[0])
    found = front(
        count, tokens, doc_ids,
        (w_query, w_key, w_value, w_slots, w_output, w_hidden, w_return),
        [flat(a) for a in (gain_first, shift_first, gain_second, shift_second, bias_return)],
        flat(bias_hidden), cotangent,
    )
    grad_input, *sums = back(
        count, tokens, *(found[name] for name in ("qkvf_out", "do", "p", "s", "z", "kept", "dy")),
        doc_ids, found["vec"], found["w_out"].reshape(D, 4 * D).astype(BF16),
        found["pack"].reshape(-1, part, D), found["pack_r"].reshape(-1, part, 640), found["gsmall"],
    )
    out, grad_input, *grads = finish(count, part, found["y"], grad_input, *sums)
    return (out, grad_input, *grads[:7], *(a.reshape(-1) for a in grads[7:]))


def solution(mesh):
    tall, flat, one = P(("fsdp", "seq"), None), P("fsdp", None), P("fsdp")
    return jax.shard_map(
        on_device,
        mesh=mesh,
        in_specs=(tall, P("fsdp", "seq")) + (flat,) * 7 + (one,) * 6 + (tall,),
        out_specs=(tall, tall) + (flat,) * 7 + (one,) * 6,
        check_vma=False,
    )
```

```python
import functools
import types

import jax
import jax.numpy as jnp
from jax import lax
from jax.experimental import pallas as pl
from jax.experimental.pallas import tpu as pltpu
from jax.sharding import PartitionSpec as P

D = 512
H = 8
M = 64
FF = 2048
C = 256
GROUP = 256
EPS = 1e-05
SCALE = 0.125
F32 = jnp.float32
BF16 = jnp.bfloat16
FEED_ROWS = 512
FEED_LANES = 256
FRONT = 4
MIB = 1024 * 1024


def dot(a, b):
    return lax.dot_general(a, b, (((1,), (0,)), ((), ())), preferred_element_type=F32)


def dot_nt(a, b):
    return lax.dot_general(a, b, (((1,), (1,)), ((), ())), preferred_element_type=F32)


def dot_tn(a, b):
    return lax.dot_general(a, b, (((0,), (0,)), ((), ())), preferred_element_type=F32)


def lane_heads(rows, lanes):
    return lax.broadcasted_iota(jnp.int32, (rows, lanes), 1) // M


def stacked(values):
    heads = lane_heads(C, GROUP)
    zero = jnp.zeros_like(values)
    return jnp.concatenate([jnp.where(heads == h, values, zero) for h in range(4)], axis=0)


def select(values):
    heads = lane_heads(C, GROUP)
    out = values[3 * C :]
    for h in (2, 1, 0):
        out = jnp.where(heads == h, values[h * C : (h + 1) * C], out)
    return out


def masked(values, mask):
    return jnp.concatenate(
        [values[h * C : (h + 1) * C].astype(BF16) * mask for h in range(4)], axis=0
    )


def expand(compact):
    rows = lax.broadcasted_iota(jnp.int32, (GROUP, GROUP), 0) // M
    full = jnp.concatenate([compact] * 4, axis=0)
    return jnp.where(rows == lane_heads(GROUP, GROUP), full, jnp.zeros_like(full))


def compacted(full):
    heads = lane_heads(M, GROUP)
    out = full[3 * M :]
    for h in (2, 1, 0):
        out = jnp.where(heads == h, full[h * M : (h + 1) * M], out)
    return out


def split(values):
    high = values.astype(BF16)
    return high, (values - high.astype(F32)).astype(BF16)


def ones_block():
    rows = lax.broadcasted_iota(jnp.int32, (GROUP, GROUP), 0) // M
    return (rows == lane_heads(GROUP, GROUP)).astype(BF16)


def head_sums(values):
    high, low = split(values)
    ones = ones_block()
    return dot(high, ones) + dot(low, ones)


def head_max(values):
    left = lane_heads(C, 128) == 0
    out = []
    for p in range(2):
        pair = values[:, p * 128 : (p + 1) * 128]
        one = jnp.max(jnp.where(left, pair, -jnp.inf), axis=1, keepdims=True)
        two = jnp.max(jnp.where(left, -jnp.inf, pair), axis=1, keepdims=True)
        out.append(jnp.where(left, one, two))
    return jnp.concatenate(out, axis=1)


def wide(values, times):
    return jnp.concatenate([values] * times, axis=1)


def visible(doc_col, doc_row):
    same = wide(doc_col, 2) == doc_row
    here = lax.broadcasted_iota(jnp.int32, (C, C), 0)
    there = lax.broadcasted_iota(jnp.int32, (C, C), 1)
    return jnp.where(same & (here >= there), 1.0, 0.0).astype(BF16)


def visible_back(doc_col, doc_row):
    same = wide(doc_col, 2) == doc_row
    here = lax.broadcasted_iota(jnp.int32, (C, C), 0)
    there = lax.broadcasted_iota(jnp.int32, (C, C), 1)
    return jnp.where(same & (there >= here), 1.0, 0.0).astype(BF16)


def flag(doc_col, doc):
    return jnp.where(doc_col == doc[:, :128], 1.0, 0.0)


def norm_parts(values):
    centre = jnp.mean(values, axis=-1, keepdims=True)
    centred = values - centre
    spread = jnp.mean(centred * centred, axis=-1, keepdims=True)
    scale = lax.rsqrt(spread + EPS)
    return centred * scale, scale


def norm_back(unit, scale, gain, grad):
    inner = grad * gain
    return scale * (
        inner
        - jnp.mean(inner, axis=-1, keepdims=True)
        - unit * jnp.mean(inner * unit, axis=-1, keepdims=True)
    )


def groups(values):
    return values[:, :GROUP], values[:, GROUP:]


def state_terms(slots, left, right):
    one, two = [], []
    for g in range(2):
        lanes = slice(g * GROUP, (g + 1) * GROUP)
        both = dot_tn(slots[:, lanes], jnp.concatenate([left[:, lanes], right[:, lanes]], axis=1))
        one.append(compacted(both[:, :GROUP]))
        two.append(compacted(both[:, GROUP:]))
    return jnp.concatenate(one, axis=1), jnp.concatenate(two, axis=1)


def lanes_of(g):
    return slice(g * GROUP, (g + 1) * GROUP)


def part_of(ref, part, g):
    return ref[:, part * D + g * GROUP : part * D + (g + 1) * GROUP]


def affinities(qkvf_ref, g, vis):
    return masked(dot_nt(stacked(part_of(qkvf_ref, 0, g)), part_of(qkvf_ref, 1, g)), vis)


def attend_body(
    n, qkvf_ref, slots, vis, affine_ref, col, edge_ref, state, o_ref, p_ref, s_ref, z_ref, kept_ref
):
    kept_ref[0] = state[0:128]
    first = edge_ref[pl.ds(0, 1)]
    before = edge_ref[pl.ds(8 + jnp.maximum(n - 1, 0), 1)]
    last = jnp.where(n == 0, first, before)
    newest = edge_ref[pl.ds(8 + n, 1)]
    carried = wide(flag(col, last), 2)
    norm = dot(vis, slots)
    key_states = [expand(state[0:64, lanes_of(g)]).astype(BF16) for g in range(2)]
    value_states = [expand(state[64:128, lanes_of(g)]).astype(BF16) for g in range(2)]
    norm_state = state[128:129]

    def scores(g, affinity):
        lanes = lanes_of(g)
        numer = select(dot(affinity, slots[:, lanes]))
        numer = numer + carried * dot_nt(part_of(qkvf_ref, 0, g), key_states[g])
        inverse = 1.0 / (norm[:, lanes] + carried * norm_state[:, lanes])
        return numer * inverse * SCALE, inverse

    def grow(score):
        return jnp.exp(score - head_max(score))

    def read(g, score, inverse, grown):
        lanes = lanes_of(g)
        probs = grown / head_sums(grown)
        p_ref[:, lanes] = probs
        s_ref[:, lanes] = score
        z_ref[:, lanes] = inverse
        return (probs * inverse).astype(BF16)

    def mixing(g, reading):
        return masked(dot_nt(stacked(reading), slots[:, lanes_of(g)]), vis)

    def mixed(g, reading, mix):
        out = select(dot(mix, part_of(qkvf_ref, 2, g))) + carried * dot(reading, value_states[g])
        o_ref[:, lanes_of(g)] = out.astype(BF16)

    score, inverse = scores(0, affine_ref[...])
    affinity = affinities(qkvf_ref, 1, vis)
    grown = grow(score)
    score_two, inverse_two = scores(1, affinity)
    reading = read(0, score, inverse, grown)
    tail = wide(flag(col, newest), 4).astype(BF16) * slots
    new_keys, new_values = state_terms(tail, qkvf_ref[:, D : 2 * D], qkvf_ref[:, 2 * D : 3 * D])
    same = jnp.where(last == newest, 1.0, 0.0)
    state[0:64] = same * state[0:64] + new_keys
    state[64:128] = same * state[64:128] + new_values
    state[128:129] = same * state[128:129] + jnp.sum(tail.astype(F32), axis=0, keepdims=True)
    grown = grow(score_two)
    mix = mixing(0, reading)
    reading_two = read(1, score_two, inverse_two, grown)
    mixed(0, reading, mix)
    mix = mixing(1, reading_two)
    mixed(1, reading_two, mix)


MESH_ID = pl.DeviceIdType.MESH


def places():
    seq, at = lax.axis_index("seq"), lax.axis_index("fsdp")
    core = lax.rem(seq, 2)
    return seq, at, seq + 1 - 2 * core, lax.rem(seq + 2, 4)


def push(src, dst, send, recv, **device):
    return pltpu.make_async_remote_copy(
        src_ref=src, dst_ref=dst, send_sem=send, recv_sem=recv,
        device_id=device, device_id_type=MESH_ID,
    )


def greet(count):
    seq, at, _, _ = places()
    barrier = pltpu.get_barrier_semaphore()
    for k in range(1, count):
        pl.semaphore_signal(barrier, inc=1, device_id={"fsdp": at ^ k}, device_id_type=MESH_ID)
    for k in range(1, 4):
        pl.semaphore_signal(barrier, inc=1, device_id={"seq": seq ^ k}, device_id_type=MESH_ID)


def met(count):
    pl.semaphore_wait(pltpu.get_barrier_semaphore(), count - 1 + 3)


class Gather:
    def __init__(self, count, mine, held, base, width, four, sems):
        self.count, self.mine, self.held, self.four = count, mine, held, four
        self.far, self.near, self.core, self.chip, self.onward, self.local = sems
        self.seq, self.at, self.sibling, self.beside = places()
        self.base, self.share = base, width // (4 if four else 2)
        self.evens = range(0, count, 2)

    def lanes(self, seq):
        place = seq if self.four else lax.rem(seq, 2)
        return pl.ds(pl.multiple_of(self.base + place * self.share, 128), self.share)

    def part(self, k, seq):
        return self.held.at[self.at ^ k, :, self.lanes(seq)]

    def source(self, k):
        if k:
            return self.part(k, self.seq)
        return self.mine.at[:, self.lanes(self.seq)]

    def own(self):
        return pltpu.make_async_copy(self.source(0), self.part(0, self.seq), self.local)

    def over(self, sems, k, **device):
        return push(self.source(k), self.part(k, self.seq), sems[0].at[k], sems[1].at[k], **device)

    def come(self, sems, k, owner):
        here = self.part(owner, self.seq)
        return push(here, here, sems[0].at[k], sems[1].at[k], seq=self.sibling)

    def far_out(self, k):
        return push(
            self.source(0), self.part(0, self.seq), self.far[0].at[k], self.far[1].at[k],
            fsdp=self.at ^ k,
        )

    def far_in(self, k):
        return self.come(self.far, k, k)

    def near_out(self, k):
        return self.over(self.near, k, fsdp=self.at ^ 1)

    def near_in(self, k):
        return self.come(self.near, k, k ^ 1)

    def start(self):
        self.own().start()
        for k in self.evens[1:]:
            self.far_out(k).start()
        self.near_out(0).start()

    def second(self):
        for k in self.evens[1:]:
            self.far_in(k).wait_recv()
            self.near_out(k).start()

    def hop(self, sems, source, target):
        here = self.held.at[:, :, self.lanes(source)]
        return push(here, here, sems[0].at[0], sems[1].at[0], seq=target)

    def third(self):
        self.own().wait()
        for k in self.evens:
            self.near_in(k).wait_recv()
        self.hop(self.core, self.seq, self.sibling).start()
        if self.four:
            self.hop(self.chip, self.seq, self.beside).start()

    def fourth(self):
        self.hop(self.chip, self.beside, self.beside).wait_recv()
        self.hop(self.onward, self.beside, self.sibling).start()

    def finish(self):
        self.hop(self.core, self.sibling, self.sibling).wait_recv()
        self.hop(self.core, self.seq, self.sibling).wait_send()
        if self.four:
            self.hop(self.onward, lax.rem(self.sibling + 2, 4), self.sibling).wait_recv()
            self.hop(self.chip, self.seq, self.beside).wait_send()
            self.hop(self.onward, self.beside, self.sibling).wait_send()

    def core_out(self, k):
        return self.over(self.core, k, seq=self.sibling)

    def core_in(self, k):
        here = self.part(k, self.sibling)
        return push(here, here, self.core[0].at[k], self.core[1].at[k], seq=self.sibling)

    def at_once(self, between):
        self.start()
        self.core_out(0).start()
        for k in self.evens[1:]:
            self.far_in(k).wait_recv()
            self.near_out(k).start()
            self.core_out(k).start()
        between()
        for k in self.evens:
            self.near_in(k).wait_recv()
            self.core_out(k ^ 1).start()
        self.own().wait()
        for k in range(self.count):
            self.core_in(k).wait_recv()

    def drain(self, each=False):
        for k in self.evens:
            self.near_out(k).wait_send()
            if k:
                self.far_out(k).wait_send()
        if each:
            for k in range(self.count):
                self.core_out(k).wait_send()


def gather_sems(count, each):
    n = count if each else 1
    pair = lambda size: [pltpu.SemaphoreType.DMA((size,)), pltpu.SemaphoreType.DMA((size,))]
    return pair(count) + pair(count) + pair(n) + pair(1) + pair(1) + [pltpu.SemaphoreType.DMA]


def bundle(refs):
    return [(refs[2 * n], refs[2 * n + 1]) for n in range(5)] + [refs[10]]


class States:
    def __init__(self, big, small, sems):
        self.refs, self.sems = (big, small), sems
        self.seq, _, self.sibling, self.beside = places()

    def hop(self, n, source, target):
        out = []
        for m, ref in enumerate(self.refs):
            here = ref.at[source]
            out.append(push(here, here, self.sems[0].at[n, m], self.sems[1].at[n, m], seq=target))
        return out

    def start(self):
        for copy in self.hop(0, self.seq, self.sibling) + self.hop(1, self.seq, self.beside):
            copy.start()

    def forward(self):
        for copy in self.hop(1, self.beside, self.beside):
            copy.wait_recv()
        for copy in self.hop(2, self.beside, self.sibling):
            copy.start()

    def finish(self):
        for copy in self.hop(0, self.sibling, self.sibling):
            copy.wait_recv()
        for copy in self.hop(2, lax.rem(self.sibling + 2, 4), self.sibling):
            copy.wait_recv()

    def drain(self):
        for copy in (
            self.hop(0, self.seq, self.sibling)
            + self.hop(1, self.seq, self.beside)
            + self.hop(2, self.beside, self.sibling)
        ):
            copy.wait_send()


def doc_parts(doc_ref, col_ref, edge_ref):
    here = lax.broadcasted_iota(jnp.int32, (C, C), 0)
    there = lax.broadcasted_iota(jnp.int32, (C, C), 1)
    eye = jnp.where(here == there, 1.0, 0.0).astype(BF16)
    for n in range(doc_ref.shape[1] // C):
        row = doc_ref[:, n * C : (n + 1) * C].astype(F32)
        col_ref[n * C : (n + 1) * C] = dot_nt(eye, jnp.broadcast_to(row, (128, C)).astype(BF16))
        low = jnp.min(row, axis=1, keepdims=True)
        high = jnp.max(row, axis=1, keepdims=True)
        edge_ref[n : n + 1] = jnp.broadcast_to(low, (1, D))
        edge_ref[n + 8 : n + 9] = jnp.broadcast_to(high, (1, D))


def spread_small(vec_refs, bias_ref, out_ref):
    def repeat(values):
        width = values.shape[1]
        rows = lax.broadcasted_iota(jnp.int32, (width, 128), 0)
        lanes = lax.broadcasted_iota(jnp.int32, (width, 128), 1)
        pick = jnp.where(lax.rem(lanes, width) == rows, 1.0, 0.0).astype(BF16)
        return dot(jnp.broadcast_to(values, (8, width)).astype(BF16), pick)[0:1]

    out_ref[...] = jnp.zeros_like(out_ref)
    for n, ref in enumerate(vec_refs):
        out_ref[n : n + 1] = repeat(ref[...])
    for b in range(max(bias_ref.shape[1] // 128, 1)):
        out_ref[5 + b : 6 + b] = repeat(bias_ref[:, b * 128 : (b + 1) * 128])


def join_small(count, part, gathered, vec_ref, bias_ref):
    lanes = lax.broadcasted_iota(jnp.int32, (8, D), 1)
    total = jnp.zeros((8, D), F32)
    for f in range(count):
        total = jnp.where(lanes // part == f, wide(gathered[f], 4), total)
    vec_ref[...] = total
    size = 4 * part
    for r in range(4):
        at = lanes[0:1] + r * D
        row = jnp.zeros((1, D), F32)
        for f in range(r * D // size, -(-(r + 1) * D // size)):
            for b in range(max(size // 128, 1)):
                use = (at // size == f) & (lax.rem(at, size) // 128 == b)
                row = jnp.where(use, wide(gathered[f, 5 + b : 6 + b], 4), row)
        bias_ref[0:1, r * D : (r + 1) * D] = row


ROOT = 0.7978845608028654
CUBE = 0.044715


def gelu_both(u):
    square = u * u
    bent = jnp.tanh(ROOT * u * (1.0 + CUBE * square))
    half = 0.5 * (1.0 + bent)
    slope = half + 0.5 * u * (1.0 - bent * bent) * (ROOT * (1.0 + 3.0 * CUBE * square))
    return u * half, slope


def feed_start(values, attended, vec_ref, w_out):
    middle = values.astype(F32) + dot(attended, w_out())
    unit, _ = norm_parts(middle)
    return middle, (unit * vec_ref[2:3] + vec_ref[3:4]).astype(BF16)


def feed_body(
    middle, hidden, attended, cot, vec_ref, bias_ref, w_out, w_hidden, w_return,
    y_ref, dy_ref, do_ref, gsmall_ref, gwo_ref, gwh_ref, gwr_ref,
):
    out = middle + vec_ref[4:5]
    grad_hidden = jnp.zeros_like(middle)
    cot32 = cot.astype(F32)
    tiles = FF // FEED_LANES

    def into(j):
        cols = slice(j * FEED_LANES, (j + 1) * FEED_LANES)
        inner = dot(hidden, w_hidden(j)) + bias_ref[0:1, cols]
        return inner, dot_nt(cot, w_return(j))

    def bend(inner, grad):
        gated, slope = gelu_both(inner)
        return gated.astype(BF16), (grad * slope).astype(BF16)

    def outof(j, active, low):
        cols = slice(j * FEED_LANES, (j + 1) * FEED_LANES)
        there = slice(cols.start % D, cols.start % D + FEED_LANES)
        row = 8 + cols.start // D
        gwr_ref[:, cols] += dot_tn(cot, active)
        gsmall_ref[row : row + 1, there] += jnp.sum(low.astype(F32), axis=0, keepdims=True)
        gwh_ref[:, cols] += dot_tn(hidden, low)
        return dot(active, w_return(j)), dot_nt(low, w_hidden(j))

    coming = into(0)
    for j in range(tiles):
        bent = bend(*coming)
        if j + 1 < tiles:
            coming = into(j + 1)
        to_out, to_hidden = outof(j, *bent)
        out = out + to_out
        grad_hidden = grad_hidden + to_hidden
        if j == tiles // 2:
            unit, scale = norm_parts(middle)
    y_ref[...] = out.astype(BF16)
    gsmall_ref[2:3] += jnp.sum(grad_hidden * unit, axis=0, keepdims=True)
    gsmall_ref[3:4] += jnp.sum(grad_hidden, axis=0, keepdims=True)
    gsmall_ref[4:5] += jnp.sum(cot32, axis=0, keepdims=True)
    grad_middle = cot32 + norm_back(unit, scale, vec_ref[2:3], grad_hidden)
    dy_ref[...] = grad_middle
    branch = grad_middle.astype(BF16)
    gwo_ref[...] += dot_tn(attended, branch)
    do_ref[...] = dot_nt(branch, w_out()).astype(BF16)


def pack_grads(count, part, gwo_ref, gwh_ref, gwr_ref, put, done=lambda first, slabs: None):
    half = count // 2
    for q in range(4):
        x, c = q // 2, q % 2
        hidden_part = gwh_ref[:, q * 512 : (q + 1) * 512].reshape(half, 2, part, 512)
        out_part = gwo_ref[:, q * 128 : (q + 1) * 128].reshape(half, 2, part, 128)
        turned = gwr_ref[q * 128 : (q + 1) * 128].T.reshape(half, 2, 4, part, 128)
        for y in range(2):
            over_x, over_y = ((c * 2 + x) * 2 + y) * half, ((c * 2 + y) * 2 + x) * half
            put(0, over_x, slice(0, 512), hidden_part[:, y])
            put(1, over_y, slice(512, 640), out_part[:, y])
            for j in range(4):
                put(1, over_y, slice(j * 128, (j + 1) * 128), turned[:, y, j])
            done((over_x, over_y), half)


def feed_kernel(
    x_ref, o_ref, g_ref, small_ref, bias_ref, wo_ref, wh_ref, wr_ref,
    y_ref, dy_ref, do_ref, pack_ref, pack_r_ref, gsmall_ref, gwo_ref, gwh_ref, gwr_ref,
):
    step = pl.program_id(0)
    count, part = wh_ref.shape[0], wh_ref.shape[1]

    @pl.when(step == 0)
    def _():
        for ref in (gwo_ref, gwh_ref, gwr_ref, gsmall_ref):
            ref[...] = jnp.zeros_like(ref)

    views = weight_views(wo_ref, wh_ref, wr_ref)
    feed_body(
        *feed_start(x_ref[...], o_ref[...], small_ref, views[0]), o_ref[...], g_ref[...], small_ref,
        bias_ref, *views, y_ref, dy_ref, do_ref, gsmall_ref, gwo_ref, gwh_ref, gwr_ref,
    )

    @pl.when(step == pl.num_programs(0) - 1)
    def _():
        def put(which, slab, lanes, values):
            ref = (pack_ref, pack_r_ref)[which]
            n = values.shape[0] * part
            ref[slab * part : slab * part + n, lanes] = values.reshape(n, -1).astype(ref.dtype)

        pack_grads(count, part, gwo_ref, gwh_ref, gwr_ref, put)


def weight_views(wo_ref, wh_ref, wr_ref):
    def w_out():
        return wo_ref[...].reshape(D, D).astype(BF16)

    def w_hidden(j):
        cols = slice(j * FEED_LANES, (j + 1) * FEED_LANES)
        return wh_ref[:, :, cols].reshape(D, FEED_LANES).astype(BF16)

    def w_return(j):
        n = FEED_LANES // wr_ref.shape[1]
        return wr_ref[j * n : (j + 1) * n].reshape(FEED_LANES, D).astype(BF16)

    return w_out, w_hidden, w_return


def front_kernel(count, joined, names, *refs):
    r = types.SimpleNamespace(**dict(zip(names, refs)))
    sems = refs[len(names) :]
    x_ref, doc_ref, vec_out, bias_out = r.x, r.doc, r.vec, r.bias
    qkvf, hidden, w_all, mine = r.qkvf, r.hidden, r.w_all, r.mine
    mine_o, mine_h, mine_r, spread, smalls = r.mine_o, r.mine_h, r.mine_r, r.spread, r.smalls
    col_ref, edge_ref, state, tail = r.col, r.edge, r.state, r.tail
    tails, tail_rows = r.tails, r.tail_rows
    slots = r.o if joined else r.slots
    step = pl.program_id(0)
    seq, at, _, _ = places()
    link = mine.dtype
    groups_of_sems = []
    for _ in range(5):
        groups_of_sems.append(bundle(sems[:11]))
        sems = sems[11:]
    small_send, small_recv, state_send, state_recv, out_sem, stage_sem, fed_sem, pack_sem = sems
    main = Gather(count, mine, w_all, D, 3 * D, False, groups_of_sems[0])
    q_piece = Gather(count, mine, w_all, 0, D, False, groups_of_sems[1])
    o_piece = Gather(count, mine_o, r.wo_all, 0, D, True, groups_of_sems[2])
    h_piece = Gather(count, mine_h, r.wh_all, 0, FF, True, groups_of_sems[3])
    r_piece = Gather(count, mine_r, r.wr_all, 0, D, False, groups_of_sems[4])
    later = (q_piece, o_piece, h_piece, r_piece)
    states = States(tails, tail_rows, (state_send, state_recv))

    def small_copy(k, owner):
        return push(
            spread, smalls.at[owner], small_send.at[k], small_recv.at[k], fsdp=at ^ k
        )

    def save():
        return (
            pltpu.make_async_copy(qkvf, r.qkvf_out, out_sem.at[0]),
            pltpu.make_async_copy(w_all, r.w_out, out_sem.at[1]),
        )

    @pl.when(step == 0)
    def _():
        greet(count)
        for n, ref in enumerate((r.w0, r.w1, r.w2, r.w3)):
            mine[:, n * D : (n + 1) * D] = ref[...].astype(BF16).astype(link)
        spread_small((r.v0, r.v1, r.v2, r.v3, r.v4), r.bias_in, spread)
        doc_parts(doc_ref, col_ref, edge_ref)
        tail[...] = jnp.zeros_like(tail)
        met(count)
        for k in range(1, count):
            small_copy(k, at).start()

        def between():
            mine_o[...] = r.w4[...].astype(BF16).astype(link)
            mine_h[...] = r.w5[...].astype(BF16).astype(link)
            mine_r[...] = r.w6[...].astype(BF16).astype(link)
            smalls[at] = spread[...]
            for k in range(1, count):
                small_copy(k, at ^ k).wait_recv()
            join_small(count, r.v0.shape[1], smalls, vec_out, bias_out)
            q_piece.start()
            o_piece.start()

            @pl.loop(0, 8)
            def _(n):
                here = pl.ds(pl.multiple_of(n * C, C), C)
                unit, _ = norm_parts(x_ref[here].astype(F32))
                hidden[here] = (unit * vec_out[0:1] + vec_out[1:2]).astype(BF16)
                r.seen[n] = visible(col_ref[here], doc_ref[:, here].astype(F32))

            if joined:
                for ref in (r.gwo, r.gwh, r.gwr, r.gsmall):
                    ref[...] = jnp.zeros_like(ref)

        main.at_once(between)
        q_piece.second()
        h_piece.start()

    @pl.when(step < FRONT)
    def _():
        size = 8 // FRONT * C
        here = pl.ds(pl.multiple_of(step * size, size), size)
        weights = w_all[:, :, D:].reshape(D, 3 * D).astype(BF16)
        rows = dot(hidden[here], weights).astype(BF16)
        qkvf[here, D:] = rows
        slots = wide(flag(col_ref[here], edge_ref[15:16]), 4) * jnp.exp(rows[:, 2 * D :].astype(F32))
        slots = slots.astype(BF16)
        keys, values = state_terms(slots, rows[:, 0:D], rows[:, D : 2 * D])
        tail[0:64] += keys
        tail[64:128] += values
        tail[128:129] += jnp.sum(slots.astype(F32), axis=0, keepdims=True)

    @pl.when(step == 1)
    def _():
        o_piece.second()
        r_piece.start()

    @pl.when(step == FRONT - 2)
    def _():
        q_piece.third()

    @pl.when(step == FRONT - 1)
    def _():
        tails[seq] = tail[0:128].astype(link)
        tail_rows[seq, 0:1] = tail[128:129]
        tail_rows[seq, 1:2] = edge_ref[15:16]
        tail_rows[seq, 2:8] = jnp.zeros((6, D), F32)
        states.start()

        @pl.loop(0, 8)
        def _(n):
            here = pl.ds(pl.multiple_of(n * C, C), C)
            slots[here] = jnp.exp(qkvf[here, 3 * D :].astype(F32)).astype(BF16)

        q_piece.finish()
        h_piece.second()

        @pl.loop(0, FRONT)
        def _(n):
            size = 8 // FRONT * C
            here = pl.ds(pl.multiple_of(n * size, size), size)
            weights = w_all[:, :, 0:D].reshape(D, D).astype(BF16)
            qkvf[here, 0:D] = dot(hidden[here], weights).astype(BF16)

        for copy in save():
            copy.start()
        o_piece.third()

        @pl.loop(0, 8)
        def _(n):
            rows = qkvf.at[pl.ds(pl.multiple_of(n * C, C), C)]
            r.affine[n] = affinities(rows, 0, r.seen[n])

        states.forward()
        states.finish()
        first = edge_ref[0:1]
        state[...] = jnp.zeros_like(state)
        for n in range(4):
            use = jnp.where(tail_rows[n, 1:2] == first, 1.0, 0.0) * (n < seq).astype(F32)
            state[0:128] += use * tails[n].astype(F32)
            state[128:129] += use * tail_rows[n, 0:1]
        h_piece.third()

    per = 8 // FRONT

    def kept_copies(n):
        here = pl.ds(pl.multiple_of(n * C, C), C)
        slot = lax.rem(n, 2)
        return [
            pltpu.make_async_copy(r.stage.at[slot, k], out.at[here], stage_sem.at[slot, k])
            for k, out in enumerate((r.p, r.s, r.z))
        ]

    @pl.when((step >= FRONT) & (step < 2 * FRONT))
    def _():
        @pl.loop(0, per, unroll=True)
        def _(u):
            n = (step - FRONT) * per + u
            slot = lax.rem(n, 2)

            @pl.when(n >= 2)
            def _():
                for copy in kept_copies(n - 2):
                    copy.wait()

            here = pl.ds(pl.multiple_of(n * C, C), C)
            block = pl.ds(pl.multiple_of(u * C, C), C)
            attend_body(
                n, qkvf.at[here], slots[here], r.seen[n], r.affine.at[n], col_ref[here], edge_ref, state,
                r.o.at[here if joined else block], *(r.stage.at[slot, k] for k in range(3)),
                r.kept.at[pl.ds(u, 1)],
            )
            for copy in kept_copies(n):
                copy.start()

            @pl.when(n == 0)
            def _():
                o_piece.fourth()

            @pl.when(n == per - 1)
            def _():
                r_piece.second()

            @pl.when(n == 6)
            def _():
                h_piece.fourth()

    @pl.when(step == 2 * FRONT - 1)
    def _():
        r_piece.third()
        o_piece.finish()
        for copy in save():
            copy.wait()

    def complete():
        h_piece.finish()
        r_piece.finish()
        for piece in later:
            piece.drain()
        main.drain(True)
        states.drain()
        for k in range(1, count):
            small_copy(k, at).wait_send()
        for n in (6, 7):
            for copy in kept_copies(n):
                copy.wait()

    if not joined:
        pl.when(step == 2 * FRONT - 1)(complete)
        return

    views = weight_views(r.wo_all, r.wh_all, r.wr_all)

    @pl.when(step == 2 * FRONT - 1)
    def _():
        @pl.loop(0, x_ref.shape[0] // FEED_ROWS)
        def _(n):
            here = pl.ds(pl.multiple_of(n * FEED_ROWS, FEED_ROWS), FEED_ROWS)
            r.middle[here], hidden[here] = feed_start(x_ref[here], r.o[here], vec_out, views[0])

        complete()

    fed = step - 2 * FRONT

    def fed_copies(n):
        here = pl.ds(pl.multiple_of(n * FEED_ROWS, FEED_ROWS), FEED_ROWS)
        slot = lax.rem(n, 2)
        pairs = ((r.held_y, r.y), (r.held_dy, r.dy), (r.held_do, r.do))
        return [
            pltpu.make_async_copy(held.at[slot], out.at[here], fed_sem.at[slot, k])
            for k, (held, out) in enumerate(pairs)
        ]

    @pl.when(fed >= 2)
    def _():
        for copy in fed_copies(fed - 2):
            copy.wait()

    @pl.when(fed >= 0)
    def _():
        here = pl.ds(pl.multiple_of(fed * FEED_ROWS, FEED_ROWS), FEED_ROWS)
        slot = lax.rem(fed, 2)
        feed_body(
            r.middle[here], hidden[here], r.o[here], r.g[...], vec_out, bias_out, *views,
            r.held_y.at[slot], r.held_dy.at[slot], r.held_do.at[slot], r.gsmall, r.gwo, r.gwh, r.gwr,
        )
        for copy in fed_copies(fed):
            copy.start()

    @pl.when(step == pl.num_programs(0) - 1)
    def _():
        part = mine.shape[0]

        def put(which, slab, lanes, values):
            n = values.shape[0] * part
            at_lane = D * which + lanes.start
            qkvf[slab * part : slab * part + n, at_lane : at_lane + values.shape[2]] = (
                values.reshape(n, -1).astype(BF16)
            )

        copies = []

        def done(first, slabs):
            for slab, lanes, out in zip(first, (slice(0, D), slice(D, 1152)), (r.pack, r.pack_r)):
                here = pl.ds(slab * part, slabs * part)
                copies.append(
                    pltpu.make_async_copy(qkvf.at[here, lanes], out.at[here], pack_sem.at[len(copies)])
                )
                copies[-1].start()

        pack_grads(count, part, r.gwo, r.gwh, r.gwr, put, done)
        last = x_ref.shape[0] // FEED_ROWS - 1
        for copy in (*fed_copies(last - 1), *fed_copies(last), *copies):
            copy.wait()


def front(count, tokens, doc_ids, weights, vectors, bias, cotangent):
    rows = tokens.shape[0]
    part = weights[0].shape[0]
    link = BF16 if part % 16 == 0 else F32
    joined = link == BF16
    per = 8 // FRONT
    once = lambda a: pl.BlockSpec(a.shape, lambda i: (0,) * a.ndim)
    late = lambda i: jnp.clip(i - FRONT, 0, FRONT - 1)
    tall = pl.BlockSpec((per * C, D), lambda i: (late(i), 0))
    fed = pl.BlockSpec((FEED_ROWS, D), lambda i: (jnp.maximum(i - 2 * FRONT, 0), 0))
    anywhere = pl.BlockSpec(memory_space=pl.ANY)
    vmem, dma = pltpu.VMEM, pltpu.SemaphoreType.DMA
    ins = {"x": (tokens, once(tokens)), "doc": (doc_ids, once(doc_ids))}
    ins |= {f"w{n}": (a, once(a)) for n, a in enumerate(weights)}
    ins |= {f"v{n}": (a, once(a)) for n, a in enumerate(vectors)}
    ins["bias_in"] = (bias, once(bias))
    wide_rows, slabs = shape_of((rows, D), F32), 4 * count
    outs = {
        "qkvf_out": (shape_of((rows, 4 * D), BF16), anywhere),
        "p": (wide_rows, anywhere),
        "s": (wide_rows, anywhere),
        "z": (wide_rows, anywhere),
        "kept": (
            shape_of((8, 128, D), F32), pl.BlockSpec((per, 128, D), lambda i: (late(i), 0, 0)),
        ),
        "w_out": (shape_of((count, part, 4 * D), link), anywhere),
        "vec": (shape_of((8, D), F32), whole(8, D)),
    }
    scratch = {
        "qkvf": vmem((rows, 4 * D), BF16),
        "hidden": vmem((rows, D), BF16),
        "w_all": vmem((count, part, 4 * D), link),
        "mine": vmem((part, 4 * D), link),
        "mine_o": vmem((part, D), link),
        "mine_h": vmem((part, FF), link),
        "mine_r": vmem((4 * part, D), link),
        "spread": vmem((8, 128), F32),
        "smalls": vmem((count, 8, 128), F32),
        "col": vmem((rows, 128), F32),
        "edge": vmem((16, D), F32),
        "state": vmem((136, D), F32),
        "tail": vmem((136, D), F32),
        "tails": vmem((4, 128, D), link),
        "tail_rows": vmem((4, 8, D), F32),
        "stage": vmem((2, 3, C, D), F32),
        "seen": vmem((8, C, C), BF16),
        "affine": vmem((8, 4 * C, C), BF16),
    }
    gathered = {
        "wo_all": (count, part, D), "wh_all": (count, part, FF), "wr_all": (count, 4 * part, D),
    }
    if joined:
        ins["g"] = (cotangent, fed)
        outs |= {
            "y": (shape_of((rows, D), BF16), anywhere),
            "dy": (wide_rows, anywhere),
            "do": (shape_of((rows, D), BF16), anywhere),
            "pack": (shape_of((slabs * part, D), BF16), anywhere),
            "pack_r": (shape_of((slabs * part, 640), BF16), anywhere),
            "gsmall": (shape_of((16, D), F32), whole(16, D)),
        }
        scratch |= {name: vmem(shape, link) for name, shape in gathered.items()}
        scratch |= {
            "held_y": vmem((2, FEED_ROWS, D), BF16), "held_dy": vmem((2, FEED_ROWS, D), F32),
            "held_do": vmem((2, FEED_ROWS, D), BF16),
            "middle": vmem((rows, D), F32),
            "o": vmem((rows, D), BF16), "bias": vmem((1, FF), F32), "gwo": vmem((D, D), F32),
            "gwh": vmem((D, FF), F32), "gwr": vmem((D, FF), F32),
        }
    else:
        outs |= {name: (shape_of(shape, link), anywhere) for name, shape in gathered.items()}
        outs |= {
            "o": (shape_of((rows, D), BF16), tall), "bias": (shape_of((1, FF), F32), whole(1, FF)),
        }
        scratch["slots"] = vmem((rows, D), BF16)
    found = pl.pallas_call(
        functools.partial(front_kernel, count, joined, (*ins, *outs, *scratch)),
        grid=(2 * FRONT + (rows // FEED_ROWS if joined else 0),),
        in_specs=[spec for _, spec in ins.values()],
        out_specs=[spec for _, spec in outs.values()],
        out_shape=[shape for shape, _ in outs.values()],
        scratch_shapes=list(scratch.values())
        + gather_sems(count, True)
        + gather_sems(count, False) * 4
        + [dma((count,)), dma((count,)), dma((3, 2)), dma((3, 2)), dma((2,)), dma((2, 3)), dma((2, 3))]
        + [dma((16,))],
        compiler_params=pltpu.CompilerParams(
            vmem_limit_bytes=62 * MIB, collective_id=1, has_side_effects=True
        ),
        name="front",
    )(*(a for a, _ in ins.values()))
    found = dict(zip(outs, found))
    if not joined:
        found |= feed(count, part, tokens, found, cotangent, link)
    return found


def feed(count, part, tokens, found, cotangent, link):
    rows, slabs = tokens.shape[0], 4 * count
    tall = pl.BlockSpec((256, D), lambda i: (i, 0))
    weights = [found[name] for name in ("wo_all", "wh_all", "wr_all")]
    names = ("y", "dy", "do", "pack", "pack_r", "gsmall")
    return dict(
        zip(
            names,
            pl.pallas_call(
                feed_kernel,
                grid=(rows // 256,),
                in_specs=[tall] * 3
                + [whole(8, D), whole(1, FF)]
                + [whole(*a.shape) for a in weights],
                out_specs=[tall] * 3
                + [whole(slabs * part, D), whole(slabs * part, 640), whole(16, D)],
                out_shape=[
                    shape_of((rows, D), BF16),
                    shape_of((rows, D), F32),
                    shape_of((rows, D), BF16),
                    shape_of((slabs * part, D), link),
                    shape_of((slabs * part, 640), link),
                    shape_of((16, D), F32),
                ],
                scratch_shapes=[
                    pltpu.VMEM((D, D), F32), pltpu.VMEM((D, FF), F32), pltpu.VMEM((D, FF), F32),
                ],
                compiler_params=PARAMS,
                name="feed",
            )(tokens, found["o"], cotangent, found["vec"], found["bias"], *weights),
        )
    )


def row_body(
    n, qkvf_ref, do_ref, p_ref, s_ref, z_ref, kept_ref, col, row, edge_ref,
    r_ref, dn_ref, dz_ref, head_ref, aside,
):
    first = edge_ref[pl.ds(0, 1)]
    before = edge_ref[pl.ds(8 + jnp.maximum(n - 1, 0), 1)]
    last = jnp.where(n == 0, first, before)
    vis = visible(col, row)
    carried = wide(flag(col, last), 2)
    slots = jnp.exp(qkvf_ref[:, 3 * D :].astype(F32)).astype(BF16)
    own = wide(flag(col, first), 2)
    states = [expand(kept_ref[0, 64:128, lanes_of(g)]).astype(BF16) for g in range(2)]

    def mixing(g):
        return masked(dot_nt(stacked(do_ref[:, lanes_of(g)]), part_of(qkvf_ref, 2, g)), vis)

    def to_reading(g, back_mix):
        lanes = lanes_of(g)
        back = select(dot(back_mix, slots[:, lanes]))
        return back + carried * dot_nt(do_ref[:, lanes], states[g])

    def to_scores(g, back_reading):
        lanes = lanes_of(g)
        probs, score, inverse = p_ref[:, lanes], s_ref[:, lanes], z_ref[:, lanes]
        shared = back_reading * inverse * probs
        back_score = shared - probs * head_sums(shared)
        back_numer = back_score * inverse * SCALE
        back_total = -(shared + back_score * score) * inverse
        reading = (probs * inverse).astype(BF16)
        r_ref[:, lanes] = reading
        dn_ref[:, lanes] = back_numer
        dz_ref[:, lanes] = back_total
        return back_numer, back_total, reading

    def to_state(g, back_numer, back_total, reading):
        lanes = lanes_of(g)
        head_ref[0:64, lanes] += compacted(
            dot_tn((own * back_numer).astype(BF16), part_of(qkvf_ref, 0, g))
        )
        head_ref[64:128, lanes] += compacted(
            dot_tn((own * reading.astype(F32)).astype(BF16), do_ref[:, lanes])
        )
        head_ref[128:129, lanes] += jnp.sum(own * back_total, axis=0, keepdims=True)

    back_mix = mixing(0)
    back_mix_two = mixing(1)
    aside()
    back_reading = to_reading(0, back_mix)
    back_reading_two = to_reading(1, back_mix_two)
    parts = to_scores(0, back_reading)
    to_state(0, *parts)
    parts = to_scores(1, back_reading_two)
    to_state(1, *parts)


def query_body(n, qkvf_ref, kept_ref, col, row, edge_ref, dn_ref, dq_ref):
    first = edge_ref[pl.ds(0, 1)]
    before = edge_ref[pl.ds(8 + jnp.maximum(n - 1, 0), 1)]
    last = jnp.where(n == 0, first, before)
    vis = visible(col, row)
    carried = wide(flag(col, last), 2)
    slots = jnp.exp(qkvf_ref[:, 3 * D :].astype(F32)).astype(BF16)
    lows = [dn_ref[:, lanes_of(g)].astype(BF16) for g in range(2)]
    states = [expand(kept_ref[0, 0:64, lanes_of(g)]).astype(BF16) for g in range(2)]

    def affine(g):
        return masked(dot_nt(stacked(lows[g]), slots[:, lanes_of(g)]), vis)

    def to_queries(g, back_affinity):
        out = select(dot(back_affinity, part_of(qkvf_ref, 1, g))) + carried * dot(lows[g], states[g])
        dq_ref[:, lanes_of(g)] = out.astype(BF16)

    one, two = affine(0), affine(1)
    to_queries(0, one)
    to_queries(1, two)


def column_body(
    n, qkvf_ref, do_ref, r_ref, dn_ref, dz_ref, col, row, edge_ref, state, snap, snap_rows, d_ref
):
    newest = edge_ref[15:16]
    after = edge_ref[pl.ds(jnp.minimum(n + 1, 7), 1)]
    following = jnp.where(n == 7, newest, after)
    first = edge_ref[pl.ds(n, 1)]
    vis = visible_back(col, row)
    carried = wide(flag(col, following), 2)
    own = wide(flag(col, first), 2)
    kept = jnp.where(following == first, 1.0, 0.0)[:, :GROUP]
    snap[n] = state[0:128].astype(BF16)
    snap_rows[pl.ds(n, 1)] = state[128:129]
    key_states = [expand(state[0:64, lanes_of(g)]).astype(BF16) for g in range(2)]
    value_states = [expand(state[64:128, lanes_of(g)]).astype(BF16) for g in range(2)]
    slots = jnp.exp(qkvf_ref[:, 3 * D :].astype(F32)).astype(BF16)
    numers = [dn_ref[:, lanes_of(g)] for g in range(2)]

    def mixing(g, apart):
        return masked(dot_nt(apart, r_ref[:, lanes_of(g)]), vis)

    def affine(g, apart):
        return masked(dot_nt(apart, numers[g].astype(BF16)), vis)

    def to_values(g, mix):
        lanes = lanes_of(g)
        out = select(dot(mix, do_ref[:, lanes])) + carried * dot(slots[:, lanes], value_states[g])
        d_ref[:, 2 * D + g * GROUP : 2 * D + (g + 1) * GROUP] = out.astype(BF16)

    def to_keys(g, back_affinity):
        lanes = lanes_of(g)
        out = select(dot(back_affinity, part_of(qkvf_ref, 0, g)))
        out = out + carried * dot(slots[:, lanes], key_states[g])
        d_ref[:, D + g * GROUP : D + (g + 1) * GROUP] = out.astype(BF16)

    def to_state(g):
        lanes = lanes_of(g)
        state[0:64, lanes] = kept * state[0:64, lanes] + compacted(
            dot_tn((own * numers[g]).astype(BF16), part_of(qkvf_ref, 0, g))
        )
        state[64:128, lanes] = kept * state[64:128, lanes] + compacted(
            dot_tn((own * r_ref[:, lanes].astype(F32)).astype(BF16), do_ref[:, lanes])
        )
        state[128:129, lanes] = kept * state[128:129, lanes] + jnp.sum(
            own * dz_ref[:, lanes], axis=0, keepdims=True
        )

    apart = stacked(slots[:, lanes_of(0)])
    mix = mixing(0, apart)
    back_affinity = affine(0, apart)
    apart = stacked(slots[:, lanes_of(1)])
    mix_two = mixing(1, apart)
    to_values(0, mix)
    affinity_two = affine(1, apart)
    to_keys(0, back_affinity)
    to_state(0)
    to_values(1, mix_two)
    to_keys(1, affinity_two)
    to_state(1)


def slot_body(n, qkvf_ref, do_ref, r_ref, dn_ref, dz_ref, col, row, edge_ref, snap, snap_rows, d_ref):
    newest = edge_ref[15:16]
    after = edge_ref[pl.ds(jnp.minimum(n + 1, 7), 1)]
    following = jnp.where(n == 7, newest, after)
    vis = visible_back(col, row)
    carried = wide(flag(col, following), 2)
    left = lane_heads(C, 128) == 0
    norm_state = snap_rows[pl.ds(n, 1)]
    key_states = [expand(snap[n, 0:64, lanes_of(g)]) for g in range(2)]
    value_states = [expand(snap[n, 64:128, lanes_of(g)]) for g in range(2)]

    def mixing(g):
        return masked(dot_nt(stacked(part_of(qkvf_ref, 2, g)), do_ref[:, lanes_of(g)]), vis)

    def affine(g):
        return masked(dot_nt(stacked(part_of(qkvf_ref, 1, g)), part_of(qkvf_ref, 0, g)), vis)

    def from_mix(g, back_mix):
        return select(dot(back_mix, r_ref[:, lanes_of(g)]))

    def from_affinity(g, affinity):
        high, low = split(dn_ref[:, lanes_of(g)])
        parts = []
        for p in range(2):
            pair = slice(p * 128, (p + 1) * 128)
            both = dot(
                affinity[p * 512 : (p + 1) * 512],
                jnp.concatenate([high[:, pair], low[:, pair]], axis=1),
            )
            both = both[:, :128] + both[:, 128:]
            parts.append(jnp.where(left, both[:C], both[C:]))
        return jnp.concatenate(parts, axis=1)

    def from_totals():
        high, low = split(dz_ref[...])
        return dot(vis, high) + dot(vis, low)

    def from_state(g):
        return carried * (
            dot_nt(part_of(qkvf_ref, 1, g), key_states[g])
            + dot_nt(part_of(qkvf_ref, 2, g), value_states[g])
            + norm_state[:, lanes_of(g)]
        )

    def to_slots(g, back_slots):
        written = jnp.exp(part_of(qkvf_ref, 3, g).astype(F32))
        d_ref[:, 3 * D + g * GROUP : 3 * D + (g + 1) * GROUP] = (back_slots * written).astype(BF16)

    norm = from_totals()
    mix = mixing(0)
    affinity = affine(0)
    mix_two = mixing(1)
    total = from_mix(0, mix)
    affinity_two = affine(1)
    total = total + from_affinity(0, affinity)
    total_two = from_mix(1, mix_two)
    to_slots(0, total + norm[:, lanes_of(0)] + from_state(0))
    total_two = total_two + from_affinity(1, affinity_two)
    to_slots(1, total_two + norm[:, lanes_of(1)] + from_state(1))


class Scatter:
    def __init__(self, count, source, own, axes, direct, out, buffers):
        self.axes, self.direct, self.out = axes, direct, out
        self.seq, self.at, self.sibling, self.beside = places()
        self.source, self.own = source, own
        self.core = lax.rem(self.seq, 2)
        self.total, self.local, self.last, self.done = buffers[:4]
        self.stages = []
        size = source.shape[0]
        base = 0
        for n, axis in enumerate(axes):
            ways = {"core": 2, "x": 2, "y": 2, "z": count // 2, "all": count}[axis]
            size = size // ways
            me = {
                "core": self.core, "x": self.seq // 2, "y": lax.rem(self.at, 2), "z": self.at // 2,
                "all": self.at,
            }[axis]
            held = source
            if own is not None and n > 0:
                held = own
            come, sems = buffers[4 + 2 * n], buffers[5 + 2 * n]
            self.stages.append((axis, ways, size, base, me, held, come, sems))
            if own is None or n > 0:
                base = base + me * size

    def copies(self, n, halves=(0, 1)):
        axis, ways, size, base, me, held, come, sems = self.stages[n]
        if axis == "x":
            for half in halves:
                first, some = half * (size // 2), size // 2
                yield push(
                    held.at[pl.ds(base + (me ^ 1) * size + first, some)],
                    come.at[0, pl.ds(first, some)],
                    sems.at[0, half], sems.at[1, half], seq=self.beside,
                )
            return
        for k in range(1, ways):
            if axis == "core":
                device = {"seq": self.sibling}
            else:
                device = {"fsdp": self.at ^ (2 * k if axis == "z" else k)}
            yield push(
                held.at[pl.ds(base + (me ^ k) * size, size)], come.at[k - 1],
                sems.at[0, k - 1], sems.at[1, k - 1], **device,
            )

    def copy_own(self):
        size = self.source.shape[0] // 2
        return pltpu.make_async_copy(
            self.source.at[pl.ds(self.core * size, size)], self.own, self.local
        )

    def start(self):
        for copy in self.copies(0):
            copy.start()
        if self.own is not None:
            self.copy_own().start()

    def advance(self, n, halves=(0, 1)):
        axis, ways, size, base, me, held, come, sems = self.stages[n]
        for copy in self.copies(n):
            copy.wait_recv()
        mine = held
        first = base + me * size
        if n == 0 and self.own is not None:
            self.copy_own().wait()
            mine, first = self.own, 0

        def added(slab):
            total = mine[first + slab].astype(F32)
            for k in range(1, ways):
                total = total + come[k - 1, slab].astype(F32)
            return total

        if n + 1 == len(self.stages):
            self.total[...] = added(0)
            self.copy_done().start()
            for copy in self.sent():
                copy.start()
            return

        @pl.loop(0, size)
        def _(slab):
            mine[first + slab] = added(slab).astype(mine.dtype)

        for copy in self.copies(n + 1, halves):
            copy.start()

    def copy_done(self):
        return pltpu.make_async_copy(self.total, self.out.at[self.seq], self.done)

    def sent(self):
        other = lax.rem(self.sibling + 2, 4)
        for n, target in enumerate((self.sibling, self.beside, other)[: 3 if self.direct else 2]):
            yield push(
                self.total, self.out.at[self.seq], self.last.at[0, n], self.last.at[1, n], seq=target
            )

    def forwarded(self, source):
        here = self.out.at[source]
        return push(here, here, self.last.at[0, 2], self.last.at[1, 2], seq=self.sibling)

    def come_in(self, n, source):
        here = self.out.at[source]
        return push(here, here, self.last.at[0, n], self.last.at[1, n], seq=source)

    def forward(self):
        self.come_in(1, self.beside).wait_recv()
        self.forwarded(self.beside).start()

    def finish(self):
        other = lax.rem(self.sibling + 2, 4)
        self.come_in(0, self.sibling).wait_recv()
        if self.direct:
            self.come_in(1, self.beside).wait_recv()
        else:
            self.forwarded(self.beside).wait_send()
        self.forwarded(other).wait_recv()
        self.copy_done().wait()
        for copy in self.sent():
            copy.wait_send()
        for n in range(len(self.stages)):
            for copy in self.copies(n):
                copy.wait_send()


def scatter_scratch(count, part, lanes, link, axes, hbm):
    vmem, dma = pltpu.VMEM, pltpu.SemaphoreType.DMA
    size = 2 * 4 * count // 2
    out = [vmem((size // 2, part, lanes), link)] if hbm else []
    out += [vmem((part, lanes), F32), dma, dma((2, 3)), dma]
    for axis in axes:
        ways = {"core": 2, "x": 2, "y": 2, "z": count // 2, "all": count}[axis]
        size = size // ways
        out += [vmem((ways - 1, size, part, lanes), link), dma((2, max(ways - 1, 2)))]
    return out


OVER_X = ("core", "x", "y", "z")
OVER_Y = ("core", "y", "x", "z")
SHORT = ("core", "x", "all")


class SmallSum:
    def __init__(self, count, mine, from_seq, half, from_fsdp, sems):
        self.count, self.mine, self.from_seq = count, mine, from_seq
        self.half, self.from_fsdp, self.sems = half, from_fsdp, sems
        self.seq, self.at, _, _ = places()

    def lanes(self, owner):
        if self.from_fsdp.shape[2] == D:
            return pl.ds(0, D)
        first = owner * (D // self.count) // 128 * 128
        return pl.ds(pl.multiple_of(first, 128), 128)

    def over_seq(self, k, slot):
        return push(
            self.mine, self.from_seq.at[slot], self.sems[0].at[0, k], self.sems[0].at[1, k],
            seq=self.seq ^ k,
        )

    def over_fsdp(self, k):
        return push(
            self.half.at[:, self.lanes(self.at ^ k)], self.from_fsdp.at[self.at],
            self.sems[1].at[0, k], self.sems[1].at[1, k], fsdp=self.at ^ k,
        )

    def fsdp_in(self, k):
        here = self.from_fsdp.at[self.at ^ k]
        return push(here, here, self.sems[1].at[0, k], self.sems[1].at[1, k], fsdp=self.at ^ k)

    def start(self):
        for k in range(1, 4):
            self.over_seq(k, self.seq).start()
        self.from_seq[self.seq] = self.mine[...]

    def second(self):
        for k in range(1, 4):
            self.over_seq(k, self.seq ^ k).wait_recv()
        total = self.from_seq[0]
        for n in range(1, 4):
            total = total + self.from_seq[n]
        self.half[...] = total
        for k in range(1, self.count):
            self.over_fsdp(k).start()
        self.from_fsdp[self.at] = self.half[:, self.lanes(self.at)]

    def finish(self, out_ref):
        for k in range(1, self.count):
            self.fsdp_in(k).wait_recv()
        total = self.from_fsdp[0]
        for n in range(1, self.count):
            total = total + self.from_fsdp[n]
        out_ref[...] = total
        for k in range(1, 4):
            self.over_seq(k, self.seq).wait_send()
        for k in range(1, self.count):
            self.over_fsdp(k).wait_send()


def small_scratch(count, rows, lanes):
    vmem, dma = pltpu.VMEM, pltpu.SemaphoreType.DMA
    return [
        vmem((4, rows, D), F32), vmem((rows, D), F32), vmem((count, rows, lanes), F32),
        dma((2, 4)), dma((2, count)),
    ]


QUERY, COLUMN, SLOT, INPUT = 8, 16, 24, 32


def back_kernel(
    count, per, x_ref, xs_ref, qkvf_ref, do_ref, p_ref, s_ref, z_ref, kept_ref, dy_ref, doc_ref,
    small_ref, w_ref, ffg_ref, ffr_ref, ffs_ref,
    gi_ref, ff_out, fr_out, q_out, kv_out, f_out, s1_out, s2_out,
    gi_held, gi_sem, scores, scores_sem, d_all, h_turned, reading, numer, total, col_ref, edge_ref, head, state, heads, head_rows,
    snap, snap_rows, w_held, w_sem, q_piece, kv_piece, f_piece, last_small, *rest,
):
    step = pl.program_id(0)
    seq, at, _, _ = places()
    link = q_piece.dtype

    def take(size):
        nonlocal rest
        out, rest = rest[:size], rest[size:]
        return out

    (own,) = take(1)
    ff = Scatter(count, ffg_ref, own, OVER_X, False, ff_out, take(12))
    (own,) = take(1)
    fr = Scatter(count, ffr_ref, own, OVER_Y, False, fr_out, take(12))
    for_q = Scatter(count, q_piece, None, OVER_X, False, q_out, take(12))
    for_kv = Scatter(count, kv_piece, None, OVER_X, False, kv_out, take(12))
    for_f = Scatter(count, f_piece, None, SHORT, True, f_out, take(10))
    small_one = SmallSum(count, ffs_ref, *take(3), take(2))
    small_two = SmallSum(count, last_small, *take(3), take(2))
    states = States(heads, head_rows, take(2))

    def chunk(u, first, turned=False):
        n = step * per + u - first
        n = 7 - n if turned else n
        here = pl.ds(pl.multiple_of(n * C, C), C)
        block = pl.ds(pl.multiple_of((per - 1 - u if turned else u) * C, C), C)
        return n, here, block, col_ref[here], doc_ref[:, here].astype(F32)

    def fetch():
        return pltpu.make_async_copy(w_ref, w_held, w_sem)

    def fetch_scores(n):
        slot, here = lax.rem(n, 2), pl.ds(pl.multiple_of(n * per * C, per * C), per * C)
        return [
            pltpu.make_async_copy(ref.at[here], scores.at[slot, k], scores_sem.at[slot, k])
            for k, ref in enumerate((p_ref, s_ref, z_ref))
        ]

    def give(n):
        here = pl.ds(pl.multiple_of(n * per * C, per * C), per * C)
        slot = lax.rem(n, 2)
        return pltpu.make_async_copy(gi_held.at[slot], gi_ref.at[here], gi_sem.at[slot])

    def weight_grad(piece, d_lanes, lanes, short=False):
        grad = dot(h_turned[...], d_all[:, d_lanes])
        half, part = count // 2, piece.shape[1]
        for q in range(4):
            x, c = q // 2, q % 2
            share = grad[:, q * 128 : (q + 1) * 128].reshape(half, 2, part, 128).astype(link)
            if short:
                first = (c * 2 + x) * count
                piece[first : first + count, :, lanes] = share.reshape(count, part, 128)
                continue
            for y in range(2):
                first = ((c * 2 + x) * 2 + y) * half
                piece[first : first + half, :, lanes] = share[:, y]

    @pl.when(step == 0)
    def _():
        greet(count)
        for n in range(2):
            for copy in fetch_scores(n):
                copy.start()
        fetch().start()
        doc_parts(doc_ref, col_ref, edge_ref)
        head[...] = jnp.zeros_like(head)
        last_small[...] = jnp.zeros_like(last_small)

    def turn():
        weight_grad(q_piece, slice(0, D), slice(0, 128))
        for_q.start()
        states.finish()
        newest = edge_ref[15:16]
        state[...] = jnp.zeros_like(state)
        for n in range(4):
            use = jnp.where(head_rows[n, 1:2] == newest, 1.0, 0.0) * (n > seq).astype(F32)
            state[0:128] += use * heads[n].astype(F32)
            state[128:129] += use * head_rows[n, 0:1]

    def send_states():
        heads[seq] = head[0:128].astype(link)
        head_rows[seq, 0:1] = head[128:129]
        head_rows[seq, 1:2] = edge_ref[0:1]
        head_rows[seq, 2:8] = jnp.zeros((6, D), F32)
        states.start()

    def key_value_grads():
        weight_grad(kv_piece, slice(D, 2 * D), slice(0, 128))
        weight_grad(kv_piece, slice(2 * D, 3 * D), slice(128, 256))
        for_kv.start()

    def slot_grads():
        weight_grad(f_piece, slice(3 * D, 4 * D), slice(0, 128), True)
        for_f.start()

    def last():
        small_two.start()
        small_one.finish(s1_out)
        for piece in (ff, for_q):
            piece.forward()
        small_two.second()
        for_f.advance(2)
        for_kv.forward()
        for piece in (ff, fr, for_q):
            piece.finish()
        states.drain()
        small_two.finish(s2_out)
        for_kv.finish()
        for_f.finish()
        for n in (8 // per - 2, 8 // per - 1):
            give(n).wait()

    def rest_of_ff():
        for copy in ff.copies(1, (1,)):
            copy.start()

    def begin():
        met(count)
        ff.start()
        small_one.start()

    schedule = {
        0: [begin],
        1: [fr.start],
        3: [lambda: ff.advance(0, (0,)), small_one.second],
        5: [lambda: fr.advance(0)],
        QUERY - 1: [send_states],
        QUERY + 5: [states.forward, rest_of_ff],
        QUERY + 7: [turn],
        COLUMN + 1: [lambda: fr.advance(1), lambda: for_q.advance(0)],
        COLUMN + 2: [lambda: ff.advance(1)],
        COLUMN + 6: [lambda: fr.advance(2)],
        SLOT: [lambda: ff.advance(2)],
        COLUMN + 7: [key_value_grads, lambda: for_q.advance(1)],
        SLOT + 1: [lambda: for_kv.advance(0), lambda: for_q.advance(2)],
        SLOT + 6: [lambda: for_kv.advance(1), lambda: fr.advance(3)],
        SLOT + 7: [slot_grads],
        INPUT + 1: [lambda: for_f.advance(0), lambda: for_kv.advance(2)],
        INPUT + 3: [lambda: ff.advance(3), lambda: for_q.advance(3), fr.forward],
        INPUT + 5: [lambda: for_f.advance(1), lambda: for_kv.advance(3)],
        INPUT + 7: [last],
    }

    @pl.when(step < QUERY // per)
    def _():
        for copy in fetch_scores(step):
            copy.wait()

    @pl.loop(0, per)
    def _(u):
        at_chunk = step * per + u

        def events(first):
            for when, actions in schedule.items():
                if first <= when < first + 8:

                    @pl.when(at_chunk == when)
                    def _(actions=actions):
                        for action in actions:
                            action()

        @pl.when(at_chunk < QUERY)
        def _():
            n, here, block, col, row = chunk(u, 0)
            kept_scores = [scores.at[lax.rem(step, 2), k, block] for k in range(3)]

            def aside():
                unit, _ = norm_parts(x_ref[block].astype(F32))
                h_turned[:, here] = (unit * small_ref[0:1] + small_ref[1:2]).astype(BF16).T

            row_body(
                n, qkvf_ref.at[block], do_ref.at[block], *kept_scores, kept_ref.at[pl.ds(u, 1)],
                col, row, edge_ref,
                reading.at[here], numer.at[here], total.at[here], head, aside,
            )
            events(0)

        @pl.when((at_chunk >= QUERY) & (at_chunk < COLUMN))
        def _():
            n, here, block, col, row = chunk(u, QUERY)
            query_body(
                n, qkvf_ref.at[block], kept_ref.at[pl.ds(u, 1)], col, row, edge_ref,
                numer.at[here], d_all.at[here, 0:D],
            )
            events(QUERY)

        @pl.when((at_chunk >= COLUMN) & (at_chunk < SLOT))
        def _():
            n, here, block, col, row = chunk(u, COLUMN, True)
            column_body(
                n, qkvf_ref.at[block], do_ref.at[block], reading.at[here], numer.at[here],
                total.at[here], col, row, edge_ref, state, snap, snap_rows, d_all.at[here],
            )
            events(COLUMN)

        @pl.when((at_chunk >= SLOT) & (at_chunk < INPUT))
        def _():
            n, here, block, col, row = chunk(u, SLOT, True)
            slot_body(
                n, qkvf_ref.at[block], do_ref.at[block], reading.at[here], numer.at[here],
                total.at[here], col, row, edge_ref, snap, snap_rows, d_all.at[here],
            )
            events(SLOT)

        @pl.when((at_chunk >= INPUT) & (u == 0))
        def _():
            nth = step - INPUT // per

            @pl.when(nth >= 2)
            def _():
                give(nth - 2).wait()

            @pl.when(nth == 0)
            def _():
                fetch().wait()

            size = xs_ref.shape[0]
            here = pl.ds(pl.multiple_of(nth * size, size), size)
            grad = dot_nt(d_all[here], w_held[...])
            unit, scale = norm_parts(xs_ref[...].astype(F32))
            last_small[0:1] += jnp.sum(grad * unit, axis=0, keepdims=True)
            last_small[1:2] += jnp.sum(grad, axis=0, keepdims=True)
            gi_held[lax.rem(nth, 2)] = dy_ref[...] + norm_back(unit, scale, small_ref[0:1], grad)
            give(nth).start()

        @pl.when(at_chunk >= INPUT)
        def _():
            events(INPUT)

    @pl.when(step + 2 < QUERY // per)
    def _():
        for copy in fetch_scores(step + 2):
            copy.start()


def back(
    count, tokens, qkvf, do, probs, score, inverse, kept, dy, doc_ids, small, w_all, ffg, ffr, ffs
):
    rows = tokens.shape[0]
    part, link = ffg.shape[1], ffg.dtype
    per = 2 if link == BF16 else 1
    size = per * C
    blocks = 8 // per
    once = lambda a: pl.BlockSpec(a.shape, lambda i: (0,) * a.ndim)
    anywhere = pl.BlockSpec(memory_space=pl.ANY)
    vmem, dma = pltpu.VMEM, pltpu.SemaphoreType.DMA

    def early(i):
        return jnp.minimum(i, blocks - 1)

    def twice(i):
        return jnp.where(i < blocks, i, jnp.clip(i - blocks, 0, blocks - 1))

    def turned(i):
        return blocks - 1 - lax.rem(jnp.clip(i - 2 * blocks, 0, 2 * blocks - 1), blocks)

    def always(i):
        return jnp.where(i < 2 * blocks, twice(i), turned(i))

    def both(i):
        return jnp.where(i < blocks, i, turned(i))

    late = lambda i: (jnp.maximum(i - 4 * blocks, 0), 0)
    tall = pl.BlockSpec((size, D), late)
    some = lambda lanes, order: pl.BlockSpec((size, lanes), lambda i: (order(i), 0))
    slabs = 4 * count
    return pl.pallas_call(
        functools.partial(back_kernel, count, per),
        grid=(5 * blocks,),
        in_specs=[some(D, early), tall, some(4 * D, always), some(D, both)]
        + [anywhere] * 3
        + [pl.BlockSpec((per, 128, D), lambda i: (twice(i), 0, 0)), tall]
        + [once(doc_ids), once(small), anywhere, anywhere, anywhere, once(ffs)],
        out_specs=[anywhere] * 6 + [whole(16, D), whole(8, 128)],
        out_shape=[
            shape_of((rows, D), F32),
            shape_of((4, part, D), F32),
            shape_of((4, part, 640), F32),
            shape_of((4, part, 128), F32),
            shape_of((4, part, 256), F32),
            shape_of((4, part, 128), F32),
            shape_of((16, D), F32),
            shape_of((8, 128), F32),
        ],
        scratch_shapes=[
            vmem((2, size, D), F32),
            dma((2,)),
            vmem((2, 3, size, D), F32),
            dma((2, 3)),
            vmem((rows, 4 * D), BF16),
            vmem((D, rows), BF16),
            vmem((rows, D), BF16),
            vmem((rows, D), F32),
            vmem((rows, D), F32),
            vmem((rows, 128), F32),
            vmem((16, D), F32),
            vmem((136, D), F32),
            vmem((136, D), F32),
            vmem((4, 128, D), link),
            vmem((4, 8, D), F32),
            vmem((8, 128, D), BF16),
            vmem((8, D), F32),
            vmem(w_all.shape, BF16),
            dma,
            vmem((slabs, part, 128), link),
            vmem((slabs, part, 256), link),
            vmem((slabs, part, 128), link),
            vmem((8, D), F32),
        ]
        + scatter_scratch(count, part, D, link, OVER_X, True)
        + scatter_scratch(count, part, 640, link, OVER_Y, True)
        + scatter_scratch(count, part, 128, link, OVER_X, False)
        + scatter_scratch(count, part, 256, link, OVER_X, False)
        + scatter_scratch(count, part, 128, link, SHORT, False)
        + small_scratch(count, 16, D)
        + small_scratch(count, 8, 128)
        + [dma((3, 2)), dma((3, 2))],
        compiler_params=pltpu.CompilerParams(
            vmem_limit_bytes=(62 if link == BF16 else 63) * MIB, collective_id=2, has_side_effects=True
        ),
        name="back",
    )(
        tokens, tokens, qkvf, do, probs, score, inverse, kept, dy, doc_ids, small, w_all, ffg, ffr,
        ffs,
    )


def finish_kernel(count, part, *refs):
    at = lax.axis_index("fsdp")
    y_ref, gi_ref, *sums = refs[:7]
    s1_ref, s2_ref, y_out, gi_out, *rest = refs[7:]
    outs, (held_y, held, *rest) = rest[:13], rest[13:]
    ff_ref, fr_ref, q_ref, kv_ref, f_ref = rest[:5]
    staged, sems, sum_sems = rest[5:12], rest[12], rest[13]

    def move(n, out):
        source, through, target, here = gi_ref, held, gi_out, pl.ds(n * 512, 512)
        if n >= 4:
            source, through, target, here = y_ref, held_y, y_out, pl.ds((n - 4) * 1024, 1024)
        if out:
            return pltpu.make_async_copy(through.at[here], target.at[here], sems.at[1, n])
        return pltpu.make_async_copy(source.at[here], through.at[here], sems.at[0, n])

    def bring(n):
        return pltpu.make_async_copy(sums[n], rest[n], sum_sems.at[0, n])

    def give(n):
        return pltpu.make_async_copy(staged[n], outs[n], sum_sems.at[1, n])

    def pick(row, size):
        out = row(0, size)
        for f in range(1, count):
            out = jnp.where(at == f, row(f * size, size), out)
        return out

    def bias(start, size):
        r = start // D
        return s1_ref[8 + r : 9 + r, start - r * D : start - r * D + size]

    def row_of_sums(ref, n):
        return lambda start, size: ref[
            n : n + 1, start % ref.shape[1] : start % ref.shape[1] + size
        ]

    for n in range(5):
        bring(n).start()
    for n in range(6):
        move(n, False).start()
    for n in range(5):
        bring(n).wait()
    for n in range(4):
        lanes = slice(n * 128, (n + 1) * 128)
        staged[0][:, lanes] = q_ref[n]
        staged[1][:, lanes] = kv_ref[n, :, 0:128]
        staged[2][:, lanes] = kv_ref[n, :, 128:256]
        staged[3][:, lanes] = f_ref[n]
        staged[4][:, lanes] = fr_ref[n, :, 512:640]
        staged[5][:, n * 512 : (n + 1) * 512] = ff_ref[n]
        for j in range(4):
            staged[6][j * part : (j + 1) * part, lanes] = fr_ref[n, :, j * 128 : (j + 1) * 128]
    for n in range(7):
        give(n).start()
    for n in range(6):
        move(n, False).wait()
        move(n, True).start()
    outs[7][...] = pick(row_of_sums(s2_ref, 0), part)
    outs[8][...] = pick(row_of_sums(s2_ref, 1), part)
    outs[9][...] = pick(row_of_sums(s1_ref, 2), part)
    outs[10][...] = pick(row_of_sums(s1_ref, 3), part)
    outs[11][...] = pick(bias, 4 * part)
    outs[12][...] = pick(row_of_sums(s1_ref, 4), part)
    for n in range(7):
        give(n).wait()
    for n in range(6):
        move(n, True).wait()


def finish(count, part, out, grad_input, *sums):
    once = lambda shape: pl.BlockSpec(shape, lambda: (0,) * len(shape))
    anywhere = pl.BlockSpec(memory_space=pl.ANY)
    vmem, dma = pltpu.VMEM, pltpu.SemaphoreType.DMA
    large = [(part, D)] * 5 + [(part, FF), (4 * part, D)]
    small = [(1, part)] * 4 + [(1, 4 * part), (1, part)]
    return pl.pallas_call(
        functools.partial(finish_kernel, count, part),
        in_specs=[anywhere] * 7 + [once(a.shape) for a in sums[5:]],
        out_specs=[anywhere] * 9 + [once(s) for s in small],
        out_shape=[shape_of(out.shape, BF16)]
        + [shape_of(s, F32) for s in (grad_input.shape, *large, *small)],
        scratch_shapes=[vmem(out.shape, BF16), vmem(grad_input.shape, F32)]
        + [vmem(a.shape, F32) for a in sums[:5]]
        + [vmem(s, F32) for s in large]
        + [dma((2, 6)), dma((2, 7))],
        compiler_params=PARAMS,
        name="finish",
    )(out, grad_input, *sums)


def rows_of(lanes, order=lambda i: i):
    return pl.BlockSpec((C, lanes), lambda i: (order(i), 0))


def whole(*shape):
    return pl.BlockSpec(shape, lambda i: (0,) * len(shape))


def row_of(order=lambda i: i):
    return pl.BlockSpec((1, C), lambda i: (0, order(i)))


def shape_of(shape, kind):
    return jax.ShapeDtypeStruct(shape, kind)


PARAMS = pltpu.CompilerParams(vmem_limit_bytes=62 * MIB)


def on_device(
    tokens, doc_ids, w_query, w_key, w_value, w_slots, w_output, w_hidden, w_return,
    gain_first, shift_first, gain_second, shift_second, bias_hidden, bias_return, cotangent,
):
    rows = tokens.shape[0]
    count = lax.axis_size("fsdp")
    part = gain_first.shape[0]
    flat = lambda a: a.reshape(1, a.shape[0])
    found = front(
        count, tokens, doc_ids,
        (w_query, w_key, w_value, w_slots, w_output, w_hidden, w_return),
        [flat(a) for a in (gain_first, shift_first, gain_second, shift_second, bias_return)],
        flat(bias_hidden), cotangent,
    )
    grad_input, *sums = back(
        count, tokens, *(found[name] for name in ("qkvf_out", "do", "p", "s", "z", "kept", "dy")),
        doc_ids, found["vec"], found["w_out"].reshape(D, 4 * D).astype(BF16),
        found["pack"].reshape(-1, part, D), found["pack_r"].reshape(-1, part, 640), found["gsmall"],
    )
    out, grad_input, *grads = finish(count, part, found["y"], grad_input, *sums)
    return (out, grad_input, *grads[:7], *(a.reshape(-1) for a in grads[7:]))


def solution(mesh):
    tall, flat, one = P(("fsdp", "seq"), None), P("fsdp", None), P("fsdp")
    return jax.shard_map(
        on_device,
        mesh=mesh,
        in_specs=(tall, P("fsdp", "seq")) + (flat,) * 7 + (one,) * 6 + (tall,),
        out_specs=(tall, tall) + (flat,) * 7 + (one,) * 6,
        check_vma=False,
    )
```
